32 devices in a mesh: fsdp: 8 (over y, x, core), ctx: 4 (over z).
Axes of the slice: x: 2, y: 2, z: 4, core: 2. Of those that a mesh axis runs over, the one named last changes fastest.
Arguments:
- tokens: bfloat16 [4096, 2048], P(('fsdp', 'ctx')), may hold values from -6 to 6
- per_layer: bfloat16 [4096, 256], P(('fsdp', 'ctx')), may hold values from -6 to 6
- segments: int32 [4096], P(('fsdp', 'ctx')), may hold values from 0 to 23, as said below
- positions: int32 [4096], P(('fsdp', 'ctx')), may hold values from 0 to 509, as said below
- cotangent: bfloat16 [4096, 2048], P(('fsdp', 'ctx')), may hold values from -6 to 6
- query_weight: bfloat16 [2048, 2048], P('fsdp'), may hold values from -0.125 to 0.125
- key_matrix: bfloat16 [2048, 512], P('fsdp'), may hold values from -0.125 to 0.125
- value_matrix: bfloat16 [2048, 512], P('fsdp'), may hold values from -0.125 to 0.125
- output_weight: bfloat16 [2048, 2048], P('fsdp'), may hold values from -0.125 to 0.125
- laurel_down: bfloat16 [2048, 64], P('fsdp'), may hold values from -0.125 to 0.125
- laurel_up: bfloat16 [64, 2048], P('fsdp'), may hold values from -0.75 to 0.75
- vector_gate: bfloat16 [2048, 256], P('fsdp'), may hold values from -0.125 to 0.125
- vector_out: bfloat16 [256, 2048], P('fsdp'), may hold values from -0.375 to 0.375
- norm_input: bfloat16 [2048], P('fsdp'), may hold values from 0.25 to 1.75
- norm_attention: bfloat16 [2048], P('fsdp'), may hold values from 0.25 to 1.75
- norm_laurel: bfloat16 [2048], P('fsdp'), may hold values from 0.25 to 1.75
- norm_before: bfloat16 [2048], P('fsdp'), may hold values from 0.25 to 1.75
- norm_after: bfloat16 [2048], P('fsdp'), may hold values from 0.25 to 1.75
- norm_vector: bfloat16 [2048], P('fsdp'), may hold values from 0.25 to 1.75
- query_norm_gain: bfloat16 [256], P('fsdp'), may hold values from 0.25 to 1.75
- norm_key: bfloat16 [256], P('fsdp'), may hold values from 0.25 to 1.75
- hidden_gate: bfloat16 [8192, 2048], P('fsdp'), may hold values from -0.125 to 0.125
- hidden_up: bfloat16 [8192, 2048], P('fsdp'), may hold values from -0.125 to 0.125
- hidden_down: bfloat16 [8192, 2048], P('fsdp'), may hold values from -0.0625 to 0.0625
Outputs:
- output: bfloat16 [4096, 2048], P(('fsdp', 'ctx'))
- grad_tokens: float32 [4096, 2048], P(('fsdp', 'ctx'))
- grad_per_layer: float32 [4096, 256], P(('fsdp', 'ctx'))
- grad_query_weight: float32 [2048, 2048], P('fsdp')
- grad_key_weight: float32 [2048, 512], P('fsdp')
- grad_value_weight: float32 [2048, 512], P('fsdp')
- grad_output_weight: float32 [2048, 2048], P('fsdp')
- grad_laurel_down: float32 [2048, 64], P('fsdp')
- grad_laurel_up: float32 [64, 2048], P('fsdp')
- grad_vector_gate: float32 [2048, 256], P('fsdp')
- grad_vector_out: float32 [256, 2048], P('fsdp')
- grad_norm_input: float32 [2048], P('fsdp')
- grad_norm_attention: float32 [2048], P('fsdp')
- grad_norm_laurel: float32 [2048], P('fsdp')
- grad_norm_before: float32 [2048], P('fsdp')
- grad_norm_after: float32 [2048], P('fsdp')
- grad_norm_vector: float32 [2048], P('fsdp')
- grad_norm_query: float32 [256], P('fsdp')
- grad_norm_key: float32 [256], P('fsdp')
- grad_hidden_gate: float32 [8192, 2048], P('fsdp')
- grad_hidden_up: float32 [8192, 2048], P('fsdp')
- grad_hidden_down: float32 [8192, 2048], P('fsdp')
The draws below stay inside these ranges and needn't reach their ends.
Inputs may be any that keep to these rules, and one draw needn't show every extreme that they name: `segments`: within each sequence of 512 tokens the segment numbers never fall; sequence s uses 3 s, 3 s + 1 and 3 s + 2, and the middle document begins in the sequence's first 128 tokens, never at its first token, and ends in its last 128, never at its last token. `positions`: each token's distance from the first token of its document; the largest is reached in every draw.
All inputs are finite; a program needn't handle non-finite values.
Results may differ from the reference program's by a relative error of at most 0.025.
Values may be sent and summed in bfloat16 or wider, within the bound.
A program may use at most 256 MiB of HBM per device.

```python
import math
import jax
import jax.numpy as jnp
from jax import lax

MODEL_WIDTH = 2048
QUERY_HEADS = 8
KEY_VALUE_HEADS = 2
HEAD_SIZE = 256
FF = 8192
RANK = 64
PLD = 256
WINDOW = 1024
TOK_DEV = 128
SEQS = 8
LENGTH = 512
TOKENS = 4096


def document_layout(key):
    first_key, second_key, third_key = jax.random.split(key, 3)
    open_at = jax.random.randint(first_key, (SEQS, 1), 1, TOK_DEV // 2 + 1)
    close_at = LENGTH - jax.random.randint(second_key, (SEQS, 1), 1, TOK_DEV // 2 + 1)
    widest = jax.random.randint(third_key, (), 0, SEQS)
    chosen = jnp.arange(SEQS, dtype=jnp.int32)[:, None] == widest
    open_at = jnp.where(chosen, 1, open_at)
    close_at = jnp.where(chosen, LENGTH - 1, close_at)
    token_location = jnp.arange(LENGTH, dtype=jnp.int32)[None, :]
    in_middle = (token_location >= open_at).astype(jnp.int32)
    in_last = (token_location >= close_at).astype(jnp.int32)
    segment_ids = in_middle + in_last + 3 * jnp.arange(SEQS, dtype=jnp.int32)[:, None]
    doc_start = jnp.where(in_last == 1, close_at, jnp.where(in_middle == 1, open_at, 0))
    return (segment_ids.reshape(-1), (token_location - doc_start).reshape(-1))


def draw_segments(key, part):
    return document_layout(key)[0]


def draw_positions(key, part):
    return document_layout(key)[1]


def level_of(own_key, extent, cuts, low, top_value):
    factor_of, own = 1.0, jax.random.fold_in(own_key, 6)
    for position, shards_of in cuts:
        heights = jnp.exp(jax.random.uniform(jax.random.fold_in(own, position), (shards_of,), jnp.float32, low / len(cuts), top_value / len(cuts)))
        factor_of = factor_of * jnp.repeat(heights, extent[position] // shards_of).reshape([-1 if axis == position else 1 for axis in range(len(extent))])
    return factor_of


def centred(own_key, shape, width, limit, pieces=(), kind=jnp.bfloat16):
    factor_of = level_of(own_key, shape, pieces, -0.22, 0.18) if pieces else 1.0
    array = jax.random.normal(own_key, shape, jnp.float32) * width * factor_of
    return jnp.minimum(jnp.maximum(array, -limit), limit).astype(kind)


def setup_inputs(seed: int = 0) -> dict:
    arg_keys = jax.random.split(jax.random.key(seed), 25)
    return {
        "tokens": centred(arg_keys[0], (TOKENS, MODEL_WIDTH), 1.0, 6.0, ((0, 32),)),
        "per_layer": centred(arg_keys[1], (TOKENS, PLD), 1.0, 6.0, ((0, 32),)),
        "segments": draw_segments(jax.random.fold_in(arg_keys[24], 71), 0),
        "positions": draw_positions(jax.random.fold_in(arg_keys[24], 71), 0),
        "cotangent": centred(arg_keys[4], (TOKENS, MODEL_WIDTH), 1.0, 6.0, ((0, 32),)),
        "query_weight": centred(arg_keys[5], (MODEL_WIDTH, QUERY_HEADS * HEAD_SIZE), MODEL_WIDTH ** -0.5, 0.125, ((0, 8),)),
        "key_matrix": centred(arg_keys[6], (MODEL_WIDTH, KEY_VALUE_HEADS * HEAD_SIZE), MODEL_WIDTH ** -0.5, 0.125, ((0, 8),)),
        "value_matrix": centred(arg_keys[7], (MODEL_WIDTH, KEY_VALUE_HEADS * HEAD_SIZE), MODEL_WIDTH ** -0.5, 0.125, ((0, 8),)),
        "output_weight": centred(arg_keys[8], (QUERY_HEADS * HEAD_SIZE, MODEL_WIDTH), (QUERY_HEADS * HEAD_SIZE) ** -0.5, 0.125, ((0, 8),)),
        "laurel_down": centred(arg_keys[9], (MODEL_WIDTH, RANK), MODEL_WIDTH ** -0.5, 0.125, ((0, 8),)),
        "laurel_up": centred(arg_keys[10], (RANK, MODEL_WIDTH), RANK ** -0.5, 0.75, ((0, 8),)),
        "vector_gate": centred(arg_keys[11], (MODEL_WIDTH, PLD), MODEL_WIDTH ** -0.5, 0.125, ((0, 8),)),
        "vector_out": centred(arg_keys[12], (PLD, MODEL_WIDTH), PLD ** -0.5, 0.375, ((0, 8),)),
        "norm_input": jnp.clip(1.0 + 0.15 * jax.random.normal(arg_keys[13], (MODEL_WIDTH,), jnp.float32), 0.25, 1.75).astype(jnp.bfloat16),
        "norm_attention": jnp.clip(1.0 + 0.15 * jax.random.normal(arg_keys[14], (MODEL_WIDTH,), jnp.float32), 0.25, 1.75).astype(jnp.bfloat16),
        "norm_laurel": jnp.clip(1.0 + 0.15 * jax.random.normal(arg_keys[15], (MODEL_WIDTH,), jnp.float32), 0.25, 1.75).astype(jnp.bfloat16),
        "norm_before": jnp.clip(1.0 + 0.15 * jax.random.normal(arg_keys[16], (MODEL_WIDTH,), jnp.float32), 0.25, 1.75).astype(jnp.bfloat16),
        "norm_after": jnp.clip(1.0 + 0.15 * jax.random.normal(arg_keys[17], (MODEL_WIDTH,), jnp.float32), 0.25, 1.75).astype(jnp.bfloat16),
        "norm_vector": jnp.clip(1.0 + 0.15 * jax.random.normal(arg_keys[18], (MODEL_WIDTH,), jnp.float32), 0.25, 1.75).astype(jnp.bfloat16),
        "query_norm_gain": jnp.clip(1.0 + 0.15 * jax.random.normal(arg_keys[19], (HEAD_SIZE,), jnp.float32), 0.25, 1.75).astype(jnp.bfloat16),
        "norm_key": jnp.clip(1.0 + 0.15 * jax.random.normal(arg_keys[20], (HEAD_SIZE,), jnp.float32), 0.25, 1.75).astype(jnp.bfloat16),
        "hidden_gate": centred(arg_keys[21], (FF, MODEL_WIDTH), MODEL_WIDTH ** -0.5, 0.125, ((0, 8),)),
        "hidden_up": centred(arg_keys[22], (FF, MODEL_WIDTH), MODEL_WIDTH ** -0.5, 0.125, ((0, 8),)),
        "hidden_down": centred(arg_keys[23], (FF, MODEL_WIDTH), FF ** -0.5, 0.0625, ((0, 8),)),
    }


@jax.custom_vjp
def lowered_input(v):
    return lax.optimization_barrier(v.astype(jnp.bfloat16)).astype(jnp.float32)

@jax.custom_vjp
def lowered_backward(v):
    return v

def low_keep(v):
    return (lowered_input(v), None)

def low_pass(kept, grad):
    return (grad,)

def back_keep(v):
    return (v, None)

def back_low(kept, grad):
    return (lowered_input(grad),)
lowered_input.defvjp(low_keep, low_pass)
lowered_backward.defvjp(back_keep, back_low)
epsilon = 1e-06
rope_base = 10000.0
inv_root = 0.7071067811865476
precise = lax.Precision.HIGHEST

def root_mean_norm(value, gain):
    factor = lax.rsqrt(lax.optimization_barrier(jnp.mean(value * value, axis=-1, keepdims=True)) + epsilon)
    return value * factor * gain

def gelu_tanh(value):
    return jax.nn.gelu(value, approximate=True)

def rotary_apply(value, token_position):
    half_size = value.shape[-1] // 2
    frequency = rope_base ** (-2.0 * jnp.arange(half_size, dtype=jnp.float32) / value.shape[-1])
    angle = token_position.astype(jnp.float32)[:, None] * frequency[None, :]
    cosine = jnp.cos(angle)[:, None, :]
    sine_part = jnp.sin(angle)[:, None, :]
    first_half = value[..., :half_size]
    second_half = value[..., half_size:]
    return jnp.concatenate([first_half * cosine - second_half * sine_part, second_half * cosine + first_half * sine_part], axis=-1)

def matrix_product(left, right):
    return jnp.dot(left, right, precision=precise)

def attend(query_lowered, key_lowered, value_lowered, document_segment):
    length = query_lowered.shape[0]
    rows_per_block = math.gcd(length, 512)
    count_of_blocks = length // rows_per_block
    token_location = jnp.arange(length, dtype=jnp.int32)
    score_scale = HEAD_SIZE ** (-0.5)

    def single_block(block_inputs):
        query_part, segment_part, place_part = block_inputs
        scores = lowered_backward(score_scale * jnp.einsum('tgfd,kgd->gftk', query_part, key_lowered, precision=precise))
        key_gap = place_part[:, None] - token_location[None, :]
        allowed = (segment_part[:, None] == document_segment[None, :]) & (key_gap >= 0) & (key_gap < WINDOW)
        scores = jnp.where(allowed, scores, -1e+30)
        soft_low = lowered_input(jax.nn.softmax(scores, axis=-1))
        return jnp.einsum('gftk,kgd->tgfd', soft_low, value_lowered, precision=precise)
    output_blocks = lax.map(jax.checkpoint(single_block), (query_lowered.reshape(count_of_blocks, rows_per_block, KEY_VALUE_HEADS, QUERY_HEADS // KEY_VALUE_HEADS, HEAD_SIZE), document_segment.reshape(count_of_blocks, rows_per_block), token_location.reshape(count_of_blocks, rows_per_block)))
    return output_blocks.reshape(length, QUERY_HEADS * HEAD_SIZE)

def decoder_layer(source, vectors, params, document_segment, token_position):
    query_weight, key_matrix, value_matrix, output_weight, laurel_down, laurel_up, vector_gate, vector_out, norm_input, norm_attention, norm_laurel, norm_before, norm_after, norm_vector, query_norm_gain, norm_key, hidden_gate, hidden_up, hidden_down = params
    normed = root_mean_norm(source, norm_input)
    lowered_normed = lowered_input(normed)
    query_linear = lowered_backward(matrix_product(lowered_normed, query_weight)).reshape(-1, QUERY_HEADS, HEAD_SIZE)
    key_linear = lowered_backward(matrix_product(lowered_normed, key_matrix)).reshape(-1, KEY_VALUE_HEADS, HEAD_SIZE)
    value_lowered = lowered_input(lowered_backward(matrix_product(lowered_normed, value_matrix))).reshape(-1, KEY_VALUE_HEADS, HEAD_SIZE)
    query_lowered = lowered_input(rotary_apply(root_mean_norm(query_linear, query_norm_gain), token_position)).reshape(-1, KEY_VALUE_HEADS, QUERY_HEADS // KEY_VALUE_HEADS, HEAD_SIZE)
    key_lowered = lowered_input(rotary_apply(root_mean_norm(key_linear, norm_key), token_position))
    attended_low = lowered_input(lowered_backward(attend(query_lowered, key_lowered, value_lowered, document_segment)))
    attn_lin = lowered_backward(matrix_product(attended_low, output_weight))
    residual_one = source + root_mean_norm(attn_lin, norm_attention)
    laurel_mid = lowered_input(lowered_backward(matrix_product(lowered_normed, laurel_down)))
    laurel_lin = lowered_backward(matrix_product(laurel_mid, laurel_up))
    mixed = (residual_one + normed + root_mean_norm(laurel_lin, norm_laurel)) * inv_root
    ffn_in = lowered_input(root_mean_norm(mixed, norm_before))
    gate_value = lowered_backward(matrix_product(ffn_in, hidden_gate.T))
    up_value = lowered_backward(matrix_product(ffn_in, hidden_up.T))
    hidden_low = lowered_input(gelu_tanh(gate_value) * up_value)
    feed_value = lowered_backward(matrix_product(hidden_low, hidden_down))
    residual_two = mixed + root_mean_norm(feed_value, norm_after)
    vector_lin = lowered_backward(matrix_product(lowered_input(residual_two), vector_gate))
    gated_low = lowered_input(gelu_tanh(vector_lin) * vectors)
    vector_back = lowered_backward(matrix_product(gated_low, vector_out))
    return residual_two + root_mean_norm(vector_back, norm_vector)

def reference(tokens, per_layer, segments, positions, cotangent, query_weight, key_matrix, value_matrix, output_weight, laurel_down, laurel_up, vector_gate, vector_out, norm_input, norm_attention, norm_laurel, norm_before, norm_after, norm_vector, query_norm_gain, norm_key, hidden_gate, hidden_up, hidden_down):
    params = tuple((weight.astype(jnp.float32) for weight in (query_weight, key_matrix, value_matrix, output_weight, laurel_down, laurel_up, vector_gate, vector_out, norm_input, norm_attention, norm_laurel, norm_before, norm_after, norm_vector, query_norm_gain, norm_key, hidden_gate, hidden_up, hidden_down)))
    source_all = tokens.astype(jnp.float32).reshape(SEQS, LENGTH, MODEL_WIDTH)
    vectors_all = per_layer.astype(jnp.float32).reshape(SEQS, LENGTH, PLD)
    upstream_all = cotangent.astype(jnp.float32).reshape(SEQS, LENGTH, MODEL_WIDTH)
    segment_all = segments.reshape(SEQS, LENGTH)
    position_all = positions.reshape(SEQS, LENGTH)

    def one_sequence(totals, sequence_inputs):
        source, vectors, document_segment, token_position, upstream = sequence_inputs

        def layer_only(source_in, vectors_in, params_in):
            return decoder_layer(source_in, vectors_in, params_in, document_segment, token_position)
        result, pullback = jax.vjp(layer_only, source, vectors, params)
        d_source, d_vectors, d_params = pullback(upstream)
        totals = jax.tree.map(lambda total_sum, addend: total_sum + addend, totals, d_params)
        return (totals, (result.astype(jnp.bfloat16), d_source, d_vectors))
    zero_grads = jax.tree.map(jnp.zeros_like, params)
    totals, (results, d_sources, d_vectors) = lax.scan(one_sequence, zero_grads, (source_all, vectors_all, segment_all, position_all, upstream_all))
    return (results.reshape(TOKENS, MODEL_WIDTH), d_sources.reshape(TOKENS, MODEL_WIDTH), d_vectors.reshape(TOKENS, PLD), totals[0], totals[1], totals[2], totals[3], totals[4], totals[5], totals[6], totals[7], totals[8], totals[9], totals[10], totals[11], totals[12], totals[13], totals[14], totals[15], totals[16], totals[17], totals[18])
```

```python
import functools

import jax
import jax.numpy as jnp
from jax import lax
from jax.experimental import pallas as pl
from jax.experimental.pallas import tpu as pltpu
from jax.sharding import PartitionSpec as P

QUERY_HEADS = 8
KEY_VALUE_HEADS = 2
HEAD_SIZE = 256
WINDOW = 1024


epsilon = 1e-06
rope_base = 10000.0
inv_root = 0.7071067811865476
gelu_scale = 0.7978845608028654
gelu_cubic = 0.044715


def from_behind(value, axis, steps):
    count = lax.axis_size(axis)
    initial, last = (max(0, -steps), min(count, count - steps))
    return lax.ppermute(value, axis, [(source, source + steps) for source in range(initial, last)])


def other_blocks(value, axis):
    count = lax.axis_size(axis)
    return jnp.concatenate(
        [
            lax.ppermute(value, axis, [(source, (source + step) % count) for source in range(count)])
            for step in range(1, count)
        ],
        axis=0,
    )


def root_mean_norm(value, gain):
    factor = lax.rsqrt(jnp.mean(value * value, axis=-1, keepdims=True) + epsilon)
    return value * factor * gain


def gelu_tanh(value):
    return jax.nn.gelu(value, approximate=True)


def gated(gate_value, up_value):
    return gelu_tanh(gate_value) * up_value


def rotary_apply(value, token_position):
    half_size = value.shape[-1] // 2
    frequency = rope_base ** (-2.0 * jnp.arange(half_size, dtype=jnp.float32) / value.shape[-1])
    angle = token_position.astype(jnp.float32)[:, None] * frequency[None, :]
    cosine = jnp.cos(angle)[:, None, :]
    sine_part = jnp.sin(angle)[:, None, :]
    first_half = value[..., :half_size]
    second_half = value[..., half_size:]
    return jnp.concatenate(
        [
            first_half * cosine - second_half * sine_part,
            second_half * cosine + first_half * sine_part,
        ],
        axis=-1,
    )


def matrix_product(left, right):
    return jnp.dot(left, right, preferred_element_type=jnp.float32)


def product_back(left, right):
    return lax.dot_general(
        left, right, (((1,), (1,)), ((), ())), preferred_element_type=jnp.float32
    )


def product_rows(left, right):
    return lax.dot_general(
        left, right, (((0,), (0,)), ((), ())), preferred_element_type=jnp.float32
    )


def norm_grad(value, gain, upstream):
    unused, pullback = jax.vjp(root_mean_norm, value, gain)
    return pullback(upstream)


def gated_grad(gate_value, up_value, upstream):
    unused, pullback = jax.vjp(gated, gate_value, up_value)
    return pullback(upstream)


def gather(value, axis):
    return lax.all_gather(value, axis, axis=0, tiled=True)


def feature_slices(value):
    count = lax.axis_size("fsdp")
    rows = value.shape[0]
    return lax.all_to_all(
        value.reshape(rows, count, -1), "fsdp", split_axis=1, concat_axis=0, tiled=True
    ).reshape(count * rows, -1)


def scatter_sum(value):
    return lax.psum_scatter(
        value.astype(jnp.bfloat16), "fsdp", scatter_dimension=0, tiled=True
    ).astype(jnp.float32)


def gelu_parts(gate):
    square = gate * gate
    bend = jnp.tanh(gelu_scale * gate * (1.0 + gelu_cubic * square))
    half_up = 0.5 * (1.0 + bend)
    slope = half_up + 0.5 * gate * (1.0 - bend * bend) * (
        gelu_scale * (1.0 + 3.0 * gelu_cubic * square)
    )
    return gate * half_up, slope


def across(me, stride):
    return me + stride - 2 * stride * ((me // stride) % 2)


def across_many(me, bits):
    for stride in (1, 2, 4):
        if bits & stride:
            me = across(me, stride)
    return me


def feed_kernel(forward, rows_of, others, *refs):
    half = rows_of // 2
    if forward:
        (own, gate_hbm, up_hbm, down_hbm, features, total, rows_hbm, far_hbm, slices_hbm, hidden_hbm, lift_hbm, bend_hbm), rest = refs[:12], refs[12:]
        weights_hbm, kept_hbm, made_hbm = (gate_hbm, up_hbm, down_hbm), (), (hidden_hbm, lift_hbm, bend_hbm)
    else:
        (own, down_hbm, gate_hbm, up_hbm, lift_hbm, bend_hbm, total, rows_hbm, far_hbm, d_gate_hbm, d_up_hbm), rest = refs[:11], refs[11:]
        weights_hbm, kept_hbm, made_hbm = (down_hbm, gate_hbm, up_hbm), (lift_hbm, bend_hbm), (d_gate_hbm, d_up_hbm)
    count_kept, count_made = len(kept_hbm), len(made_hbm)
    weights = rest[:3]
    kept = rest[3 : 3 + count_kept]
    made = rest[3 + count_kept : 3 + count_kept + count_made]
    (rows, part, sib_in, chip_sum, relay_in, relay_sum, last_in, send_sem, recv_sem, in_sem, out_sem, far_send, far_recv, *slice_sems) = rest[
        3 + count_kept + count_made :
    ]
    hidden = weights[0].shape[0]
    width = own.shape[1]
    me = lax.axis_index("fsdp")
    sibling, beside, above = across(me, 1), across(me, 2), across(me, 4)

    loads = [
        pltpu.make_async_copy(source, target, in_sem.at[index])
        for index, (source, target) in enumerate(zip(weights_hbm + kept_hbm, tuple(weights) + tuple(kept)))
    ]
    for load in loads:
        load.start()

    block = lax.axis_index("ctx")
    partners = range(1, 8) if forward else (1, 2, 4)
    barrier = pltpu.get_barrier_semaphore()
    for distance in partners:
        partner = across_many(me, distance)
        pl.semaphore_signal(barrier, inc=1, device_id={"fsdp": partner}, device_id_type=pl.DeviceIdType.MESH)
    for distance in range(1, others + 1):
        partner = (block + distance) % (others + 1)
        pl.semaphore_signal(barrier, inc=1, device_id={"ctx": partner}, device_id_type=pl.DeviceIdType.MESH)
    pl.semaphore_wait(barrier, len(partners) + others)

    def send(index, source, target, partner):
        return pltpu.make_async_remote_copy(
            src_ref=source,
            dst_ref=target,
            send_sem=send_sem.at[index],
            recv_sem=recv_sem.at[index],
            device_id={"fsdp": partner},
            device_id_type=pl.DeviceIdType.MESH,
        )

    low, high = pl.ds(0, half), pl.ds(half, half)
    mine, theirs = pl.ds(0, rows_of), pl.ds(rows_of, rows_of)
    copies = [
        send(0, own, rows.at[0, theirs], sibling),
        send(1, own.at[low], rows.at[1, low], beside),
        send(2, own.at[low], rows.at[1, high], above),
        send(3, own.at[high], rows.at[2, low], beside),
        send(4, own.at[high], rows.at[2, high], above),
        send(5, rows.at[1, mine], rows.at[1, theirs], sibling),
        send(6, rows.at[2, mine], rows.at[2, theirs], sibling),
        send(7, rows.at[1, low], rows.at[3, low], above),
        send(8, rows.at[2, high], rows.at[3, high], beside),
        send(9, rows.at[3, mine], rows.at[3, theirs], sibling),
        send(10, part.at[0, theirs], sib_in.at[0], sibling),
        send(11, part.at[1, theirs], sib_in.at[1], sibling),
        send(12, part.at[2, theirs], sib_in.at[2], sibling),
        send(13, part.at[3, theirs], sib_in.at[3], sibling),
        send(14, chip_sum.at[0, high], last_in.at[2], above),
        send(15, chip_sum.at[1, low], last_in.at[1], beside),
        send(16, chip_sum.at[2, low], relay_in.at[0], above),
        send(17, chip_sum.at[2, high], relay_in.at[1], beside),
        send(18, relay_sum.at[0], last_in.at[0], beside),
        send(19, relay_sum.at[1], last_in.at[3], above),
    ]
    outs = []

    def write_out(source, target):
        copy = pltpu.make_async_copy(source, target, out_sem.at[len(outs)])
        copy.start()
        outs.append(copy)

    for index in range(5):
        copies[index].start()
    far = [
        pltpu.make_async_remote_copy(
            src_ref=own,
            dst_ref=far_hbm.at[distance - 1],
            send_sem=far_send.at[distance - 1],
            recv_sem=far_recv.at[distance - 1],
            device_id={"ctx": (block + distance) % (others + 1)},
            device_id_type=pl.DeviceIdType.MESH,
        )
        for distance in range(1, others + 1)
    ]
    for copy in far:
        copy.start()
    rows[0, mine] = own[...]
    slices = []
    if forward:
        share = features.shape[1] // 8

        def share_of(device):
            return features.at[:, pl.ds(pl.multiple_of(device * share, share), share)]

        own_slice = pltpu.make_async_copy(share_of(me), slices_hbm.at[me], slice_sems[2])
        own_slice.start()
        slices = [
            pltpu.make_async_remote_copy(
                src_ref=share_of(across_many(me, distance)),
                dst_ref=slices_hbm.at[me],
                send_sem=slice_sems[0].at[distance - 1],
                recv_sem=slice_sems[1].at[distance - 1],
                device_id={"fsdp": across_many(me, distance)},
                device_id_type=pl.DeviceIdType.MESH,
            )
            for distance in range(1, 8)
        ]

    tile = min(hidden, 1024)
    wide = min(width, 1024)

    def first_stage(group):
        span = pl.ds(group * 2 * rows_of, 2 * rows_of)

        def step(index, carry):
            columns = pl.ds(pl.multiple_of(index * tile, tile), tile)
            left = rows[group]

            def back(weight):
                return lax.dot_general(
                    left, weight[columns, :], (((1,), (1,)), ((), ())), preferred_element_type=jnp.float32
                )

            if forward:
                gate, up = back(weights[0]), back(weights[1])
                value, slope = gelu_parts(gate)
                made[0][span, columns] = (value * up).astype(jnp.bfloat16)
                made[1][span, columns] = value.astype(jnp.bfloat16)
                made[2][span, columns] = (slope * up).astype(jnp.bfloat16)
            else:
                d_hidden = back(weights[0])
                made[0][span, columns] = (d_hidden * kept[1][span, columns].astype(jnp.float32)).astype(jnp.bfloat16)
                made[1][span, columns] = (d_hidden * kept[0][span, columns].astype(jnp.float32)).astype(jnp.bfloat16)
            return carry

        lax.fori_loop(0, hidden // tile, step, 0)

    def second_stage(group):
        span = pl.ds(group * 2 * rows_of, 2 * rows_of)

        def step(index, carry):
            columns = pl.ds(pl.multiple_of(index * wide, wide), wide)
            if forward:
                value = jnp.dot(made[0][span, :], weights[2][:, columns], preferred_element_type=jnp.float32)
            else:
                value = jnp.dot(made[0][span, :], weights[1][:, columns], preferred_element_type=jnp.float32)
                value = value + jnp.dot(made[1][span, :], weights[2][:, columns], preferred_element_type=jnp.float32)
            part[group, :, columns] = value.astype(jnp.bfloat16)
            return carry

        lax.fori_loop(0, width // wide, step, 0)

    def keep_out(group):
        span = pl.ds(group * 2 * rows_of, 2 * rows_of)
        write_out(rows.at[group], rows_hbm.at[span])
        for source, target in zip(made, made_hbm):
            write_out(source.at[span], target.at[span])

    def add_chip(group):
        chip_sum[group - 1] = (
            part[group, mine].astype(jnp.float32) + sib_in[group].astype(jnp.float32)
        ).astype(jnp.bfloat16)

    copies[0].wait_recv()
    loads[0].wait()
    if forward:
        loads[1].wait()
    else:
        loads[3].wait()
        loads[4].wait()
    first_stage(0)
    if forward:
        loads[2].wait()
    else:
        loads[1].wait()
        loads[2].wait()
    second_stage(0)
    copies[10].start()
    keep_out(0)
    copies[1].wait_recv()
    copies[7].start()
    copies[2].wait_recv()
    copies[5].start()
    copies[5].wait_recv()
    first_stage(1)
    second_stage(1)
    copies[11].start()
    keep_out(1)
    copies[3].wait_recv()
    copies[4].wait_recv()
    copies[8].start()
    copies[6].start()
    copies[11].wait_recv()
    add_chip(1)
    copies[14].start()
    copies[6].wait_recv()
    first_stage(2)
    second_stage(2)
    copies[12].start()
    keep_out(2)
    for copy in slices:
        copy.start()
    copies[7].wait_recv()
    copies[8].wait_recv()
    copies[9].start()
    copies[12].wait_recv()
    add_chip(2)
    copies[15].start()
    copies[9].wait_recv()
    first_stage(3)
    second_stage(3)
    copies[13].start()
    keep_out(3)
    copies[13].wait_recv()
    add_chip(3)
    copies[16].start()
    copies[17].start()
    copies[10].wait_recv()
    total[...] = part[0, mine].astype(jnp.float32) + sib_in[0].astype(jnp.float32)
    copies[16].wait_recv()
    relay_sum[0] = (chip_sum[0, low].astype(jnp.float32) + relay_in[0].astype(jnp.float32)).astype(jnp.bfloat16)
    copies[18].start()
    copies[17].wait_recv()
    relay_sum[1] = (chip_sum[1, high].astype(jnp.float32) + relay_in[1].astype(jnp.float32)).astype(jnp.bfloat16)
    copies[19].start()
    copies[14].wait_recv()
    total[low] = total[low] + last_in[2].astype(jnp.float32)
    copies[15].wait_recv()
    total[high] = total[high] + last_in[1].astype(jnp.float32)
    copies[18].wait_recv()
    total[low] = total[low] + last_in[0].astype(jnp.float32)
    copies[19].wait_recv()
    total[high] = total[high] + last_in[3].astype(jnp.float32)
    for copy in copies:
        copy.wait_send()
    for copy in outs:
        copy.wait()
    for copy in far + slices:
        copy.wait()
    if forward:
        own_slice.wait()


def feed_call(forward, own, weights, kept=(), features=None):
    rows_of, width = own.shape
    hidden = weights[0].shape[0]
    all_rows = 8 * rows_of
    others = lax.axis_size("ctx") - 1
    low = jnp.bfloat16
    count_made = 3 if forward else 2
    hbm = pl.BlockSpec(memory_space=pl.ANY)
    vmem = pl.BlockSpec(memory_space=pltpu.VMEM)
    half = rows_of // 2
    dma = pltpu.SemaphoreType.DMA
    shapes = [
        jax.ShapeDtypeStruct((rows_of, width), jnp.float32),
        jax.ShapeDtypeStruct((all_rows, width), low),
        jax.ShapeDtypeStruct((others, rows_of, width), low),
    ]
    operands = (own, *weights, *kept)
    operand_specs = [vmem] + [hbm] * (3 + len(kept))
    slice_sems = []
    if forward:
        shapes += [jax.ShapeDtypeStruct((8, rows_of, features.shape[1] // 8), low)]
        operands += (features,)
        operand_specs += [vmem]
        slice_sems = [dma((7,)), dma((7,)), dma]
    shapes += [jax.ShapeDtypeStruct((all_rows, hidden), low)] * count_made
    return pl.pallas_call(
        functools.partial(feed_kernel, forward, rows_of, others),
        out_shape=shapes,
        in_specs=operand_specs,
        out_specs=[vmem] + [hbm] * (len(shapes) - 1),
        scratch_shapes=[pltpu.VMEM((hidden, width), low)] * 3
        + [pltpu.VMEM((all_rows, hidden), low)] * (len(kept) + count_made)
        + [
            pltpu.VMEM((4, 2 * rows_of, width), low),
            pltpu.VMEM((4, 2 * rows_of, width), low),
            pltpu.VMEM((4, rows_of, width), low),
            pltpu.VMEM((3, rows_of, width), low),
            pltpu.VMEM((2, half, width), low),
            pltpu.VMEM((2, half, width), low),
            pltpu.VMEM((4, half, width), low),
            dma((20,)),
            dma((20,)),
            dma((3 + len(kept),)),
            dma((4 * (1 + count_made),)),
            dma((others,)),
            dma((others,)),
        ]
        + slice_sems,
        compiler_params=pltpu.CompilerParams(
            collective_id=1 if forward else 2,
            has_side_effects=True,
            vmem_limit_bytes=56 * 2**20,
        ),
        cost_estimate=pl.CostEstimate(
            flops=40 * all_rows * hidden * width // 2,
            bytes_accessed=6 * hidden * width + 8 * all_rows * width,
            transcendentals=0,
        ),
        name="feed_forward" if forward else "feed_backward",
    )(*operands)


def weight_grad_kernel(
    own_steps, gate, up, down, rows, d_rows, hidden, d_gate, d_up, rows_far, d_rows_far,
    grad_gate, grad_up, grad_down, hidden_tile, d_gate_tile, d_up_tile,
):
    step = pl.program_id(1)
    tile = 512
    hidden_size = gate.shape[0]
    chunk = rows.shape[1]

    @pl.when(step == 0)
    def _():
        grad_gate[...] = jnp.zeros_like(grad_gate)
        grad_up[...] = jnp.zeros_like(grad_up)
        grad_down[...] = jnp.zeros_like(grad_down)

    def accumulate(rows, d_rows):
        def body(index, carry):
            columns = pl.ds(pl.multiple_of(index * chunk, chunk), chunk)
            right, d_right = rows[:, columns], d_rows[:, columns]
            grad_gate[:, columns] += matrix_product(d_gate_tile[...], right)
            grad_up[:, columns] += matrix_product(d_up_tile[...], right)
            grad_down[:, columns] += matrix_product(hidden_tile[...], d_right)
            return carry
        lax.fori_loop(0, rows.shape[1] // chunk, body, 0)

    @pl.when(step < own_steps)
    def _():
        hidden_tile[...] = hidden[...].T
        d_gate_tile[...] = d_gate[...].T
        d_up_tile[...] = d_up[...].T
        accumulate(rows, d_rows)

    @pl.when(step >= own_steps)
    def _():
        def body(index, carry):
            span = pl.ds(pl.multiple_of(index * tile, tile), tile)
            gate_value = product_back(gate[span, :], rows_far[...])
            up_value = product_back(up[span, :], rows_far[...])
            d_hidden = product_back(down[span, :], d_rows_far[...])
            value, slope = gelu_parts(gate_value)
            hidden_tile[span, :] = (value * up_value).astype(jnp.bfloat16)
            d_gate_tile[span, :] = (d_hidden * up_value * slope).astype(jnp.bfloat16)
            d_up_tile[span, :] = (d_hidden * value).astype(jnp.bfloat16)
            return carry
        lax.fori_loop(0, hidden_size // tile, body, 0)
        accumulate(rows_far, d_rows_far)


def weight_grad_call(gate, up, down, rows, d_rows, hidden, d_gate, d_up, rows_far, d_rows_far, hid=1024, tok=256):
    size, width = gate.shape
    hid = min(hid, size)
    own_steps = rows.shape[0] // tok
    far_steps = rows_far.shape[0] // tok
    low = jnp.bfloat16
    weight = pl.BlockSpec((hid, width), lambda h, s: (h, 0))
    own = pl.BlockSpec((tok, width), lambda h, s: (jnp.minimum(s, own_steps - 1), 0))
    own_mid = pl.BlockSpec((tok, hid), lambda h, s: (jnp.minimum(s, own_steps - 1), h))
    far = pl.BlockSpec((tok, width), lambda h, s: (jnp.maximum(s - own_steps, 0), 0))
    flops = 6 * size * width * (rows.shape[0] + 2 * rows_far.shape[0])
    return pl.pallas_call(
        functools.partial(weight_grad_kernel, own_steps),
        grid=(size // hid, own_steps + far_steps),
        in_specs=[weight] * 3 + [own] * 2 + [own_mid] * 3 + [far] * 2,
        out_specs=[weight] * 3,
        out_shape=[jax.ShapeDtypeStruct((size, width), jnp.float32)] * 3,
        scratch_shapes=[pltpu.VMEM((hid, tok), low)] * 3,
        compiler_params=pltpu.CompilerParams(
            dimension_semantics=("arbitrary", "arbitrary"), vmem_limit_bytes=60 * 2**20
        ),
        cost_estimate=pl.CostEstimate(flops=flops, bytes_accessed=100 * 2**20, transcendentals=0),
        name="weight_grads",
    )(gate, up, down, rows, d_rows, hidden, d_gate, d_up, rows_far, d_rows_far)


def per_device(
    tokens,
    per_layer,
    segments,
    positions,
    cotangent,
    query_weight,
    key_matrix,
    value_matrix,
    output_weight,
    laurel_down,
    laurel_up,
    vector_gate,
    vector_out,
    norm_input,
    norm_attention,
    norm_laurel,
    norm_before,
    norm_after,
    norm_vector,
    query_norm_gain,
    norm_key,
    hidden_gate,
    hidden_up,
    hidden_down,
):
    count_of_rows = tokens.shape[0]
    shards = lax.axis_size("fsdp")
    width = tokens.shape[1]
    heads_per_group = QUERY_HEADS // KEY_VALUE_HEADS
    reach_blocks = min((WINDOW + count_of_rows - 2) // count_of_rows, lax.axis_size("ctx") - 1)
    score_scale = HEAD_SIZE ** (-0.5)
    other_rows = (lax.axis_size("ctx") - 1) * count_of_rows * shards
    gathered_plan = other_rows <= 4096
    query_width = query_weight.shape[1]
    key_width = key_matrix.shape[1]

    gain_shards = (
        norm_input,
        norm_attention,
        norm_laurel,
        norm_before,
        norm_after,
        norm_vector,
        query_norm_gain,
        norm_key,
    )
    gain_sizes = [gain.shape[0] for gain in gain_shards]
    gain_starts = [sum(gain_sizes[:index]) for index in range(len(gain_sizes))]
    gain_line = jnp.concatenate(gain_shards)
    gain_line = jnp.pad(gain_line, (0, -gain_line.shape[0] % 2048)).reshape(-1, 128)
    gains_all = gather(gain_line, "fsdp").reshape(shards, -1)
    (
        gain_input,
        gain_attention,
        gain_laurel,
        gain_before,
        gain_after,
        gain_vector,
        gain_query,
        key_norm_gain,
    ) = [
        gains_all[:, start : start + size].reshape(-1).astype(jnp.float32)
        for start, size in zip(gain_starts, gain_sizes)
    ]
    full_inward = gather(
        jnp.concatenate([query_weight, key_matrix, value_matrix, laurel_down], axis=1), "fsdp"
    )
    pieces = [output_weight, vector_gate.reshape(-1, width), vector_out, laurel_up]
    piece_sizes = [piece.shape[0] for piece in pieces]
    piece_rows = sum(piece_sizes)
    outward = jnp.pad(jnp.concatenate(pieces, axis=0), ((0, -piece_rows % 16), (0, 0)))
    outward, unused = lax.optimization_barrier((outward, full_inward[:8, :128]))
    outward = lax.all_gather(outward, "fsdp", axis=0, tiled=False)
    piece_starts = [sum(piece_sizes[:index]) for index in range(len(pieces))]
    full_output, full_vector_gate, full_vector_out, full_laurel_up = [
        outward[:, start : start + size].reshape(-1, width)
        for start, size in zip(piece_starts, piece_sizes)
    ]
    full_vector_gate = full_vector_gate.reshape(width, -1)

    source = tokens.astype(jnp.float32)
    vectors = per_layer.astype(jnp.float32)
    normed = root_mean_norm(source, gain_input)
    lowered_normed = normed.astype(jnp.bfloat16)
    def head_facing(linear, gain):
        return rotary_apply(root_mean_norm(linear, gain), positions)

    inward = matrix_product(lowered_normed, full_inward)
    query_linear = inward[:, :query_width].reshape(count_of_rows, QUERY_HEADS, HEAD_SIZE)
    key_linear = inward[:, query_width : query_width + key_width].reshape(
        count_of_rows, KEY_VALUE_HEADS, HEAD_SIZE
    )
    value_lowered = inward[:, query_width + key_width : query_width + 2 * key_width].astype(
        jnp.bfloat16
    )
    laurel_mid = inward[:, query_width + 2 * key_width :].astype(jnp.bfloat16)
    query_lowered = (
        head_facing(query_linear, gain_query)
        .astype(jnp.bfloat16)
        .reshape(count_of_rows, KEY_VALUE_HEADS, heads_per_group, HEAD_SIZE)
    )
    key_lowered = (
        head_facing(key_linear, key_norm_gain)
        .astype(jnp.bfloat16)
        .reshape(count_of_rows, KEY_VALUE_HEADS * HEAD_SIZE)
    )
    key_value = jnp.stack([key_lowered, value_lowered])
    pair_blocks = [key_value]
    for distance in range(1, reach_blocks + 1):
        pair_blocks.append(from_behind(key_value, "ctx", distance))
    window_couple = jnp.concatenate(pair_blocks, axis=1)
    window_keys = window_couple[0].reshape(-1, KEY_VALUE_HEADS, HEAD_SIZE)
    window_values = window_couple[1].reshape(-1, KEY_VALUE_HEADS, HEAD_SIZE)
    key_offset = jnp.concatenate(
        [
            distance * count_of_rows - jnp.arange(count_of_rows, dtype=jnp.int32)
            for distance in range(reach_blocks + 1)
        ]
    )
    key_gap = jnp.arange(count_of_rows, dtype=jnp.int32)[:, None] + key_offset[None, :]
    allowed = (key_gap >= 0) & (key_gap <= positions[:, None]) & (key_gap < WINDOW)

    def masked_scores():
        raw_scores = score_scale * jnp.einsum(
            "tgfd,kgd->gftk", query_lowered, window_keys, preferred_element_type=jnp.float32
        )
        return jnp.where(allowed, raw_scores, -1e30)

    scores_first = masked_scores()
    row_peak = jnp.max(scores_first, axis=-1, keepdims=True)
    exp_scores = jnp.exp(scores_first - row_peak)
    row_total = jnp.sum(exp_scores, axis=-1, keepdims=True)
    soft_low = (exp_scores / row_total).astype(jnp.bfloat16)
    log_total = row_peak + jnp.log(row_total)
    attended_low = (
        jnp.einsum("gftk,kgd->tgfd", soft_low, window_values, preferred_element_type=jnp.float32)
        .reshape(count_of_rows, QUERY_HEADS * HEAD_SIZE)
        .astype(jnp.bfloat16)
    )
    attn_lin = matrix_product(attended_low, full_output)
    residual_one = source + root_mean_norm(attn_lin, gain_attention)
    laurel_lin = matrix_product(laurel_mid, full_laurel_up)
    mixed = (residual_one + normed + root_mean_norm(laurel_lin, gain_laurel)) * inv_root
    ffn_in = root_mean_norm(mixed, gain_before).astype(jnp.bfloat16)
    if shards == 8:
        features = jnp.concatenate(
            [lowered_normed.reshape(count_of_rows, shards, -1), attended_low.reshape(count_of_rows, shards, -1)], axis=2
        ).reshape(count_of_rows, -1)
        feed_value, rows_all, rows_far, slices, hidden_all, lift_all, bend_all = feed_call(
            True, ffn_in, (hidden_gate, hidden_up, hidden_down), features=features
        )
        slices = slices.reshape(shards * count_of_rows, -1)
        normed_slices, attended_slices = jnp.split(slices, 2, axis=1)
    else:
        normed_slices = feature_slices(lowered_normed)
        attended_slices = feature_slices(attended_low)
        rows_all = gather(ffn_in, "fsdp")
        gate_all = product_back(rows_all, hidden_gate)
        up_all = product_back(rows_all, hidden_up)
        hidden_all = gated(gate_all, up_all).astype(jnp.bfloat16)
        feed_value = scatter_sum(matrix_product(hidden_all, hidden_down))
    residual_two = mixed + root_mean_norm(feed_value, gain_after)
    residual_low = residual_two.astype(jnp.bfloat16)
    vector_lin = matrix_product(residual_low, full_vector_gate)
    gated_low = gated(vector_lin, vectors).astype(jnp.bfloat16)
    vector_back = matrix_product(gated_low, full_vector_out)
    result = residual_two + root_mean_norm(vector_back, gain_vector)
    upstream = cotangent.astype(jnp.float32)
    d_vector_back, grad_gain_vector = norm_grad(vector_back, gain_vector, upstream)
    d_vector_back_low = d_vector_back.astype(jnp.bfloat16)
    grad_vector_out = product_rows(gated_low, d_vector_back_low)
    d_gated = product_back(d_vector_back_low, full_vector_out)
    d_vector_lin, d_vectors = gated_grad(vector_lin, vectors, d_gated)
    d_vector_lin_low = d_vector_lin.astype(jnp.bfloat16)
    grad_vector_gate = product_rows(residual_low, d_vector_lin_low)
    d_residual = upstream + product_back(d_vector_lin_low, full_vector_gate)
    d_feed, grad_gain_after = norm_grad(feed_value, gain_after, d_residual)
    d_feed_low = d_feed.astype(jnp.bfloat16)
    if shards == 8:
        d_ffn_in, d_rows_all, d_rows_far, d_gate_low, d_up_low = feed_call(
            False, d_feed_low, (hidden_down, hidden_gate, hidden_up), (lift_all, bend_all)
        )
    else:
        d_rows_all = gather(d_feed_low, "fsdp")
        d_hidden = product_back(d_rows_all, hidden_down)
        d_gate_all, d_up_all = gated_grad(gate_all, up_all, d_hidden)
        d_gate_low = d_gate_all.astype(jnp.bfloat16)
        d_up_low = d_up_all.astype(jnp.bfloat16)
        d_ffn_in = scatter_sum(
            matrix_product(d_gate_low, hidden_gate) + matrix_product(d_up_low, hidden_up)
        )

    if shards == 8 and gathered_plan:
        rows_far = gather(rows_far.reshape(-1, width), "fsdp")
        d_ffn_in, rows_far = lax.optimization_barrier((d_ffn_in, rows_far))
        d_rows_far = gather(d_rows_far.reshape(-1, width), "fsdp")
        grad_hidden_gate, grad_hidden_up, grad_hidden_down = weight_grad_call(
            hidden_gate,
            hidden_up,
            hidden_down,
            rows_all,
            d_rows_all,
            hidden_all,
            d_gate_low,
            d_up_low,
            rows_far,
            d_rows_far,
        )
    else:
        grad_hidden_gate, grad_hidden_up, grad_hidden_down = [
            lax.psum(grad.astype(jnp.bfloat16), "ctx").astype(jnp.float32)
            for grad in (
                product_rows(d_gate_low, rows_all),
                product_rows(d_up_low, rows_all),
                product_rows(hidden_all, d_rows_all),
            )
        ]

    d_mixed_part, grad_gain_before = norm_grad(mixed, gain_before, d_ffn_in)
    d_half = (d_residual + d_mixed_part) * inv_root
    d_laurel_lin, grad_gain_laurel = norm_grad(laurel_lin, gain_laurel, d_half)
    d_laurel_low = d_laurel_lin.astype(jnp.bfloat16)
    grad_laurel_up = product_rows(laurel_mid, d_laurel_low)
    d_laurel_mid = product_back(d_laurel_low, full_laurel_up).astype(jnp.bfloat16)
    d_attn_lin, grad_gain_attention = norm_grad(attn_lin, gain_attention, d_half)
    d_attn_low = d_attn_lin.astype(jnp.bfloat16)
    grad_output = product_rows(attended_slices, gather(d_attn_low, "fsdp"))
    small_rows = jnp.concatenate(
        [
            grad_vector_gate.reshape(shards, -1, width),
            grad_vector_out.reshape(shards, -1, width),
            grad_laurel_up.reshape(shards, -1, width),
        ],
        axis=1,
    ).astype(jnp.bfloat16)
    small_share = lax.psum_scatter(small_rows, "fsdp", scatter_dimension=0, tiled=False)

    d_attended = (
        product_back(d_attn_low, full_output)
        .astype(jnp.bfloat16)
        .reshape(count_of_rows, KEY_VALUE_HEADS, heads_per_group, HEAD_SIZE)
    )
    soft_again = jnp.exp(masked_scores() - log_total)
    d_soft = jnp.einsum(
        "tgfd,kgd->gftk", d_attended, window_values, preferred_element_type=jnp.float32
    )
    d_scores = (
        soft_again * (d_soft - jnp.sum(soft_again * d_soft, axis=-1, keepdims=True))
    ).astype(jnp.bfloat16)
    d_query = score_scale * jnp.einsum(
        "gftk,kgd->tgfd", d_scores, window_keys, preferred_element_type=jnp.float32
    )
    grad_key_rows = score_scale * jnp.einsum(
        "gftk,tgfd->kgd", d_scores, query_lowered, preferred_element_type=jnp.float32
    )
    grad_value_rows = jnp.einsum(
        "gftk,tgfd->kgd",
        soft_again.astype(jnp.bfloat16),
        d_attended,
        preferred_element_type=jnp.float32,
    )
    grad_window_couple = jnp.stack(
        [
            grad_key_rows.reshape(-1, KEY_VALUE_HEADS * HEAD_SIZE),
            grad_value_rows.reshape(-1, KEY_VALUE_HEADS * HEAD_SIZE),
        ]
    )
    grad_own_part = grad_window_couple[:, :count_of_rows]
    for distance in range(1, reach_blocks + 1):
        grad_own_part = grad_own_part + from_behind(
            grad_window_couple[:, distance * count_of_rows : (distance + 1) * count_of_rows].astype(
                jnp.bfloat16
            ),
            "ctx",
            -distance,
        ).astype(jnp.float32)
    unused, query_pull = jax.vjp(head_facing, query_linear, gain_query)
    d_query_lin, grad_gain_query = query_pull(
        d_query.reshape(count_of_rows, QUERY_HEADS, HEAD_SIZE)
    )
    unused, key_pullback_fn = jax.vjp(head_facing, key_linear, key_norm_gain)
    grad_key_linear, grad_key_norm_gain = key_pullback_fn(
        grad_own_part[0].reshape(count_of_rows, KEY_VALUE_HEADS, HEAD_SIZE)
    )
    d_inward = jnp.concatenate(
        [
            d_query_lin.reshape(count_of_rows, QUERY_HEADS * HEAD_SIZE).astype(jnp.bfloat16),
            grad_key_linear.reshape(count_of_rows, KEY_VALUE_HEADS * HEAD_SIZE).astype(
                jnp.bfloat16
            ),
            grad_own_part[1].astype(jnp.bfloat16),
            d_laurel_mid,
        ],
        axis=1,
    )
    grad_inward = product_rows(normed_slices, gather(d_inward, "fsdp"))
    d_normed = d_half + product_back(d_inward, full_inward)
    d_source_part, grad_gain_input = norm_grad(source, gain_input, d_normed)
    d_source = d_half + d_source_part

    gain_lines = jnp.concatenate(
        [
            grad.reshape(shards, -1)
            for grad in (
                grad_gain_input,
                grad_gain_attention,
                grad_gain_laurel,
                grad_gain_before,
                grad_gain_after,
                grad_gain_vector,
                grad_gain_query,
                grad_key_norm_gain,
            )
        ],
        axis=1,
    )
    gain_sums = gather(gather(gain_lines.reshape(-1, 128), "fsdp"), "ctx")
    gain_sums = jnp.sum(gain_sums.reshape(-1, *gain_lines.shape), axis=0)
    totals = lax.psum(
        jnp.concatenate(
            [
                grad_inward.astype(jnp.bfloat16).reshape(-1, 128),
                grad_output.astype(jnp.bfloat16).reshape(-1, 128),
                small_share.reshape(-1, 128),
            ],
            axis=0,
        ),
        "ctx",
    ).astype(jnp.float32)
    inward_lines = grad_inward.size // 128
    output_lines = grad_output.size // 128
    grad_inward = totals[:inward_lines].reshape(grad_inward.shape)
    grad_output = totals[inward_lines : inward_lines + output_lines].reshape(grad_output.shape)
    small_share = totals[inward_lines + output_lines :].reshape(small_share.shape)
    gate_rows = vector_gate.shape[0] * vector_gate.shape[1] // width
    out_rows = vector_out.shape[0]
    share_vector_gate = small_share[:gate_rows].reshape(vector_gate.shape)
    share_vector_out = small_share[gate_rows : gate_rows + out_rows]
    share_laurel_up = small_share[gate_rows + out_rows :]
    gain_share = lax.dynamic_index_in_dim(
        gain_sums, lax.axis_index("fsdp"), axis=0, keepdims=False
    )
    gain_grads = tuple(
        gain_share[start : start + size] for start, size in zip(gain_starts, gain_sizes)
    )
    value_start = query_width + key_width
    return (
        result.astype(jnp.bfloat16),
        d_source,
        d_vectors,
        grad_inward[:, :query_width],
        grad_inward[:, query_width:value_start],
        grad_inward[:, value_start : value_start + key_width],
        grad_output,
        grad_inward[:, value_start + key_width :],
        share_laurel_up,
        share_vector_gate,
        share_vector_out,
    ) + gain_grads + (
        grad_hidden_gate,
        grad_hidden_up,
        grad_hidden_down,
    )


def solution(mesh):
    rows = P(("fsdp", "ctx"), None)
    line = P(("fsdp", "ctx"))
    weight = P("fsdp", None)
    gain = P("fsdp")
    return jax.shard_map(
        per_device,
        mesh=mesh,
        in_specs=(rows, rows, line, line, rows) + (weight,) * 8 + (gain,) * 8 + (weight,) * 3,
        out_specs=(rows,) * 3 + (weight,) * 8 + (gain,) * 8 + (weight,) * 3,
        check_vma=False,
    )
```

```python
import functools

import jax
import jax.numpy as jnp
from jax import lax
from jax.experimental import pallas as pl
from jax.experimental.pallas import tpu as pltpu
from jax.sharding import PartitionSpec as P

QUERY_HEADS = 8
KEY_VALUE_HEADS = 2
HEAD_SIZE = 256
WINDOW = 1024


epsilon = 1e-06
rope_base = 10000.0
inv_root = 0.7071067811865476
gelu_scale = 0.7978845608028654
gelu_cubic = 0.044715


def from_behind(value, axis, steps):
    count = lax.axis_size(axis)
    initial, last = (max(0, -steps), min(count, count - steps))
    return lax.ppermute(value, axis, [(source, source + steps) for source in range(initial, last)])


def other_blocks(value, axis):
    count = lax.axis_size(axis)
    return jnp.concatenate(
        [
            lax.ppermute(value, axis, [(source, (source + step) % count) for source in range(count)])
            for step in range(1, count)
        ],
        axis=0,
    )


def root_mean_norm(value, gain):
    factor = lax.rsqrt(jnp.mean(value * value, axis=-1, keepdims=True) + epsilon)
    return value * factor * gain


def gelu_tanh(value):
    return jax.nn.gelu(value, approximate=True)


def gated(gate_value, up_value):
    return gelu_tanh(gate_value) * up_value


def rotary_apply(value, token_position):
    half_size = value.shape[-1] // 2
    frequency = rope_base ** (-2.0 * jnp.arange(half_size, dtype=jnp.float32) / value.shape[-1])
    angle = token_position.astype(jnp.float32)[:, None] * frequency[None, :]
    cosine = jnp.cos(angle)[:, None, :]
    sine_part = jnp.sin(angle)[:, None, :]
    first_half = value[..., :half_size]
    second_half = value[..., half_size:]
    return jnp.concatenate(
        [
            first_half * cosine - second_half * sine_part,
            second_half * cosine + first_half * sine_part,
        ],
        axis=-1,
    )


def rotary_tables(token_position, size):
    half_size = size // 2
    frequency = rope_base ** (-2.0 * jnp.arange(half_size, dtype=jnp.float32) / size)
    angle = token_position.astype(jnp.float32)[:, None] * frequency[None, :]
    return jnp.cos(angle), jnp.sin(angle)


def window(positions, rows_of, reach):
    key_offset = jnp.concatenate(
        [distance * rows_of - jnp.arange(rows_of, dtype=jnp.int32) for distance in range(reach + 1)]
    )
    key_gap = jnp.arange(rows_of, dtype=jnp.int32)[:, None] + key_offset[None, :]
    return key_gap, (key_gap >= 0) & (key_gap <= positions[:, None]) & (key_gap < WINDOW)


def matrix_product(left, right):
    return jnp.dot(left, right, preferred_element_type=jnp.float32)


def product_back(left, right):
    return lax.dot_general(
        left, right, (((1,), (1,)), ((), ())), preferred_element_type=jnp.float32
    )


def product_rows(left, right):
    return lax.dot_general(
        left, right, (((0,), (0,)), ((), ())), preferred_element_type=jnp.float32
    )


def norm_grad(value, gain, upstream):
    unused, pullback = jax.vjp(root_mean_norm, value, gain)
    return pullback(upstream)


def gated_grad(gate_value, up_value, upstream):
    unused, pullback = jax.vjp(gated, gate_value, up_value)
    return pullback(upstream)


def gather(value, axis):
    return lax.all_gather(value, axis, axis=0, tiled=True)


def feature_slices(value):
    count = lax.axis_size("fsdp")
    rows = value.shape[0]
    return lax.all_to_all(
        value.reshape(rows, count, -1), "fsdp", split_axis=1, concat_axis=0, tiled=True
    ).reshape(count * rows, -1)


def scatter_sum(value):
    return lax.psum_scatter(
        value.astype(jnp.bfloat16), "fsdp", scatter_dimension=0, tiled=True
    ).astype(jnp.float32)


def gelu_parts(gate):
    square = gate * gate
    bend = jnp.tanh(gelu_scale * gate * (1.0 + gelu_cubic * square))
    half_up = 0.5 * (1.0 + bend)
    slope = half_up + 0.5 * gate * (1.0 - bend * bend) * (
        gelu_scale * (1.0 + 3.0 * gelu_cubic * square)
    )
    return gate * half_up, slope


def across(me, stride):
    return me + stride - 2 * stride * ((me // stride) % 2)


def across_many(me, bits):
    for stride in (1, 2, 4):
        if bits & stride:
            me = across(me, stride)
    return me


def feed_kernel(forward, rows_of, others, *refs):
    half = rows_of // 2
    if forward:
        (own, gate_hbm, up_hbm, down_hbm, features, total, rows_hbm, far_hbm, slices_hbm, hidden_hbm, lift_hbm, bend_hbm), rest = refs[:12], refs[12:]
        weights_hbm, kept_hbm, made_hbm = (gate_hbm, up_hbm, down_hbm), (), (hidden_hbm, lift_hbm, bend_hbm)
    else:
        (own, down_hbm, gate_hbm, up_hbm, lift_hbm, bend_hbm, total, rows_hbm, far_hbm, d_gate_hbm, d_up_hbm), rest = refs[:11], refs[11:]
        weights_hbm, kept_hbm, made_hbm = (down_hbm, gate_hbm, up_hbm), (lift_hbm, bend_hbm), (d_gate_hbm, d_up_hbm)
    count_kept, count_made = len(kept_hbm), len(made_hbm)
    weights = rest[:3]
    kept = rest[3 : 3 + count_kept]
    made = rest[3 + count_kept : 3 + count_kept + count_made]
    (rows, part, sib_in, chip_sum, relay_in, relay_sum, last_in, send_sem, recv_sem, in_sem, out_sem, far_send, far_recv, *slice_sems) = rest[
        3 + count_kept + count_made :
    ]
    hidden = weights[0].shape[0]
    width = own.shape[1]
    me = lax.axis_index("fsdp")
    sibling, beside, above = across(me, 1), across(me, 2), across(me, 4)

    loads = [
        pltpu.make_async_copy(source, target, in_sem.at[index])
        for index, (source, target) in enumerate(zip(weights_hbm + kept_hbm, tuple(weights) + tuple(kept)))
    ]
    for load in loads:
        load.start()

    block = lax.axis_index("ctx")
    partners = range(1, 8) if forward else (1, 2, 4)
    barrier = pltpu.get_barrier_semaphore()
    for distance in partners:
        partner = across_many(me, distance)
        pl.semaphore_signal(barrier, inc=1, device_id={"fsdp": partner}, device_id_type=pl.DeviceIdType.MESH)
    for distance in range(1, others + 1):
        partner = (block + distance) % (others + 1)
        pl.semaphore_signal(barrier, inc=1, device_id={"ctx": partner}, device_id_type=pl.DeviceIdType.MESH)
    pl.semaphore_wait(barrier, len(partners) + others)

    def send(index, source, target, partner):
        return pltpu.make_async_remote_copy(
            src_ref=source,
            dst_ref=target,
            send_sem=send_sem.at[index],
            recv_sem=recv_sem.at[index],
            device_id={"fsdp": partner},
            device_id_type=pl.DeviceIdType.MESH,
        )

    low, high = pl.ds(0, half), pl.ds(half, half)
    mine, theirs = pl.ds(0, rows_of), pl.ds(rows_of, rows_of)
    copies = [
        send(0, own, rows.at[0, theirs], sibling),
        send(1, own.at[low], rows.at[1, low], beside),
        send(2, own.at[low], rows.at[1, high], above),
        send(3, own.at[high], rows.at[2, low], beside),
        send(4, own.at[high], rows.at[2, high], above),
        send(5, rows.at[1, mine], rows.at[1, theirs], sibling),
        send(6, rows.at[2, mine], rows.at[2, theirs], sibling),
        send(7, rows.at[1, low], rows.at[3, low], above),
        send(8, rows.at[2, high], rows.at[3, high], beside),
        send(9, rows.at[3, mine], rows.at[3, theirs], sibling),
        send(10, part.at[0, theirs], sib_in.at[0], sibling),
        send(11, part.at[1, theirs], sib_in.at[1], sibling),
        send(12, part.at[2, theirs], sib_in.at[2], sibling),
        send(13, part.at[3, theirs], sib_in.at[3], sibling),
        send(14, chip_sum.at[0, high], last_in.at[2], above),
        send(15, chip_sum.at[1, low], last_in.at[1], beside),
        send(16, chip_sum.at[2, low], relay_in.at[0], above),
        send(17, chip_sum.at[2, high], relay_in.at[1], beside),
        send(18, relay_sum.at[0], last_in.at[0], beside),
        send(19, relay_sum.at[1], last_in.at[3], above),
    ]
    outs = []

    def write_out(source, target):
        copy = pltpu.make_async_copy(source, target, out_sem.at[len(outs)])
        copy.start()
        outs.append(copy)

    for index in range(5):
        copies[index].start()
    far = [
        pltpu.make_async_remote_copy(
            src_ref=own,
            dst_ref=far_hbm.at[distance - 1],
            send_sem=far_send.at[distance - 1],
            recv_sem=far_recv.at[distance - 1],
            device_id={"ctx": (block + distance) % (others + 1)},
            device_id_type=pl.DeviceIdType.MESH,
        )
        for distance in range(1, others + 1)
    ]
    for copy in far:
        copy.start()
    rows[0, mine] = own[...]
    slices = []
    if forward:
        share = features.shape[1] // 8

        def share_of(device):
            return features.at[:, pl.ds(pl.multiple_of(device * share, share), share)]

        own_slice = pltpu.make_async_copy(share_of(me), slices_hbm.at[me], slice_sems[2])
        own_slice.start()
        slices = [
            pltpu.make_async_remote_copy(
                src_ref=share_of(across_many(me, distance)),
                dst_ref=slices_hbm.at[me],
                send_sem=slice_sems[0].at[distance - 1],
                recv_sem=slice_sems[1].at[distance - 1],
                device_id={"fsdp": across_many(me, distance)},
                device_id_type=pl.DeviceIdType.MESH,
            )
            for distance in range(1, 8)
        ]

    tile = min(hidden, 1024)
    wide = min(width, 1024)

    def first_stage(group):
        span = pl.ds(group * 2 * rows_of, 2 * rows_of)

        def step(index, carry):
            columns = pl.ds(pl.multiple_of(index * tile, tile), tile)
            left = rows[group]

            def back(weight):
                return lax.dot_general(
                    left, weight[columns, :], (((1,), (1,)), ((), ())), preferred_element_type=jnp.float32
                )

            if forward:
                gate, up = back(weights[0]), back(weights[1])
                value, slope = gelu_parts(gate)
                made[0][span, columns] = (value * up).astype(jnp.bfloat16)
                made[1][span, columns] = value.astype(jnp.bfloat16)
                made[2][span, columns] = (slope * up).astype(jnp.bfloat16)
            else:
                d_hidden = back(weights[0])
                made[0][span, columns] = (d_hidden * kept[1][span, columns].astype(jnp.float32)).astype(jnp.bfloat16)
                made[1][span, columns] = (d_hidden * kept[0][span, columns].astype(jnp.float32)).astype(jnp.bfloat16)
            return carry

        lax.fori_loop(0, hidden // tile, step, 0)

    def second_stage(group):
        span = pl.ds(group * 2 * rows_of, 2 * rows_of)

        def step(index, carry):
            columns = pl.ds(pl.multiple_of(index * wide, wide), wide)
            if forward:
                value = jnp.dot(made[0][span, :], weights[2][:, columns], preferred_element_type=jnp.float32)
            else:
                value = jnp.dot(made[0][span, :], weights[1][:, columns], preferred_element_type=jnp.float32)
                value = value + jnp.dot(made[1][span, :], weights[2][:, columns], preferred_element_type=jnp.float32)
            part[group, :, columns] = value.astype(jnp.bfloat16)
            return carry

        lax.fori_loop(0, width // wide, step, 0)

    def keep_out(group):
        span = pl.ds(group * 2 * rows_of, 2 * rows_of)
        write_out(rows.at[group], rows_hbm.at[span])
        for source, target in zip(made, made_hbm):
            write_out(source.at[span], target.at[span])

    def add_chip(group):
        chip_sum[group - 1] = (
            part[group, mine].astype(jnp.float32) + sib_in[group].astype(jnp.float32)
        ).astype(jnp.bfloat16)

    copies[0].wait_recv()
    loads[0].wait()
    if forward:
        loads[1].wait()
    else:
        loads[3].wait()
        loads[4].wait()
    first_stage(0)
    if forward:
        loads[2].wait()
    else:
        loads[1].wait()
        loads[2].wait()
    second_stage(0)
    copies[10].start()
    keep_out(0)
    copies[1].wait_recv()
    copies[7].start()
    copies[2].wait_recv()
    copies[5].start()
    copies[5].wait_recv()
    first_stage(1)
    second_stage(1)
    copies[11].start()
    keep_out(1)
    copies[3].wait_recv()
    copies[4].wait_recv()
    copies[8].start()
    copies[6].start()
    copies[11].wait_recv()
    add_chip(1)
    copies[14].start()
    copies[6].wait_recv()
    first_stage(2)
    second_stage(2)
    copies[12].start()
    keep_out(2)
    for copy in slices:
        copy.start()
    copies[7].wait_recv()
    copies[8].wait_recv()
    copies[9].start()
    copies[12].wait_recv()
    add_chip(2)
    copies[15].start()
    copies[9].wait_recv()
    first_stage(3)
    second_stage(3)
    copies[13].start()
    keep_out(3)
    copies[13].wait_recv()
    add_chip(3)
    copies[16].start()
    copies[17].start()
    copies[10].wait_recv()
    total[...] = part[0, mine].astype(jnp.float32) + sib_in[0].astype(jnp.float32)
    copies[16].wait_recv()
    relay_sum[0] = (chip_sum[0, low].astype(jnp.float32) + relay_in[0].astype(jnp.float32)).astype(jnp.bfloat16)
    copies[18].start()
    copies[17].wait_recv()
    relay_sum[1] = (chip_sum[1, high].astype(jnp.float32) + relay_in[1].astype(jnp.float32)).astype(jnp.bfloat16)
    copies[19].start()
    copies[14].wait_recv()
    total[low] = total[low] + last_in[2].astype(jnp.float32)
    copies[15].wait_recv()
    total[high] = total[high] + last_in[1].astype(jnp.float32)
    copies[18].wait_recv()
    total[low] = total[low] + last_in[0].astype(jnp.float32)
    copies[19].wait_recv()
    total[high] = total[high] + last_in[3].astype(jnp.float32)
    for copy in copies:
        copy.wait_send()
    for copy in outs:
        copy.wait()
    for copy in far + slices:
        copy.wait()
    if forward:
        own_slice.wait()


def turn(value, cosine, sine, direction=1.0):
    middle = value.shape[1] // 2
    first, second = value[:, :middle], value[:, middle:]
    sine = sine * direction
    return jnp.concatenate([first * cosine - second * sine, second * cosine + first * sine], axis=1)


def window_mask(positions, rows_of, blocks):
    query_row = lax.broadcasted_iota(jnp.int32, (rows_of, blocks * rows_of), 0)
    column = lax.broadcasted_iota(jnp.int32, (rows_of, blocks * rows_of), 1)
    behind = column // rows_of
    gap = query_row + 2 * behind * rows_of - column
    return (gap >= 0) & (gap <= positions) & (gap < WINDOW)


def greet(me, partners, block, others):
    barrier = pltpu.get_barrier_semaphore()
    for distance in partners:
        pl.semaphore_signal(
            barrier, inc=1, device_id={"fsdp": across_many(me, distance)}, device_id_type=pl.DeviceIdType.MESH
        )
    for distance in range(1, others + 1):
        pl.semaphore_signal(
            barrier,
            inc=1,
            device_id={"ctx": (block + distance) % (others + 1)},
            device_id_type=pl.DeviceIdType.MESH,
        )
    pl.semaphore_wait(barrier, len(partners) + others)


def push(source, target, send_sem, recv_sem, place):
    return pltpu.make_async_remote_copy(
        src_ref=source,
        dst_ref=target,
        send_sem=send_sem,
        recv_sem=recv_sem,
        device_id=place,
        device_id_type=pl.DeviceIdType.MESH,
    )


def spread_copies(own, slots, send_sem, recv_sem, me):
    half = own.shape[0] // 2
    low, high = pl.ds(0, half), pl.ds(half, half)
    sibling, beside, above = across(me, 1), across(me, 2), across(me, 4)
    plan = [
        (own, slots.at[1], sibling),
        (own.at[low], slots.at[2, low], beside),
        (own.at[low], slots.at[4, low], above),
        (own.at[high], slots.at[2, high], beside),
        (own.at[high], slots.at[4, high], above),
        (slots.at[2, low], slots.at[3, low], sibling),
        (slots.at[4, low], slots.at[5, low], sibling),
        (slots.at[2, high], slots.at[3, high], sibling),
        (slots.at[4, high], slots.at[5, high], sibling),
        (slots.at[2, low], slots.at[6, low], above),
        (slots.at[4, high], slots.at[6, high], beside),
        (slots.at[6, low], slots.at[7, low], sibling),
        (slots.at[6, high], slots.at[7, high], sibling),
    ]
    return [
        push(source, target, send_sem.at[index], recv_sem.at[index], {"fsdp": partner})
        for index, (source, target, partner) in enumerate(plan)
    ]


def attend_kernel(
    others, reach, source, gain_lines, positions, cosine, sine, inward_own, outward_own,
    normed, normed_low, gains, linear, query_low, key_value, attended, middle, attn_lin, inward_all, outward_all,
    gain_slots, inward_slots, outward_slots, inward, lin_sum,
    gain_send, gain_recv, in_send, in_recv, out_send, out_recv, kv_send, kv_recv, in_copy, out_copy,
):
    rows_of, width = source.shape
    me, block = lax.axis_index("fsdp"), lax.axis_index("ctx")
    greet(me, range(1, 8), block, others)
    gain_copies = [
        push(gain_lines, gain_slots.at[distance], gain_send.at[distance - 1], gain_recv.at[distance - 1],
             {"fsdp": across_many(me, distance)})
        for distance in range(1, 8)
    ]
    for copy in gain_copies:
        copy.start()
    spread_in = spread_copies(inward_own, inward_slots, in_send, in_recv, me)
    spread_out = spread_copies(outward_own, outward_slots, out_send, out_recv, me)
    for index in range(5):
        spread_in[index].start()
    inward_slots[0] = inward_own[...]
    outward_slots[0] = outward_own[...]

    value = source[...].astype(jnp.float32)
    factor = lax.rsqrt(jnp.mean(value * value, axis=-1, keepdims=True) + epsilon)
    for copy in gain_copies:
        copy.wait_recv()
    gain_slots[0] = gain_lines[...]
    gains[...] = jnp.sum(gain_slots[...].astype(jnp.float32), axis=0)
    value = value * factor * gains[0:1, :]
    normed[...] = value
    normed_low[...] = value.astype(jnp.bfloat16)

    depth = inward_own.shape[0]
    head_rows = width // 8
    written = []

    def add_inward(slot):
        device = across_many(me, slot)
        part = normed_low[:, pl.ds(pl.multiple_of(device * depth, depth), depth)]
        for start in range(0, inward.shape[1], 640):
            span = pl.ds(start, 640)
            product = jnp.dot(part, inward_slots[slot, :, span], preferred_element_type=jnp.float32)
            inward[:, span] = product if slot == 0 else inward[:, span] + product
        copy = pltpu.make_async_copy(
            inward_slots.at[slot], inward_all.at[pl.ds(pl.multiple_of(device * depth, depth), depth)], in_copy.at[slot]
        )
        copy.start()
        written.append(copy)

    def add_outward(slot):
        device = across_many(me, slot)
        part = attended[:, pl.ds(pl.multiple_of(device * head_rows, head_rows), head_rows)]
        for start in range(0, width, 512):
            span = pl.ds(start, 512)
            product = jnp.dot(part, outward_slots[slot, pl.ds(0, head_rows), span], preferred_element_type=jnp.float32)
            lin_sum[:, span] = product if slot == 0 else lin_sum[:, span] + product

    def write_outward(slot):
        copy = pltpu.make_async_copy(
            outward_slots.at[slot], outward_all.at[across_many(me, slot)], out_copy.at[slot]
        )
        copy.start()
        written.append(copy)

    add_inward(0)
    spread_in[0].wait_recv()
    add_inward(1)
    spread_in[1].wait_recv()
    spread_in[9].start()
    spread_in[5].start()
    spread_in[2].wait_recv()
    spread_in[6].start()
    spread_in[3].wait_recv()
    spread_in[7].start()
    spread_in[4].wait_recv()
    spread_in[10].start()
    spread_in[8].start()
    add_inward(2)
    add_inward(4)
    spread_in[5].wait_recv()
    spread_in[7].wait_recv()
    add_inward(3)
    spread_in[6].wait_recv()
    spread_in[8].wait_recv()
    add_inward(5)
    spread_in[9].wait_recv()
    spread_in[11].start()
    spread_in[10].wait_recv()
    spread_in[12].start()
    for index in range(5):
        spread_out[index].start()
    add_inward(6)
    spread_in[11].wait_recv()
    spread_in[12].wait_recv()
    add_inward(7)

    query_width, key_width = QUERY_HEADS * HEAD_SIZE, KEY_VALUE_HEADS * HEAD_SIZE
    own_rows = pl.ds(0, rows_of)

    def head(start, gain):
        lane = inward[:, pl.ds(start, HEAD_SIZE)]
        scale = lax.rsqrt(jnp.mean(lane * lane, axis=-1, keepdims=True) + epsilon)
        return turn(lane * scale * gain, cosine[...], sine[...]).astype(jnp.bfloat16)

    for index in range(KEY_VALUE_HEADS):
        key_value[own_rows, pl.ds(index * HEAD_SIZE, HEAD_SIZE)] = head(
            query_width + index * HEAD_SIZE, gains[7:8, 0:HEAD_SIZE]
        )
    key_value[own_rows, pl.ds(key_width, key_width)] = inward[:, pl.ds(query_width + key_width, key_width)].astype(
        jnp.bfloat16
    )
    for distance in range(1, reach + 1):
        copy = push(
            key_value.at[own_rows],
            key_value.at[pl.ds(distance * rows_of, rows_of)],
            kv_send.at[distance - 1],
            kv_recv.at[distance - 1],
            {"ctx": (block + distance) % (others + 1)},
        )

        @pl.when(block + distance <= others)
        def _():
            copy.start()

        @pl.when(block < distance)
        def _():
            key_value[pl.ds(distance * rows_of, rows_of), :] = jnp.zeros((rows_of, 2 * key_width), jnp.bfloat16)

    for index in range(QUERY_HEADS):
        query_low[:, pl.ds(index * HEAD_SIZE, HEAD_SIZE)] = head(index * HEAD_SIZE, gains[6:7, 0:HEAD_SIZE])
    linear[...] = inward[:, pl.ds(0, query_width + key_width)]
    middle[...] = inward[:, pl.ds(query_width + 2 * key_width, middle.shape[1])].astype(jnp.bfloat16)

    spread_out[0].wait_recv()
    spread_out[1].wait_recv()
    spread_out[9].start()
    spread_out[5].start()
    spread_out[2].wait_recv()
    spread_out[6].start()
    for distance in range(1, reach + 1):
        copy = push(
            key_value.at[own_rows],
            key_value.at[pl.ds(distance * rows_of, rows_of)],
            kv_send.at[distance - 1],
            kv_recv.at[distance - 1],
            {"ctx": (block + distance) % (others + 1)},
        )

        @pl.when(block >= distance)
        def _():
            copy.wait_recv()

    allowed = window_mask(positions[...], rows_of, reach + 1)
    per_group = QUERY_HEADS // KEY_VALUE_HEADS
    for index in range(QUERY_HEADS):
        group = index // per_group
        columns = pl.ds(index * HEAD_SIZE, HEAD_SIZE)
        scores = product_back(query_low[:, columns], key_value[:, pl.ds(group * HEAD_SIZE, HEAD_SIZE)])
        scores = jnp.where(allowed, scores * HEAD_SIZE ** (-0.5), -1e30)
        grown = jnp.exp(scores - jnp.max(scores, axis=-1, keepdims=True))
        soft = (grown / jnp.sum(grown, axis=-1, keepdims=True)).astype(jnp.bfloat16)
        attended[:, columns] = jnp.dot(
            soft, key_value[:, pl.ds(key_width + group * HEAD_SIZE, HEAD_SIZE)], preferred_element_type=jnp.float32
        ).astype(jnp.bfloat16)

    add_outward(0)
    add_outward(1)
    write_outward(0)
    write_outward(1)
    spread_out[3].wait_recv()
    spread_out[7].start()
    spread_out[4].wait_recv()
    spread_out[10].start()
    spread_out[8].start()
    add_outward(2)
    add_outward(4)
    spread_out[5].wait_recv()
    spread_out[7].wait_recv()
    add_outward(3)
    spread_out[6].wait_recv()
    spread_out[8].wait_recv()
    add_outward(5)
    for slot in range(2, 6):
        write_outward(slot)
    spread_out[9].wait_recv()
    spread_out[11].start()
    spread_out[10].wait_recv()
    spread_out[12].start()
    add_outward(6)
    write_outward(6)
    spread_out[11].wait_recv()
    spread_out[12].wait_recv()
    add_outward(7)
    write_outward(7)
    attn_lin[...] = lin_sum[...]
    for copy in gain_copies + spread_in + spread_out:
        copy.wait_send()
    for copy in written:
        copy.wait()
    for distance in range(1, reach + 1):
        copy = push(
            key_value.at[own_rows],
            key_value.at[pl.ds(distance * rows_of, rows_of)],
            kv_send.at[distance - 1],
            kv_recv.at[distance - 1],
            {"ctx": (block + distance) % (others + 1)},
        )

        @pl.when(block + distance <= others)
        def _():
            copy.wait_send()


def attend_call(reach, source, gain_lines, positions, cosine, sine, inward_own, outward_own):
    rows_of, width = source.shape
    others = lax.axis_size("ctx") - 1
    low, full = jnp.bfloat16, jnp.float32
    hbm = pl.BlockSpec(memory_space=pl.ANY)
    vmem = pl.BlockSpec(memory_space=pltpu.VMEM)
    dma = pltpu.SemaphoreType.DMA
    depth, columns = inward_own.shape
    query_width, key_width = QUERY_HEADS * HEAD_SIZE, KEY_VALUE_HEADS * HEAD_SIZE
    tail = columns - query_width - 2 * key_width
    shapes = [
        jax.ShapeDtypeStruct((rows_of, width), full),
        jax.ShapeDtypeStruct((rows_of, width), low),
        jax.ShapeDtypeStruct(gain_lines.shape, full),
        jax.ShapeDtypeStruct((rows_of, query_width + key_width), full),
        jax.ShapeDtypeStruct((rows_of, query_width), low),
        jax.ShapeDtypeStruct(((reach + 1) * rows_of, 2 * key_width), low),
        jax.ShapeDtypeStruct((rows_of, query_width), low),
        jax.ShapeDtypeStruct((rows_of, tail), low),
        jax.ShapeDtypeStruct((rows_of, width), full),
        jax.ShapeDtypeStruct((8 * depth, columns), low),
        jax.ShapeDtypeStruct((8, *outward_own.shape), low),
    ]
    return pl.pallas_call(
        functools.partial(attend_kernel, others, reach),
        out_shape=shapes,
        in_specs=[vmem] * 7,
        out_specs=[vmem] * 9 + [hbm] * 2,
        scratch_shapes=[
            pltpu.VMEM((8, *gain_lines.shape), low),
            pltpu.VMEM((8, depth, columns), low),
            pltpu.VMEM((8, *outward_own.shape), low),
            pltpu.VMEM((rows_of, columns), full),
            pltpu.VMEM((rows_of, width), full),
            dma((7,)),
            dma((7,)),
            dma((13,)),
            dma((13,)),
            dma((13,)),
            dma((13,)),
            dma((max(reach, 1),)),
            dma((max(reach, 1),)),
            dma((8,)),
            dma((8,)),
        ],
        compiler_params=pltpu.CompilerParams(collective_id=3, has_side_effects=True, vmem_limit_bytes=56 * 2**20),
        cost_estimate=pl.CostEstimate(
            flops=60 * rows_of * width * columns, bytes_accessed=20 * depth * columns, transcendentals=0
        ),
        name="attend_forward",
    )(source, gain_lines, positions, cosine, sine, inward_own, outward_own)


def turn_norm_grad(upstream, linear, gain, cosine, sine):
    scale = lax.rsqrt(jnp.mean(linear * linear, axis=-1, keepdims=True) + epsilon)
    unit = linear * scale
    back = turn(upstream, cosine, sine, -1.0)
    grad_gain = jnp.sum(back * unit, axis=0, keepdims=True)
    back = back * gain
    return scale * (back - unit * jnp.mean(back * unit, axis=-1, keepdims=True)), grad_gain


def attend_back_kernel(
    others, reach, d_lin, query_low, key_value, linear, gains, positions, cosine, sine, d_middle, features,
    source, d_half, gain_rows, outward_all, inward_all,
    d_source, grad_inward, grad_output, grad_gains,
    outward, inward, d_attended, d_key_value, parcel, arrived, d_query, d_rest, lin_slots, query_slots, rest_slots,
    ordered, d_normed, gain_parcel, gain_arrived, load_sem, lin_send, lin_recv, query_send, query_recv, rest_send, rest_recv, kv_send, kv_recv, gain_send, gain_recv,
):
    rows_of, width = d_lin.shape
    me, block = lax.axis_index("fsdp"), lax.axis_index("ctx")
    query_width, key_width = QUERY_HEADS * HEAD_SIZE, KEY_VALUE_HEADS * HEAD_SIZE
    per_group = QUERY_HEADS // KEY_VALUE_HEADS
    depth = width // 8
    loads = [
        pltpu.make_async_copy(outward_all.at[index, pl.ds(0, depth)], outward.at[index], load_sem.at[index])
        for index in range(8)
    ]
    loads.append(pltpu.make_async_copy(inward_all, inward, load_sem.at[8]))
    for load in loads:
        load.start()
    greet(me, range(1, 8), block, others)
    spread_lin = spread_copies(d_lin, lin_slots, lin_send, lin_recv, me)
    spread_query = spread_copies(d_query, query_slots, query_send, query_recv, me)
    spread_rest = spread_copies(d_rest, rest_slots, rest_send, rest_recv, me)
    for index in range(5):
        spread_lin[index].start()
    lin_slots[0] = d_lin[...]
    for slot in range(8):
        device = across_many(me, slot)
        ordered[pl.ds(slot * rows_of, rows_of), :] = features[
            pl.ds(pl.multiple_of(device * rows_of, rows_of), rows_of), :
        ]
    for index in range(8):
        loads[index].wait()
        d_attended[:, pl.ds(index * depth, depth)] = product_back(d_lin[...], outward[index]).astype(jnp.bfloat16)

    allowed = window_mask(positions[...], rows_of, reach + 1)
    scale = HEAD_SIZE ** (-0.5)

    def one_head(index):
        group = index // per_group
        columns = pl.ds(index * HEAD_SIZE, HEAD_SIZE)
        keys = pl.ds(group * HEAD_SIZE, HEAD_SIZE)
        values = pl.ds(key_width + group * HEAD_SIZE, HEAD_SIZE)
        scores = product_back(query_low[:, columns], key_value[:, keys])
        scores = jnp.where(allowed, scores * scale, -1e30)
        grown = jnp.exp(scores - jnp.max(scores, axis=-1, keepdims=True))
        soft = grown / jnp.sum(grown, axis=-1, keepdims=True)
        d_soft = product_back(d_attended[:, columns], key_value[:, values])
        d_scores = (soft * (d_soft - jnp.sum(soft * d_soft, axis=-1, keepdims=True))).astype(jnp.bfloat16)
        upstream = scale * jnp.dot(d_scores, key_value[:, keys], preferred_element_type=jnp.float32)
        d_key = scale * product_rows(d_scores, query_low[:, columns])
        d_value = product_rows(soft.astype(jnp.bfloat16), d_attended[:, columns])
        if index % per_group == 0:
            d_key_value[:, keys] = d_key
            d_key_value[:, values] = d_value
        else:
            d_key_value[:, keys] += d_key
            d_key_value[:, values] += d_value
        d_head, grad_gain = turn_norm_grad(upstream, linear[:, columns], gains[6:7, 0:HEAD_SIZE], cosine[...], sine[...])
        d_query[:, columns] = d_head.astype(jnp.bfloat16)
        return grad_gain

    query_gain = one_head(0)
    for index in range(1, per_group):
        query_gain = query_gain + one_head(index)
    spread_lin[0].wait_recv()
    spread_lin[1].wait_recv()
    spread_lin[9].start()
    spread_lin[5].start()
    spread_lin[2].wait_recv()
    spread_lin[6].start()
    for index in range(per_group, QUERY_HEADS):
        query_gain = query_gain + one_head(index)
    parcel[...] = d_key_value[pl.ds(rows_of, reach * rows_of), :].astype(jnp.bfloat16)

    def return_copy(distance):
        span = pl.ds((distance - 1) * rows_of, rows_of)
        return push(
            parcel.at[span],
            arrived.at[span],
            kv_send.at[distance - 1],
            kv_recv.at[distance - 1],
            {"ctx": (block + others + 1 - distance) % (others + 1)},
        )

    for distance in range(1, reach + 1):
        copy = return_copy(distance)

        @pl.when(block >= distance)
        def _():
            copy.start()

        @pl.when(block + distance > others)
        def _():
            arrived[pl.ds((distance - 1) * rows_of, rows_of), :] = jnp.zeros((rows_of, 2 * key_width), jnp.bfloat16)

    spread_lin[3].wait_recv()
    spread_lin[7].start()
    spread_lin[4].wait_recv()
    spread_lin[10].start()
    spread_lin[8].start()
    for index in range(5):
        spread_query[index].start()
    query_slots[0] = d_query[...]
    loads[8].wait()
    d_normed[...] = product_back(d_query[...], inward[:, pl.ds(0, query_width)])
    spread_lin[9].wait_recv()
    spread_lin[11].start()
    spread_lin[10].wait_recv()
    spread_lin[12].start()
    spread_query[0].wait_recv()
    spread_query[1].wait_recv()
    spread_query[9].start()
    spread_query[5].start()
    spread_query[2].wait_recv()
    spread_query[6].start()
    for index in (5, 6, 7, 8, 11, 12):
        spread_lin[index].wait_recv()
    grad_output[...] = product_rows(
        ordered[:, pl.ds(depth, depth)], lin_slots[...].reshape(8 * rows_of, width)
    ).astype(jnp.bfloat16)

    for distance in range(1, reach + 1):
        copy = return_copy(distance)

        @pl.when(block + distance <= others)
        def _():
            copy.wait_recv()

    total = d_key_value[pl.ds(0, rows_of), :]
    for distance in range(1, reach + 1):
        total = total + arrived[pl.ds((distance - 1) * rows_of, rows_of), :].astype(jnp.float32)
    for index in range(KEY_VALUE_HEADS):
        columns = pl.ds(index * HEAD_SIZE, HEAD_SIZE)
        d_head, grad_gain = turn_norm_grad(
            total[:, index * HEAD_SIZE : (index + 1) * HEAD_SIZE],
            linear[:, pl.ds(query_width + index * HEAD_SIZE, HEAD_SIZE)],
            gains[7:8, 0:HEAD_SIZE],
            cosine[...],
            sine[...],
        )
        d_rest[:, columns] = d_head.astype(jnp.bfloat16)
        key_gain = grad_gain if index == 0 else key_gain + grad_gain
    d_rest[:, pl.ds(key_width, key_width)] = total[:, key_width:].astype(jnp.bfloat16)
    d_rest[:, pl.ds(2 * key_width, d_middle.shape[1])] = d_middle[...]
    spread_query[3].wait_recv()
    spread_query[7].start()
    spread_query[4].wait_recv()
    spread_query[10].start()
    spread_query[8].start()
    for index in range(5):
        spread_rest[index].start()
    rest_slots[0] = d_rest[...]
    rest_width = d_rest.shape[1]
    d_normed[...] += product_back(d_rest[...], inward[:, pl.ds(query_width, rest_width)])
    value = source[...].astype(jnp.float32)
    factor = lax.rsqrt(jnp.mean(value * value, axis=-1, keepdims=True) + epsilon)
    unit = value * factor
    upstream = d_half[...] + d_normed[...]
    for index in range(8):
        columns = slice(index * depth, (index + 1) * depth)
        gain_parcel[index, 0:8, :] = gain_rows[0:8, columns]
        gain_parcel[index, 0:1, :] = jnp.sum(upstream[:, columns] * unit[:, columns], axis=0, keepdims=True)
        gain_parcel[index, 6:7, :] = query_gain
        gain_parcel[index, 7:8, :] = key_gain
    gain_copies = [
        push(
            gain_parcel.at[across_many(me, distance)],
            gain_arrived.at[distance],
            gain_send.at[distance - 1],
            gain_recv.at[distance - 1],
            {"fsdp": across_many(me, distance)},
        )
        for distance in range(1, 8)
    ]
    for copy in gain_copies:
        copy.start()
    gain_arrived[0] = gain_parcel[me]
    upstream = upstream * gains[0:1, :]
    d_source[...] = d_half[...] + factor * (upstream - unit * jnp.mean(upstream * unit, axis=-1, keepdims=True))
    spread_rest[0].wait_recv()
    spread_rest[1].wait_recv()
    spread_rest[9].start()
    spread_rest[5].start()
    spread_rest[2].wait_recv()
    spread_rest[6].start()
    spread_query[9].wait_recv()
    spread_query[11].start()
    spread_query[10].wait_recv()
    spread_query[12].start()
    spread_rest[3].wait_recv()
    spread_rest[7].start()
    spread_rest[4].wait_recv()
    spread_rest[10].start()
    spread_rest[8].start()
    for index in (5, 6, 7, 8, 11, 12):
        spread_query[index].wait_recv()
    grad_inward[:, pl.ds(0, query_width)] = product_rows(
        ordered[:, pl.ds(0, depth)], query_slots[...].reshape(8 * rows_of, query_width)
    ).astype(jnp.bfloat16)
    spread_rest[9].wait_recv()
    spread_rest[11].start()
    spread_rest[10].wait_recv()
    spread_rest[12].start()
    for index in (5, 6, 7, 8, 11, 12):
        spread_rest[index].wait_recv()
    grad_inward[:, pl.ds(query_width, rest_width)] = product_rows(
        ordered[:, pl.ds(0, depth)], rest_slots[...].reshape(8 * rows_of, rest_width)
    ).astype(jnp.bfloat16)
    for copy in gain_copies:
        copy.wait_recv()
    grad_gains[...] = jnp.sum(gain_arrived[...], axis=0)
    for copy in spread_lin + spread_query + spread_rest + gain_copies:
        copy.wait_send()
    for distance in range(1, reach + 1):
        copy = return_copy(distance)

        @pl.when(block >= distance)
        def _():
            copy.wait_send()


def attend_back_call(
    reach, d_lin, query_low, key_value, linear, gains, positions, cosine, sine, d_middle, features,
    source, d_half, gain_rows, outward_all, inward_all,
):
    rows_of, width = d_lin.shape
    others = lax.axis_size("ctx") - 1
    low, full = jnp.bfloat16, jnp.float32
    hbm = pl.BlockSpec(memory_space=pl.ANY)
    vmem = pl.BlockSpec(memory_space=pltpu.VMEM)
    dma = pltpu.SemaphoreType.DMA
    columns = inward_all.shape[1]
    query_width, key_width = QUERY_HEADS * HEAD_SIZE, KEY_VALUE_HEADS * HEAD_SIZE
    rest_width = columns - query_width
    depth = width // 8
    shapes = [
        jax.ShapeDtypeStruct((rows_of, width), full),
        jax.ShapeDtypeStruct((depth, columns), low),
        jax.ShapeDtypeStruct((depth, width), low),
        jax.ShapeDtypeStruct((8, depth), full),
    ]
    spans = max(reach, 1)
    return pl.pallas_call(
        functools.partial(attend_back_kernel, others, reach),
        out_shape=shapes,
        in_specs=[vmem] * 13 + [hbm] * 2,
        out_specs=[vmem] * 4,
        scratch_shapes=[
            pltpu.VMEM((8, depth, width), low),
            pltpu.VMEM((width, columns), low),
            pltpu.VMEM((rows_of, query_width), low),
            pltpu.VMEM(((reach + 1) * rows_of, 2 * key_width), full),
            pltpu.VMEM((spans * rows_of, 2 * key_width), low),
            pltpu.VMEM((spans * rows_of, 2 * key_width), low),
            pltpu.VMEM((rows_of, query_width), low),
            pltpu.VMEM((rows_of, rest_width), low),
            pltpu.VMEM((8, rows_of, width), low),
            pltpu.VMEM((8, rows_of, query_width), low),
            pltpu.VMEM((8, rows_of, rest_width), low),
            pltpu.VMEM((8 * rows_of, 2 * depth), low),
            pltpu.VMEM((rows_of, width), full),
            pltpu.VMEM((8, 8, depth), full),
            pltpu.VMEM((8, 8, depth), full),
            dma((9,)),
            dma((13,)),
            dma((13,)),
            dma((13,)),
            dma((13,)),
            dma((13,)),
            dma((13,)),
            dma((spans,)),
            dma((spans,)),
            dma((7,)),
            dma((7,)),
        ],
        compiler_params=pltpu.CompilerParams(collective_id=4, has_side_effects=True, vmem_limit_bytes=60 * 2**20),
        cost_estimate=pl.CostEstimate(
            flops=40 * rows_of * width * columns, bytes_accessed=6 * width * columns, transcendentals=0
        ),
        name="attend_backward",
    )(
        d_lin, query_low, key_value, linear, gains, positions, cosine, sine, d_middle, features,
        source, d_half, gain_rows, outward_all, inward_all,
    )


def feed_call(forward, own, weights, kept=(), features=None):
    rows_of, width = own.shape
    hidden = weights[0].shape[0]
    all_rows = 8 * rows_of
    others = lax.axis_size("ctx") - 1
    low = jnp.bfloat16
    count_made = 3 if forward else 2
    hbm = pl.BlockSpec(memory_space=pl.ANY)
    vmem = pl.BlockSpec(memory_space=pltpu.VMEM)
    half = rows_of // 2
    dma = pltpu.SemaphoreType.DMA
    shapes = [
        jax.ShapeDtypeStruct((rows_of, width), jnp.float32),
        jax.ShapeDtypeStruct((all_rows, width), low),
        jax.ShapeDtypeStruct((others, rows_of, width), low),
    ]
    operands = (own, *weights, *kept)
    operand_specs = [vmem] + [hbm] * (3 + len(kept))
    slice_sems = []
    if forward:
        shapes += [jax.ShapeDtypeStruct((8, rows_of, features.shape[1] // 8), low)]
        operands += (features,)
        operand_specs += [vmem]
        slice_sems = [dma((7,)), dma((7,)), dma]
    shapes += [jax.ShapeDtypeStruct((all_rows, hidden), low)] * count_made
    return pl.pallas_call(
        functools.partial(feed_kernel, forward, rows_of, others),
        out_shape=shapes,
        in_specs=operand_specs,
        out_specs=[vmem] + [hbm] * (len(shapes) - 1),
        scratch_shapes=[pltpu.VMEM((hidden, width), low)] * 3
        + [pltpu.VMEM((all_rows, hidden), low)] * (len(kept) + count_made)
        + [
            pltpu.VMEM((4, 2 * rows_of, width), low),
            pltpu.VMEM((4, 2 * rows_of, width), low),
            pltpu.VMEM((4, rows_of, width), low),
            pltpu.VMEM((3, rows_of, width), low),
            pltpu.VMEM((2, half, width), low),
            pltpu.VMEM((2, half, width), low),
            pltpu.VMEM((4, half, width), low),
            dma((20,)),
            dma((20,)),
            dma((3 + len(kept),)),
            dma((4 * (1 + count_made),)),
            dma((others,)),
            dma((others,)),
        ]
        + slice_sems,
        compiler_params=pltpu.CompilerParams(
            collective_id=1 if forward else 2,
            has_side_effects=True,
            vmem_limit_bytes=56 * 2**20,
        ),
        cost_estimate=pl.CostEstimate(
            flops=40 * all_rows * hidden * width // 2,
            bytes_accessed=6 * hidden * width + 8 * all_rows * width,
            transcendentals=0,
        ),
        name="feed_forward" if forward else "feed_backward",
    )(*operands)


def weight_grad_kernel(
    own_steps, gate, up, down, rows, d_rows, hidden, d_gate, d_up, rows_far, d_rows_far,
    grad_gate, grad_up, grad_down, hidden_tile, d_gate_tile, d_up_tile,
):
    step = pl.program_id(1)
    tile = 512
    hidden_size = gate.shape[0]
    chunk = rows.shape[1]

    @pl.when(step == 0)
    def _():
        grad_gate[...] = jnp.zeros_like(grad_gate)
        grad_up[...] = jnp.zeros_like(grad_up)
        grad_down[...] = jnp.zeros_like(grad_down)

    def accumulate(rows, d_rows):
        def body(index, carry):
            columns = pl.ds(pl.multiple_of(index * chunk, chunk), chunk)
            right, d_right = rows[:, columns], d_rows[:, columns]
            grad_gate[:, columns] += matrix_product(d_gate_tile[...], right)
            grad_up[:, columns] += matrix_product(d_up_tile[...], right)
            grad_down[:, columns] += matrix_product(hidden_tile[...], d_right)
            return carry
        lax.fori_loop(0, rows.shape[1] // chunk, body, 0)

    @pl.when(step < own_steps)
    def _():
        hidden_tile[...] = hidden[...].T
        d_gate_tile[...] = d_gate[...].T
        d_up_tile[...] = d_up[...].T
        accumulate(rows, d_rows)

    @pl.when(step >= own_steps)
    def _():
        def body(index, carry):
            span = pl.ds(pl.multiple_of(index * tile, tile), tile)
            gate_value = product_back(gate[span, :], rows_far[...])
            up_value = product_back(up[span, :], rows_far[...])
            d_hidden = product_back(down[span, :], d_rows_far[...])
            value, slope = gelu_parts(gate_value)
            hidden_tile[span, :] = (value * up_value).astype(jnp.bfloat16)
            d_gate_tile[span, :] = (d_hidden * up_value * slope).astype(jnp.bfloat16)
            d_up_tile[span, :] = (d_hidden * value).astype(jnp.bfloat16)
            return carry
        lax.fori_loop(0, hidden_size // tile, body, 0)
        accumulate(rows_far, d_rows_far)


def weight_grad_call(gate, up, down, rows, d_rows, hidden, d_gate, d_up, rows_far, d_rows_far, hid=1024, tok=256):
    size, width = gate.shape
    hid = min(hid, size)
    own_steps = rows.shape[0] // tok
    far_steps = rows_far.shape[0] // tok
    low = jnp.bfloat16
    weight = pl.BlockSpec((hid, width), lambda h, s: (h, 0))
    own = pl.BlockSpec((tok, width), lambda h, s: (jnp.minimum(s, own_steps - 1), 0))
    own_mid = pl.BlockSpec((tok, hid), lambda h, s: (jnp.minimum(s, own_steps - 1), h))
    far = pl.BlockSpec((tok, width), lambda h, s: (jnp.maximum(s - own_steps, 0), 0))
    flops = 6 * size * width * (rows.shape[0] + 2 * rows_far.shape[0])
    return pl.pallas_call(
        functools.partial(weight_grad_kernel, own_steps),
        grid=(size // hid, own_steps + far_steps),
        in_specs=[weight] * 3 + [own] * 2 + [own_mid] * 3 + [far] * 2,
        out_specs=[weight] * 3,
        out_shape=[jax.ShapeDtypeStruct((size, width), jnp.float32)] * 3,
        scratch_shapes=[pltpu.VMEM((hid, tok), low)] * 3,
        compiler_params=pltpu.CompilerParams(
            dimension_semantics=("arbitrary", "arbitrary"), vmem_limit_bytes=60 * 2**20
        ),
        cost_estimate=pl.CostEstimate(flops=flops, bytes_accessed=100 * 2**20, transcendentals=0),
        name="weight_grads",
    )(gate, up, down, rows, d_rows, hidden, d_gate, d_up, rows_far, d_rows_far)


def per_device(
    tokens,
    per_layer,
    segments,
    positions,
    cotangent,
    query_weight,
    key_matrix,
    value_matrix,
    output_weight,
    laurel_down,
    laurel_up,
    vector_gate,
    vector_out,
    norm_input,
    norm_attention,
    norm_laurel,
    norm_before,
    norm_after,
    norm_vector,
    query_norm_gain,
    norm_key,
    hidden_gate,
    hidden_up,
    hidden_down,
):
    count_of_rows = tokens.shape[0]
    shards = lax.axis_size("fsdp")
    width = tokens.shape[1]
    heads_per_group = QUERY_HEADS // KEY_VALUE_HEADS
    reach_blocks = min((WINDOW + count_of_rows - 2) // count_of_rows, lax.axis_size("ctx") - 1)
    score_scale = HEAD_SIZE ** (-0.5)
    other_rows = (lax.axis_size("ctx") - 1) * count_of_rows * shards
    gathered_plan = other_rows <= 4096
    query_width = query_weight.shape[1]
    key_width = key_matrix.shape[1]

    gain_shards = (
        norm_input,
        norm_attention,
        norm_laurel,
        norm_before,
        norm_after,
        norm_vector,
        query_norm_gain,
        norm_key,
    )
    gain_sizes = [gain.shape[0] for gain in gain_shards]
    gain_starts = [sum(gain_sizes[:index]) for index in range(len(gain_sizes))]
    pieces = [output_weight, vector_gate.reshape(-1, width), vector_out, laurel_up]
    piece_sizes = [piece.shape[0] for piece in pieces]
    piece_starts = [sum(piece_sizes[:index]) for index in range(len(pieces))]
    outward = jnp.concatenate(pieces, axis=0)
    outward = jnp.pad(outward, ((0, -outward.shape[0] % 32), (0, 0)))
    inward_weight = jnp.concatenate([query_weight, key_matrix, value_matrix, laurel_down], axis=1)
    inward_weight = jnp.pad(inward_weight, ((0, 0), (0, -inward_weight.shape[1] % 128)))
    source = tokens.astype(jnp.float32)
    vectors = per_layer.astype(jnp.float32)
    rank = laurel_down.shape[1]
    unused, allowed = window(positions, count_of_rows, reach_blocks)

    def head_facing(linear, gain):
        return rotary_apply(root_mean_norm(linear, gain), positions)

    if shards == 8:
        me = lax.axis_index("fsdp")
        gain_lines = jnp.stack(
            [
                lax.dynamic_update_slice(jnp.zeros((width,), gain.dtype), gain, (me * gain.shape[0],))
                for gain in gain_shards
            ]
        )
        gain_lines = jnp.pad(gain_lines, ((0, 16 - len(gain_shards)), (0, 0)))
        cosine, sine_part = rotary_tables(positions, HEAD_SIZE)
        (
            normed,
            lowered_normed,
            gains_all,
            linear,
            query_lowered,
            key_value,
            attended_low,
            laurel_mid,
            attn_lin,
            full_inward,
            outward,
        ) = attend_call(
            reach_blocks, tokens, gain_lines, positions[:, None], cosine, sine_part, inward_weight, outward
        )
        gains = [gains_all[index, : size * shards] for index, size in enumerate(gain_sizes)]
        laurel_mid = laurel_mid[:, :rank]
        window_keys, window_values = key_value[:, :key_width], key_value[:, key_width:]
    else:
        gain_line = jnp.concatenate(gain_shards)
        gain_line = jnp.pad(gain_line, (0, -gain_line.shape[0] % 2048)).reshape(-1, 128)
        gains_all = gather(gain_line, "fsdp").reshape(shards, -1)
        gains = [
            gains_all[:, start : start + size].reshape(-1).astype(jnp.float32)
            for start, size in zip(gain_starts, gain_sizes)
        ]
        full_inward = gather(inward_weight, "fsdp")
        outward = lax.all_gather(outward, "fsdp", axis=0, tiled=False)
        normed = root_mean_norm(source, gains[0])
        lowered_normed = normed.astype(jnp.bfloat16)
        inward = matrix_product(lowered_normed, full_inward)
        linear = inward[:, : query_width + key_width]
        value_lowered = inward[:, query_width + key_width : query_width + 2 * key_width].astype(jnp.bfloat16)
        laurel_mid = inward[:, query_width + 2 * key_width :][:, :rank].astype(jnp.bfloat16)
        query_lowered = head_facing(
            linear[:, :query_width].reshape(count_of_rows, QUERY_HEADS, HEAD_SIZE), gains[6]
        ).astype(jnp.bfloat16)
        key_lowered = head_facing(
            linear[:, query_width:].reshape(count_of_rows, KEY_VALUE_HEADS, HEAD_SIZE), gains[7]
        ).astype(jnp.bfloat16)
        key_value = jnp.stack([key_lowered.reshape(count_of_rows, -1), value_lowered])
        pair_blocks = [key_value]
        for distance in range(1, reach_blocks + 1):
            pair_blocks.append(from_behind(key_value, "ctx", distance))
        window_couple = jnp.concatenate(pair_blocks, axis=1)
        window_keys, window_values = window_couple[0], window_couple[1]
    (
        gain_input,
        gain_attention,
        gain_laurel,
        gain_before,
        gain_after,
        gain_vector,
        gain_query,
        key_norm_gain,
    ) = gains
    full_output, full_vector_gate, full_vector_out, full_laurel_up = [
        outward[:, start : start + size].reshape(-1, width)
        for start, size in zip(piece_starts, piece_sizes)
    ]
    full_vector_gate = full_vector_gate.reshape(width, -1)
    if shards != 8:
        query_linear = linear[:, :query_width].reshape(count_of_rows, QUERY_HEADS, HEAD_SIZE)
        key_linear = linear[:, query_width:].reshape(count_of_rows, KEY_VALUE_HEADS, HEAD_SIZE)
        query_lowered = query_lowered.reshape(count_of_rows, KEY_VALUE_HEADS, heads_per_group, HEAD_SIZE)
        window_keys = window_keys.reshape(-1, KEY_VALUE_HEADS, HEAD_SIZE)
        window_values = window_values.reshape(-1, KEY_VALUE_HEADS, HEAD_SIZE)

        def masked_scores():
            raw_scores = score_scale * jnp.einsum(
                "tgfd,kgd->gftk", query_lowered, window_keys, preferred_element_type=jnp.float32
            )
            return jnp.where(allowed, raw_scores, -1e30)

        scores_first = masked_scores()
        row_peak = jnp.max(scores_first, axis=-1, keepdims=True)
        exp_scores = jnp.exp(scores_first - row_peak)
        row_total = jnp.sum(exp_scores, axis=-1, keepdims=True)
        log_total = row_peak + jnp.log(row_total)
        soft_low = (exp_scores / row_total).astype(jnp.bfloat16)
        attended_low = (
            jnp.einsum("gftk,kgd->tgfd", soft_low, window_values, preferred_element_type=jnp.float32)
            .reshape(count_of_rows, QUERY_HEADS * HEAD_SIZE)
            .astype(jnp.bfloat16)
        )
        attn_lin = matrix_product(attended_low, full_output)
    residual_one = source + root_mean_norm(attn_lin, gain_attention)
    laurel_lin = matrix_product(laurel_mid, full_laurel_up)
    mixed = (residual_one + normed + root_mean_norm(laurel_lin, gain_laurel)) * inv_root
    ffn_in = root_mean_norm(mixed, gain_before).astype(jnp.bfloat16)
    if shards == 8:
        features = jnp.concatenate(
            [lowered_normed.reshape(count_of_rows, shards, -1), attended_low.reshape(count_of_rows, shards, -1)], axis=2
        ).reshape(count_of_rows, -1)
        feed_value, rows_all, rows_far, slices, hidden_all, lift_all, bend_all = feed_call(
            True, ffn_in, (hidden_gate, hidden_up, hidden_down), features=features
        )
        slices = slices.reshape(shards * count_of_rows, -1)
        normed_slices, attended_slices = jnp.split(slices, 2, axis=1)
    else:
        normed_slices = feature_slices(lowered_normed)
        attended_slices = feature_slices(attended_low)
        rows_all = gather(ffn_in, "fsdp")
        gate_all = product_back(rows_all, hidden_gate)
        up_all = product_back(rows_all, hidden_up)
        hidden_all = gated(gate_all, up_all).astype(jnp.bfloat16)
        feed_value = scatter_sum(matrix_product(hidden_all, hidden_down))
    residual_two = mixed + root_mean_norm(feed_value, gain_after)
    residual_low = residual_two.astype(jnp.bfloat16)
    vector_lin = matrix_product(residual_low, full_vector_gate)
    gated_low = gated(vector_lin, vectors).astype(jnp.bfloat16)
    vector_back = matrix_product(gated_low, full_vector_out)
    result = residual_two + root_mean_norm(vector_back, gain_vector)
    upstream = cotangent.astype(jnp.float32)
    d_vector_back, grad_gain_vector = norm_grad(vector_back, gain_vector, upstream)
    d_vector_back_low = d_vector_back.astype(jnp.bfloat16)
    grad_vector_out = product_rows(gated_low, d_vector_back_low)
    d_gated = product_back(d_vector_back_low, full_vector_out)
    d_vector_lin, d_vectors = gated_grad(vector_lin, vectors, d_gated)
    d_vector_lin_low = d_vector_lin.astype(jnp.bfloat16)
    grad_vector_gate = product_rows(residual_low, d_vector_lin_low)
    d_residual = upstream + product_back(d_vector_lin_low, full_vector_gate)
    d_feed, grad_gain_after = norm_grad(feed_value, gain_after, d_residual)
    d_feed_low = d_feed.astype(jnp.bfloat16)
    if shards == 8:
        d_ffn_in, d_rows_all, d_rows_far, d_gate_low, d_up_low = feed_call(
            False, d_feed_low, (hidden_down, hidden_gate, hidden_up), (lift_all, bend_all)
        )
    else:
        d_rows_all = gather(d_feed_low, "fsdp")
        d_hidden = product_back(d_rows_all, hidden_down)
        d_gate_all, d_up_all = gated_grad(gate_all, up_all, d_hidden)
        d_gate_low = d_gate_all.astype(jnp.bfloat16)
        d_up_low = d_up_all.astype(jnp.bfloat16)
        d_ffn_in = scatter_sum(
            matrix_product(d_gate_low, hidden_gate) + matrix_product(d_up_low, hidden_up)
        )

    if shards == 8 and gathered_plan:
        rows_far = gather(rows_far.reshape(-1, width), "fsdp")
        d_ffn_in, rows_far = lax.optimization_barrier((d_ffn_in, rows_far))
        d_rows_far = gather(d_rows_far.reshape(-1, width), "fsdp")
        grad_hidden_gate, grad_hidden_up, grad_hidden_down = weight_grad_call(
            hidden_gate,
            hidden_up,
            hidden_down,
            rows_all,
            d_rows_all,
            hidden_all,
            d_gate_low,
            d_up_low,
            rows_far,
            d_rows_far,
        )
    else:
        grad_hidden_gate, grad_hidden_up, grad_hidden_down = [
            lax.psum(grad.astype(jnp.bfloat16), "ctx").astype(jnp.float32)
            for grad in (
                product_rows(d_gate_low, rows_all),
                product_rows(d_up_low, rows_all),
                product_rows(hidden_all, d_rows_all),
            )
        ]

    d_mixed_part, grad_gain_before = norm_grad(mixed, gain_before, d_ffn_in)
    d_half = (d_residual + d_mixed_part) * inv_root
    d_laurel_lin, grad_gain_laurel = norm_grad(laurel_lin, gain_laurel, d_half)
    d_laurel_low = d_laurel_lin.astype(jnp.bfloat16)
    grad_laurel_up = product_rows(laurel_mid, d_laurel_low)
    d_laurel_mid = product_back(d_laurel_low, full_laurel_up).astype(jnp.bfloat16)
    d_attn_lin, grad_gain_attention = norm_grad(attn_lin, gain_attention, d_half)
    d_attn_low = d_attn_lin.astype(jnp.bfloat16)
    small_rows = jnp.concatenate(
        [
            grad_vector_gate.reshape(shards, -1, width),
            grad_vector_out.reshape(shards, -1, width),
            grad_laurel_up.reshape(shards, -1, width),
        ],
        axis=1,
    ).astype(jnp.bfloat16)
    small_share = lax.psum_scatter(small_rows, "fsdp", scatter_dimension=0, tiled=False)

    if shards == 8:
        empty = jnp.zeros((width,), jnp.float32)
        gain_rows = jnp.stack(
            [
                empty,
                grad_gain_attention,
                grad_gain_laurel,
                grad_gain_before,
                grad_gain_after,
                grad_gain_vector,
                empty,
                empty,
            ]
        )
        d_middle = jnp.pad(d_laurel_mid, ((0, 0), (0, full_inward.shape[1] - query_width - 2 * key_width - rank)))
        d_source, grad_inward, grad_output, gain_shares = attend_back_call(
            reach_blocks, d_attn_low, query_lowered, key_value, linear, gains_all, positions[:, None], cosine, sine_part,
            d_middle, slices, tokens, d_half, gain_rows, outward, full_inward,
        )
        gain_shares = [
            lax.dynamic_slice_in_dim(gain_shares[index], me * size, size) if index >= 6 else gain_shares[index]
            for index, size in enumerate(gain_sizes)
        ]
        gain_share = jnp.concatenate(gain_shares)
    else:
        d_attended = (
            product_back(d_attn_low, full_output)
            .astype(jnp.bfloat16)
            .reshape(count_of_rows, KEY_VALUE_HEADS, heads_per_group, HEAD_SIZE)
        )
        soft_again = jnp.exp(masked_scores() - log_total)
        d_soft = jnp.einsum(
            "tgfd,kgd->gftk", d_attended, window_values, preferred_element_type=jnp.float32
        )
        d_scores = (
            soft_again * (d_soft - jnp.sum(soft_again * d_soft, axis=-1, keepdims=True))
        ).astype(jnp.bfloat16)
        d_query = score_scale * jnp.einsum(
            "gftk,kgd->tgfd", d_scores, window_keys, preferred_element_type=jnp.float32
        )
        grad_key_rows = score_scale * jnp.einsum(
            "gftk,tgfd->kgd", d_scores, query_lowered, preferred_element_type=jnp.float32
        )
        grad_value_rows = jnp.einsum(
            "gftk,tgfd->kgd",
            soft_again.astype(jnp.bfloat16),
            d_attended,
            preferred_element_type=jnp.float32,
        )
        grad_window_couple = jnp.stack(
            [
                grad_key_rows.reshape(-1, KEY_VALUE_HEADS * HEAD_SIZE),
                grad_value_rows.reshape(-1, KEY_VALUE_HEADS * HEAD_SIZE),
            ]
        )
        grad_own_part = grad_window_couple[:, :count_of_rows]
        for distance in range(1, reach_blocks + 1):
            grad_own_part = grad_own_part + from_behind(
                grad_window_couple[:, distance * count_of_rows : (distance + 1) * count_of_rows].astype(
                    jnp.bfloat16
                ),
                "ctx",
                -distance,
            ).astype(jnp.float32)
        unused, query_pull = jax.vjp(head_facing, query_linear, gain_query)
        d_query_lin, grad_gain_query = query_pull(
            d_query.reshape(count_of_rows, QUERY_HEADS, HEAD_SIZE)
        )
        unused, key_pullback_fn = jax.vjp(head_facing, key_linear, key_norm_gain)
        grad_key_linear, grad_key_norm_gain = key_pullback_fn(
            grad_own_part[0].reshape(count_of_rows, KEY_VALUE_HEADS, HEAD_SIZE)
        )
        d_inward = jnp.concatenate(
            [
                d_query_lin.reshape(count_of_rows, QUERY_HEADS * HEAD_SIZE).astype(jnp.bfloat16),
                grad_key_linear.reshape(count_of_rows, KEY_VALUE_HEADS * HEAD_SIZE).astype(
                    jnp.bfloat16
                ),
                grad_own_part[1].astype(jnp.bfloat16),
                d_laurel_mid,
                jnp.zeros((count_of_rows, full_inward.shape[1] - query_width - 2 * key_width - rank), jnp.bfloat16),
            ],
            axis=1,
        )
        grad_inward = product_rows(normed_slices, gather(d_inward, "fsdp")).astype(jnp.bfloat16)
        grad_output = product_rows(attended_slices, gather(d_attn_low, "fsdp")).astype(jnp.bfloat16)
        d_normed = d_half + product_back(d_inward, full_inward)
        d_source_part, grad_gain_input = norm_grad(source, gain_input, d_normed)
        d_source = d_half + d_source_part
        gain_lines = jnp.concatenate(
            [
                grad.reshape(shards, -1)
                for grad in (
                    grad_gain_input,
                    grad_gain_attention,
                    grad_gain_laurel,
                    grad_gain_before,
                    grad_gain_after,
                    grad_gain_vector,
                    grad_gain_query,
                    grad_key_norm_gain,
                )
            ],
            axis=1,
        )
        gain_share = lax.psum_scatter(gain_lines, "fsdp", scatter_dimension=0, tiled=False)
    gain_count = gain_share.shape[0]
    gain_share = jnp.pad(gain_share, (0, -gain_count % 2048)).astype(jnp.bfloat16)
    totals = lax.psum(
        jnp.concatenate(
            [
                grad_inward.reshape(-1, 128),
                grad_output.reshape(-1, 128),
                small_share.reshape(-1, 128),
                gain_share.reshape(-1, 128),
            ],
            axis=0,
        ),
        "ctx",
    ).astype(jnp.float32)
    inward_lines = grad_inward.size // 128
    output_lines = grad_output.size // 128
    grad_inward = totals[:inward_lines].reshape(grad_inward.shape)
    grad_output = totals[inward_lines : inward_lines + output_lines].reshape(grad_output.shape)
    small_lines = inward_lines + output_lines + small_share.size // 128
    small_share = totals[inward_lines + output_lines : small_lines].reshape(small_share.shape)
    gain_share = totals[small_lines:].reshape(-1)[:gain_count]
    gate_rows = vector_gate.shape[0] * vector_gate.shape[1] // width
    out_rows = vector_out.shape[0]
    share_vector_gate = small_share[:gate_rows].reshape(vector_gate.shape)
    share_vector_out = small_share[gate_rows : gate_rows + out_rows]
    share_laurel_up = small_share[gate_rows + out_rows :]
    gain_grads = tuple(
        gain_share[start : start + size] for start, size in zip(gain_starts, gain_sizes)
    )
    value_start = query_width + key_width
    return (
        result.astype(jnp.bfloat16),
        d_source,
        d_vectors,
        grad_inward[:, :query_width],
        grad_inward[:, query_width:value_start],
        grad_inward[:, value_start : value_start + key_width],
        grad_output,
        grad_inward[:, value_start + key_width : value_start + key_width + rank],
        share_laurel_up,
        share_vector_gate,
        share_vector_out,
    ) + gain_grads + (
        grad_hidden_gate,
        grad_hidden_up,
        grad_hidden_down,
    )


def solution(mesh):
    rows = P(("fsdp", "ctx"), None)
    line = P(("fsdp", "ctx"))
    weight = P("fsdp", None)
    gain = P("fsdp")
    return jax.shard_map(
        per_device,
        mesh=mesh,
        in_specs=(rows, rows, line, line, rows) + (weight,) * 8 + (gain,) * 8 + (weight,) * 3,
        out_specs=(rows,) * 3 + (weight,) * 8 + (gain,) * 8 + (weight,) * 3,
        check_vma=False,
    )
```

```python
import functools

import jax
import jax.numpy as jnp
from jax import lax
from jax.experimental import pallas as pl
from jax.experimental.pallas import tpu as pltpu
from jax.sharding import PartitionSpec as P

QUERY_HEADS = 8
KEY_VALUE_HEADS = 2
HEAD_SIZE = 256
WINDOW = 1024


epsilon = 1e-06
rope_base = 10000.0
inv_root = 0.7071067811865476
gelu_scale = 0.7978845608028654
gelu_cubic = 0.044715


def from_behind(value, axis, steps):
    count = lax.axis_size(axis)
    initial, last = (max(0, -steps), min(count, count - steps))
    return lax.ppermute(value, axis, [(source, source + steps) for source in range(initial, last)])


def other_blocks(value, axis):
    count = lax.axis_size(axis)
    return jnp.concatenate(
        [
            lax.ppermute(value, axis, [(source, (source + step) % count) for source in range(count)])
            for step in range(1, count)
        ],
        axis=0,
    )


def root_mean_norm(value, gain):
    factor = lax.rsqrt(jnp.mean(value * value, axis=-1, keepdims=True) + epsilon)
    return value * factor * gain


def gelu_tanh(value):
    return jax.nn.gelu(value, approximate=True)


def gated(gate_value, up_value):
    return gelu_tanh(gate_value) * up_value


def rotary_apply(value, token_position):
    half_size = value.shape[-1] // 2
    frequency = rope_base ** (-2.0 * jnp.arange(half_size, dtype=jnp.float32) / value.shape[-1])
    angle = token_position.astype(jnp.float32)[:, None] * frequency[None, :]
    cosine = jnp.cos(angle)[:, None, :]
    sine_part = jnp.sin(angle)[:, None, :]
    first_half = value[..., :half_size]
    second_half = value[..., half_size:]
    return jnp.concatenate(
        [
            first_half * cosine - second_half * sine_part,
            second_half * cosine + first_half * sine_part,
        ],
        axis=-1,
    )


def rotary_tables(token_position, size):
    half_size = size // 2
    frequency = rope_base ** (-2.0 * jnp.arange(half_size, dtype=jnp.float32) / size)
    angle = token_position.astype(jnp.float32)[:, None] * frequency[None, :]
    return jnp.cos(angle), jnp.sin(angle)


def window(positions, rows_of, reach):
    key_offset = jnp.concatenate(
        [distance * rows_of - jnp.arange(rows_of, dtype=jnp.int32) for distance in range(reach + 1)]
    )
    key_gap = jnp.arange(rows_of, dtype=jnp.int32)[:, None] + key_offset[None, :]
    return key_gap, (key_gap >= 0) & (key_gap <= positions[:, None]) & (key_gap < WINDOW)


def matrix_product(left, right):
    return jnp.dot(left, right, preferred_element_type=jnp.float32)


def product_back(left, right):
    return lax.dot_general(
        left, right, (((1,), (1,)), ((), ())), preferred_element_type=jnp.float32
    )


def product_rows(left, right):
    return lax.dot_general(
        left, right, (((0,), (0,)), ((), ())), preferred_element_type=jnp.float32
    )


def norm_grad(value, gain, upstream):
    unused, pullback = jax.vjp(root_mean_norm, value, gain)
    return pullback(upstream)


def gated_grad(gate_value, up_value, upstream):
    unused, pullback = jax.vjp(gated, gate_value, up_value)
    return pullback(upstream)


def gather(value, axis):
    return lax.all_gather(value, axis, axis=0, tiled=True)


def feature_slices(value):
    count = lax.axis_size("fsdp")
    rows = value.shape[0]
    return lax.all_to_all(
        value.reshape(rows, count, -1), "fsdp", split_axis=1, concat_axis=0, tiled=True
    ).reshape(count * rows, -1)


def scatter_sum(value):
    return lax.psum_scatter(
        value.astype(jnp.bfloat16), "fsdp", scatter_dimension=0, tiled=True
    ).astype(jnp.float32)


def gelu_parts(gate):
    square = gate * gate
    bend = jnp.tanh(gelu_scale * gate * (1.0 + gelu_cubic * square))
    half_up = 0.5 * (1.0 + bend)
    slope = half_up + 0.5 * gate * (1.0 - bend * bend) * (
        gelu_scale * (1.0 + 3.0 * gelu_cubic * square)
    )
    return gate * half_up, slope


def across(me, stride):
    return me + stride - 2 * stride * ((me // stride) % 2)


def across_many(me, bits):
    for stride in (1, 2, 4):
        if bits & stride:
            me = across(me, stride)
    return me


def feed_kernel(forward, rows_of, others, *refs):
    half = rows_of // 2
    if forward:
        (own, gate_hbm, up_hbm, down_hbm, features, total, rows_hbm, far_hbm, near_hbm, slices_hbm, hidden_hbm, lift_hbm, bend_hbm), rest = refs[:13], refs[13:]
        weights_hbm, kept_hbm, made_hbm = (gate_hbm, up_hbm, down_hbm), (), (hidden_hbm, lift_hbm, bend_hbm)
    else:
        (own, down_hbm, gate_hbm, up_hbm, lift_hbm, bend_hbm, forward_rows, total, rows_hbm, far_hbm, near_hbm, d_gate_hbm, d_up_hbm), rest = refs[:13], refs[13:]
        weights_hbm, kept_hbm, made_hbm = (down_hbm, gate_hbm, up_hbm), (lift_hbm, bend_hbm), (d_gate_hbm, d_up_hbm)
    count_kept, count_made = len(kept_hbm), len(made_hbm)
    weights = rest[:3]
    kept = rest[3 : 3 + count_kept]
    made = rest[3 + count_kept : 3 + count_kept + count_made]
    (rows, part, sib_in, chip_sum, relay_in, relay_sum, last_in, send_sem, recv_sem, in_sem, out_sem, far_send, far_recv, near_send, near_recv, *slice_sems) = rest[
        3 + count_kept + count_made :
    ]
    hidden = weights[0].shape[0]
    width = own.shape[1]
    me = lax.axis_index("fsdp")
    sibling, beside, above = across(me, 1), across(me, 2), across(me, 4)

    loads = [
        pltpu.make_async_copy(source, target, in_sem.at[index])
        for index, (source, target) in enumerate(zip(weights_hbm + kept_hbm, tuple(weights) + tuple(kept)))
    ]
    for load in loads:
        load.start()

    block = lax.axis_index("ctx")
    greet(me, range(1, 8) if forward else (1, 2, 4), block, others)

    def send(index, source, target, partner):
        return pltpu.make_async_remote_copy(
            src_ref=source,
            dst_ref=target,
            send_sem=send_sem.at[index],
            recv_sem=recv_sem.at[index],
            device_id={"fsdp": partner},
            device_id_type=pl.DeviceIdType.MESH,
        )

    low, high = pl.ds(0, half), pl.ds(half, half)
    mine, theirs = pl.ds(0, rows_of), pl.ds(rows_of, rows_of)
    copies = [
        send(0, own, rows.at[0, theirs], sibling),
        send(1, own.at[low], rows.at[1, low], beside),
        send(2, own.at[low], rows.at[1, high], above),
        send(3, own.at[high], rows.at[2, low], beside),
        send(4, own.at[high], rows.at[2, high], above),
        send(5, rows.at[1, mine], rows.at[1, theirs], sibling),
        send(6, rows.at[2, mine], rows.at[2, theirs], sibling),
        send(7, rows.at[1, low], rows.at[3, low], above),
        send(8, rows.at[2, high], rows.at[3, high], beside),
        send(9, rows.at[3, mine], rows.at[3, theirs], sibling),
        send(10, part.at[0, theirs], sib_in.at[0], sibling),
        send(11, part.at[1, theirs], sib_in.at[1], sibling),
        send(12, part.at[2, theirs], sib_in.at[2], sibling),
        send(13, part.at[3, theirs], sib_in.at[3], sibling),
        send(14, chip_sum.at[0, high], last_in.at[2], above),
        send(15, chip_sum.at[1, low], last_in.at[1], beside),
        send(16, chip_sum.at[2, low], relay_in.at[0], above),
        send(17, chip_sum.at[2, high], relay_in.at[1], beside),
        send(18, relay_sum.at[0], last_in.at[0], beside),
        send(19, relay_sum.at[1], last_in.at[3], above),
    ]
    outs = []

    def write_out(source, target):
        copy = pltpu.make_async_copy(source, target, out_sem.at[len(outs)])
        copy.start()
        outs.append(copy)

    for index in range(5):
        copies[index].start()
    far = [
        push(own, far_hbm.at[index], far_send.at[index], far_recv.at[index], {"ctx": across_many(block, 2 + index)})
        for index in range(2)
    ]
    for copy in far:
        copy.start()
    def near_source(index):
        if forward:
            return rows.at[1, mine] if index else own
        return forward_rows.at[pl.ds((2 + index) * 2 * rows_of, rows_of)]

    near = [
        push(near_source(index), near_hbm.at[index, mine], near_send.at[index], near_recv.at[index], {"ctx": across(block, 1)})
        for index in range(2)
    ]
    near_share = [
        push(
            near_hbm.at[index, mine],
            near_hbm.at[index, theirs],
            near_send.at[2 + index],
            near_recv.at[2 + index],
            {"fsdp": sibling},
        )
        for index in range(2)
    ]
    near[0].start()
    if not forward:
        near[1].start()
    rows[0, mine] = own[...]
    slices = []
    if forward:
        share = features.shape[1] // 8

        def share_of(device):
            return features.at[:, pl.ds(pl.multiple_of(device * share, share), share)]

        own_slice = pltpu.make_async_copy(share_of(me), slices_hbm.at[me], slice_sems[2])
        own_slice.start()
        slices = [
            pltpu.make_async_remote_copy(
                src_ref=share_of(across_many(me, distance)),
                dst_ref=slices_hbm.at[me],
                send_sem=slice_sems[0].at[distance - 1],
                recv_sem=slice_sems[1].at[distance - 1],
                device_id={"fsdp": across_many(me, distance)},
                device_id_type=pl.DeviceIdType.MESH,
            )
            for distance in range(1, 8)
        ]

    tile = min(hidden, 1024)
    wide = min(width, 1024)

    def first_stage(group):
        span = pl.ds(group * 2 * rows_of, 2 * rows_of)

        def step(index, carry):
            columns = pl.ds(pl.multiple_of(index * tile, tile), tile)
            left = rows[group]

            def back(weight):
                return lax.dot_general(
                    left, weight[columns, :], (((1,), (1,)), ((), ())), preferred_element_type=jnp.float32
                )

            if forward:
                gate, up = back(weights[0]), back(weights[1])
                value, slope = gelu_parts(gate)
                made[0][span, columns] = (value * up).astype(jnp.bfloat16)
                made[1][span, columns] = value.astype(jnp.bfloat16)
                made[2][span, columns] = (slope * up).astype(jnp.bfloat16)
            else:
                d_hidden = back(weights[0])
                made[0][span, columns] = (d_hidden * kept[1][span, columns].astype(jnp.float32)).astype(jnp.bfloat16)
                made[1][span, columns] = (d_hidden * kept[0][span, columns].astype(jnp.float32)).astype(jnp.bfloat16)
            return carry

        lax.fori_loop(0, hidden // tile, step, 0)

    def second_stage(group):
        span = pl.ds(group * 2 * rows_of, 2 * rows_of)

        def step(index, carry):
            columns = pl.ds(pl.multiple_of(index * wide, wide), wide)
            if forward:
                value = jnp.dot(made[0][span, :], weights[2][:, columns], preferred_element_type=jnp.float32)
            else:
                value = jnp.dot(made[0][span, :], weights[1][:, columns], preferred_element_type=jnp.float32)
                value = value + jnp.dot(made[1][span, :], weights[2][:, columns], preferred_element_type=jnp.float32)
            part[group, :, columns] = value.astype(jnp.bfloat16)
            return carry

        lax.fori_loop(0, width // wide, step, 0)

    def keep_out(group):
        span = pl.ds(group * 2 * rows_of, 2 * rows_of)
        write_out(rows.at[group], rows_hbm.at[span])
        for source, target in zip(made, made_hbm):
            write_out(source.at[span], target.at[span])

    def add_chip(group):
        chip_sum[group - 1] = (
            part[group, mine].astype(jnp.float32) + sib_in[group].astype(jnp.float32)
        ).astype(jnp.bfloat16)

    copies[0].wait_recv()
    loads[0].wait()
    if forward:
        loads[1].wait()
    else:
        loads[3].wait()
        loads[4].wait()
    first_stage(0)
    if forward:
        loads[2].wait()
    else:
        loads[1].wait()
        loads[2].wait()
    second_stage(0)
    copies[10].start()
    keep_out(0)
    copies[1].wait_recv()
    copies[7].start()
    copies[2].wait_recv()
    copies[5].start()
    if forward:
        near[1].start()
    copies[5].wait_recv()
    first_stage(1)
    second_stage(1)
    copies[11].start()
    keep_out(1)
    copies[3].wait_recv()
    copies[4].wait_recv()
    copies[8].start()
    copies[6].start()
    copies[11].wait_recv()
    add_chip(1)
    copies[14].start()
    copies[6].wait_recv()
    first_stage(2)
    second_stage(2)
    copies[12].start()
    keep_out(2)
    for copy in slices:
        copy.start()
    copies[7].wait_recv()
    copies[8].wait_recv()
    copies[9].start()
    copies[12].wait_recv()
    add_chip(2)
    copies[15].start()
    copies[9].wait_recv()
    first_stage(3)
    second_stage(3)
    copies[13].start()
    keep_out(3)
    copies[13].wait_recv()
    add_chip(3)
    copies[16].start()
    copies[17].start()
    copies[10].wait_recv()
    total[...] = part[0, mine].astype(jnp.float32) + sib_in[0].astype(jnp.float32)
    copies[16].wait_recv()
    relay_sum[0] = (chip_sum[0, low].astype(jnp.float32) + relay_in[0].astype(jnp.float32)).astype(jnp.bfloat16)
    copies[18].start()
    copies[17].wait_recv()
    relay_sum[1] = (chip_sum[1, high].astype(jnp.float32) + relay_in[1].astype(jnp.float32)).astype(jnp.bfloat16)
    copies[19].start()
    copies[14].wait_recv()
    total[low] = total[low] + last_in[2].astype(jnp.float32)
    copies[15].wait_recv()
    total[high] = total[high] + last_in[1].astype(jnp.float32)
    for index in range(2):
        near[index].wait_recv()
        near_share[index].start()
    copies[18].wait_recv()
    total[low] = total[low] + last_in[0].astype(jnp.float32)
    copies[19].wait_recv()
    total[high] = total[high] + last_in[3].astype(jnp.float32)
    for copy in copies:
        copy.wait_send()
    for copy in outs:
        copy.wait()
    for copy in far + slices:
        copy.wait()
    for index in range(2):
        near[index].wait_send()
        near_share[index].wait()
    if forward:
        own_slice.wait()


def turn(value, cosine, sine, direction=1.0):
    middle = value.shape[1] // 2
    first, second = value[:, :middle], value[:, middle:]
    sine = sine * direction
    return jnp.concatenate([first * cosine - second * sine, second * cosine + first * sine], axis=1)


def window_mask(positions, rows_of, blocks):
    query_row = lax.broadcasted_iota(jnp.int32, (rows_of, blocks * rows_of), 0)
    column = lax.broadcasted_iota(jnp.int32, (rows_of, blocks * rows_of), 1)
    behind = column // rows_of
    gap = query_row + 2 * behind * rows_of - column
    return (gap >= 0) & (gap <= positions) & (gap < WINDOW)


def greet(me, partners, block, others):
    barrier = pltpu.get_barrier_semaphore()
    for distance in partners:
        pl.semaphore_signal(
            barrier, inc=1, device_id={"fsdp": across_many(me, distance)}, device_id_type=pl.DeviceIdType.MESH
        )
    for distance in range(1, others + 1):
        pl.semaphore_signal(
            barrier,
            inc=1,
            device_id={"ctx": (block + distance) % (others + 1)},
            device_id_type=pl.DeviceIdType.MESH,
        )
    pl.semaphore_wait(barrier, len(partners) + others)


def push(source, target, send_sem, recv_sem, place):
    return pltpu.make_async_remote_copy(
        src_ref=source,
        dst_ref=target,
        send_sem=send_sem,
        recv_sem=recv_sem,
        device_id=place,
        device_id_type=pl.DeviceIdType.MESH,
    )


def spread_copies(own, slots, send_sem, recv_sem, me):
    half = own.shape[0] // 2
    low, high = pl.ds(0, half), pl.ds(half, half)
    sibling, beside, above = across(me, 1), across(me, 2), across(me, 4)
    plan = [
        (own, slots.at[1], sibling),
        (own.at[low], slots.at[2, low], beside),
        (own.at[low], slots.at[4, low], above),
        (own.at[high], slots.at[2, high], beside),
        (own.at[high], slots.at[4, high], above),
        (slots.at[2, low], slots.at[3, low], sibling),
        (slots.at[4, low], slots.at[5, low], sibling),
        (slots.at[2, high], slots.at[3, high], sibling),
        (slots.at[4, high], slots.at[5, high], sibling),
        (slots.at[2, low], slots.at[6, low], above),
        (slots.at[4, high], slots.at[6, high], beside),
        (slots.at[6, low], slots.at[7, low], sibling),
        (slots.at[6, high], slots.at[7, high], sibling),
    ]
    return [
        push(source, target, send_sem.at[index], recv_sem.at[index], {"fsdp": partner})
        for index, (source, target, partner) in enumerate(plan)
    ]


def attend_kernel(
    others, reach, source, gain_lines, positions, cosine, sine, inward_own, outward_own, vector_own,
    normed, normed_low, gains, linear, query_low, key_value, attended, middle, attn_lin,
    inward_all, outward_all, gate_all, vector_all, laurel_all,
    gain_slots, inward_slots, outward_slots, vector_slots, inward, lin_sum,
    gain_send, gain_recv, in_send, in_recv, out_send, out_recv, vec_send, vec_recv, kv_send, kv_recv,
    in_copy, out_copy, gate_copy, vec_copy, laurel_copy,
):
    rows_of, width = source.shape
    me, block = lax.axis_index("fsdp"), lax.axis_index("ctx")
    greet(me, range(1, 8), block, others)
    gain_copies = [
        push(gain_lines, gain_slots.at[distance], gain_send.at[distance - 1], gain_recv.at[distance - 1],
             {"fsdp": across_many(me, distance)})
        for distance in range(1, 8)
    ]
    for copy in gain_copies:
        copy.start()
    spread_in = spread_copies(inward_own, inward_slots, in_send, in_recv, me)
    spread_out = spread_copies(outward_own, outward_slots, out_send, out_recv, me)
    spread_vec = spread_copies(vector_own, vector_slots, vec_send, vec_recv, me)
    for index in range(5):
        spread_in[index].start()
    inward_slots[0] = inward_own[...]
    outward_slots[0] = outward_own[...]
    vector_slots[0] = vector_own[...]

    value = source[...].astype(jnp.float32)
    factor = lax.rsqrt(jnp.mean(value * value, axis=-1, keepdims=True) + epsilon)
    for copy in gain_copies:
        copy.wait_recv()
    gain_slots[0] = gain_lines[...]
    gains[...] = jnp.sum(gain_slots[...].astype(jnp.float32), axis=0)
    value = value * factor * gains[0:1, :]
    normed[...] = value
    normed_low[...] = value.astype(jnp.bfloat16)

    depth = inward_own.shape[0]
    head_rows = width // 8
    written = []

    def add_inward(slot):
        device = across_many(me, slot)
        part = normed_low[:, pl.ds(pl.multiple_of(device * depth, depth), depth)]
        for start in range(0, inward.shape[1], 640):
            span = pl.ds(start, 640)
            product = jnp.dot(part, inward_slots[slot, :, span], preferred_element_type=jnp.float32)
            inward[:, span] = product if slot == 0 else inward[:, span] + product
        copy = pltpu.make_async_copy(
            inward_slots.at[slot], inward_all.at[pl.ds(pl.multiple_of(device * depth, depth), depth)], in_copy.at[slot]
        )
        copy.start()
        written.append(copy)

    def add_outward(slot):
        device = across_many(me, slot)
        part = attended[:, pl.ds(pl.multiple_of(device * head_rows, head_rows), head_rows)]
        for start in range(0, width, 512):
            span = pl.ds(start, 512)
            product = jnp.dot(part, outward_slots[slot, pl.ds(0, head_rows), span], preferred_element_type=jnp.float32)
            lin_sum[:, span] = product if slot == 0 else lin_sum[:, span] + product

    def write_outward(slot):
        device = across_many(me, slot)
        rows = pl.ds(pl.multiple_of(device * head_rows, head_rows), head_rows)
        copies = [
            pltpu.make_async_copy(outward_slots.at[slot, :, pl.ds(0, width)], outward_all.at[rows], out_copy.at[slot]),
            pltpu.make_async_copy(
                outward_slots.at[slot, :, pl.ds(width, gate_all.shape[1])], gate_all.at[rows], gate_copy.at[slot]
            ),
        ]
        for copy in copies:
            copy.start()
        written.extend(copies)

    def write_vector(slot):
        device = across_many(me, slot)
        size = vector_all.shape[0] // 8
        rows = pl.ds(pl.multiple_of(device * size, size), size)
        copies = [
            pltpu.make_async_copy(vector_slots.at[slot, pl.ds(0, size)], vector_all.at[rows], vec_copy.at[slot]),
            pltpu.make_async_copy(
                vector_slots.at[slot, pl.ds(size, laurel_all.shape[1])], laurel_all.at[device], laurel_copy.at[slot]
            ),
        ]
        for copy in copies:
            copy.start()
        written.extend(copies)

    add_inward(0)
    spread_in[0].wait_recv()
    add_inward(1)
    spread_in[1].wait_recv()
    spread_in[9].start()
    spread_in[5].start()
    spread_in[2].wait_recv()
    spread_in[6].start()
    spread_in[3].wait_recv()
    spread_in[7].start()
    spread_in[4].wait_recv()
    spread_in[10].start()
    spread_in[8].start()
    add_inward(2)
    add_inward(4)
    spread_in[5].wait_recv()
    spread_in[7].wait_recv()
    add_inward(3)
    spread_in[6].wait_recv()
    spread_in[8].wait_recv()
    add_inward(5)
    spread_in[9].wait_recv()
    spread_in[11].start()
    spread_in[10].wait_recv()
    spread_in[12].start()
    for index in range(5):
        spread_out[index].start()
    add_inward(6)
    spread_in[11].wait_recv()
    spread_in[12].wait_recv()
    add_inward(7)

    query_width, key_width = QUERY_HEADS * HEAD_SIZE, KEY_VALUE_HEADS * HEAD_SIZE
    own_rows = pl.ds(0, rows_of)

    def head(start, gain):
        lane = inward[:, pl.ds(start, HEAD_SIZE)]
        scale = lax.rsqrt(jnp.mean(lane * lane, axis=-1, keepdims=True) + epsilon)
        return turn(lane * scale * gain, cosine[...], sine[...]).astype(jnp.bfloat16)

    for index in range(KEY_VALUE_HEADS):
        key_value[own_rows, pl.ds(index * HEAD_SIZE, HEAD_SIZE)] = head(
            query_width + index * HEAD_SIZE, gains[7:8, 0:HEAD_SIZE]
        )
    key_value[own_rows, pl.ds(key_width, key_width)] = inward[:, pl.ds(query_width + key_width, key_width)].astype(
        jnp.bfloat16
    )
    for distance in range(1, reach + 1):
        copy = push(
            key_value.at[own_rows],
            key_value.at[pl.ds(distance * rows_of, rows_of)],
            kv_send.at[distance - 1],
            kv_recv.at[distance - 1],
            {"ctx": (block + distance) % (others + 1)},
        )

        @pl.when(block + distance <= others)
        def _():
            copy.start()

        @pl.when(block < distance)
        def _():
            key_value[pl.ds(distance * rows_of, rows_of), :] = jnp.zeros((rows_of, 2 * key_width), jnp.bfloat16)

    for index in range(QUERY_HEADS):
        query_low[:, pl.ds(index * HEAD_SIZE, HEAD_SIZE)] = head(index * HEAD_SIZE, gains[6:7, 0:HEAD_SIZE])
    linear[...] = inward[:, pl.ds(0, query_width + key_width)]
    middle[...] = inward[:, pl.ds(query_width + 2 * key_width, middle.shape[1])].astype(jnp.bfloat16)

    spread_out[0].wait_recv()
    spread_out[1].wait_recv()
    spread_out[9].start()
    spread_out[5].start()
    spread_out[2].wait_recv()
    spread_out[6].start()
    for distance in range(1, reach + 1):
        copy = push(
            key_value.at[own_rows],
            key_value.at[pl.ds(distance * rows_of, rows_of)],
            kv_send.at[distance - 1],
            kv_recv.at[distance - 1],
            {"ctx": (block + distance) % (others + 1)},
        )

        @pl.when(block >= distance)
        def _():
            copy.wait_recv()

    allowed = window_mask(positions[...], rows_of, reach + 1)
    per_group = QUERY_HEADS // KEY_VALUE_HEADS
    for index in range(QUERY_HEADS):
        group = index // per_group
        columns = pl.ds(index * HEAD_SIZE, HEAD_SIZE)
        scores = product_back(query_low[:, columns], key_value[:, pl.ds(group * HEAD_SIZE, HEAD_SIZE)])
        scores = jnp.where(allowed, scores * HEAD_SIZE ** (-0.5), -1e30)
        grown = jnp.exp(scores - jnp.max(scores, axis=-1, keepdims=True))
        soft = (grown / jnp.sum(grown, axis=-1, keepdims=True)).astype(jnp.bfloat16)
        attended[:, columns] = jnp.dot(
            soft, key_value[:, pl.ds(key_width + group * HEAD_SIZE, HEAD_SIZE)], preferred_element_type=jnp.float32
        ).astype(jnp.bfloat16)

    add_outward(0)
    add_outward(1)
    write_outward(0)
    write_outward(1)
    spread_out[3].wait_recv()
    spread_out[7].start()
    spread_out[4].wait_recv()
    spread_out[10].start()
    spread_out[8].start()
    for index in range(5):
        spread_vec[index].start()
    add_outward(2)
    add_outward(4)
    spread_out[5].wait_recv()
    spread_out[7].wait_recv()
    add_outward(3)
    spread_out[6].wait_recv()
    spread_out[8].wait_recv()
    add_outward(5)
    for slot in range(2, 6):
        write_outward(slot)
    spread_out[9].wait_recv()
    spread_out[11].start()
    spread_out[10].wait_recv()
    spread_out[12].start()
    add_outward(6)
    write_outward(6)
    for index in range(5):
        spread_vec[index].wait_recv()
    for index in range(5, 11):
        spread_vec[index].start()
    spread_out[11].wait_recv()
    spread_out[12].wait_recv()
    add_outward(7)
    write_outward(7)
    attn_lin[...] = lin_sum[...]
    for index in range(5, 11):
        spread_vec[index].wait_recv()
    spread_vec[11].start()
    spread_vec[12].start()
    spread_vec[11].wait_recv()
    spread_vec[12].wait_recv()
    for slot in range(8):
        write_vector(slot)
    for copy in gain_copies + spread_in + spread_out + spread_vec:
        copy.wait_send()
    for copy in written:
        copy.wait()
    for distance in range(1, reach + 1):
        copy = push(
            key_value.at[own_rows],
            key_value.at[pl.ds(distance * rows_of, rows_of)],
            kv_send.at[distance - 1],
            kv_recv.at[distance - 1],
            {"ctx": (block + distance) % (others + 1)},
        )

        @pl.when(block + distance <= others)
        def _():
            copy.wait_send()


def attend_call(reach, source, gain_lines, positions, cosine, sine, inward_own, outward_own, vector_own, vector_rows):
    rows_of, width = source.shape
    others = lax.axis_size("ctx") - 1
    low, full = jnp.bfloat16, jnp.float32
    hbm = pl.BlockSpec(memory_space=pl.ANY)
    vmem = pl.BlockSpec(memory_space=pltpu.VMEM)
    dma = pltpu.SemaphoreType.DMA
    depth, columns = inward_own.shape
    query_width, key_width = QUERY_HEADS * HEAD_SIZE, KEY_VALUE_HEADS * HEAD_SIZE
    tail = columns - query_width - 2 * key_width
    shapes = [
        jax.ShapeDtypeStruct((rows_of, width), full),
        jax.ShapeDtypeStruct((rows_of, width), low),
        jax.ShapeDtypeStruct(gain_lines.shape, full),
        jax.ShapeDtypeStruct((rows_of, query_width + key_width), full),
        jax.ShapeDtypeStruct((rows_of, query_width), low),
        jax.ShapeDtypeStruct(((reach + 1) * rows_of, 2 * key_width), low),
        jax.ShapeDtypeStruct((rows_of, query_width), low),
        jax.ShapeDtypeStruct((rows_of, tail), low),
        jax.ShapeDtypeStruct((rows_of, width), full),
        jax.ShapeDtypeStruct((8 * depth, columns), low),
        jax.ShapeDtypeStruct((8 * outward_own.shape[0], width), low),
        jax.ShapeDtypeStruct((8 * outward_own.shape[0], outward_own.shape[1] - width), low),
        jax.ShapeDtypeStruct((8 * vector_rows, width), low),
        jax.ShapeDtypeStruct((8, 16, width), low),
    ]
    return pl.pallas_call(
        functools.partial(attend_kernel, others, reach),
        out_shape=shapes,
        in_specs=[vmem] * 8,
        out_specs=[vmem] * 9 + [hbm] * 5,
        scratch_shapes=[
            pltpu.VMEM((8, *gain_lines.shape), low),
            pltpu.VMEM((8, depth, columns), low),
            pltpu.VMEM((8, *outward_own.shape), low),
            pltpu.VMEM((8, *vector_own.shape), low),
            pltpu.VMEM((rows_of, columns), full),
            pltpu.VMEM((rows_of, width), full),
            dma((7,)),
            dma((7,)),
            dma((13,)),
            dma((13,)),
            dma((13,)),
            dma((13,)),
            dma((13,)),
            dma((13,)),
            dma((max(reach, 1),)),
            dma((max(reach, 1),)),
        ]
        + [dma((8,))] * 5,
        compiler_params=pltpu.CompilerParams(collective_id=3, has_side_effects=True, vmem_limit_bytes=56 * 2**20),
        cost_estimate=pl.CostEstimate(
            flops=60 * rows_of * width * columns, bytes_accessed=20 * depth * columns, transcendentals=0
        ),
        name="attend_forward",
    )(source, gain_lines, positions, cosine, sine, inward_own, outward_own, vector_own)


def turn_norm_grad(upstream, linear, gain, cosine, sine):
    scale = lax.rsqrt(jnp.mean(linear * linear, axis=-1, keepdims=True) + epsilon)
    unit = linear * scale
    back = turn(upstream, cosine, sine, -1.0)
    grad_gain = jnp.sum(back * unit, axis=0, keepdims=True)
    back = back * gain
    return scale * (back - unit * jnp.mean(back * unit, axis=-1, keepdims=True)), grad_gain


def attend_back_kernel(
    others, reach, d_lin, query_low, key_value, linear, gains, positions, cosine, sine, d_middle, features,
    source, d_half, gain_rows, laurel_rows, gate_parts, out_parts, outward_all, inward_all, d_rows,
    d_source, grad_wide, grad_small, near_hbm,
    outward, inward, d_attended, d_key_value, parcel, arrived, d_query, d_rest, lin_slots, query_slots, rest_slots,
    ordered, d_normed, gain_parcel, gain_arrived, laurel_arrived, load_sem, lin_send, lin_recv, query_send, query_recv, rest_send, rest_recv, kv_send, kv_recv, gain_send, gain_recv, laurel_send, laurel_recv, near_send, near_recv,
    gate_in, gate_sum, gate_arrived, out_in, out_sum, out_arrived, pair_send, pair_recv, chip_send, chip_recv,
):
    rows_of, width = d_lin.shape
    me, block = lax.axis_index("fsdp"), lax.axis_index("ctx")
    query_width, key_width = QUERY_HEADS * HEAD_SIZE, KEY_VALUE_HEADS * HEAD_SIZE
    per_group = QUERY_HEADS // KEY_VALUE_HEADS
    depth = width // 8
    loads = [
        pltpu.make_async_copy(outward_all.at[pl.ds(index * depth, depth)], outward.at[index], load_sem.at[index])
        for index in range(8)
    ]
    loads.append(pltpu.make_async_copy(inward_all, inward, load_sem.at[8]))
    for load in loads:
        load.start()
    greet(me, range(1, 8), block, others)
    mine, theirs = pl.ds(0, rows_of), pl.ds(rows_of, rows_of)
    near = [
        push(
            d_rows.at[pl.ds(group * 2 * rows_of, rows_of)],
            near_hbm.at[group, mine],
            near_send.at[group],
            near_recv.at[group],
            {"ctx": across(block, 1)},
        )
        for group in range(4)
    ]
    near_share = [
        push(
            near_hbm.at[group, mine],
            near_hbm.at[group, theirs],
            near_send.at[4 + group],
            near_recv.at[4 + group],
            {"fsdp": across(me, 1)},
        )
        for group in range(4)
    ]
    for copy in near[:2]:
        copy.start()
    vector_parts = ((gate_parts, gate_in, gate_sum, gate_arrived), (out_parts, out_in, out_sum, out_arrived))
    chips = (0, 2, 4, 6)
    pair_copies = []
    chip_copies = []
    for kind, (parts, pair_in, pair_sum, arrived_parts) in enumerate(vector_parts):
        for index, chip in enumerate(chips):
            place = 4 * kind + index
            pair_copies.append(
                push(
                    parts.at[across_many(me, chip + 1)],
                    pair_in.at[index],
                    pair_send.at[place],
                    pair_recv.at[place],
                    {"fsdp": across(me, 1)},
                )
            )
            if chip:
                place = 3 * kind + index - 1
                chip_copies.append(
                    push(
                        pair_sum.at[index - 1],
                        arrived_parts.at[index - 1],
                        chip_send.at[place],
                        chip_recv.at[place],
                        {"fsdp": across_many(me, chip)},
                    )
                )
    for copy in pair_copies:
        copy.start()
    spread_lin = spread_copies(d_lin, lin_slots, lin_send, lin_recv, me)
    spread_query = spread_copies(d_query, query_slots, query_send, query_recv, me)
    spread_rest = spread_copies(d_rest, rest_slots, rest_send, rest_recv, me)
    for index in range(5):
        spread_lin[index].start()
    lin_slots[0] = d_lin[...]
    laurel_copies = [
        push(
            laurel_rows.at[across_many(me, distance)],
            laurel_arrived.at[distance],
            laurel_send.at[distance - 1],
            laurel_recv.at[distance - 1],
            {"fsdp": across_many(me, distance)},
        )
        for distance in range(1, 8)
    ]
    laurel_arrived[0] = laurel_rows[me]
    for slot in range(8):
        device = across_many(me, slot)
        ordered[pl.ds(slot * rows_of, rows_of), :] = features[
            pl.ds(pl.multiple_of(device * rows_of, rows_of), rows_of), :
        ]
    for index in range(8):
        loads[index].wait()
        d_attended[:, pl.ds(index * depth, depth)] = product_back(d_lin[...], outward[index]).astype(jnp.bfloat16)

    allowed = window_mask(positions[...], rows_of, reach + 1)
    scale = HEAD_SIZE ** (-0.5)

    def one_head(index):
        group = index // per_group
        columns = pl.ds(index * HEAD_SIZE, HEAD_SIZE)
        keys = pl.ds(group * HEAD_SIZE, HEAD_SIZE)
        values = pl.ds(key_width + group * HEAD_SIZE, HEAD_SIZE)
        scores = product_back(query_low[:, columns], key_value[:, keys])
        scores = jnp.where(allowed, scores * scale, -1e30)
        grown = jnp.exp(scores - jnp.max(scores, axis=-1, keepdims=True))
        soft = grown / jnp.sum(grown, axis=-1, keepdims=True)
        d_soft = product_back(d_attended[:, columns], key_value[:, values])
        d_scores = (soft * (d_soft - jnp.sum(soft * d_soft, axis=-1, keepdims=True))).astype(jnp.bfloat16)
        upstream = scale * jnp.dot(d_scores, key_value[:, keys], preferred_element_type=jnp.float32)
        d_key = scale * product_rows(d_scores, query_low[:, columns])
        d_value = product_rows(soft.astype(jnp.bfloat16), d_attended[:, columns])
        if index % per_group == 0:
            d_key_value[:, keys] = d_key
            d_key_value[:, values] = d_value
        else:
            d_key_value[:, keys] += d_key
            d_key_value[:, values] += d_value
        d_head, grad_gain = turn_norm_grad(upstream, linear[:, columns], gains[6:7, 0:HEAD_SIZE], cosine[...], sine[...])
        d_query[:, columns] = d_head.astype(jnp.bfloat16)
        return grad_gain

    query_gain = one_head(0)
    for index in range(1, per_group):
        query_gain = query_gain + one_head(index)
    spread_lin[0].wait_recv()
    spread_lin[1].wait_recv()
    spread_lin[9].start()
    spread_lin[5].start()
    spread_lin[2].wait_recv()
    spread_lin[6].start()
    for index in range(per_group, QUERY_HEADS):
        query_gain = query_gain + one_head(index)
    parcel[...] = d_key_value[pl.ds(rows_of, reach * rows_of), :].astype(jnp.bfloat16)

    def return_copy(distance):
        span = pl.ds((distance - 1) * rows_of, rows_of)
        return push(
            parcel.at[span],
            arrived.at[span],
            kv_send.at[distance - 1],
            kv_recv.at[distance - 1],
            {"ctx": (block + others + 1 - distance) % (others + 1)},
        )

    for distance in range(1, reach + 1):
        copy = return_copy(distance)

        @pl.when(block >= distance)
        def _():
            copy.start()

        @pl.when(block + distance > others)
        def _():
            arrived[pl.ds((distance - 1) * rows_of, rows_of), :] = jnp.zeros((rows_of, 2 * key_width), jnp.bfloat16)

    for copy in near[2:]:
        copy.start()
    spread_lin[3].wait_recv()
    spread_lin[7].start()
    spread_lin[4].wait_recv()
    spread_lin[10].start()
    spread_lin[8].start()
    for index in range(5):
        spread_query[index].start()
    for copy in pair_copies:
        copy.wait_recv()
    for parts, pair_in, pair_sum, arrived_parts in vector_parts:
        for index, chip in enumerate(chips):
            if chip:
                pair_sum[index - 1] = (
                    parts[across_many(me, chip)].astype(jnp.float32) + pair_in[index].astype(jnp.float32)
                ).astype(jnp.bfloat16)
    for copy in chip_copies:
        copy.start()
    query_slots[0] = d_query[...]
    loads[8].wait()
    d_normed[...] = product_back(d_query[...], inward[:, pl.ds(0, query_width)])
    spread_lin[9].wait_recv()
    spread_lin[11].start()
    spread_lin[10].wait_recv()
    spread_lin[12].start()
    spread_query[0].wait_recv()
    spread_query[1].wait_recv()
    spread_query[9].start()
    spread_query[5].start()
    spread_query[2].wait_recv()
    spread_query[6].start()
    for index in (5, 6, 7, 8, 11, 12):
        spread_lin[index].wait_recv()
    grad_wide[:, pl.ds(inward.shape[1], width)] = product_rows(
        ordered[:, pl.ds(depth, depth)], lin_slots[...].reshape(8 * rows_of, width)
    ).astype(jnp.bfloat16)

    for distance in range(1, reach + 1):
        copy = return_copy(distance)

        @pl.when(block + distance <= others)
        def _():
            copy.wait_recv()

    total = d_key_value[pl.ds(0, rows_of), :]
    for distance in range(1, reach + 1):
        total = total + arrived[pl.ds((distance - 1) * rows_of, rows_of), :].astype(jnp.float32)
    for index in range(KEY_VALUE_HEADS):
        columns = pl.ds(index * HEAD_SIZE, HEAD_SIZE)
        d_head, grad_gain = turn_norm_grad(
            total[:, index * HEAD_SIZE : (index + 1) * HEAD_SIZE],
            linear[:, pl.ds(query_width + index * HEAD_SIZE, HEAD_SIZE)],
            gains[7:8, 0:HEAD_SIZE],
            cosine[...],
            sine[...],
        )
        d_rest[:, columns] = d_head.astype(jnp.bfloat16)
        key_gain = grad_gain if index == 0 else key_gain + grad_gain
    d_rest[:, pl.ds(key_width, key_width)] = total[:, key_width:].astype(jnp.bfloat16)
    d_rest[:, pl.ds(2 * key_width, d_middle.shape[1])] = d_middle[...]
    spread_query[3].wait_recv()
    spread_query[7].start()
    spread_query[4].wait_recv()
    spread_query[10].start()
    spread_query[8].start()
    for index in range(5):
        spread_rest[index].start()
    rest_slots[0] = d_rest[...]
    rest_width = d_rest.shape[1]
    d_normed[...] += product_back(d_rest[...], inward[:, pl.ds(query_width, rest_width)])
    value = source[...].astype(jnp.float32)
    factor = lax.rsqrt(jnp.mean(value * value, axis=-1, keepdims=True) + epsilon)
    unit = value * factor
    upstream = d_half[...] + d_normed[...]
    for index in range(8):
        columns = slice(index * depth, (index + 1) * depth)
        gain_parcel[index, 0:8, :] = gain_rows[0:8, columns]
        gain_parcel[index, 0:1, :] = jnp.sum(upstream[:, columns] * unit[:, columns], axis=0, keepdims=True)
        gain_parcel[index, 6:7, :] = query_gain
        gain_parcel[index, 7:8, :] = key_gain
    gain_copies = [
        push(
            gain_parcel.at[across_many(me, distance)],
            gain_arrived.at[distance],
            gain_send.at[distance - 1],
            gain_recv.at[distance - 1],
            {"fsdp": across_many(me, distance)},
        )
        for distance in range(1, 8)
    ]
    for copy in gain_copies + laurel_copies:
        copy.start()
    gain_arrived[0] = gain_parcel[me]
    upstream = upstream * gains[0:1, :]
    d_source[...] = d_half[...] + factor * (upstream - unit * jnp.mean(upstream * unit, axis=-1, keepdims=True))
    spread_rest[0].wait_recv()
    spread_rest[1].wait_recv()
    spread_rest[9].start()
    spread_rest[5].start()
    spread_rest[2].wait_recv()
    spread_rest[6].start()
    spread_query[9].wait_recv()
    spread_query[11].start()
    spread_query[10].wait_recv()
    spread_query[12].start()
    spread_rest[3].wait_recv()
    spread_rest[7].start()
    spread_rest[4].wait_recv()
    spread_rest[10].start()
    spread_rest[8].start()
    for index in (5, 6, 7, 8, 11, 12):
        spread_query[index].wait_recv()
    grad_wide[:, pl.ds(0, query_width)] = product_rows(
        ordered[:, pl.ds(0, depth)], query_slots[...].reshape(8 * rows_of, query_width)
    ).astype(jnp.bfloat16)
    spread_rest[9].wait_recv()
    spread_rest[11].start()
    spread_rest[10].wait_recv()
    spread_rest[12].start()
    for index in (5, 6, 7, 8, 11, 12):
        spread_rest[index].wait_recv()
    grad_wide[:, pl.ds(query_width, rest_width)] = product_rows(
        ordered[:, pl.ds(0, depth)], rest_slots[...].reshape(8 * rows_of, rest_width)
    ).astype(jnp.bfloat16)
    for copy, share in zip(near, near_share):
        copy.wait_recv()
        share.start()
    for copy in gain_copies + laurel_copies + chip_copies:
        copy.wait_recv()
    totals = []
    for parts, pair_in, pair_sum, arrived_parts in vector_parts:
        total = parts[me].astype(jnp.float32) + pair_in[0].astype(jnp.float32)
        for index in range(3):
            total = total + arrived_parts[index].astype(jnp.float32)
        totals.append(total.astype(jnp.bfloat16))
    grad_wide[:, pl.ds(inward.shape[1] + width, totals[0].shape[1])] = totals[0]
    laurel_size = laurel_rows.shape[1]
    tail = jnp.concatenate(
        [jnp.sum(laurel_arrived[...], axis=0), jnp.pad(jnp.sum(gain_arrived[...], axis=0), ((0, 0), (0, width - depth)))],
        axis=0,
    )
    out_size = totals[1].shape[0]
    grad_small[pl.ds(0, out_size), :] = totals[1]
    grad_small[pl.ds(out_size, laurel_size + 8), :] = tail.astype(jnp.bfloat16)
    for copy in near_share:
        copy.wait_recv()
    for copy in (
        spread_lin + spread_query + spread_rest + gain_copies + laurel_copies + near + near_share + pair_copies + chip_copies
    ):
        copy.wait_send()
    for distance in range(1, reach + 1):
        copy = return_copy(distance)

        @pl.when(block >= distance)
        def _():
            copy.wait_send()


def attend_back_call(
    reach, d_lin, query_low, key_value, linear, gains, positions, cosine, sine, d_middle, features,
    source, d_half, gain_rows, laurel_rows, gate_parts, out_parts, outward_all, inward_all, d_rows,
):
    rows_of, width = d_lin.shape
    others = lax.axis_size("ctx") - 1
    low, full = jnp.bfloat16, jnp.float32
    hbm = pl.BlockSpec(memory_space=pl.ANY)
    vmem = pl.BlockSpec(memory_space=pltpu.VMEM)
    dma = pltpu.SemaphoreType.DMA
    columns = inward_all.shape[1]
    query_width, key_width = QUERY_HEADS * HEAD_SIZE, KEY_VALUE_HEADS * HEAD_SIZE
    rest_width = columns - query_width
    depth = width // 8
    shapes = [
        jax.ShapeDtypeStruct((rows_of, width), full),
        jax.ShapeDtypeStruct((depth, columns + width + gate_parts.shape[2]), low),
        jax.ShapeDtypeStruct((out_parts.shape[1] + laurel_rows.shape[1] + 8, width), low),
        jax.ShapeDtypeStruct((4, 2 * rows_of, width), low),
    ]
    spans = max(reach, 1)
    return pl.pallas_call(
        functools.partial(attend_back_kernel, others, reach),
        out_shape=shapes,
        in_specs=[vmem] * 16 + [hbm] * 3,
        out_specs=[vmem] * 3 + [hbm],
        scratch_shapes=[
            pltpu.VMEM((8, depth, width), low),
            pltpu.VMEM((width, columns), low),
            pltpu.VMEM((rows_of, query_width), low),
            pltpu.VMEM(((reach + 1) * rows_of, 2 * key_width), full),
            pltpu.VMEM((spans * rows_of, 2 * key_width), low),
            pltpu.VMEM((spans * rows_of, 2 * key_width), low),
            pltpu.VMEM((rows_of, query_width), low),
            pltpu.VMEM((rows_of, rest_width), low),
            pltpu.VMEM((8, rows_of, width), low),
            pltpu.VMEM((8, rows_of, query_width), low),
            pltpu.VMEM((8, rows_of, rest_width), low),
            pltpu.VMEM((8 * rows_of, 2 * depth), low),
            pltpu.VMEM((rows_of, width), full),
            pltpu.VMEM((8, 8, depth), full),
            pltpu.VMEM((8, 8, depth), full),
            pltpu.VMEM(laurel_rows.shape, full),
            dma((9,)),
            dma((13,)),
            dma((13,)),
            dma((13,)),
            dma((13,)),
            dma((13,)),
            dma((13,)),
            dma((spans,)),
            dma((spans,)),
            dma((7,)),
            dma((7,)),
            dma((7,)),
            dma((7,)),
            dma((8,)),
            dma((8,)),
        ]
        + [
            pltpu.VMEM((count, *parts.shape[1:]), low)
            for parts in (gate_parts, out_parts)
            for count in (4, 3, 3)
        ]
        + [dma((8,)), dma((8,)), dma((6,)), dma((6,))],
        compiler_params=pltpu.CompilerParams(collective_id=4, has_side_effects=True, vmem_limit_bytes=60 * 2**20),
        cost_estimate=pl.CostEstimate(
            flops=40 * rows_of * width * columns, bytes_accessed=6 * width * columns, transcendentals=0
        ),
        name="attend_backward",
    )(
        d_lin, query_low, key_value, linear, gains, positions, cosine, sine, d_middle, features,
        source, d_half, gain_rows, laurel_rows, gate_parts, out_parts, outward_all, inward_all, d_rows,
    )


def feed_call(forward, own, weights, kept=(), features=None, forward_rows=None):
    rows_of, width = own.shape
    hidden = weights[0].shape[0]
    all_rows = 8 * rows_of
    others = lax.axis_size("ctx") - 1
    low = jnp.bfloat16
    count_made = 3 if forward else 2
    hbm = pl.BlockSpec(memory_space=pl.ANY)
    vmem = pl.BlockSpec(memory_space=pltpu.VMEM)
    half = rows_of // 2
    dma = pltpu.SemaphoreType.DMA
    shapes = [
        jax.ShapeDtypeStruct((rows_of, width), jnp.float32),
        jax.ShapeDtypeStruct((all_rows, width), low),
        jax.ShapeDtypeStruct((2, rows_of, width), low),
        jax.ShapeDtypeStruct((2, 2 * rows_of, width), low),
    ]
    operands = (own, *weights, *kept)
    operand_specs = [vmem] + [hbm] * (3 + len(kept))
    slice_sems = []
    if forward:
        shapes += [jax.ShapeDtypeStruct((8, rows_of, features.shape[1] // 8), low)]
        operands += (features,)
        operand_specs += [vmem]
        slice_sems = [dma((7,)), dma((7,)), dma]
    else:
        operands += (forward_rows,)
        operand_specs += [hbm]
    shapes += [jax.ShapeDtypeStruct((all_rows, hidden), low)] * count_made
    return pl.pallas_call(
        functools.partial(feed_kernel, forward, rows_of, others),
        out_shape=shapes,
        in_specs=operand_specs,
        out_specs=[vmem] + [hbm] * (len(shapes) - 1),
        scratch_shapes=[pltpu.VMEM((hidden, width), low)] * 3
        + [pltpu.VMEM((all_rows, hidden), low)] * (len(kept) + count_made)
        + [
            pltpu.VMEM((4, 2 * rows_of, width), low),
            pltpu.VMEM((4, 2 * rows_of, width), low),
            pltpu.VMEM((4, rows_of, width), low),
            pltpu.VMEM((3, rows_of, width), low),
            pltpu.VMEM((2, half, width), low),
            pltpu.VMEM((2, half, width), low),
            pltpu.VMEM((4, half, width), low),
            dma((20,)),
            dma((20,)),
            dma((3 + len(kept),)),
            dma((4 * (1 + count_made),)),
            dma((2,)),
            dma((2,)),
            dma((4,)),
            dma((4,)),
        ]
        + slice_sems,
        compiler_params=pltpu.CompilerParams(
            collective_id=1 if forward else 2,
            has_side_effects=True,
            vmem_limit_bytes=56 * 2**20,
        ),
        cost_estimate=pl.CostEstimate(
            flops=40 * all_rows * hidden * width // 2,
            bytes_accessed=6 * hidden * width + 8 * all_rows * width,
            transcendentals=0,
        ),
        name="feed_forward" if forward else "feed_backward",
    )(*operands)


def weight_grad_kernel(
    own_steps, near_steps, gate, up, down, rows, d_rows, hidden, d_gate, d_up,
    rows_near, rows_next, d_rows_near, rows_far, d_rows_far,
    grad_gate, grad_up, grad_down, hidden_tile, d_gate_tile, d_up_tile,
):
    step = pl.program_id(1)
    tile = 512
    hidden_size = gate.shape[0]
    chunk = rows.shape[1]

    @pl.when(step == 0)
    def _():
        grad_gate[...] = jnp.zeros_like(grad_gate)
        grad_up[...] = jnp.zeros_like(grad_up)
        grad_down[...] = jnp.zeros_like(grad_down)

    def accumulate(rows, d_rows):
        def body(index, carry):
            columns = pl.ds(pl.multiple_of(index * chunk, chunk), chunk)
            right, d_right = rows[:, columns], d_rows[:, columns]
            grad_gate[:, columns] += matrix_product(d_gate_tile[...], right)
            grad_up[:, columns] += matrix_product(d_up_tile[...], right)
            grad_down[:, columns] += matrix_product(hidden_tile[...], d_right)
            return carry
        lax.fori_loop(0, rows.shape[1] // chunk, body, 0)

    @pl.when(step < own_steps)
    def _():
        hidden_tile[...] = hidden[...].T
        d_gate_tile[...] = d_gate[...].T
        d_up_tile[...] = d_up[...].T
        accumulate(rows, d_rows)

    def other_rows(rows, d_rows):
        def body(index, carry):
            span = pl.ds(pl.multiple_of(index * tile, tile), tile)
            gate_value = product_back(gate[span, :], rows[...])
            up_value = product_back(up[span, :], rows[...])
            d_hidden = product_back(down[span, :], d_rows[...])
            value, slope = gelu_parts(gate_value)
            hidden_tile[span, :] = (value * up_value).astype(jnp.bfloat16)
            d_gate_tile[span, :] = (d_hidden * up_value * slope).astype(jnp.bfloat16)
            d_up_tile[span, :] = (d_hidden * value).astype(jnp.bfloat16)
            return carry

        lax.fori_loop(0, hidden_size // tile, body, 0)
        accumulate(rows, d_rows)

    @pl.when((step >= own_steps) & (step < own_steps + near_steps // 2))
    def _():
        other_rows(rows_near, d_rows_near)

    @pl.when((step >= own_steps + near_steps // 2) & (step < own_steps + near_steps))
    def _():
        other_rows(rows_next, d_rows_near)

    @pl.when(step >= own_steps + near_steps)
    def _():
        other_rows(rows_far, d_rows_far)


def weight_grad_call(
    gate, up, down, rows, d_rows, hidden, d_gate, d_up, rows_near, rows_next, d_rows_near, rows_far, d_rows_far,
    hid=1024, tok=256,
):
    size, width = gate.shape
    hid = min(hid, size)
    own_steps, near_steps, far_steps = [value.shape[0] // tok for value in (rows, d_rows_near, rows_far)]
    low = jnp.bfloat16

    def stream(first, steps, columns, across):
        def place(h, s):
            return jnp.clip(s - first, 0, steps - 1), h if across else 0

        return pl.BlockSpec((tok, columns), place)

    weight = pl.BlockSpec((hid, width), lambda h, s: (h, 0))
    own = stream(0, own_steps, width, False)
    own_mid = stream(0, own_steps, hid, True)
    near_one = stream(own_steps, near_steps // 2, width, False)
    near_two = stream(own_steps + near_steps // 2, near_steps // 2, width, False)
    near = stream(own_steps, near_steps, width, False)
    far = stream(own_steps + near_steps, far_steps, width, False)
    flops = 6 * size * width * (rows.shape[0] + 2 * d_rows_near.shape[0] + 2 * rows_far.shape[0])
    return pl.pallas_call(
        functools.partial(weight_grad_kernel, own_steps, near_steps),
        grid=(size // hid, own_steps + near_steps + far_steps),
        in_specs=[weight] * 3 + [own] * 2 + [own_mid] * 3 + [near_one, near_two, near] + [far] * 2,
        out_specs=[weight] * 3,
        out_shape=[jax.ShapeDtypeStruct((size, width), jnp.float32)] * 3,
        scratch_shapes=[pltpu.VMEM((hid, tok), low)] * 3,
        compiler_params=pltpu.CompilerParams(
            dimension_semantics=("arbitrary", "arbitrary"), vmem_limit_bytes=62 * 2**20
        ),
        cost_estimate=pl.CostEstimate(flops=flops, bytes_accessed=100 * 2**20, transcendentals=0),
        name="weight_grads",
    )(
        gate, up, down, rows, d_rows, hidden, d_gate, d_up, rows_near, rows_next, d_rows_near, rows_far, d_rows_far
    )


def per_device(
    tokens,
    per_layer,
    segments,
    positions,
    cotangent,
    query_weight,
    key_matrix,
    value_matrix,
    output_weight,
    laurel_down,
    laurel_up,
    vector_gate,
    vector_out,
    norm_input,
    norm_attention,
    norm_laurel,
    norm_before,
    norm_after,
    norm_vector,
    query_norm_gain,
    norm_key,
    hidden_gate,
    hidden_up,
    hidden_down,
):
    count_of_rows = tokens.shape[0]
    shards = lax.axis_size("fsdp")
    width = tokens.shape[1]
    heads_per_group = QUERY_HEADS // KEY_VALUE_HEADS
    reach_blocks = min((WINDOW + count_of_rows - 2) // count_of_rows, lax.axis_size("ctx") - 1)
    score_scale = HEAD_SIZE ** (-0.5)
    fused = shards == 8 and lax.axis_size("ctx") == 4
    query_width = query_weight.shape[1]
    key_width = key_matrix.shape[1]

    gain_shards = (
        norm_input,
        norm_attention,
        norm_laurel,
        norm_before,
        norm_after,
        norm_vector,
        query_norm_gain,
        norm_key,
    )
    gain_sizes = [gain.shape[0] for gain in gain_shards]
    gain_starts = [sum(gain_sizes[:index]) for index in range(len(gain_sizes))]
    inward_weight = jnp.concatenate([query_weight, key_matrix, value_matrix, laurel_down], axis=1)
    inward_weight = jnp.pad(inward_weight, ((0, 0), (0, -inward_weight.shape[1] % 128)))
    source = tokens.astype(jnp.float32)
    vectors = per_layer.astype(jnp.float32)
    rank = laurel_down.shape[1]
    unused, allowed = window(positions, count_of_rows, reach_blocks)

    def head_facing(linear, gain):
        return rotary_apply(root_mean_norm(linear, gain), positions)

    if fused:
        me = lax.axis_index("fsdp")
        gain_lines = jnp.stack(
            [
                lax.dynamic_update_slice(jnp.zeros((width,), gain.dtype), gain, (me * gain.shape[0],))
                for gain in gain_shards
            ]
        )
        gain_lines = jnp.pad(gain_lines, ((0, 16 - len(gain_shards)), (0, 0)))
        cosine, sine_part = rotary_tables(positions, HEAD_SIZE)
        (
            normed,
            lowered_normed,
            gains_all,
            linear,
            query_lowered,
            key_value,
            attended_low,
            laurel_mid,
            attn_lin,
            full_inward,
            full_output,
            full_vector_gate,
            full_vector_out,
            full_laurel_up,
        ) = attend_call(
            reach_blocks,
            tokens,
            gain_lines,
            positions[:, None],
            cosine,
            sine_part,
            inward_weight,
            jnp.concatenate([output_weight, vector_gate], axis=1),
            jnp.concatenate([vector_out, laurel_up, jnp.zeros((24, width), jnp.bfloat16)], axis=0),
            vector_out.shape[0],
        )
        full_laurel_up = full_laurel_up[:, : laurel_up.shape[0]].reshape(-1, width)
        gains = [gains_all[index, : size * shards] for index, size in enumerate(gain_sizes)]
        laurel_mid = laurel_mid[:, :rank]
        window_keys, window_values = key_value[:, :key_width], key_value[:, key_width:]
    else:
        gain_line = jnp.concatenate(gain_shards)
        gain_line = jnp.pad(gain_line, (0, -gain_line.shape[0] % 2048)).reshape(-1, 128)
        gains_all = gather(gain_line, "fsdp").reshape(shards, -1)
        gains = [
            gains_all[:, start : start + size].reshape(-1).astype(jnp.float32)
            for start, size in zip(gain_starts, gain_sizes)
        ]
        full_inward = gather(inward_weight, "fsdp")
        full_output, full_vector_gate, full_vector_out, full_laurel_up = [
            gather(value, "fsdp") for value in (output_weight, vector_gate, vector_out, laurel_up)
        ]
        normed = root_mean_norm(source, gains[0])
        lowered_normed = normed.astype(jnp.bfloat16)
        inward = matrix_product(lowered_normed, full_inward)
        linear = inward[:, : query_width + key_width]
        value_lowered = inward[:, query_width + key_width : query_width + 2 * key_width].astype(jnp.bfloat16)
        laurel_mid = inward[:, query_width + 2 * key_width :][:, :rank].astype(jnp.bfloat16)
        query_lowered = head_facing(
            linear[:, :query_width].reshape(count_of_rows, QUERY_HEADS, HEAD_SIZE), gains[6]
        ).astype(jnp.bfloat16)
        key_lowered = head_facing(
            linear[:, query_width:].reshape(count_of_rows, KEY_VALUE_HEADS, HEAD_SIZE), gains[7]
        ).astype(jnp.bfloat16)
        key_value = jnp.stack([key_lowered.reshape(count_of_rows, -1), value_lowered])
        pair_blocks = [key_value]
        for distance in range(1, reach_blocks + 1):
            pair_blocks.append(from_behind(key_value, "ctx", distance))
        window_couple = jnp.concatenate(pair_blocks, axis=1)
        window_keys, window_values = window_couple[0], window_couple[1]
    (
        gain_input,
        gain_attention,
        gain_laurel,
        gain_before,
        gain_after,
        gain_vector,
        gain_query,
        key_norm_gain,
    ) = gains
    if not fused:
        query_linear = linear[:, :query_width].reshape(count_of_rows, QUERY_HEADS, HEAD_SIZE)
        key_linear = linear[:, query_width:].reshape(count_of_rows, KEY_VALUE_HEADS, HEAD_SIZE)
        query_lowered = query_lowered.reshape(count_of_rows, KEY_VALUE_HEADS, heads_per_group, HEAD_SIZE)
        window_keys = window_keys.reshape(-1, KEY_VALUE_HEADS, HEAD_SIZE)
        window_values = window_values.reshape(-1, KEY_VALUE_HEADS, HEAD_SIZE)

        def masked_scores():
            raw_scores = score_scale * jnp.einsum(
                "tgfd,kgd->gftk", query_lowered, window_keys, preferred_element_type=jnp.float32
            )
            return jnp.where(allowed, raw_scores, -1e30)

        scores_first = masked_scores()
        row_peak = jnp.max(scores_first, axis=-1, keepdims=True)
        exp_scores = jnp.exp(scores_first - row_peak)
        row_total = jnp.sum(exp_scores, axis=-1, keepdims=True)
        log_total = row_peak + jnp.log(row_total)
        soft_low = (exp_scores / row_total).astype(jnp.bfloat16)
        attended_low = (
            jnp.einsum("gftk,kgd->tgfd", soft_low, window_values, preferred_element_type=jnp.float32)
            .reshape(count_of_rows, QUERY_HEADS * HEAD_SIZE)
            .astype(jnp.bfloat16)
        )
        attn_lin = matrix_product(attended_low, full_output)
    residual_one = source + root_mean_norm(attn_lin, gain_attention)
    laurel_lin = matrix_product(laurel_mid, full_laurel_up)
    mixed = (residual_one + normed + root_mean_norm(laurel_lin, gain_laurel)) * inv_root
    ffn_in = root_mean_norm(mixed, gain_before).astype(jnp.bfloat16)
    if fused:
        features = jnp.concatenate(
            [lowered_normed.reshape(count_of_rows, shards, -1), attended_low.reshape(count_of_rows, shards, -1)], axis=2
        ).reshape(count_of_rows, -1)
        feed_value, rows_all, rows_far, rows_near, slices, hidden_all, lift_all, bend_all = feed_call(
            True, ffn_in, (hidden_gate, hidden_up, hidden_down), features=features
        )
        slices = slices.reshape(shards * count_of_rows, -1)
        normed_slices, attended_slices = jnp.split(slices, 2, axis=1)
    else:
        normed_slices = feature_slices(lowered_normed)
        attended_slices = feature_slices(attended_low)
        rows_all = gather(ffn_in, "fsdp")
        gate_all = product_back(rows_all, hidden_gate)
        up_all = product_back(rows_all, hidden_up)
        hidden_all = gated(gate_all, up_all).astype(jnp.bfloat16)
        feed_value = scatter_sum(matrix_product(hidden_all, hidden_down))
    residual_two = mixed + root_mean_norm(feed_value, gain_after)
    residual_low = residual_two.astype(jnp.bfloat16)
    vector_lin = matrix_product(residual_low, full_vector_gate)
    gated_low = gated(vector_lin, vectors).astype(jnp.bfloat16)
    vector_back = matrix_product(gated_low, full_vector_out)
    result = residual_two + root_mean_norm(vector_back, gain_vector)
    upstream = cotangent.astype(jnp.float32)
    d_vector_back, grad_gain_vector = norm_grad(vector_back, gain_vector, upstream)
    d_vector_back_low = d_vector_back.astype(jnp.bfloat16)
    grad_vector_out = product_rows(gated_low, d_vector_back_low)
    d_gated = product_back(d_vector_back_low, full_vector_out)
    d_vector_lin, d_vectors = gated_grad(vector_lin, vectors, d_gated)
    d_vector_lin_low = d_vector_lin.astype(jnp.bfloat16)
    grad_vector_gate = product_rows(residual_low, d_vector_lin_low)
    if fused:
        rows_far = gather(rows_far.reshape(-1, width), "fsdp")
    d_residual = upstream + product_back(d_vector_lin_low, full_vector_gate)
    d_feed, grad_gain_after = norm_grad(feed_value, gain_after, d_residual)
    d_feed_low = d_feed.astype(jnp.bfloat16)
    if fused:
        d_ffn_in, d_rows_all, d_rows_far, rows_next, d_gate_low, d_up_low = feed_call(
            False, d_feed_low, (hidden_down, hidden_gate, hidden_up), (lift_all, bend_all), forward_rows=rows_all
        )
        d_ffn_in, rows_far = lax.optimization_barrier((d_ffn_in, rows_far))
        d_rows_far = gather(d_rows_far.reshape(-1, width), "fsdp")
    else:
        d_rows_all = gather(d_feed_low, "fsdp")
        d_hidden = product_back(d_rows_all, hidden_down)
        d_gate_all, d_up_all = gated_grad(gate_all, up_all, d_hidden)
        d_gate_low = d_gate_all.astype(jnp.bfloat16)
        d_up_low = d_up_all.astype(jnp.bfloat16)
        d_ffn_in = scatter_sum(
            matrix_product(d_gate_low, hidden_gate) + matrix_product(d_up_low, hidden_up)
        )

    if not fused:
        grad_hidden_gate, grad_hidden_up, grad_hidden_down = [
            lax.psum(grad.astype(jnp.bfloat16), "ctx").astype(jnp.float32)
            for grad in (
                product_rows(d_gate_low, rows_all),
                product_rows(d_up_low, rows_all),
                product_rows(hidden_all, d_rows_all),
            )
        ]

    d_mixed_part, grad_gain_before = norm_grad(mixed, gain_before, d_ffn_in)
    d_half = (d_residual + d_mixed_part) * inv_root
    d_laurel_lin, grad_gain_laurel = norm_grad(laurel_lin, gain_laurel, d_half)
    d_laurel_low = d_laurel_lin.astype(jnp.bfloat16)
    grad_laurel_up = product_rows(laurel_mid, d_laurel_low)
    d_laurel_mid = product_back(d_laurel_low, full_laurel_up).astype(jnp.bfloat16)
    d_attn_lin, grad_gain_attention = norm_grad(attn_lin, gain_attention, d_half)
    d_attn_low = d_attn_lin.astype(jnp.bfloat16)
    if fused:
        empty = jnp.zeros((width,), jnp.float32)
        gain_rows = jnp.stack(
            [
                empty,
                grad_gain_attention,
                grad_gain_laurel,
                grad_gain_before,
                grad_gain_after,
                grad_gain_vector,
                empty,
                empty,
            ]
        )
        d_middle = jnp.pad(d_laurel_mid, ((0, 0), (0, full_inward.shape[1] - query_width - 2 * key_width - rank)))
        d_source, grad_wide, grad_small, d_rows_near = attend_back_call(
            reach_blocks, d_attn_low, query_lowered, key_value, linear, gains_all, positions[:, None], cosine, sine_part,
            d_middle, slices, tokens, d_half, gain_rows, grad_laurel_up.reshape(shards, -1, width),
            grad_vector_gate.astype(jnp.bfloat16).reshape(shards, -1, grad_vector_gate.shape[1]),
            grad_vector_out.astype(jnp.bfloat16).reshape(shards, -1, width),
            full_output, full_inward,
            d_rows_all,
        )
        grad_hidden_gate, grad_hidden_up, grad_hidden_down = weight_grad_call(
            hidden_gate,
            hidden_up,
            hidden_down,
            rows_all,
            d_rows_all,
            hidden_all,
            d_gate_low,
            d_up_low,
            rows_near.reshape(-1, width),
            rows_next.reshape(-1, width),
            d_rows_near.reshape(-1, width),
            rows_far,
            d_rows_far,
        )
    else:
        d_attended = (
            product_back(d_attn_low, full_output)
            .astype(jnp.bfloat16)
            .reshape(count_of_rows, KEY_VALUE_HEADS, heads_per_group, HEAD_SIZE)
        )
        soft_again = jnp.exp(masked_scores() - log_total)
        d_soft = jnp.einsum(
            "tgfd,kgd->gftk", d_attended, window_values, preferred_element_type=jnp.float32
        )
        d_scores = (
            soft_again * (d_soft - jnp.sum(soft_again * d_soft, axis=-1, keepdims=True))
        ).astype(jnp.bfloat16)
        d_query = score_scale * jnp.einsum(
            "gftk,kgd->tgfd", d_scores, window_keys, preferred_element_type=jnp.float32
        )
        grad_key_rows = score_scale * jnp.einsum(
            "gftk,tgfd->kgd", d_scores, query_lowered, preferred_element_type=jnp.float32
        )
        grad_value_rows = jnp.einsum(
            "gftk,tgfd->kgd",
            soft_again.astype(jnp.bfloat16),
            d_attended,
            preferred_element_type=jnp.float32,
        )
        grad_window_couple = jnp.stack(
            [
                grad_key_rows.reshape(-1, KEY_VALUE_HEADS * HEAD_SIZE),
                grad_value_rows.reshape(-1, KEY_VALUE_HEADS * HEAD_SIZE),
            ]
        )
        grad_own_part = grad_window_couple[:, :count_of_rows]
        for distance in range(1, reach_blocks + 1):
            grad_own_part = grad_own_part + from_behind(
                grad_window_couple[:, distance * count_of_rows : (distance + 1) * count_of_rows].astype(
                    jnp.bfloat16
                ),
                "ctx",
                -distance,
            ).astype(jnp.float32)
        unused, query_pull = jax.vjp(head_facing, query_linear, gain_query)
        d_query_lin, grad_gain_query = query_pull(
            d_query.reshape(count_of_rows, QUERY_HEADS, HEAD_SIZE)
        )
        unused, key_pullback_fn = jax.vjp(head_facing, key_linear, key_norm_gain)
        grad_key_linear, grad_key_norm_gain = key_pullback_fn(
            grad_own_part[0].reshape(count_of_rows, KEY_VALUE_HEADS, HEAD_SIZE)
        )
        d_inward = jnp.concatenate(
            [
                d_query_lin.reshape(count_of_rows, QUERY_HEADS * HEAD_SIZE).astype(jnp.bfloat16),
                grad_key_linear.reshape(count_of_rows, KEY_VALUE_HEADS * HEAD_SIZE).astype(
                    jnp.bfloat16
                ),
                grad_own_part[1].astype(jnp.bfloat16),
                d_laurel_mid,
                jnp.zeros((count_of_rows, full_inward.shape[1] - query_width - 2 * key_width - rank), jnp.bfloat16),
            ],
            axis=1,
        )
        grad_inward = product_rows(normed_slices, gather(d_inward, "fsdp")).astype(jnp.bfloat16)
        grad_output = product_rows(attended_slices, gather(d_attn_low, "fsdp")).astype(jnp.bfloat16)
        grad_wide = jnp.concatenate([grad_inward, grad_output], axis=1)
        small_rows = jnp.concatenate(
            [
                grad_vector_gate.reshape(shards, -1, width),
                grad_vector_out.reshape(shards, -1, width),
                grad_laurel_up.reshape(shards, -1, width),
            ],
            axis=1,
        ).astype(jnp.bfloat16)
        grad_small = lax.psum_scatter(small_rows, "fsdp", scatter_dimension=0, tiled=False)
        d_normed = d_half + product_back(d_inward, full_inward)
        d_source_part, grad_gain_input = norm_grad(source, gain_input, d_normed)
        d_source = d_half + d_source_part
        gain_lines = jnp.concatenate(
            [
                grad.reshape(shards, -1)
                for grad in (
                    grad_gain_input,
                    grad_gain_attention,
                    grad_gain_laurel,
                    grad_gain_before,
                    grad_gain_after,
                    grad_gain_vector,
                    grad_gain_query,
                    grad_key_norm_gain,
                )
            ],
            axis=1,
        )
        gain_share = lax.psum_scatter(gain_lines, "fsdp", scatter_dimension=0, tiled=False)
        gain_count = gain_share.shape[0]
        gain_share = jnp.pad(gain_share, (0, -gain_count % width)).astype(jnp.bfloat16)
        grad_small = jnp.concatenate([grad_small, gain_share.reshape(-1, width)], axis=0)

    grad_wide, grad_small = [value.astype(jnp.float32) for value in lax.psum((grad_wide, grad_small), "ctx")]
    inward_width = full_inward.shape[1]
    grad_inward = grad_wide[:, :inward_width]
    grad_output = grad_wide[:, inward_width : inward_width + width]
    out_rows, laurel_rows = vector_out.shape[0], laurel_up.shape[0]
    if fused:
        share_vector_gate = grad_wide[:, inward_width + width :]
        gain_start = out_rows + laurel_rows
        share_vector_out = grad_small[:out_rows]
        share_laurel_up = grad_small[out_rows:gain_start]
        gain_lines = grad_small[gain_start:]
        gain_grads = tuple(
            lax.dynamic_slice_in_dim(gain_lines[index], me * size, size) if index >= 6 else gain_lines[index, :size]
            for index, size in enumerate(gain_sizes)
        )
    else:
        gate_rows = vector_gate.shape[0] * vector_gate.shape[1] // width
        share_vector_gate = grad_small[:gate_rows].reshape(vector_gate.shape)
        share_vector_out = grad_small[gate_rows : gate_rows + out_rows]
        gain_start = gate_rows + out_rows + laurel_rows
        share_laurel_up = grad_small[gate_rows + out_rows : gain_start]
        gain_share = grad_small[gain_start:].reshape(-1)
        gain_grads = tuple(
            gain_share[start : start + size] for start, size in zip(gain_starts, gain_sizes)
        )
    value_start = query_width + key_width
    return (
        result.astype(jnp.bfloat16),
        d_source,
        d_vectors,
        grad_inward[:, :query_width],
        grad_inward[:, query_width:value_start],
        grad_inward[:, value_start : value_start + key_width],
        grad_output,
        grad_inward[:, value_start + key_width : value_start + key_width + rank],
        share_laurel_up,
        share_vector_gate,
        share_vector_out,
    ) + gain_grads + (
        grad_hidden_gate,
        grad_hidden_up,
        grad_hidden_down,
    )


def solution(mesh):
    rows = P(("fsdp", "ctx"), None)
    line = P(("fsdp", "ctx"))
    weight = P("fsdp", None)
    gain = P("fsdp")
    return jax.shard_map(
        per_device,
        mesh=mesh,
        in_specs=(rows, rows, line, line, rows) + (weight,) * 8 + (gain,) * 8 + (weight,) * 3,
        out_specs=(rows,) * 3 + (weight,) * 8 + (gain,) * 8 + (weight,) * 3,
        check_vma=False,
    )
```

```python
import functools

import jax
import jax.numpy as jnp
from jax import lax
from jax.experimental import pallas as pl
from jax.experimental.pallas import tpu as pltpu
from jax.sharding import PartitionSpec as P

QUERY_HEADS = 8
KEY_VALUE_HEADS = 2
HEAD_SIZE = 256
WINDOW = 1024


epsilon = 1e-06
rope_base = 10000.0
inv_root = 0.7071067811865476
gelu_scale = 0.7978845608028654
gelu_cubic = 0.044715


def from_behind(value, axis, steps):
    count = lax.axis_size(axis)
    initial, last = (max(0, -steps), min(count, count - steps))
    return lax.ppermute(value, axis, [(source, source + steps) for source in range(initial, last)])


def other_blocks(value, axis):
    count = lax.axis_size(axis)
    return jnp.concatenate(
        [
            lax.ppermute(value, axis, [(source, (source + step) % count) for source in range(count)])
            for step in range(1, count)
        ],
        axis=0,
    )


def root_mean_norm(value, gain):
    factor = lax.rsqrt(jnp.mean(value * value, axis=-1, keepdims=True) + epsilon)
    return value * factor * gain


def gelu_tanh(value):
    return jax.nn.gelu(value, approximate=True)


def gated(gate_value, up_value):
    return gelu_tanh(gate_value) * up_value


def rotary_apply(value, token_position):
    half_size = value.shape[-1] // 2
    frequency = rope_base ** (-2.0 * jnp.arange(half_size, dtype=jnp.float32) / value.shape[-1])
    angle = token_position.astype(jnp.float32)[:, None] * frequency[None, :]
    cosine = jnp.cos(angle)[:, None, :]
    sine_part = jnp.sin(angle)[:, None, :]
    first_half = value[..., :half_size]
    second_half = value[..., half_size:]
    return jnp.concatenate(
        [
            first_half * cosine - second_half * sine_part,
            second_half * cosine + first_half * sine_part,
        ],
        axis=-1,
    )


def rotary_tables(token_position, size):
    half_size = size // 2
    frequency = rope_base ** (-2.0 * jnp.arange(half_size, dtype=jnp.float32) / size)
    angle = token_position.astype(jnp.float32)[:, None] * frequency[None, :]
    return jnp.cos(angle), jnp.sin(angle)


def window(positions, rows_of, reach):
    key_offset = jnp.concatenate(
        [distance * rows_of - jnp.arange(rows_of, dtype=jnp.int32) for distance in range(reach + 1)]
    )
    key_gap = jnp.arange(rows_of, dtype=jnp.int32)[:, None] + key_offset[None, :]
    return key_gap, (key_gap >= 0) & (key_gap <= positions[:, None]) & (key_gap < WINDOW)


def matrix_product(left, right):
    return jnp.dot(left, right, preferred_element_type=jnp.float32)


def product_back(left, right):
    return lax.dot_general(
        left, right, (((1,), (1,)), ((), ())), preferred_element_type=jnp.float32
    )


def product_rows(left, right):
    return lax.dot_general(
        left, right, (((0,), (0,)), ((), ())), preferred_element_type=jnp.float32
    )


def norm_grad(value, gain, upstream):
    unused, pullback = jax.vjp(root_mean_norm, value, gain)
    return pullback(upstream)


def gated_grad(gate_value, up_value, upstream):
    unused, pullback = jax.vjp(gated, gate_value, up_value)
    return pullback(upstream)


def gather(value, axis):
    return lax.all_gather(value, axis, axis=0, tiled=True)


def feature_slices(value):
    count = lax.axis_size("fsdp")
    rows = value.shape[0]
    return lax.all_to_all(
        value.reshape(rows, count, -1), "fsdp", split_axis=1, concat_axis=0, tiled=True
    ).reshape(count * rows, -1)


def scatter_sum(value):
    return lax.psum_scatter(
        value.astype(jnp.bfloat16), "fsdp", scatter_dimension=0, tiled=True
    ).astype(jnp.float32)


def gelu_parts(gate):
    square = gate * gate
    bend = jnp.tanh(gelu_scale * gate * (1.0 + gelu_cubic * square))
    half_up = 0.5 * (1.0 + bend)
    slope = half_up + 0.5 * gate * (1.0 - bend * bend) * (
        gelu_scale * (1.0 + 3.0 * gelu_cubic * square)
    )
    return gate * half_up, slope


def across(me, stride):
    return me + stride - 2 * stride * ((me // stride) % 2)


def across_many(me, bits):
    for stride in (1, 2, 4):
        if bits & stride:
            me = across(me, stride)
    return me


def feed_kernel(forward, rows_of, others, *refs):
    half = rows_of // 2
    if forward:
        (own, gate_hbm, up_hbm, down_hbm, features, gate_own, out_own, total, rows_hbm, far_hbm, near_hbm, slices_hbm, gate_all, out_all, hidden_hbm, lift_hbm, bend_hbm), rest = refs[:17], refs[17:]
        weights_hbm, kept_hbm, made_hbm = (gate_hbm, up_hbm, down_hbm), (), (hidden_hbm, lift_hbm, bend_hbm)
    else:
        (own, down_hbm, gate_hbm, up_hbm, lift_hbm, bend_hbm, forward_rows, total, rows_hbm, far_hbm, near_hbm, d_gate_hbm, d_up_hbm), rest = refs[:13], refs[13:]
        weights_hbm, kept_hbm, made_hbm = (down_hbm, gate_hbm, up_hbm), (lift_hbm, bend_hbm), (d_gate_hbm, d_up_hbm)
    count_kept, count_made = len(kept_hbm), len(made_hbm)
    weights = rest[:3]
    kept = rest[3 : 3 + count_kept]
    made = rest[3 + count_kept : 3 + count_kept + count_made]
    (rows, part, sib_in, chip_sum, relay_in, relay_sum, last_in, send_sem, recv_sem, in_sem, out_sem, far_send, far_recv, near_send, near_recv, *extra) = rest[
        3 + count_kept + count_made :
    ]
    hidden = weights[0].shape[0]
    width = own.shape[1]
    me = lax.axis_index("fsdp")
    sibling, beside, above = across(me, 1), across(me, 2), across(me, 4)

    loads = [
        pltpu.make_async_copy(source, target, in_sem.at[index])
        for index, (source, target) in enumerate(zip(weights_hbm + kept_hbm, tuple(weights) + tuple(kept)))
    ]
    for load in loads:
        load.start()

    block = lax.axis_index("ctx")
    greet(me, range(1, 8) if forward else (1, 2, 4), block, others)

    def send(index, source, target, partner):
        return pltpu.make_async_remote_copy(
            src_ref=source,
            dst_ref=target,
            send_sem=send_sem.at[index],
            recv_sem=recv_sem.at[index],
            device_id={"fsdp": partner},
            device_id_type=pl.DeviceIdType.MESH,
        )

    low, high = pl.ds(0, half), pl.ds(half, half)
    mine, theirs = pl.ds(0, rows_of), pl.ds(rows_of, rows_of)
    copies = [
        send(0, own, rows.at[0, theirs], sibling),
        send(1, own.at[low], rows.at[1, low], beside),
        send(2, own.at[low], rows.at[1, high], above),
        send(3, own.at[high], rows.at[2, low], beside),
        send(4, own.at[high], rows.at[2, high], above),
        send(5, rows.at[1, mine], rows.at[1, theirs], sibling),
        send(6, rows.at[2, mine], rows.at[2, theirs], sibling),
        send(7, rows.at[1, low], rows.at[3, low], above),
        send(8, rows.at[2, high], rows.at[3, high], beside),
        send(9, rows.at[3, mine], rows.at[3, theirs], sibling),
        send(10, part.at[0, theirs], sib_in.at[0], sibling),
        send(11, part.at[1, theirs], sib_in.at[1], sibling),
        send(12, part.at[2, theirs], sib_in.at[2], sibling),
        send(13, part.at[3, theirs], sib_in.at[3], sibling),
        send(14, chip_sum.at[0, high], last_in.at[2], above),
        send(15, chip_sum.at[1, low], last_in.at[1], beside),
        send(16, chip_sum.at[2, low], relay_in.at[0], above),
        send(17, chip_sum.at[2, high], relay_in.at[1], beside),
        send(18, relay_sum.at[0], last_in.at[0], beside),
        send(19, relay_sum.at[1], last_in.at[3], above),
    ]
    outs = []

    def write_out(source, target):
        copy = pltpu.make_async_copy(source, target, out_sem.at[len(outs)])
        copy.start()
        outs.append(copy)

    for index in range(5):
        copies[index].start()
    spreads = []
    if forward:
        gate_slots, out_slots, gate_send, gate_recv, vec_send, vec_recv, gate_out, vec_out = extra[3:]
        spreads = [
            spread_copies(gate_own, gate_slots, gate_send, gate_recv, me),
            spread_copies(out_own, out_slots, vec_send, vec_recv, me),
        ]
        for spread in spreads:
            for index in range(5):
                spread[index].start()
        gate_slots[0] = gate_own[...]
        out_slots[0] = out_own[...]
    far = [
        push(own, far_hbm.at[index], far_send.at[index], far_recv.at[index], {"ctx": across_many(block, 2 + index)})
        for index in range(2)
    ]
    for copy in far:
        copy.start()
    def near_source(index):
        if forward:
            return rows.at[1, mine] if index else own
        return forward_rows.at[pl.ds((2 + index) * 2 * rows_of, rows_of)]

    near = [
        push(near_source(index), near_hbm.at[index, mine], near_send.at[index], near_recv.at[index], {"ctx": across(block, 1)})
        for index in range(2)
    ]
    near_share = [
        push(
            near_hbm.at[index, mine],
            near_hbm.at[index, theirs],
            near_send.at[2 + index],
            near_recv.at[2 + index],
            {"fsdp": sibling},
        )
        for index in range(2)
    ]
    near[0].start()
    if not forward:
        near[1].start()
    rows[0, mine] = own[...]
    slices = []
    if forward:
        share = features.shape[1] // 8

        def share_of(device):
            return features.at[:, pl.ds(pl.multiple_of(device * share, share), share)]

        own_slice = pltpu.make_async_copy(share_of(me), slices_hbm.at[me], extra[2])
        own_slice.start()
        slices = [
            pltpu.make_async_remote_copy(
                src_ref=share_of(across_many(me, distance)),
                dst_ref=slices_hbm.at[me],
                send_sem=extra[0].at[distance - 1],
                recv_sem=extra[1].at[distance - 1],
                device_id={"fsdp": across_many(me, distance)},
                device_id_type=pl.DeviceIdType.MESH,
            )
            for distance in range(1, 8)
        ]

    tile = min(hidden, 1024)
    wide = min(width, 1024)

    def first_stage(group):
        span = pl.ds(group * 2 * rows_of, 2 * rows_of)

        def step(index, carry):
            columns = pl.ds(pl.multiple_of(index * tile, tile), tile)
            left = rows[group]

            def back(weight):
                return lax.dot_general(
                    left, weight[columns, :], (((1,), (1,)), ((), ())), preferred_element_type=jnp.float32
                )

            if forward:
                gate, up = back(weights[0]), back(weights[1])
                value, slope = gelu_parts(gate)
                made[0][span, columns] = (value * up).astype(jnp.bfloat16)
                made[1][span, columns] = value.astype(jnp.bfloat16)
                made[2][span, columns] = (slope * up).astype(jnp.bfloat16)
            else:
                d_hidden = back(weights[0])
                made[0][span, columns] = (d_hidden * kept[1][span, columns].astype(jnp.float32)).astype(jnp.bfloat16)
                made[1][span, columns] = (d_hidden * kept[0][span, columns].astype(jnp.float32)).astype(jnp.bfloat16)
            return carry

        lax.fori_loop(0, hidden // tile, step, 0)

    def second_stage(group):
        span = pl.ds(group * 2 * rows_of, 2 * rows_of)

        def step(index, carry):
            columns = pl.ds(pl.multiple_of(index * wide, wide), wide)
            if forward:
                value = jnp.dot(made[0][span, :], weights[2][:, columns], preferred_element_type=jnp.float32)
            else:
                value = jnp.dot(made[0][span, :], weights[1][:, columns], preferred_element_type=jnp.float32)
                value = value + jnp.dot(made[1][span, :], weights[2][:, columns], preferred_element_type=jnp.float32)
            part[group, :, columns] = value.astype(jnp.bfloat16)
            return carry

        lax.fori_loop(0, width // wide, step, 0)

    def keep_out(group):
        span = pl.ds(group * 2 * rows_of, 2 * rows_of)
        write_out(rows.at[group], rows_hbm.at[span])
        for source, target in zip(made, made_hbm):
            write_out(source.at[span], target.at[span])

    def add_chip(group):
        chip_sum[group - 1] = (
            part[group, mine].astype(jnp.float32) + sib_in[group].astype(jnp.float32)
        ).astype(jnp.bfloat16)

    copies[0].wait_recv()
    loads[0].wait()
    if forward:
        loads[1].wait()
    else:
        loads[3].wait()
        loads[4].wait()
    first_stage(0)
    if forward:
        loads[2].wait()
    else:
        loads[1].wait()
        loads[2].wait()
    second_stage(0)
    copies[10].start()
    keep_out(0)
    copies[1].wait_recv()
    copies[7].start()
    copies[2].wait_recv()
    copies[5].start()
    if forward:
        near[1].start()
    copies[5].wait_recv()
    first_stage(1)
    second_stage(1)
    copies[11].start()
    keep_out(1)
    copies[3].wait_recv()
    copies[4].wait_recv()
    copies[8].start()
    copies[6].start()
    copies[11].wait_recv()
    add_chip(1)
    copies[14].start()
    copies[6].wait_recv()
    first_stage(2)
    second_stage(2)
    copies[12].start()
    keep_out(2)
    for copy in slices:
        copy.start()
    for spread in spreads:
        for index in range(1, 5):
            spread[index].wait_recv()
        for index in range(5, 11):
            spread[index].start()
    copies[7].wait_recv()
    copies[8].wait_recv()
    copies[9].start()
    copies[12].wait_recv()
    add_chip(2)
    copies[15].start()
    copies[9].wait_recv()
    first_stage(3)
    second_stage(3)
    copies[13].start()
    keep_out(3)
    copies[13].wait_recv()
    add_chip(3)
    copies[16].start()
    copies[17].start()
    for spread in spreads:
        for index in (9, 10):
            spread[index].wait_recv()
        for index in (11, 12):
            spread[index].start()
    copies[10].wait_recv()
    total[...] = part[0, mine].astype(jnp.float32) + sib_in[0].astype(jnp.float32)
    copies[16].wait_recv()
    relay_sum[0] = (chip_sum[0, low].astype(jnp.float32) + relay_in[0].astype(jnp.float32)).astype(jnp.bfloat16)
    copies[18].start()
    copies[17].wait_recv()
    relay_sum[1] = (chip_sum[1, high].astype(jnp.float32) + relay_in[1].astype(jnp.float32)).astype(jnp.bfloat16)
    copies[19].start()
    copies[14].wait_recv()
    total[low] = total[low] + last_in[2].astype(jnp.float32)
    copies[15].wait_recv()
    total[high] = total[high] + last_in[1].astype(jnp.float32)
    for index in range(2):
        near[index].wait_recv()
        near_share[index].start()
    copies[18].wait_recv()
    total[low] = total[low] + last_in[0].astype(jnp.float32)
    copies[19].wait_recv()
    total[high] = total[high] + last_in[3].astype(jnp.float32)
    if forward:
        for spread, slots, target, sems in (
            (spreads[0], gate_slots, gate_all, gate_out),
            (spreads[1], out_slots, out_all, vec_out),
        ):
            for index in (0, 5, 6, 7, 8, 11, 12):
                spread[index].wait_recv()
            size = slots.shape[1]
            for slot in range(8):
                place = pl.ds(pl.multiple_of(across_many(me, slot) * size, size), size)
                copy = pltpu.make_async_copy(slots.at[slot], target.at[place], sems.at[slot])
                copy.start()
                outs.append(copy)
            for copy in spread:
                copy.wait_send()
    for copy in copies:
        copy.wait_send()
    for copy in outs:
        copy.wait()
    for copy in far + slices:
        copy.wait()
    for index in range(2):
        near[index].wait_send()
        near_share[index].wait()
    if forward:
        own_slice.wait()


def turn(value, cosine, sine, direction=1.0):
    middle = value.shape[1] // 2
    first, second = value[:, :middle], value[:, middle:]
    sine = sine * direction
    return jnp.concatenate([first * cosine - second * sine, second * cosine + first * sine], axis=1)


def window_mask(positions, rows_of, blocks):
    query_row = lax.broadcasted_iota(jnp.int32, (rows_of, blocks * rows_of), 0)
    column = lax.broadcasted_iota(jnp.int32, (rows_of, blocks * rows_of), 1)
    behind = column // rows_of
    gap = query_row + 2 * behind * rows_of - column
    return (gap >= 0) & (gap <= positions) & (gap < WINDOW)


def greet(me, partners, block, others):
    barrier = pltpu.get_barrier_semaphore()
    for distance in partners:
        pl.semaphore_signal(
            barrier, inc=1, device_id={"fsdp": across_many(me, distance)}, device_id_type=pl.DeviceIdType.MESH
        )
    for distance in range(1, others + 1):
        pl.semaphore_signal(
            barrier,
            inc=1,
            device_id={"ctx": (block + distance) % (others + 1)},
            device_id_type=pl.DeviceIdType.MESH,
        )
    pl.semaphore_wait(barrier, len(partners) + others)


def push(source, target, send_sem, recv_sem, place):
    return pltpu.make_async_remote_copy(
        src_ref=source,
        dst_ref=target,
        send_sem=send_sem,
        recv_sem=recv_sem,
        device_id=place,
        device_id_type=pl.DeviceIdType.MESH,
    )


def spread_copies(own, slots, send_sem, recv_sem, me):
    half = own.shape[0] // 2
    low, high = pl.ds(0, half), pl.ds(half, half)
    sibling, beside, above = across(me, 1), across(me, 2), across(me, 4)
    plan = [
        (own, slots.at[1], sibling),
        (own.at[low], slots.at[2, low], beside),
        (own.at[low], slots.at[4, low], above),
        (own.at[high], slots.at[2, high], beside),
        (own.at[high], slots.at[4, high], above),
        (slots.at[2, low], slots.at[3, low], sibling),
        (slots.at[4, low], slots.at[5, low], sibling),
        (slots.at[2, high], slots.at[3, high], sibling),
        (slots.at[4, high], slots.at[5, high], sibling),
        (slots.at[2, low], slots.at[6, low], above),
        (slots.at[4, high], slots.at[6, high], beside),
        (slots.at[6, low], slots.at[7, low], sibling),
        (slots.at[6, high], slots.at[7, high], sibling),
    ]
    return [
        push(source, target, send_sem.at[index], recv_sem.at[index], {"fsdp": partner})
        for index, (source, target, partner) in enumerate(plan)
    ]


def attend_kernel(
    others, reach, source, gain_lines, positions, cosine, sine, inward_own, outward_own,
    normed, gains, linear, query_low, key_value, features, middle, attn_lin, laurel_all, inward_all, outward_all,
    gain_slots, inward_slots, outward_slots, normed_low, attended, inward, lin_sum,
    gain_send, gain_recv, in_send, in_recv, out_send, out_recv, kv_send, kv_recv, in_copy, out_copy,
):
    rows_of, width = source.shape
    me, block = lax.axis_index("fsdp"), lax.axis_index("ctx")
    greet(me, range(1, 8), block, others)
    gain_copies = [
        push(gain_lines, gain_slots.at[distance], gain_send.at[distance - 1], gain_recv.at[distance - 1],
             {"fsdp": across_many(me, distance)})
        for distance in range(1, 8)
    ]
    for copy in gain_copies:
        copy.start()
    spread_in = spread_copies(inward_own, inward_slots, in_send, in_recv, me)
    spread_out = spread_copies(outward_own, outward_slots, out_send, out_recv, me)
    for index in range(5):
        spread_in[index].start()
    inward_slots[0] = inward_own[...]
    outward_slots[0] = outward_own[...]

    value = source[...].astype(jnp.float32)
    factor = lax.rsqrt(jnp.mean(value * value, axis=-1, keepdims=True) + epsilon)
    for copy in gain_copies:
        copy.wait_recv()
    gain_slots[0] = gain_lines[...]
    lines = gain_slots[...].astype(jnp.float32)
    gains[...] = jnp.sum(lines, axis=0)[0:8]
    laurel_size = laurel_all.shape[0] // 8
    for slot in range(8):
        device = across_many(me, slot)
        laurel_all[pl.ds(pl.multiple_of(device * laurel_size, laurel_size), laurel_size), :] = lines[slot, 8:16]
    value = value * factor * gains[0:1, :]
    normed[...] = value
    normed_low[...] = value.astype(jnp.bfloat16)
    share = width // 8
    for index in range(8):
        features[:, pl.ds(2 * index * share, share)] = normed_low[:, pl.ds(index * share, share)]

    depth = inward_own.shape[0]
    head_rows = width // 8
    written = []

    def add_inward(slot):
        device = across_many(me, slot)
        part = normed_low[:, pl.ds(pl.multiple_of(device * depth, depth), depth)]
        for start in range(0, inward.shape[1], 640):
            span = pl.ds(start, 640)
            product = jnp.dot(part, inward_slots[slot, :, span], preferred_element_type=jnp.float32)
            inward[:, span] = product if slot == 0 else inward[:, span] + product
        copy = pltpu.make_async_copy(
            inward_slots.at[slot], inward_all.at[pl.ds(pl.multiple_of(device * depth, depth), depth)], in_copy.at[slot]
        )
        copy.start()
        written.append(copy)

    def add_outward(slot):
        device = across_many(me, slot)
        part = attended[:, pl.ds(pl.multiple_of(device * head_rows, head_rows), head_rows)]
        for start in range(0, width, 512):
            span = pl.ds(start, 512)
            product = jnp.dot(part, outward_slots[slot, pl.ds(0, head_rows), span], preferred_element_type=jnp.float32)
            lin_sum[:, span] = product if slot == 0 else lin_sum[:, span] + product

    def write_outward(slot):
        device = across_many(me, slot)
        rows = pl.ds(pl.multiple_of(device * head_rows, head_rows), head_rows)
        copy = pltpu.make_async_copy(outward_slots.at[slot], outward_all.at[rows], out_copy.at[slot])
        copy.start()
        written.append(copy)

    add_inward(0)
    spread_in[0].wait_recv()
    add_inward(1)
    spread_in[1].wait_recv()
    spread_in[9].start()
    spread_in[5].start()
    spread_in[2].wait_recv()
    spread_in[6].start()
    spread_in[3].wait_recv()
    spread_in[7].start()
    spread_in[4].wait_recv()
    spread_in[10].start()
    spread_in[8].start()
    add_inward(2)
    add_inward(4)
    spread_in[5].wait_recv()
    spread_in[7].wait_recv()
    add_inward(3)
    spread_in[6].wait_recv()
    spread_in[8].wait_recv()
    add_inward(5)
    spread_in[9].wait_recv()
    spread_in[11].start()
    spread_in[10].wait_recv()
    spread_in[12].start()
    for index in range(5):
        spread_out[index].start()
    add_inward(6)
    spread_in[11].wait_recv()
    spread_in[12].wait_recv()
    add_inward(7)

    query_width, key_width = QUERY_HEADS * HEAD_SIZE, KEY_VALUE_HEADS * HEAD_SIZE
    own_rows = pl.ds(0, rows_of)

    def head(start, gain):
        lane = inward[:, pl.ds(start, HEAD_SIZE)]
        scale = lax.rsqrt(jnp.mean(lane * lane, axis=-1, keepdims=True) + epsilon)
        return turn(lane * scale * gain, cosine[...], sine[...]).astype(jnp.bfloat16)

    for index in range(KEY_VALUE_HEADS):
        key_value[own_rows, pl.ds(index * HEAD_SIZE, HEAD_SIZE)] = head(
            query_width + index * HEAD_SIZE, gains[7:8, 0:HEAD_SIZE]
        )
    key_value[own_rows, pl.ds(key_width, key_width)] = inward[:, pl.ds(query_width + key_width, key_width)].astype(
        jnp.bfloat16
    )
    for distance in range(1, reach + 1):
        copy = push(
            key_value.at[own_rows],
            key_value.at[pl.ds(distance * rows_of, rows_of)],
            kv_send.at[distance - 1],
            kv_recv.at[distance - 1],
            {"ctx": (block + distance) % (others + 1)},
        )

        @pl.when(block + distance <= others)
        def _():
            copy.start()

        @pl.when(block < distance)
        def _():
            key_value[pl.ds(distance * rows_of, rows_of), :] = jnp.zeros((rows_of, 2 * key_width), jnp.bfloat16)

    for index in range(QUERY_HEADS):
        query_low[:, pl.ds(index * HEAD_SIZE, HEAD_SIZE)] = head(index * HEAD_SIZE, gains[6:7, 0:HEAD_SIZE])
    linear[...] = inward[:, pl.ds(0, query_width + key_width)]
    middle[...] = inward[:, pl.ds(query_width + 2 * key_width, middle.shape[1])].astype(jnp.bfloat16)

    spread_out[0].wait_recv()
    spread_out[1].wait_recv()
    spread_out[9].start()
    spread_out[5].start()
    spread_out[2].wait_recv()
    spread_out[6].start()
    for distance in range(1, reach + 1):
        copy = push(
            key_value.at[own_rows],
            key_value.at[pl.ds(distance * rows_of, rows_of)],
            kv_send.at[distance - 1],
            kv_recv.at[distance - 1],
            {"ctx": (block + distance) % (others + 1)},
        )

        @pl.when(block >= distance)
        def _():
            copy.wait_recv()

    allowed = window_mask(positions[...], rows_of, reach + 1)
    per_group = QUERY_HEADS // KEY_VALUE_HEADS
    for index in range(QUERY_HEADS):
        group = index // per_group
        columns = pl.ds(index * HEAD_SIZE, HEAD_SIZE)
        scores = product_back(query_low[:, columns], key_value[:, pl.ds(group * HEAD_SIZE, HEAD_SIZE)])
        scores = jnp.where(allowed, scores * HEAD_SIZE ** (-0.5), -1e30)
        grown = jnp.exp(scores - jnp.max(scores, axis=-1, keepdims=True))
        soft = (grown / jnp.sum(grown, axis=-1, keepdims=True)).astype(jnp.bfloat16)
        attended[:, columns] = jnp.dot(
            soft, key_value[:, pl.ds(key_width + group * HEAD_SIZE, HEAD_SIZE)], preferred_element_type=jnp.float32
        ).astype(jnp.bfloat16)

    for index in range(8):
        features[:, pl.ds((2 * index + 1) * share, share)] = attended[:, pl.ds(index * share, share)]
    add_outward(0)
    add_outward(1)
    write_outward(0)
    write_outward(1)
    spread_out[3].wait_recv()
    spread_out[7].start()
    spread_out[4].wait_recv()
    spread_out[10].start()
    spread_out[8].start()
    add_outward(2)
    add_outward(4)
    spread_out[5].wait_recv()
    spread_out[7].wait_recv()
    add_outward(3)
    spread_out[6].wait_recv()
    spread_out[8].wait_recv()
    add_outward(5)
    for slot in range(2, 6):
        write_outward(slot)
    spread_out[9].wait_recv()
    spread_out[11].start()
    spread_out[10].wait_recv()
    spread_out[12].start()
    add_outward(6)
    write_outward(6)
    spread_out[11].wait_recv()
    spread_out[12].wait_recv()
    add_outward(7)
    write_outward(7)
    attn_lin[...] = lin_sum[...]
    for copy in gain_copies + spread_in + spread_out:
        copy.wait_send()
    for copy in written:
        copy.wait()
    for distance in range(1, reach + 1):
        copy = push(
            key_value.at[own_rows],
            key_value.at[pl.ds(distance * rows_of, rows_of)],
            kv_send.at[distance - 1],
            kv_recv.at[distance - 1],
            {"ctx": (block + distance) % (others + 1)},
        )

        @pl.when(block + distance <= others)
        def _():
            copy.wait_send()


def attend_call(reach, source, gain_lines, positions, cosine, sine, inward_own, outward_own):
    rows_of, width = source.shape
    others = lax.axis_size("ctx") - 1
    low, full = jnp.bfloat16, jnp.float32
    hbm = pl.BlockSpec(memory_space=pl.ANY)
    vmem = pl.BlockSpec(memory_space=pltpu.VMEM)
    dma = pltpu.SemaphoreType.DMA
    depth, columns = inward_own.shape
    query_width, key_width = QUERY_HEADS * HEAD_SIZE, KEY_VALUE_HEADS * HEAD_SIZE
    tail = columns - query_width - 2 * key_width
    shapes = [
        jax.ShapeDtypeStruct((rows_of, width), full),
        jax.ShapeDtypeStruct((8, width), full),
        jax.ShapeDtypeStruct((rows_of, query_width + key_width), full),
        jax.ShapeDtypeStruct((rows_of, query_width), low),
        jax.ShapeDtypeStruct(((reach + 1) * rows_of, 2 * key_width), low),
        jax.ShapeDtypeStruct((rows_of, 2 * width), low),
        jax.ShapeDtypeStruct((rows_of, tail), low),
        jax.ShapeDtypeStruct((rows_of, width), full),
        jax.ShapeDtypeStruct((64, width), full),
        jax.ShapeDtypeStruct((8 * depth, columns), low),
        jax.ShapeDtypeStruct((8 * outward_own.shape[0], width), low),
    ]
    return pl.pallas_call(
        functools.partial(attend_kernel, others, reach),
        out_shape=shapes,
        in_specs=[vmem] * 7,
        out_specs=[vmem] * 9 + [hbm] * 2,
        scratch_shapes=[
            pltpu.VMEM((8, *gain_lines.shape), low),
            pltpu.VMEM((8, depth, columns), low),
            pltpu.VMEM((8, *outward_own.shape), low),
            pltpu.VMEM((rows_of, width), low),
            pltpu.VMEM((rows_of, query_width), low),
            pltpu.VMEM((rows_of, columns), full),
            pltpu.VMEM((rows_of, width), full),
            dma((7,)),
            dma((7,)),
            dma((13,)),
            dma((13,)),
            dma((13,)),
            dma((13,)),
            dma((max(reach, 1),)),
            dma((max(reach, 1),)),
            dma((8,)),
            dma((8,)),
        ],
        compiler_params=pltpu.CompilerParams(collective_id=3, has_side_effects=True, vmem_limit_bytes=56 * 2**20),
        cost_estimate=pl.CostEstimate(
            flops=60 * rows_of * width * columns, bytes_accessed=20 * depth * columns, transcendentals=0
        ),
        name="attend_forward",
    )(source, gain_lines, positions, cosine, sine, inward_own, outward_own)


def turn_norm_grad(upstream, linear, gain, cosine, sine):
    scale = lax.rsqrt(jnp.mean(linear * linear, axis=-1, keepdims=True) + epsilon)
    unit = linear * scale
    back = turn(upstream, cosine, sine, -1.0)
    grad_gain = jnp.sum(back * unit, axis=0, keepdims=True)
    back = back * gain
    return scale * (back - unit * jnp.mean(back * unit, axis=-1, keepdims=True)), grad_gain


def attend_back_kernel(
    others, reach, d_lin, query_low, key_value, linear, gains, positions, cosine, sine, middle, d_middle, features,
    source, d_half, gain_rows, residual, d_vector, gated_value, d_back, d_laurel, outward_all, inward_all, d_rows,
    d_source, grad_wide, grad_small, near_hbm,
    outward, inward, d_attended, d_key_value, parcel, arrived, d_query, d_rest, lin_slots, query_slots, rest_slots,
    ordered, d_normed, gain_parcel, gain_arrived, laurel_arrived, load_sem, lin_send, lin_recv, query_send, query_recv, rest_send, rest_recv, kv_send, kv_recv, gain_send, gain_recv, laurel_send, laurel_recv, near_send, near_recv,
    gate_in, gate_sum, gate_arrived, out_in, out_sum, out_arrived, pair_send, pair_recv, chip_send, chip_recv,
    gate_parts, out_parts, laurel_rows,
):
    rows_of, width = d_lin.shape
    me, block = lax.axis_index("fsdp"), lax.axis_index("ctx")
    query_width, key_width = QUERY_HEADS * HEAD_SIZE, KEY_VALUE_HEADS * HEAD_SIZE
    per_group = QUERY_HEADS // KEY_VALUE_HEADS
    depth = width // 8
    loads = [
        pltpu.make_async_copy(outward_all.at[pl.ds(index * depth, depth)], outward.at[index], load_sem.at[index])
        for index in range(8)
    ]
    loads.append(pltpu.make_async_copy(inward_all, inward, load_sem.at[8]))
    for load in loads:
        load.start()
    greet(me, range(1, 8), block, others)
    mine, theirs = pl.ds(0, rows_of), pl.ds(rows_of, rows_of)
    near = [
        push(
            d_rows.at[pl.ds(group * 2 * rows_of, rows_of)],
            near_hbm.at[group, mine],
            near_send.at[group],
            near_recv.at[group],
            {"ctx": across(block, 1)},
        )
        for group in range(4)
    ]
    near_share = [
        push(
            near_hbm.at[group, mine],
            near_hbm.at[group, theirs],
            near_send.at[4 + group],
            near_recv.at[4 + group],
            {"fsdp": across(me, 1)},
        )
        for group in range(4)
    ]
    for copy in near[:2]:
        copy.start()
    vector_parts = ((gate_parts, gate_in, gate_sum, gate_arrived), (out_parts, out_in, out_sum, out_arrived))
    chips = (0, 2, 4, 6)
    pair_copies = []
    chip_copies = []
    for kind, (parts, pair_in, pair_sum, arrived_parts) in enumerate(vector_parts):
        for index, chip in enumerate(chips):
            place = 4 * kind + index
            pair_copies.append(
                push(
                    parts.at[across_many(me, chip + 1)],
                    pair_in.at[index],
                    pair_send.at[place],
                    pair_recv.at[place],
                    {"fsdp": across(me, 1)},
                )
            )
            if chip:
                place = 3 * kind + index - 1
                chip_copies.append(
                    push(
                        pair_sum.at[index - 1],
                        arrived_parts.at[index - 1],
                        chip_send.at[place],
                        chip_recv.at[place],
                        {"fsdp": across_many(me, chip)},
                    )
                )
    spread_lin = spread_copies(d_lin, lin_slots, lin_send, lin_recv, me)
    spread_query = spread_copies(d_query, query_slots, query_send, query_recv, me)
    spread_rest = spread_copies(d_rest, rest_slots, rest_send, rest_recv, me)
    for index in range(5):
        spread_lin[index].start()
    lin_slots[0] = d_lin[...]
    for index in range(8):
        gate_parts[index] = product_rows(residual[:, pl.ds(index * depth, depth)], d_vector[...]).astype(jnp.bfloat16)
    out_parts[...] = product_rows(gated_value[...], d_back[...]).reshape(out_parts.shape).astype(jnp.bfloat16)
    laurel_rows[...] = product_rows(middle[...], d_laurel[...])[0 : 8 * laurel_rows.shape[1]].reshape(laurel_rows.shape)
    for copy in pair_copies:
        copy.start()
    laurel_copies = [
        push(
            laurel_rows.at[across_many(me, distance)],
            laurel_arrived.at[distance],
            laurel_send.at[distance - 1],
            laurel_recv.at[distance - 1],
            {"fsdp": across_many(me, distance)},
        )
        for distance in range(1, 8)
    ]
    laurel_arrived[0] = laurel_rows[me]
    for slot in range(8):
        device = across_many(me, slot)
        ordered[pl.ds(slot * rows_of, rows_of), :] = features[
            pl.ds(pl.multiple_of(device * rows_of, rows_of), rows_of), :
        ]
    for index in range(8):
        loads[index].wait()
        d_attended[:, pl.ds(index * depth, depth)] = product_back(d_lin[...], outward[index]).astype(jnp.bfloat16)

    allowed = window_mask(positions[...], rows_of, reach + 1)
    scale = HEAD_SIZE ** (-0.5)

    def one_head(index):
        group = index // per_group
        columns = pl.ds(index * HEAD_SIZE, HEAD_SIZE)
        keys = pl.ds(group * HEAD_SIZE, HEAD_SIZE)
        values = pl.ds(key_width + group * HEAD_SIZE, HEAD_SIZE)
        scores = product_back(query_low[:, columns], key_value[:, keys])
        scores = jnp.where(allowed, scores * scale, -1e30)
        grown = jnp.exp(scores - jnp.max(scores, axis=-1, keepdims=True))
        soft = grown / jnp.sum(grown, axis=-1, keepdims=True)
        d_soft = product_back(d_attended[:, columns], key_value[:, values])
        d_scores = (soft * (d_soft - jnp.sum(soft * d_soft, axis=-1, keepdims=True))).astype(jnp.bfloat16)
        upstream = scale * jnp.dot(d_scores, key_value[:, keys], preferred_element_type=jnp.float32)
        d_key = scale * product_rows(d_scores, query_low[:, columns])
        d_value = product_rows(soft.astype(jnp.bfloat16), d_attended[:, columns])
        if index % per_group == 0:
            d_key_value[:, keys] = d_key
            d_key_value[:, values] = d_value
        else:
            d_key_value[:, keys] += d_key
            d_key_value[:, values] += d_value
        d_head, grad_gain = turn_norm_grad(upstream, linear[:, columns], gains[6:7, 0:HEAD_SIZE], cosine[...], sine[...])
        d_query[:, columns] = d_head.astype(jnp.bfloat16)
        return grad_gain

    query_gain = one_head(0)
    for index in range(1, per_group):
        query_gain = query_gain + one_head(index)
    spread_lin[0].wait_recv()
    spread_lin[1].wait_recv()
    spread_lin[9].start()
    spread_lin[5].start()
    spread_lin[2].wait_recv()
    spread_lin[6].start()
    for index in range(per_group, QUERY_HEADS):
        query_gain = query_gain + one_head(index)
    parcel[...] = d_key_value[pl.ds(rows_of, reach * rows_of), :].astype(jnp.bfloat16)

    def return_copy(distance):
        span = pl.ds((distance - 1) * rows_of, rows_of)
        return push(
            parcel.at[span],
            arrived.at[span],
            kv_send.at[distance - 1],
            kv_recv.at[distance - 1],
            {"ctx": (block + others + 1 - distance) % (others + 1)},
        )

    for distance in range(1, reach + 1):
        copy = return_copy(distance)

        @pl.when(block >= distance)
        def _():
            copy.start()

        @pl.when(block + distance > others)
        def _():
            arrived[pl.ds((distance - 1) * rows_of, rows_of), :] = jnp.zeros((rows_of, 2 * key_width), jnp.bfloat16)

    for copy in near[2:]:
        copy.start()
    spread_lin[3].wait_recv()
    spread_lin[7].start()
    spread_lin[4].wait_recv()
    spread_lin[10].start()
    spread_lin[8].start()
    for index in range(5):
        spread_query[index].start()
    for copy in pair_copies:
        copy.wait_recv()
    for parts, pair_in, pair_sum, arrived_parts in vector_parts:
        for index, chip in enumerate(chips):
            if chip:
                pair_sum[index - 1] = (
                    parts[across_many(me, chip)].astype(jnp.float32) + pair_in[index].astype(jnp.float32)
                ).astype(jnp.bfloat16)
    for copy in chip_copies:
        copy.start()
    query_slots[0] = d_query[...]
    loads[8].wait()
    d_normed[...] = product_back(d_query[...], inward[:, pl.ds(0, query_width)])
    spread_lin[9].wait_recv()
    spread_lin[11].start()
    spread_lin[10].wait_recv()
    spread_lin[12].start()
    spread_query[0].wait_recv()
    spread_query[1].wait_recv()
    spread_query[9].start()
    spread_query[5].start()
    spread_query[2].wait_recv()
    spread_query[6].start()
    for index in (5, 6, 7, 8, 11, 12):
        spread_lin[index].wait_recv()
    grad_wide[:, pl.ds(inward.shape[1], width)] = product_rows(
        ordered[:, pl.ds(depth, depth)], lin_slots[...].reshape(8 * rows_of, width)
    ).astype(jnp.bfloat16)

    for distance in range(1, reach + 1):
        copy = return_copy(distance)

        @pl.when(block + distance <= others)
        def _():
            copy.wait_recv()

    total = d_key_value[pl.ds(0, rows_of), :]
    for distance in range(1, reach + 1):
        total = total + arrived[pl.ds((distance - 1) * rows_of, rows_of), :].astype(jnp.float32)
    for index in range(KEY_VALUE_HEADS):
        columns = pl.ds(index * HEAD_SIZE, HEAD_SIZE)
        d_head, grad_gain = turn_norm_grad(
            total[:, index * HEAD_SIZE : (index + 1) * HEAD_SIZE],
            linear[:, pl.ds(query_width + index * HEAD_SIZE, HEAD_SIZE)],
            gains[7:8, 0:HEAD_SIZE],
            cosine[...],
            sine[...],
        )
        d_rest[:, columns] = d_head.astype(jnp.bfloat16)
        key_gain = grad_gain if index == 0 else key_gain + grad_gain
    d_rest[:, pl.ds(key_width, key_width)] = total[:, key_width:].astype(jnp.bfloat16)
    d_rest[:, pl.ds(2 * key_width, d_middle.shape[1])] = d_middle[...]
    spread_query[3].wait_recv()
    spread_query[7].start()
    spread_query[4].wait_recv()
    spread_query[10].start()
    spread_query[8].start()
    for index in range(5):
        spread_rest[index].start()
    rest_slots[0] = d_rest[...]
    rest_width = d_rest.shape[1]
    d_normed[...] += product_back(d_rest[...], inward[:, pl.ds(query_width, rest_width)])
    value = source[...].astype(jnp.float32)
    factor = lax.rsqrt(jnp.mean(value * value, axis=-1, keepdims=True) + epsilon)
    unit = value * factor
    upstream = d_half[...] + d_normed[...]
    for index in range(8):
        columns = slice(index * depth, (index + 1) * depth)
        gain_parcel[index, 0:8, :] = gain_rows[0:8, columns]
        gain_parcel[index, 0:1, :] = jnp.sum(upstream[:, columns] * unit[:, columns], axis=0, keepdims=True)
        gain_parcel[index, 6:7, :] = query_gain
        gain_parcel[index, 7:8, :] = key_gain
    gain_copies = [
        push(
            gain_parcel.at[across_many(me, distance)],
            gain_arrived.at[distance],
            gain_send.at[distance - 1],
            gain_recv.at[distance - 1],
            {"fsdp": across_many(me, distance)},
        )
        for distance in range(1, 8)
    ]
    for copy in gain_copies + laurel_copies:
        copy.start()
    gain_arrived[0] = gain_parcel[me]
    upstream = upstream * gains[0:1, :]
    d_source[...] = d_half[...] + factor * (upstream - unit * jnp.mean(upstream * unit, axis=-1, keepdims=True))
    spread_rest[0].wait_recv()
    spread_rest[1].wait_recv()
    spread_rest[9].start()
    spread_rest[5].start()
    spread_rest[2].wait_recv()
    spread_rest[6].start()
    spread_query[9].wait_recv()
    spread_query[11].start()
    spread_query[10].wait_recv()
    spread_query[12].start()
    spread_rest[3].wait_recv()
    spread_rest[7].start()
    spread_rest[4].wait_recv()
    spread_rest[10].start()
    spread_rest[8].start()
    for index in (5, 6, 7, 8, 11, 12):
        spread_query[index].wait_recv()
    grad_wide[:, pl.ds(0, query_width)] = product_rows(
        ordered[:, pl.ds(0, depth)], query_slots[...].reshape(8 * rows_of, query_width)
    ).astype(jnp.bfloat16)
    spread_rest[9].wait_recv()
    spread_rest[11].start()
    spread_rest[10].wait_recv()
    spread_rest[12].start()
    for index in (5, 6, 7, 8, 11, 12):
        spread_rest[index].wait_recv()
    grad_wide[:, pl.ds(query_width, rest_width)] = product_rows(
        ordered[:, pl.ds(0, depth)], rest_slots[...].reshape(8 * rows_of, rest_width)
    ).astype(jnp.bfloat16)
    for copy, share in zip(near, near_share):
        copy.wait_recv()
        share.start()
    for copy in gain_copies + laurel_copies + chip_copies:
        copy.wait_recv()
    totals = []
    for parts, pair_in, pair_sum, arrived_parts in vector_parts:
        total = parts[me].astype(jnp.float32) + pair_in[0].astype(jnp.float32)
        for index in range(3):
            total = total + arrived_parts[index].astype(jnp.float32)
        totals.append(total.astype(jnp.bfloat16))
    grad_wide[:, pl.ds(inward.shape[1] + width, totals[0].shape[1])] = totals[0]
    laurel_size = laurel_rows.shape[1]
    tail = jnp.concatenate(
        [jnp.sum(laurel_arrived[...], axis=0), jnp.pad(jnp.sum(gain_arrived[...], axis=0), ((0, 0), (0, width - depth)))],
        axis=0,
    )
    out_size = totals[1].shape[0]
    grad_small[pl.ds(0, out_size), :] = totals[1]
    grad_small[pl.ds(out_size, laurel_size + 8), :] = tail.astype(jnp.bfloat16)
    for copy in near_share:
        copy.wait_recv()
    for copy in (
        spread_lin + spread_query + spread_rest + gain_copies + laurel_copies + near + near_share + pair_copies + chip_copies
    ):
        copy.wait_send()
    for distance in range(1, reach + 1):
        copy = return_copy(distance)

        @pl.when(block >= distance)
        def _():
            copy.wait_send()


def attend_back_call(
    reach, d_lin, query_low, key_value, linear, gains, positions, cosine, sine, middle, d_middle, features,
    source, d_half, gain_rows, residual, d_vector, gated_value, d_back, d_laurel, outward_all, inward_all, d_rows,
):
    rows_of, width = d_lin.shape
    others = lax.axis_size("ctx") - 1
    low, full = jnp.bfloat16, jnp.float32
    hbm = pl.BlockSpec(memory_space=pl.ANY)
    vmem = pl.BlockSpec(memory_space=pltpu.VMEM)
    dma = pltpu.SemaphoreType.DMA
    columns = inward_all.shape[1]
    query_width, key_width = QUERY_HEADS * HEAD_SIZE, KEY_VALUE_HEADS * HEAD_SIZE
    rest_width = columns - query_width
    depth = width // 8
    vector_width = d_vector.shape[1]
    part_shapes = ((depth, vector_width), (vector_width // 8, width))
    shapes = [
        jax.ShapeDtypeStruct((rows_of, width), full),
        jax.ShapeDtypeStruct((depth, columns + width + vector_width), low),
        jax.ShapeDtypeStruct((vector_width // 8 + 16, width), low),
        jax.ShapeDtypeStruct((4, 2 * rows_of, width), low),
    ]
    spans = max(reach, 1)
    return pl.pallas_call(
        functools.partial(attend_back_kernel, others, reach),
        out_shape=shapes,
        in_specs=[vmem] * 19 + [hbm] * 3,
        out_specs=[vmem] * 3 + [hbm],
        scratch_shapes=[
            pltpu.VMEM((8, depth, width), low),
            pltpu.VMEM((width, columns), low),
            pltpu.VMEM((rows_of, query_width), low),
            pltpu.VMEM(((reach + 1) * rows_of, 2 * key_width), full),
            pltpu.VMEM((spans * rows_of, 2 * key_width), low),
            pltpu.VMEM((spans * rows_of, 2 * key_width), low),
            pltpu.VMEM((rows_of, query_width), low),
            pltpu.VMEM((rows_of, rest_width), low),
            pltpu.VMEM((8, rows_of, width), low),
            pltpu.VMEM((8, rows_of, query_width), low),
            pltpu.VMEM((8, rows_of, rest_width), low),
            pltpu.VMEM((8 * rows_of, 2 * depth), low),
            pltpu.VMEM((rows_of, width), full),
            pltpu.VMEM((8, 8, depth), full),
            pltpu.VMEM((8, 8, depth), full),
            pltpu.VMEM((8, 8, width), full),
            dma((9,)),
            dma((13,)),
            dma((13,)),
            dma((13,)),
            dma((13,)),
            dma((13,)),
            dma((13,)),
            dma((spans,)),
            dma((spans,)),
            dma((7,)),
            dma((7,)),
            dma((7,)),
            dma((7,)),
            dma((8,)),
            dma((8,)),
        ]
        + [
            pltpu.VMEM((count, *shape), low)
            for shape in part_shapes
            for count in (4, 3, 3)
        ]
        + [dma((8,)), dma((8,)), dma((6,)), dma((6,))]
        + [pltpu.VMEM((8, *shape), low) for shape in part_shapes]
        + [pltpu.VMEM((8, 8, width), full)],
        compiler_params=pltpu.CompilerParams(collective_id=4, has_side_effects=True, vmem_limit_bytes=60 * 2**20),
        cost_estimate=pl.CostEstimate(
            flops=40 * rows_of * width * columns, bytes_accessed=6 * width * columns, transcendentals=0
        ),
        name="attend_backward",
    )(
        d_lin, query_low, key_value, linear, gains, positions, cosine, sine, middle, d_middle, features,
        source, d_half, gain_rows, residual, d_vector, gated_value, d_back, d_laurel, outward_all, inward_all, d_rows,
    )


def feed_call(forward, own, weights, kept=(), features=None, forward_rows=None, vectors=()):
    rows_of, width = own.shape
    hidden = weights[0].shape[0]
    all_rows = 8 * rows_of
    others = lax.axis_size("ctx") - 1
    low = jnp.bfloat16
    count_made = 3 if forward else 2
    hbm = pl.BlockSpec(memory_space=pl.ANY)
    vmem = pl.BlockSpec(memory_space=pltpu.VMEM)
    half = rows_of // 2
    dma = pltpu.SemaphoreType.DMA
    shapes = [
        jax.ShapeDtypeStruct((rows_of, width), jnp.float32),
        jax.ShapeDtypeStruct((all_rows, width), low),
        jax.ShapeDtypeStruct((2, rows_of, width), low),
        jax.ShapeDtypeStruct((2, 2 * rows_of, width), low),
    ]
    operands = (own, *weights, *kept)
    operand_specs = [vmem] + [hbm] * (3 + len(kept))
    extra = []
    if forward:
        shapes += [jax.ShapeDtypeStruct((8, rows_of, features.shape[1] // 8), low)]
        shapes += [jax.ShapeDtypeStruct((8 * value.shape[0], value.shape[1]), low) for value in vectors]
        operands += (features, *vectors)
        operand_specs += [vmem] * 3
        extra = (
            [dma((7,)), dma((7,)), dma]
            + [pltpu.VMEM((8, *value.shape), low) for value in vectors]
            + [dma((13,))] * 4
            + [dma((8,))] * 2
        )
    else:
        operands += (forward_rows,)
        operand_specs += [hbm]
    shapes += [jax.ShapeDtypeStruct((all_rows, hidden), low)] * count_made
    return pl.pallas_call(
        functools.partial(feed_kernel, forward, rows_of, others),
        out_shape=shapes,
        in_specs=operand_specs,
        out_specs=[vmem] + [hbm] * (len(shapes) - 1),
        scratch_shapes=[pltpu.VMEM((hidden, width), low)] * 3
        + [pltpu.VMEM((all_rows, hidden), low)] * (len(kept) + count_made)
        + [
            pltpu.VMEM((4, 2 * rows_of, width), low),
            pltpu.VMEM((4, 2 * rows_of, width), low),
            pltpu.VMEM((4, rows_of, width), low),
            pltpu.VMEM((3, rows_of, width), low),
            pltpu.VMEM((2, half, width), low),
            pltpu.VMEM((2, half, width), low),
            pltpu.VMEM((4, half, width), low),
            dma((20,)),
            dma((20,)),
            dma((3 + len(kept),)),
            dma((4 * (1 + count_made),)),
            dma((2,)),
            dma((2,)),
            dma((4,)),
            dma((4,)),
        ]
        + extra,
        compiler_params=pltpu.CompilerParams(
            collective_id=1 if forward else 2,
            has_side_effects=True,
            vmem_limit_bytes=56 * 2**20,
        ),
        cost_estimate=pl.CostEstimate(
            flops=40 * all_rows * hidden * width // 2,
            bytes_accessed=6 * hidden * width + 8 * all_rows * width,
            transcendentals=0,
        ),
        name="feed_forward" if forward else "feed_backward",
    )(*operands)


def weight_grad_kernel(
    own_steps, near_steps, gate, up, down, rows, d_rows, hidden, d_gate, d_up,
    rows_near, rows_next, d_rows_near, rows_far, d_rows_far,
    grad_gate, grad_up, grad_down, hidden_tile, d_gate_tile, d_up_tile,
):
    step = pl.program_id(1)
    tile = 512
    hidden_size = gate.shape[0]
    chunk = rows.shape[1]

    @pl.when(step == 0)
    def _():
        grad_gate[...] = jnp.zeros_like(grad_gate)
        grad_up[...] = jnp.zeros_like(grad_up)
        grad_down[...] = jnp.zeros_like(grad_down)

    def accumulate(rows, d_rows):
        def body(index, carry):
            columns = pl.ds(pl.multiple_of(index * chunk, chunk), chunk)
            right, d_right = rows[:, columns], d_rows[:, columns]
            grad_gate[:, columns] += matrix_product(d_gate_tile[...], right)
            grad_up[:, columns] += matrix_product(d_up_tile[...], right)
            grad_down[:, columns] += matrix_product(hidden_tile[...], d_right)
            return carry
        lax.fori_loop(0, rows.shape[1] // chunk, body, 0)

    @pl.when(step < own_steps)
    def _():
        hidden_tile[...] = hidden[...].T
        d_gate_tile[...] = d_gate[...].T
        d_up_tile[...] = d_up[...].T
        accumulate(rows, d_rows)

    def other_rows(rows, d_rows):
        def body(index, carry):
            span = pl.ds(pl.multiple_of(index * tile, tile), tile)
            gate_value = product_back(gate[span, :], rows[...])
            up_value = product_back(up[span, :], rows[...])
            d_hidden = product_back(down[span, :], d_rows[...])
            value, slope = gelu_parts(gate_value)
            hidden_tile[span, :] = (value * up_value).astype(jnp.bfloat16)
            d_gate_tile[span, :] = (d_hidden * up_value * slope).astype(jnp.bfloat16)
            d_up_tile[span, :] = (d_hidden * value).astype(jnp.bfloat16)
            return carry

        lax.fori_loop(0, hidden_size // tile, body, 0)
        accumulate(rows, d_rows)

    @pl.when((step >= own_steps) & (step < own_steps + near_steps // 2))
    def _():
        other_rows(rows_near, d_rows_near)

    @pl.when((step >= own_steps + near_steps // 2) & (step < own_steps + near_steps))
    def _():
        other_rows(rows_next, d_rows_near)

    @pl.when(step >= own_steps + near_steps)
    def _():
        other_rows(rows_far, d_rows_far)


def weight_grad_call(
    gate, up, down, rows, d_rows, hidden, d_gate, d_up, rows_near, rows_next, d_rows_near, rows_far, d_rows_far,
    hid=1024, tok=256,
):
    size, width = gate.shape
    hid = min(hid, size)
    own_steps, near_steps, far_steps = [value.shape[0] // tok for value in (rows, d_rows_near, rows_far)]
    low = jnp.bfloat16

    def stream(first, steps, columns, across):
        def place(h, s):
            return jnp.clip(s - first, 0, steps - 1), h if across else 0

        return pl.BlockSpec((tok, columns), place)

    weight = pl.BlockSpec((hid, width), lambda h, s: (h, 0))
    own = stream(0, own_steps, width, False)
    own_mid = stream(0, own_steps, hid, True)
    near_one = stream(own_steps, near_steps // 2, width, False)
    near_two = stream(own_steps + near_steps // 2, near_steps // 2, width, False)
    near = stream(own_steps, near_steps, width, False)
    far = stream(own_steps + near_steps, far_steps, width, False)
    flops = 6 * size * width * (rows.shape[0] + 2 * d_rows_near.shape[0] + 2 * rows_far.shape[0])
    return pl.pallas_call(
        functools.partial(weight_grad_kernel, own_steps, near_steps),
        grid=(size // hid, own_steps + near_steps + far_steps),
        in_specs=[weight] * 3 + [own] * 2 + [own_mid] * 3 + [near_one, near_two, near] + [far] * 2,
        out_specs=[weight] * 3,
        out_shape=[jax.ShapeDtypeStruct((size, width), jnp.float32)] * 3,
        scratch_shapes=[pltpu.VMEM((hid, tok), low)] * 3,
        compiler_params=pltpu.CompilerParams(
            dimension_semantics=("arbitrary", "arbitrary"), vmem_limit_bytes=62 * 2**20
        ),
        cost_estimate=pl.CostEstimate(flops=flops, bytes_accessed=100 * 2**20, transcendentals=0),
        name="weight_grads",
    )(
        gate, up, down, rows, d_rows, hidden, d_gate, d_up, rows_near, rows_next, d_rows_near, rows_far, d_rows_far
    )


def per_device(
    tokens,
    per_layer,
    segments,
    positions,
    cotangent,
    query_weight,
    key_matrix,
    value_matrix,
    output_weight,
    laurel_down,
    laurel_up,
    vector_gate,
    vector_out,
    norm_input,
    norm_attention,
    norm_laurel,
    norm_before,
    norm_after,
    norm_vector,
    query_norm_gain,
    norm_key,
    hidden_gate,
    hidden_up,
    hidden_down,
):
    count_of_rows = tokens.shape[0]
    shards = lax.axis_size("fsdp")
    width = tokens.shape[1]
    heads_per_group = QUERY_HEADS // KEY_VALUE_HEADS
    reach_blocks = min((WINDOW + count_of_rows - 2) // count_of_rows, lax.axis_size("ctx") - 1)
    score_scale = HEAD_SIZE ** (-0.5)
    fused = shards == 8 and lax.axis_size("ctx") == 4
    query_width = query_weight.shape[1]
    key_width = key_matrix.shape[1]

    gain_shards = (
        norm_input,
        norm_attention,
        norm_laurel,
        norm_before,
        norm_after,
        norm_vector,
        query_norm_gain,
        norm_key,
    )
    gain_sizes = [gain.shape[0] for gain in gain_shards]
    gain_starts = [sum(gain_sizes[:index]) for index in range(len(gain_sizes))]
    inward_weight = jnp.concatenate([query_weight, key_matrix, value_matrix, laurel_down], axis=1)
    inward_weight = jnp.pad(inward_weight, ((0, 0), (0, -inward_weight.shape[1] % 128)))
    source = tokens.astype(jnp.float32)
    vectors = per_layer.astype(jnp.float32)
    rank = laurel_down.shape[1]
    unused, allowed = window(positions, count_of_rows, reach_blocks)

    def head_facing(linear, gain):
        return rotary_apply(root_mean_norm(linear, gain), positions)

    if fused:
        me = lax.axis_index("fsdp")
        mine = (jnp.arange(shards) == me).astype(jnp.bfloat16)[None, :, None]

        def placed_line(shares):
            stacked = jnp.concatenate(shares).reshape(len(shares), -1)
            line = (stacked[:, None, :] * mine).reshape(len(shares), -1)
            return jnp.pad(line, ((0, 0), (0, width - line.shape[1])))

        gain_lines = jnp.concatenate([placed_line(gain_shards[:6]), placed_line(gain_shards[6:]), laurel_up], axis=0)
        cosine, sine_part = rotary_tables(positions, HEAD_SIZE)
        (
            normed,
            gains_all,
            linear,
            query_lowered,
            key_value,
            features,
            laurel_mid,
            attn_lin,
            full_laurel_up,
            full_inward,
            full_output,
        ) = attend_call(
            reach_blocks, tokens, gain_lines, positions[:, None], cosine, sine_part, inward_weight, output_weight
        )
        full_laurel_up = full_laurel_up.astype(jnp.bfloat16)
        gains = [gains_all[index, : size * shards] for index, size in enumerate(gain_sizes)]
        middle_low = laurel_mid
        laurel_mid = laurel_mid[:, :rank]
        window_keys, window_values = key_value[:, :key_width], key_value[:, key_width:]
    else:
        gain_line = jnp.concatenate(gain_shards)
        gain_line = jnp.pad(gain_line, (0, -gain_line.shape[0] % 2048)).reshape(-1, 128)
        gains_all = gather(gain_line, "fsdp").reshape(shards, -1)
        gains = [
            gains_all[:, start : start + size].reshape(-1).astype(jnp.float32)
            for start, size in zip(gain_starts, gain_sizes)
        ]
        full_inward = gather(inward_weight, "fsdp")
        full_output, full_vector_gate, full_vector_out, full_laurel_up = [
            gather(value, "fsdp") for value in (output_weight, vector_gate, vector_out, laurel_up)
        ]
        normed = root_mean_norm(source, gains[0])
        lowered_normed = normed.astype(jnp.bfloat16)
        inward = matrix_product(lowered_normed, full_inward)
        linear = inward[:, : query_width + key_width]
        value_lowered = inward[:, query_width + key_width : query_width + 2 * key_width].astype(jnp.bfloat16)
        laurel_mid = inward[:, query_width + 2 * key_width :][:, :rank].astype(jnp.bfloat16)
        query_lowered = head_facing(
            linear[:, :query_width].reshape(count_of_rows, QUERY_HEADS, HEAD_SIZE), gains[6]
        ).astype(jnp.bfloat16)
        key_lowered = head_facing(
            linear[:, query_width:].reshape(count_of_rows, KEY_VALUE_HEADS, HEAD_SIZE), gains[7]
        ).astype(jnp.bfloat16)
        key_value = jnp.stack([key_lowered.reshape(count_of_rows, -1), value_lowered])
        pair_blocks = [key_value]
        for distance in range(1, reach_blocks + 1):
            pair_blocks.append(from_behind(key_value, "ctx", distance))
        window_couple = jnp.concatenate(pair_blocks, axis=1)
        window_keys, window_values = window_couple[0], window_couple[1]
    (
        gain_input,
        gain_attention,
        gain_laurel,
        gain_before,
        gain_after,
        gain_vector,
        gain_query,
        key_norm_gain,
    ) = gains
    if not fused:
        query_linear = linear[:, :query_width].reshape(count_of_rows, QUERY_HEADS, HEAD_SIZE)
        key_linear = linear[:, query_width:].reshape(count_of_rows, KEY_VALUE_HEADS, HEAD_SIZE)
        query_lowered = query_lowered.reshape(count_of_rows, KEY_VALUE_HEADS, heads_per_group, HEAD_SIZE)
        window_keys = window_keys.reshape(-1, KEY_VALUE_HEADS, HEAD_SIZE)
        window_values = window_values.reshape(-1, KEY_VALUE_HEADS, HEAD_SIZE)

        def masked_scores():
            raw_scores = score_scale * jnp.einsum(
                "tgfd,kgd->gftk", query_lowered, window_keys, preferred_element_type=jnp.float32
            )
            return jnp.where(allowed, raw_scores, -1e30)

        scores_first = masked_scores()
        row_peak = jnp.max(scores_first, axis=-1, keepdims=True)
        exp_scores = jnp.exp(scores_first - row_peak)
        row_total = jnp.sum(exp_scores, axis=-1, keepdims=True)
        log_total = row_peak + jnp.log(row_total)
        soft_low = (exp_scores / row_total).astype(jnp.bfloat16)
        attended_low = (
            jnp.einsum("gftk,kgd->tgfd", soft_low, window_values, preferred_element_type=jnp.float32)
            .reshape(count_of_rows, QUERY_HEADS * HEAD_SIZE)
            .astype(jnp.bfloat16)
        )
        attn_lin = matrix_product(attended_low, full_output)
    residual_one = source + root_mean_norm(attn_lin, gain_attention)
    laurel_lin = matrix_product(laurel_mid, full_laurel_up)
    mixed = (residual_one + normed + root_mean_norm(laurel_lin, gain_laurel)) * inv_root
    ffn_in = root_mean_norm(mixed, gain_before).astype(jnp.bfloat16)
    if fused:
        (
            feed_value,
            rows_all,
            rows_far,
            rows_near,
            slices,
            full_vector_gate,
            full_vector_out,
            hidden_all,
            lift_all,
            bend_all,
        ) = feed_call(
            True, ffn_in, (hidden_gate, hidden_up, hidden_down), features=features, vectors=(vector_gate, vector_out)
        )
        slices = slices.reshape(shards * count_of_rows, -1)
    else:
        normed_slices = feature_slices(lowered_normed)
        attended_slices = feature_slices(attended_low)
        rows_all = gather(ffn_in, "fsdp")
        gate_all = product_back(rows_all, hidden_gate)
        up_all = product_back(rows_all, hidden_up)
        hidden_all = gated(gate_all, up_all).astype(jnp.bfloat16)
        feed_value = scatter_sum(matrix_product(hidden_all, hidden_down))
    residual_two = mixed + root_mean_norm(feed_value, gain_after)
    residual_low = residual_two.astype(jnp.bfloat16)
    vector_lin = matrix_product(residual_low, full_vector_gate)
    gated_low = gated(vector_lin, vectors).astype(jnp.bfloat16)
    vector_back = matrix_product(gated_low, full_vector_out)
    result = residual_two + root_mean_norm(vector_back, gain_vector)
    upstream = cotangent.astype(jnp.float32)
    d_vector_back, grad_gain_vector = norm_grad(vector_back, gain_vector, upstream)
    d_vector_back_low = d_vector_back.astype(jnp.bfloat16)
    grad_vector_out = product_rows(gated_low, d_vector_back_low)
    d_gated = product_back(d_vector_back_low, full_vector_out)
    d_vector_lin, d_vectors = gated_grad(vector_lin, vectors, d_gated)
    d_vector_lin_low = d_vector_lin.astype(jnp.bfloat16)
    grad_vector_gate = product_rows(residual_low, d_vector_lin_low)
    if fused:
        rows_far = gather(rows_far.reshape(-1, width), "fsdp")
    d_residual = upstream + product_back(d_vector_lin_low, full_vector_gate)
    d_feed, grad_gain_after = norm_grad(feed_value, gain_after, d_residual)
    d_feed_low = d_feed.astype(jnp.bfloat16)
    if fused:
        d_ffn_in, d_rows_all, d_rows_far, rows_next, d_gate_low, d_up_low = feed_call(
            False, d_feed_low, (hidden_down, hidden_gate, hidden_up), (lift_all, bend_all), forward_rows=rows_all
        )
        d_ffn_in, rows_far = lax.optimization_barrier((d_ffn_in, rows_far))
        d_rows_far = gather(d_rows_far.reshape(-1, width), "fsdp")
    else:
        d_rows_all = gather(d_feed_low, "fsdp")
        d_hidden = product_back(d_rows_all, hidden_down)
        d_gate_all, d_up_all = gated_grad(gate_all, up_all, d_hidden)
        d_gate_low = d_gate_all.astype(jnp.bfloat16)
        d_up_low = d_up_all.astype(jnp.bfloat16)
        d_ffn_in = scatter_sum(
            matrix_product(d_gate_low, hidden_gate) + matrix_product(d_up_low, hidden_up)
        )

    if not fused:
        grad_hidden_gate, grad_hidden_up, grad_hidden_down = [
            lax.psum(grad.astype(jnp.bfloat16), "ctx").astype(jnp.float32)
            for grad in (
                product_rows(d_gate_low, rows_all),
                product_rows(d_up_low, rows_all),
                product_rows(hidden_all, d_rows_all),
            )
        ]

    d_mixed_part, grad_gain_before = norm_grad(mixed, gain_before, d_ffn_in)
    d_half = (d_residual + d_mixed_part) * inv_root
    d_laurel_lin, grad_gain_laurel = norm_grad(laurel_lin, gain_laurel, d_half)
    d_laurel_low = d_laurel_lin.astype(jnp.bfloat16)
    grad_laurel_up = product_rows(laurel_mid, d_laurel_low)
    d_laurel_mid = product_back(d_laurel_low, full_laurel_up).astype(jnp.bfloat16)
    d_attn_lin, grad_gain_attention = norm_grad(attn_lin, gain_attention, d_half)
    d_attn_low = d_attn_lin.astype(jnp.bfloat16)
    if fused:
        empty = jnp.zeros((width,), jnp.float32)
        gain_rows = jnp.stack(
            [
                empty,
                grad_gain_attention,
                grad_gain_laurel,
                grad_gain_before,
                grad_gain_after,
                grad_gain_vector,
                empty,
                empty,
            ]
        )
        d_middle = jnp.pad(d_laurel_mid, ((0, 0), (0, full_inward.shape[1] - query_width - 2 * key_width - rank)))
        d_source, grad_wide, grad_small, d_rows_near = attend_back_call(
            reach_blocks, d_attn_low, query_lowered, key_value, linear, gains_all, positions[:, None], cosine, sine_part,
            middle_low, d_middle, slices, tokens, d_half, gain_rows, residual_low, d_vector_lin_low, gated_low,
            d_vector_back_low, d_laurel_low,
            full_output, full_inward,
            d_rows_all,
        )
        grad_hidden_gate, grad_hidden_up, grad_hidden_down = weight_grad_call(
            hidden_gate,
            hidden_up,
            hidden_down,
            rows_all,
            d_rows_all,
            hidden_all,
            d_gate_low,
            d_up_low,
            rows_near.reshape(-1, width),
            rows_next.reshape(-1, width),
            d_rows_near.reshape(-1, width),
            rows_far,
            d_rows_far,
        )
    else:
        d_attended = (
            product_back(d_attn_low, full_output)
            .astype(jnp.bfloat16)
            .reshape(count_of_rows, KEY_VALUE_HEADS, heads_per_group, HEAD_SIZE)
        )
        soft_again = jnp.exp(masked_scores() - log_total)
        d_soft = jnp.einsum(
            "tgfd,kgd->gftk", d_attended, window_values, preferred_element_type=jnp.float32
        )
        d_scores = (
            soft_again * (d_soft - jnp.sum(soft_again * d_soft, axis=-1, keepdims=True))
        ).astype(jnp.bfloat16)
        d_query = score_scale * jnp.einsum(
            "gftk,kgd->tgfd", d_scores, window_keys, preferred_element_type=jnp.float32
        )
        grad_key_rows = score_scale * jnp.einsum(
            "gftk,tgfd->kgd", d_scores, query_lowered, preferred_element_type=jnp.float32
        )
        grad_value_rows = jnp.einsum(
            "gftk,tgfd->kgd",
            soft_again.astype(jnp.bfloat16),
            d_attended,
            preferred_element_type=jnp.float32,
        )
        grad_window_couple = jnp.stack(
            [
                grad_key_rows.reshape(-1, KEY_VALUE_HEADS * HEAD_SIZE),
                grad_value_rows.reshape(-1, KEY_VALUE_HEADS * HEAD_SIZE),
            ]
        )
        grad_own_part = grad_window_couple[:, :count_of_rows]
        for distance in range(1, reach_blocks + 1):
            grad_own_part = grad_own_part + from_behind(
                grad_window_couple[:, distance * count_of_rows : (distance + 1) * count_of_rows].astype(
                    jnp.bfloat16
                ),
                "ctx",
                -distance,
            ).astype(jnp.float32)
        unused, query_pull = jax.vjp(head_facing, query_linear, gain_query)
        d_query_lin, grad_gain_query = query_pull(
            d_query.reshape(count_of_rows, QUERY_HEADS, HEAD_SIZE)
        )
        unused, key_pullback_fn = jax.vjp(head_facing, key_linear, key_norm_gain)
        grad_key_linear, grad_key_norm_gain = key_pullback_fn(
            grad_own_part[0].reshape(count_of_rows, KEY_VALUE_HEADS, HEAD_SIZE)
        )
        d_inward = jnp.concatenate(
            [
                d_query_lin.reshape(count_of_rows, QUERY_HEADS * HEAD_SIZE).astype(jnp.bfloat16),
                grad_key_linear.reshape(count_of_rows, KEY_VALUE_HEADS * HEAD_SIZE).astype(
                    jnp.bfloat16
                ),
                grad_own_part[1].astype(jnp.bfloat16),
                d_laurel_mid,
                jnp.zeros((count_of_rows, full_inward.shape[1] - query_width - 2 * key_width - rank), jnp.bfloat16),
            ],
            axis=1,
        )
        grad_inward = product_rows(normed_slices, gather(d_inward, "fsdp")).astype(jnp.bfloat16)
        grad_output = product_rows(attended_slices, gather(d_attn_low, "fsdp")).astype(jnp.bfloat16)
        grad_wide = jnp.concatenate([grad_inward, grad_output], axis=1)
        small_rows = jnp.concatenate(
            [
                grad_vector_gate.reshape(shards, -1, width),
                grad_vector_out.reshape(shards, -1, width),
                grad_laurel_up.reshape(shards, -1, width),
            ],
            axis=1,
        ).astype(jnp.bfloat16)
        grad_small = lax.psum_scatter(small_rows, "fsdp", scatter_dimension=0, tiled=False)
        d_normed = d_half + product_back(d_inward, full_inward)
        d_source_part, grad_gain_input = norm_grad(source, gain_input, d_normed)
        d_source = d_half + d_source_part
        gain_lines = jnp.concatenate(
            [
                grad.reshape(shards, -1)
                for grad in (
                    grad_gain_input,
                    grad_gain_attention,
                    grad_gain_laurel,
                    grad_gain_before,
                    grad_gain_after,
                    grad_gain_vector,
                    grad_gain_query,
                    grad_key_norm_gain,
                )
            ],
            axis=1,
        )
        gain_share = lax.psum_scatter(gain_lines, "fsdp", scatter_dimension=0, tiled=False)
        gain_count = gain_share.shape[0]
        gain_share = jnp.pad(gain_share, (0, -gain_count % width)).astype(jnp.bfloat16)
        grad_small = jnp.concatenate([grad_small, gain_share.reshape(-1, width)], axis=0)

    grad_wide, grad_small = [value.astype(jnp.float32) for value in lax.psum((grad_wide, grad_small), "ctx")]
    inward_width = full_inward.shape[1]
    grad_inward = grad_wide[:, :inward_width]
    grad_output = grad_wide[:, inward_width : inward_width + width]
    out_rows, laurel_rows = vector_out.shape[0], laurel_up.shape[0]
    if fused:
        share_vector_gate = grad_wide[:, inward_width + width :]
        gain_start = out_rows + laurel_rows
        share_vector_out = grad_small[:out_rows]
        share_laurel_up = grad_small[out_rows:gain_start]
        gain_lines = grad_small[gain_start:]
        gain_grads = tuple(
            lax.dynamic_slice_in_dim(gain_lines[index], me * size, size) if index >= 6 else gain_lines[index, :size]
            for index, size in enumerate(gain_sizes)
        )
    else:
        gate_rows = vector_gate.shape[0] * vector_gate.shape[1] // width
        share_vector_gate = grad_small[:gate_rows].reshape(vector_gate.shape)
        share_vector_out = grad_small[gate_rows : gate_rows + out_rows]
        gain_start = gate_rows + out_rows + laurel_rows
        share_laurel_up = grad_small[gate_rows + out_rows : gain_start]
        gain_share = grad_small[gain_start:].reshape(-1)
        gain_grads = tuple(
            gain_share[start : start + size] for start, size in zip(gain_starts, gain_sizes)
        )
    value_start = query_width + key_width
    return (
        result.astype(jnp.bfloat16),
        d_source,
        d_vectors,
        grad_inward[:, :query_width],
        grad_inward[:, query_width:value_start],
        grad_inward[:, value_start : value_start + key_width],
        grad_output,
        grad_inward[:, value_start + key_width : value_start + key_width + rank],
        share_laurel_up,
        share_vector_gate,
        share_vector_out,
    ) + gain_grads + (
        grad_hidden_gate,
        grad_hidden_up,
        grad_hidden_down,
    )


def solution(mesh):
    rows = P(("fsdp", "ctx"), None)
    line = P(("fsdp", "ctx"))
    weight = P("fsdp", None)
    gain = P("fsdp")
    return jax.shard_map(
        per_device,
        mesh=mesh,
        in_specs=(rows, rows, line, line, rows) + (weight,) * 8 + (gain,) * 8 + (weight,) * 3,
        out_specs=(rows,) * 3 + (weight,) * 8 + (gain,) * 8 + (weight,) * 3,
        check_vma=False,
    )
```

```python
import functools

import jax
import jax.numpy as jnp
from jax import lax
from jax.experimental import pallas as pl
from jax.experimental.pallas import tpu as pltpu
from jax.sharding import PartitionSpec as P

QUERY_HEADS = 8
KEY_VALUE_HEADS = 2
HEAD_SIZE = 256
WINDOW = 1024


epsilon = 1e-06
rope_base = 10000.0
inv_root = 0.7071067811865476
gelu_scale = 0.7978845608028654
gelu_cubic = 0.044715


def from_behind(value, axis, steps):
    count = lax.axis_size(axis)
    initial, last = (max(0, -steps), min(count, count - steps))
    return lax.ppermute(value, axis, [(source, source + steps) for source in range(initial, last)])


def other_blocks(value, axis):
    count = lax.axis_size(axis)
    return jnp.concatenate(
        [
            lax.ppermute(value, axis, [(source, (source + step) % count) for source in range(count)])
            for step in range(1, count)
        ],
        axis=0,
    )


def root_mean_norm(value, gain):
    factor = lax.rsqrt(jnp.mean(value * value, axis=-1, keepdims=True) + epsilon)
    return value * factor * gain


def gelu_tanh(value):
    return jax.nn.gelu(value, approximate=True)


def gated(gate_value, up_value):
    return gelu_tanh(gate_value) * up_value


def rotary_apply(value, token_position):
    half_size = value.shape[-1] // 2
    frequency = rope_base ** (-2.0 * jnp.arange(half_size, dtype=jnp.float32) / value.shape[-1])
    angle = token_position.astype(jnp.float32)[:, None] * frequency[None, :]
    cosine = jnp.cos(angle)[:, None, :]
    sine_part = jnp.sin(angle)[:, None, :]
    first_half = value[..., :half_size]
    second_half = value[..., half_size:]
    return jnp.concatenate(
        [
            first_half * cosine - second_half * sine_part,
            second_half * cosine + first_half * sine_part,
        ],
        axis=-1,
    )


def rotary_tables(token_position, size):
    half_size = size // 2
    frequency = rope_base ** (-2.0 * jnp.arange(half_size, dtype=jnp.float32) / size)
    angle = token_position.astype(jnp.float32)[:, None] * frequency[None, :]
    return jnp.cos(angle), jnp.sin(angle)


def window(positions, rows_of, reach):
    key_offset = jnp.concatenate(
        [distance * rows_of - jnp.arange(rows_of, dtype=jnp.int32) for distance in range(reach + 1)]
    )
    key_gap = jnp.arange(rows_of, dtype=jnp.int32)[:, None] + key_offset[None, :]
    return key_gap, (key_gap >= 0) & (key_gap <= positions[:, None]) & (key_gap < WINDOW)


def matrix_product(left, right):
    return jnp.dot(left, right, preferred_element_type=jnp.float32)


def product_back(left, right):
    return lax.dot_general(
        left, right, (((1,), (1,)), ((), ())), preferred_element_type=jnp.float32
    )


def product_rows(left, right):
    return lax.dot_general(
        left, right, (((0,), (0,)), ((), ())), preferred_element_type=jnp.float32
    )


def norm_grad(value, gain, upstream):
    unused, pullback = jax.vjp(root_mean_norm, value, gain)
    return pullback(upstream)


def gated_grad(gate_value, up_value, upstream):
    unused, pullback = jax.vjp(gated, gate_value, up_value)
    return pullback(upstream)


def gather(value, axis):
    return lax.all_gather(value, axis, axis=0, tiled=True)


def feature_slices(value):
    count = lax.axis_size("fsdp")
    rows = value.shape[0]
    return lax.all_to_all(
        value.reshape(rows, count, -1), "fsdp", split_axis=1, concat_axis=0, tiled=True
    ).reshape(count * rows, -1)


def scatter_sum(value):
    return lax.psum_scatter(
        value.astype(jnp.bfloat16), "fsdp", scatter_dimension=0, tiled=True
    ).astype(jnp.float32)


def gelu_parts(gate):
    square = gate * gate
    bend = jnp.tanh(gelu_scale * gate * (1.0 + gelu_cubic * square))
    half_up = 0.5 * (1.0 + bend)
    slope = half_up + 0.5 * gate * (1.0 - bend * bend) * (
        gelu_scale * (1.0 + 3.0 * gelu_cubic * square)
    )
    return gate * half_up, slope


def across(me, stride):
    return me + stride - 2 * stride * ((me // stride) % 2)


def across_many(me, bits):
    for stride in (1, 2, 4):
        if bits & stride:
            me = across(me, stride)
    return me


def feed_kernel(forward, rows_of, others, *refs):
    half = rows_of // 2
    if forward:
        (source, normed, attn_lin, middle, laurel, gains), refs = refs[:6], refs[6:]
        (gate_hbm, up_hbm, down_hbm, features, gate_own, out_own), refs = refs[:6], refs[6:]
        (total, mixed, laurel_lin, rows_hbm, far_hbm, near_hbm), refs = refs[:6], refs[6:]
        (slices_hbm, gate_all, out_all, hidden_hbm, lift_hbm, bend_hbm), rest = refs[:6], refs[6:]
        weights_hbm, kept_hbm, made_hbm = (gate_hbm, up_hbm, down_hbm), (), (hidden_hbm, lift_hbm, bend_hbm)
    else:
        (feed_value, mixed, gains, gate_all, out_all, vectors, cotangent), refs = refs[:7], refs[7:]
        (down_hbm, gate_hbm, up_hbm, lift_hbm, bend_hbm, forward_rows), refs = refs[:6], refs[6:]
        (total, result, d_vectors, residual_low, d_vector_low, gated_low, d_back_low, d_residual, gain_rows), refs = (
            refs[:9],
            refs[9:],
        )
        (rows_hbm, far_hbm, near_hbm, d_gate_hbm, d_up_hbm), rest = refs[:5], refs[5:]
        weights_hbm, kept_hbm, made_hbm = (down_hbm, gate_hbm, up_hbm), (lift_hbm, bend_hbm), (d_gate_hbm, d_up_hbm)
    count_kept, count_made = len(kept_hbm), len(made_hbm)
    weights = rest[:3]
    kept = rest[3 : 3 + count_kept]
    made = rest[3 + count_kept : 3 + count_kept + count_made]
    (own, rows, part, sib_in, chip_sum, relay_in, relay_sum, last_in, send_sem, recv_sem, in_sem, out_sem, far_send, far_recv, near_send, near_recv, *extra) = rest[
        3 + count_kept + count_made :
    ]
    hidden = weights[0].shape[0]
    width = weights[0].shape[1]
    me = lax.axis_index("fsdp")
    sibling, beside, above = across(me, 1), across(me, 2), across(me, 4)

    loads = [
        pltpu.make_async_copy(source, target, in_sem.at[index])
        for index, (source, target) in enumerate(zip(weights_hbm + kept_hbm, tuple(weights) + tuple(kept)))
    ]
    for load in loads:
        load.start()

    block = lax.axis_index("ctx")
    def before_feed():
        def unit(value):
            return value * lax.rsqrt(jnp.mean(value * value, axis=-1, keepdims=True) + epsilon)

        laurel_lin[...] = jnp.dot(middle[...], laurel[...].astype(jnp.bfloat16), preferred_element_type=jnp.float32)
        value = source[...].astype(jnp.float32) + unit(attn_lin[...]) * gains[1:2, :] + normed[...]
        value = (value + unit(laurel_lin[...]) * gains[2:3, :]) * inv_root
        mixed[...] = value
        own[...] = (unit(value) * gains[3:4, :]).astype(jnp.bfloat16)

    def after_feed():
        def unit(value):
            return value * lax.rsqrt(jnp.mean(value * value, axis=-1, keepdims=True) + epsilon)

        residual = mixed[...] + unit(feed_value[...]) * gains[4:5, :]
        residual_low[...] = residual.astype(jnp.bfloat16)
        vector_lin = jnp.dot(residual_low[...], gate_all[...], preferred_element_type=jnp.float32)
        value, slope = gelu_parts(vector_lin)
        per_token = vectors[...].astype(jnp.float32)
        gated_low[...] = (value * per_token).astype(jnp.bfloat16)
        vector_back = jnp.dot(gated_low[...], out_all[...], preferred_element_type=jnp.float32)
        result[...] = (residual + unit(vector_back) * gains[5:6, :]).astype(jnp.bfloat16)
        upstream = cotangent[...].astype(jnp.float32)
        d_back, grad_vector_gain = norm_rows_grad(vector_back, gains[5:6, :], upstream)
        d_back_low[...] = d_back.astype(jnp.bfloat16)
        d_gated = product_back(d_back_low[...], out_all[...])
        d_vectors[...] = d_gated * value
        d_vector_low[...] = (d_gated * per_token * slope).astype(jnp.bfloat16)
        d_residual[...] = upstream + product_back(d_vector_low[...], gate_all[...])
        d_feed, grad_after_gain = norm_rows_grad(feed_value[...], gains[4:5, :], d_residual[...])
        own[...] = d_feed.astype(jnp.bfloat16)
        gain_rows[...] = jnp.zeros_like(gain_rows)
        gain_rows[4:5, :] = grad_after_gain
        gain_rows[5:6, :] = grad_vector_gain

    greet(me, range(1, 8) if forward else (1, 2, 4), block, others, before_feed if forward else after_feed)

    def send(index, source, target, partner):
        return pltpu.make_async_remote_copy(
            src_ref=source,
            dst_ref=target,
            send_sem=send_sem.at[index],
            recv_sem=recv_sem.at[index],
            device_id={"fsdp": partner},
            device_id_type=pl.DeviceIdType.MESH,
        )

    low, high = pl.ds(0, half), pl.ds(half, half)
    mine, theirs = pl.ds(0, rows_of), pl.ds(rows_of, rows_of)
    copies = [
        send(0, own, rows.at[0, theirs], sibling),
        send(1, own.at[low], rows.at[1, low], beside),
        send(2, own.at[low], rows.at[1, high], above),
        send(3, own.at[high], rows.at[2, low], beside),
        send(4, own.at[high], rows.at[2, high], above),
        send(5, rows.at[1, mine], rows.at[1, theirs], sibling),
        send(6, rows.at[2, mine], rows.at[2, theirs], sibling),
        send(7, rows.at[1, low], rows.at[3, low], above),
        send(8, rows.at[2, high], rows.at[3, high], beside),
        send(9, rows.at[3, mine], rows.at[3, theirs], sibling),
        send(10, part.at[0, theirs], sib_in.at[0], sibling),
        send(11, part.at[1, theirs], sib_in.at[1], sibling),
        send(12, part.at[2, theirs], sib_in.at[2], sibling),
        send(13, part.at[3, theirs], sib_in.at[3], sibling),
        send(14, chip_sum.at[0, high], last_in.at[2], above),
        send(15, chip_sum.at[1, low], last_in.at[1], beside),
        send(16, chip_sum.at[2, low], relay_in.at[0], above),
        send(17, chip_sum.at[2, high], relay_in.at[1], beside),
        send(18, relay_sum.at[0], last_in.at[0], beside),
        send(19, relay_sum.at[1], last_in.at[3], above),
    ]
    outs = []

    def write_out(source, target):
        copy = pltpu.make_async_copy(source, target, out_sem.at[len(outs)])
        copy.start()
        outs.append(copy)

    for index in range(5):
        copies[index].start()
    spreads = []
    if forward:
        gate_slots, out_slots, gate_send, gate_recv, vec_send, vec_recv, gate_out, vec_out = extra[3:]
        spreads = [
            spread_copies(gate_own, gate_slots, gate_send, gate_recv, me),
            spread_copies(out_own, out_slots, vec_send, vec_recv, me),
        ]
        for spread in spreads:
            for index in range(5):
                spread[index].start()
        gate_slots[0] = gate_own[...]
        out_slots[0] = out_own[...]
    far = [
        push(own, far_hbm.at[index], far_send.at[index], far_recv.at[index], {"ctx": across_many(block, 2 + index)})
        for index in range(2)
    ]
    for copy in far:
        copy.start()
    def near_source(index):
        if forward:
            return rows.at[1, mine] if index else own
        return forward_rows.at[pl.ds((2 + index) * 2 * rows_of, rows_of)]

    near = [
        push(near_source(index), near_hbm.at[index, mine], near_send.at[index], near_recv.at[index], {"ctx": across(block, 1)})
        for index in range(2)
    ]
    near_share = [
        push(
            near_hbm.at[index, mine],
            near_hbm.at[index, theirs],
            near_send.at[2 + index],
            near_recv.at[2 + index],
            {"fsdp": sibling},
        )
        for index in range(2)
    ]
    near[0].start()
    if not forward:
        near[1].start()
    rows[0, mine] = own[...]
    slices = []
    if forward:
        share = features.shape[1] // 8

        def share_of(device):
            return features.at[:, pl.ds(pl.multiple_of(device * share, share), share)]

        own_slice = pltpu.make_async_copy(share_of(me), slices_hbm.at[me], extra[2])
        own_slice.start()
        slices = [
            pltpu.make_async_remote_copy(
                src_ref=share_of(across_many(me, distance)),
                dst_ref=slices_hbm.at[me],
                send_sem=extra[0].at[distance - 1],
                recv_sem=extra[1].at[distance - 1],
                device_id={"fsdp": across_many(me, distance)},
                device_id_type=pl.DeviceIdType.MESH,
            )
            for distance in range(1, 8)
        ]

    tile = min(hidden, 1024)
    wide = min(width, 1024)

    def first_stage(group):
        span = pl.ds(group * 2 * rows_of, 2 * rows_of)

        def step(index, carry):
            columns = pl.ds(pl.multiple_of(index * tile, tile), tile)
            left = rows[group]

            def back(weight):
                return lax.dot_general(
                    left, weight[columns, :], (((1,), (1,)), ((), ())), preferred_element_type=jnp.float32
                )

            if forward:
                gate, up = back(weights[0]), back(weights[1])
                value, slope = gelu_parts(gate)
                made[0][span, columns] = (value * up).astype(jnp.bfloat16)
                made[1][span, columns] = value.astype(jnp.bfloat16)
                made[2][span, columns] = (slope * up).astype(jnp.bfloat16)
            else:
                d_hidden = back(weights[0])
                made[0][span, columns] = (d_hidden * kept[1][span, columns].astype(jnp.float32)).astype(jnp.bfloat16)
                made[1][span, columns] = (d_hidden * kept[0][span, columns].astype(jnp.float32)).astype(jnp.bfloat16)
            return carry

        lax.fori_loop(0, hidden // tile, step, 0)

    def second_stage(group):
        span = pl.ds(group * 2 * rows_of, 2 * rows_of)

        def step(index, carry):
            columns = pl.ds(pl.multiple_of(index * wide, wide), wide)
            if forward:
                value = jnp.dot(made[0][span, :], weights[2][:, columns], preferred_element_type=jnp.float32)
            else:
                value = jnp.dot(made[0][span, :], weights[1][:, columns], preferred_element_type=jnp.float32)
                value = value + jnp.dot(made[1][span, :], weights[2][:, columns], preferred_element_type=jnp.float32)
            part[group, :, columns] = value.astype(jnp.bfloat16)
            return carry

        lax.fori_loop(0, width // wide, step, 0)

    def keep_out(group):
        span = pl.ds(group * 2 * rows_of, 2 * rows_of)
        write_out(rows.at[group], rows_hbm.at[span])
        for source, target in zip(made, made_hbm):
            write_out(source.at[span], target.at[span])

    def add_chip(group):
        chip_sum[group - 1] = (
            part[group, mine].astype(jnp.float32) + sib_in[group].astype(jnp.float32)
        ).astype(jnp.bfloat16)

    copies[0].wait_recv()
    loads[0].wait()
    if forward:
        loads[1].wait()
    else:
        loads[3].wait()
        loads[4].wait()
    first_stage(0)
    if forward:
        loads[2].wait()
    else:
        loads[1].wait()
        loads[2].wait()
    second_stage(0)
    copies[10].start()
    keep_out(0)
    copies[1].wait_recv()
    copies[7].start()
    copies[2].wait_recv()
    copies[5].start()
    if forward:
        near[1].start()
    copies[5].wait_recv()
    first_stage(1)
    second_stage(1)
    copies[11].start()
    keep_out(1)
    copies[3].wait_recv()
    copies[4].wait_recv()
    copies[8].start()
    copies[6].start()
    copies[11].wait_recv()
    add_chip(1)
    copies[14].start()
    copies[6].wait_recv()
    first_stage(2)
    second_stage(2)
    copies[12].start()
    keep_out(2)
    for copy in slices:
        copy.start()
    for spread in spreads:
        for index in range(1, 5):
            spread[index].wait_recv()
        for index in range(5, 11):
            spread[index].start()
    copies[7].wait_recv()
    copies[8].wait_recv()
    copies[9].start()
    copies[12].wait_recv()
    add_chip(2)
    copies[15].start()
    copies[9].wait_recv()
    first_stage(3)
    second_stage(3)
    copies[13].start()
    keep_out(3)
    copies[13].wait_recv()
    add_chip(3)
    copies[16].start()
    copies[17].start()
    for spread in spreads:
        for index in (9, 10):
            spread[index].wait_recv()
        for index in (11, 12):
            spread[index].start()
    copies[10].wait_recv()
    total[...] = part[0, mine].astype(jnp.float32) + sib_in[0].astype(jnp.float32)
    copies[16].wait_recv()
    relay_sum[0] = (chip_sum[0, low].astype(jnp.float32) + relay_in[0].astype(jnp.float32)).astype(jnp.bfloat16)
    copies[18].start()
    copies[17].wait_recv()
    relay_sum[1] = (chip_sum[1, high].astype(jnp.float32) + relay_in[1].astype(jnp.float32)).astype(jnp.bfloat16)
    copies[19].start()
    copies[14].wait_recv()
    total[low] = total[low] + last_in[2].astype(jnp.float32)
    copies[15].wait_recv()
    total[high] = total[high] + last_in[1].astype(jnp.float32)
    for index in range(2):
        near[index].wait_recv()
        near_share[index].start()
    copies[18].wait_recv()
    total[low] = total[low] + last_in[0].astype(jnp.float32)
    copies[19].wait_recv()
    total[high] = total[high] + last_in[3].astype(jnp.float32)
    if forward:
        for spread, slots, target, sems in (
            (spreads[0], gate_slots, gate_all, gate_out),
            (spreads[1], out_slots, out_all, vec_out),
        ):
            for index in (0, 5, 6, 7, 8, 11, 12):
                spread[index].wait_recv()
            size = slots.shape[1]
            for slot in range(8):
                place = pl.ds(pl.multiple_of(across_many(me, slot) * size, size), size)
                copy = pltpu.make_async_copy(slots.at[slot], target.at[place], sems.at[slot])
                copy.start()
                outs.append(copy)
            for copy in spread:
                copy.wait_send()
    for copy in copies:
        copy.wait_send()
    for copy in outs:
        copy.wait()
    for copy in far + slices:
        copy.wait()
    for index in range(2):
        near[index].wait_send()
        near_share[index].wait()
    if forward:
        own_slice.wait()


def turn(value, cosine, sine, direction=1.0):
    middle = value.shape[1] // 2
    first, second = value[:, :middle], value[:, middle:]
    sine = sine * direction
    return jnp.concatenate([first * cosine - second * sine, second * cosine + first * sine], axis=1)


def window_mask(positions, rows_of, blocks):
    query_row = lax.broadcasted_iota(jnp.int32, (rows_of, blocks * rows_of), 0)
    column = lax.broadcasted_iota(jnp.int32, (rows_of, blocks * rows_of), 1)
    behind = column // rows_of
    gap = query_row + 2 * behind * rows_of - column
    return (gap >= 0) & (gap <= positions) & (gap < WINDOW)


def norm_rows_grad(value, gain, upstream):
    factor = lax.rsqrt(jnp.mean(value * value, axis=-1, keepdims=True) + epsilon)
    unit = value * factor
    grad_gain = jnp.sum(upstream * unit, axis=0, keepdims=True)
    back = upstream * gain
    return factor * (back - unit * jnp.mean(back * unit, axis=-1, keepdims=True)), grad_gain


def greet(me, partners, block, others, work=None):
    barrier = pltpu.get_barrier_semaphore()
    for distance in partners:
        pl.semaphore_signal(
            barrier, inc=1, device_id={"fsdp": across_many(me, distance)}, device_id_type=pl.DeviceIdType.MESH
        )
    for distance in range(1, others + 1):
        pl.semaphore_signal(
            barrier,
            inc=1,
            device_id={"ctx": (block + distance) % (others + 1)},
            device_id_type=pl.DeviceIdType.MESH,
        )
    if work is not None:
        work()
    pl.semaphore_wait(barrier, len(partners) + others)


def push(source, target, send_sem, recv_sem, place):
    return pltpu.make_async_remote_copy(
        src_ref=source,
        dst_ref=target,
        send_sem=send_sem,
        recv_sem=recv_sem,
        device_id=place,
        device_id_type=pl.DeviceIdType.MESH,
    )


def spread_copies(own, slots, send_sem, recv_sem, me):
    half = own.shape[0] // 2
    low, high = pl.ds(0, half), pl.ds(half, half)
    sibling, beside, above = across(me, 1), across(me, 2), across(me, 4)
    plan = [
        (own, slots.at[1], sibling),
        (own.at[low], slots.at[2, low], beside),
        (own.at[low], slots.at[4, low], above),
        (own.at[high], slots.at[2, high], beside),
        (own.at[high], slots.at[4, high], above),
        (slots.at[2, low], slots.at[3, low], sibling),
        (slots.at[4, low], slots.at[5, low], sibling),
        (slots.at[2, high], slots.at[3, high], sibling),
        (slots.at[4, high], slots.at[5, high], sibling),
        (slots.at[2, low], slots.at[6, low], above),
        (slots.at[4, high], slots.at[6, high], beside),
        (slots.at[6, low], slots.at[7, low], sibling),
        (slots.at[6, high], slots.at[7, high], sibling),
    ]
    return [
        push(source, target, send_sem.at[index], recv_sem.at[index], {"fsdp": partner})
        for index, (source, target, partner) in enumerate(plan)
    ]


def attend_kernel(
    others, reach, source, gain_one, gain_two, gain_three, gain_four, gain_five, gain_six, head_gains, laurel_own,
    positions, cosine, sine, query_own, key_own, value_own, down_own, outward_own,
    normed, gains, linear, query_low, key_value, features, middle, attn_lin, laurel_all, inward_all, outward_all,
    gain_share, gain_slots, inward_slots, outward_slots, normed_low, attended, inward, lin_sum,
    gain_send, gain_recv, in_send, in_recv, out_send, out_recv, kv_send, kv_recv, in_copy, out_copy,
):
    rows_of, width = source.shape
    me, block = lax.axis_index("fsdp"), lax.axis_index("ctx")
    inward_own = inward_slots.at[0]
    gain_lines = gain_slots.at[0]

    def own_shares():
        start = 0
        for piece in (query_own, key_own, value_own, down_own):
            inward_slots[0, :, pl.ds(start, piece.shape[1])] = piece[...]
            start += piece.shape[1]
        inward_slots[0, :, pl.ds(start, inward_slots.shape[2] - start)] = jnp.zeros(
            (inward_slots.shape[1], inward_slots.shape[2] - start), jnp.bfloat16
        )
        gain_share[...] = jnp.zeros_like(gain_share)
        for index, gain in enumerate((gain_one, gain_two, gain_three, gain_four, gain_five, gain_six)):
            pieces = gain[...].astype(jnp.float32)
            size = pieces.shape[0] * 128
            for row in range(pieces.shape[0]):
                place = pl.ds(pl.multiple_of(me * size + row * 128, 128), 128)
                gain_share[index : index + 1, place] = pieces[row : row + 1, :]
        gain_share[6:8, 0:HEAD_SIZE] = head_gains[...].astype(jnp.float32)
        gain_share[8:16, :] = laurel_own[...].astype(jnp.float32)
        gain_slots[0] = gain_share[...].astype(jnp.bfloat16)

    greet(me, range(1, 8), block, others, own_shares)
    gain_copies = [
        push(gain_lines, gain_slots.at[distance], gain_send.at[distance - 1], gain_recv.at[distance - 1],
             {"fsdp": across_many(me, distance)})
        for distance in range(1, 8)
    ]
    for copy in gain_copies:
        copy.start()
    spread_in = spread_copies(inward_own, inward_slots, in_send, in_recv, me)
    spread_out = spread_copies(outward_own, outward_slots, out_send, out_recv, me)
    for index in range(5):
        spread_in[index].start()
    outward_slots[0] = outward_own[...]

    value = source[...].astype(jnp.float32)
    factor = lax.rsqrt(jnp.mean(value * value, axis=-1, keepdims=True) + epsilon)
    for copy in gain_copies:
        copy.wait_recv()
    lines = gain_slots[...].astype(jnp.float32)
    gains[...] = jnp.sum(lines, axis=0)[0:8]
    laurel_size = 8
    laurel_all[...] = jnp.zeros_like(laurel_all)
    for slot in range(8):
        device = across_many(me, slot)
        laurel_all[pl.ds(pl.multiple_of(device * laurel_size, laurel_size), laurel_size), :] = lines[slot, 8:16]
    value = value * factor * gains[0:1, :]
    normed[...] = value
    normed_low[...] = value.astype(jnp.bfloat16)
    share = width // 8
    for index in range(8):
        features[:, pl.ds(2 * index * share, share)] = normed_low[:, pl.ds(index * share, share)]

    depth = inward_own.shape[0]
    head_rows = width // 8
    written = []

    def add_inward(slot):
        device = across_many(me, slot)
        part = normed_low[:, pl.ds(pl.multiple_of(device * depth, depth), depth)]
        for start in range(0, inward.shape[1], 640):
            span = pl.ds(start, 640)
            product = jnp.dot(part, inward_slots[slot, :, span], preferred_element_type=jnp.float32)
            inward[:, span] = product if slot == 0 else inward[:, span] + product
        copy = pltpu.make_async_copy(
            inward_slots.at[slot], inward_all.at[pl.ds(pl.multiple_of(device * depth, depth), depth)], in_copy.at[slot]
        )
        copy.start()
        written.append(copy)

    def add_outward(slot):
        device = across_many(me, slot)
        part = attended[:, pl.ds(pl.multiple_of(device * head_rows, head_rows), head_rows)]
        for start in range(0, width, 512):
            span = pl.ds(start, 512)
            product = jnp.dot(part, outward_slots[slot, pl.ds(0, head_rows), span], preferred_element_type=jnp.float32)
            lin_sum[:, span] = product if slot == 0 else lin_sum[:, span] + product

    def write_outward(slot):
        device = across_many(me, slot)
        rows = pl.ds(pl.multiple_of(device * head_rows, head_rows), head_rows)
        copy = pltpu.make_async_copy(outward_slots.at[slot], outward_all.at[rows], out_copy.at[slot])
        copy.start()
        written.append(copy)

    add_inward(0)
    spread_in[0].wait_recv()
    add_inward(1)
    spread_in[1].wait_recv()
    spread_in[9].start()
    spread_in[5].start()
    spread_in[2].wait_recv()
    spread_in[6].start()
    spread_in[3].wait_recv()
    spread_in[7].start()
    spread_in[4].wait_recv()
    spread_in[10].start()
    spread_in[8].start()
    add_inward(2)
    add_inward(4)
    spread_in[5].wait_recv()
    spread_in[7].wait_recv()
    add_inward(3)
    spread_in[6].wait_recv()
    spread_in[8].wait_recv()
    add_inward(5)
    spread_in[9].wait_recv()
    spread_in[11].start()
    spread_in[10].wait_recv()
    spread_in[12].start()
    for index in range(5):
        spread_out[index].start()
    add_inward(6)
    spread_in[11].wait_recv()
    spread_in[12].wait_recv()
    add_inward(7)

    query_width, key_width = QUERY_HEADS * HEAD_SIZE, KEY_VALUE_HEADS * HEAD_SIZE
    own_rows = pl.ds(0, rows_of)

    def head(start, gain):
        lane = inward[:, pl.ds(start, HEAD_SIZE)]
        scale = lax.rsqrt(jnp.mean(lane * lane, axis=-1, keepdims=True) + epsilon)
        return turn(lane * scale * gain, cosine[...], sine[...]).astype(jnp.bfloat16)

    for index in range(KEY_VALUE_HEADS):
        key_value[own_rows, pl.ds(index * HEAD_SIZE, HEAD_SIZE)] = head(
            query_width + index * HEAD_SIZE, gains[7:8, 0:HEAD_SIZE]
        )
    key_value[own_rows, pl.ds(key_width, key_width)] = inward[:, pl.ds(query_width + key_width, key_width)].astype(
        jnp.bfloat16
    )
    for distance in range(1, reach + 1):
        copy = push(
            key_value.at[own_rows],
            key_value.at[pl.ds(distance * rows_of, rows_of)],
            kv_send.at[distance - 1],
            kv_recv.at[distance - 1],
            {"ctx": (block + distance) % (others + 1)},
        )

        @pl.when(block + distance <= others)
        def _():
            copy.start()

        @pl.when(block < distance)
        def _():
            key_value[pl.ds(distance * rows_of, rows_of), :] = jnp.zeros((rows_of, 2 * key_width), jnp.bfloat16)

    for index in range(QUERY_HEADS):
        query_low[:, pl.ds(index * HEAD_SIZE, HEAD_SIZE)] = head(index * HEAD_SIZE, gains[6:7, 0:HEAD_SIZE])
    linear[...] = inward[:, pl.ds(0, query_width + key_width)]
    middle[...] = inward[:, pl.ds(query_width + 2 * key_width, middle.shape[1])].astype(jnp.bfloat16)

    spread_out[0].wait_recv()
    spread_out[1].wait_recv()
    spread_out[9].start()
    spread_out[5].start()
    spread_out[2].wait_recv()
    spread_out[6].start()
    for distance in range(1, reach + 1):
        copy = push(
            key_value.at[own_rows],
            key_value.at[pl.ds(distance * rows_of, rows_of)],
            kv_send.at[distance - 1],
            kv_recv.at[distance - 1],
            {"ctx": (block + distance) % (others + 1)},
        )

        @pl.when(block >= distance)
        def _():
            copy.wait_recv()

    allowed = window_mask(positions[...], rows_of, reach + 1)
    per_group = QUERY_HEADS // KEY_VALUE_HEADS
    for index in range(QUERY_HEADS):
        group = index // per_group
        columns = pl.ds(index * HEAD_SIZE, HEAD_SIZE)
        scores = product_back(query_low[:, columns], key_value[:, pl.ds(group * HEAD_SIZE, HEAD_SIZE)])
        scores = jnp.where(allowed, scores * HEAD_SIZE ** (-0.5), -1e30)
        grown = jnp.exp(scores - jnp.max(scores, axis=-1, keepdims=True))
        soft = (grown / jnp.sum(grown, axis=-1, keepdims=True)).astype(jnp.bfloat16)
        attended[:, columns] = jnp.dot(
            soft, key_value[:, pl.ds(key_width + group * HEAD_SIZE, HEAD_SIZE)], preferred_element_type=jnp.float32
        ).astype(jnp.bfloat16)

    for index in range(8):
        features[:, pl.ds((2 * index + 1) * share, share)] = attended[:, pl.ds(index * share, share)]
    add_outward(0)
    add_outward(1)
    write_outward(0)
    write_outward(1)
    spread_out[3].wait_recv()
    spread_out[7].start()
    spread_out[4].wait_recv()
    spread_out[10].start()
    spread_out[8].start()
    add_outward(2)
    add_outward(4)
    spread_out[5].wait_recv()
    spread_out[7].wait_recv()
    add_outward(3)
    spread_out[6].wait_recv()
    spread_out[8].wait_recv()
    add_outward(5)
    for slot in range(2, 6):
        write_outward(slot)
    spread_out[9].wait_recv()
    spread_out[11].start()
    spread_out[10].wait_recv()
    spread_out[12].start()
    add_outward(6)
    write_outward(6)
    spread_out[11].wait_recv()
    spread_out[12].wait_recv()
    add_outward(7)
    write_outward(7)
    attn_lin[...] = lin_sum[...]
    for copy in gain_copies + spread_in + spread_out:
        copy.wait_send()
    for copy in written:
        copy.wait()
    for distance in range(1, reach + 1):
        copy = push(
            key_value.at[own_rows],
            key_value.at[pl.ds(distance * rows_of, rows_of)],
            kv_send.at[distance - 1],
            kv_recv.at[distance - 1],
            {"ctx": (block + distance) % (others + 1)},
        )

        @pl.when(block + distance <= others)
        def _():
            copy.wait_send()


def attend_call(reach, source, gains, head_gains, laurel_own, positions, cosine, sine, inward_own, outward_own):
    rows_of, width = source.shape
    others = lax.axis_size("ctx") - 1
    low, full = jnp.bfloat16, jnp.float32
    hbm = pl.BlockSpec(memory_space=pl.ANY)
    vmem = pl.BlockSpec(memory_space=pltpu.VMEM)
    dma = pltpu.SemaphoreType.DMA
    depth = inward_own[0].shape[0]
    columns = sum(piece.shape[1] for piece in inward_own)
    columns += -columns % 128
    gain_shape = (16, width)
    query_width, key_width = QUERY_HEADS * HEAD_SIZE, KEY_VALUE_HEADS * HEAD_SIZE
    tail = columns - query_width - 2 * key_width
    shapes = [
        jax.ShapeDtypeStruct((rows_of, width), full),
        jax.ShapeDtypeStruct((8, width), full),
        jax.ShapeDtypeStruct((rows_of, query_width + key_width), full),
        jax.ShapeDtypeStruct((rows_of, query_width), low),
        jax.ShapeDtypeStruct(((reach + 1) * rows_of, 2 * key_width), low),
        jax.ShapeDtypeStruct((rows_of, 2 * width), low),
        jax.ShapeDtypeStruct((rows_of, tail), low),
        jax.ShapeDtypeStruct((rows_of, width), full),
        jax.ShapeDtypeStruct((tail, width), full),
        jax.ShapeDtypeStruct((8 * depth, columns), low),
        jax.ShapeDtypeStruct((8 * outward_own.shape[0], width), low),
    ]
    return pl.pallas_call(
        functools.partial(attend_kernel, others, reach),
        out_shape=shapes,
        in_specs=[vmem] * 17,
        out_specs=[vmem] * 9 + [hbm] * 2,
        scratch_shapes=[
            pltpu.VMEM(gain_shape, full),
            pltpu.VMEM((8, *gain_shape), low),
            pltpu.VMEM((8, depth, columns), low),
            pltpu.VMEM((8, *outward_own.shape), low),
            pltpu.VMEM((rows_of, width), low),
            pltpu.VMEM((rows_of, query_width), low),
            pltpu.VMEM((rows_of, columns), full),
            pltpu.VMEM((rows_of, width), full),
            dma((7,)),
            dma((7,)),
            dma((13,)),
            dma((13,)),
            dma((13,)),
            dma((13,)),
            dma((max(reach, 1),)),
            dma((max(reach, 1),)),
            dma((8,)),
            dma((8,)),
        ],
        compiler_params=pltpu.CompilerParams(collective_id=3, has_side_effects=True, vmem_limit_bytes=56 * 2**20),
        cost_estimate=pl.CostEstimate(
            flops=60 * rows_of * width * columns, bytes_accessed=20 * depth * columns, transcendentals=0
        ),
        name="attend_forward",
    )(source, *gains, head_gains, laurel_own, positions, cosine, sine, *inward_own, outward_own)


def turn_norm_grad(upstream, linear, gain, cosine, sine):
    scale = lax.rsqrt(jnp.mean(linear * linear, axis=-1, keepdims=True) + epsilon)
    unit = linear * scale
    back = turn(upstream, cosine, sine, -1.0)
    grad_gain = jnp.sum(back * unit, axis=0, keepdims=True)
    back = back * gain
    return scale * (back - unit * jnp.mean(back * unit, axis=-1, keepdims=True)), grad_gain


def attend_back_kernel(
    others, reach, d_ffn_in, mixed, d_residual, laurel_lin, attn_lin, laurel, gain_part,
    query_low, key_value, linear, gains, positions, cosine, sine, middle, features,
    source, residual, d_vector, gated_value, d_back, outward_all, inward_all, d_rows,
    d_source, grad_wide, grad_small, near_hbm,
    d_lin, d_half, d_laurel, d_middle, gain_rows,
    outward, inward, d_attended, d_key_value, parcel, arrived, d_query, d_rest, lin_slots, query_slots, rest_slots,
    ordered, d_normed, gain_parcel, gain_arrived, laurel_arrived, load_sem, lin_send, lin_recv, query_send, query_recv, rest_send, rest_recv, kv_send, kv_recv, gain_send, gain_recv, laurel_send, laurel_recv, near_send, near_recv,
    gate_in, gate_sum, gate_arrived, out_in, out_sum, out_arrived, pair_send, pair_recv, chip_send, chip_recv,
    gate_parts, out_parts, laurel_rows,
):
    rows_of, width = source.shape
    me, block = lax.axis_index("fsdp"), lax.axis_index("ctx")
    query_width, key_width = QUERY_HEADS * HEAD_SIZE, KEY_VALUE_HEADS * HEAD_SIZE
    per_group = QUERY_HEADS // KEY_VALUE_HEADS
    depth = width // 8
    loads = [
        pltpu.make_async_copy(outward_all.at[pl.ds(index * depth, depth)], outward.at[index % 2], load_sem.at[index])
        for index in range(8)
    ]
    loads.append(pltpu.make_async_copy(inward_all, inward, load_sem.at[8]))
    for index in (0, 1, 8):
        loads[index].start()

    def before_attention():
        d_mixed, grad_before = norm_rows_grad(mixed[...], gains[3:4, :], d_ffn_in[...])
        d_half[...] = (d_residual[...] + d_mixed) * inv_root
        d_branch, grad_laurel_gain = norm_rows_grad(laurel_lin[...], gains[2:3, :], d_half[...])
        d_laurel[...] = d_branch.astype(jnp.bfloat16)
        d_middle[...] = product_back(d_laurel[...], laurel[...].astype(jnp.bfloat16)).astype(jnp.bfloat16)
        d_branch, grad_attention = norm_rows_grad(attn_lin[...], gains[1:2, :], d_half[...])
        d_lin[...] = d_branch.astype(jnp.bfloat16)
        gain_rows[...] = gain_part[...]
        gain_rows[1:2, :] = grad_attention
        gain_rows[2:3, :] = grad_laurel_gain
        gain_rows[3:4, :] = grad_before

    greet(me, range(1, 8), block, others, before_attention)
    mine, theirs = pl.ds(0, rows_of), pl.ds(rows_of, rows_of)
    near = [
        push(
            d_rows.at[pl.ds(group * 2 * rows_of, rows_of)],
            near_hbm.at[group, mine],
            near_send.at[group],
            near_recv.at[group],
            {"ctx": across(block, 1)},
        )
        for group in range(4)
    ]
    near_share = [
        push(
            near_hbm.at[group, mine],
            near_hbm.at[group, theirs],
            near_send.at[4 + group],
            near_recv.at[4 + group],
            {"fsdp": across(me, 1)},
        )
        for group in range(4)
    ]
    for copy in near[:2]:
        copy.start()
    vector_parts = ((gate_parts, gate_in, gate_sum, gate_arrived), (out_parts, out_in, out_sum, out_arrived))
    chips = (0, 2, 4, 6)
    pair_copies = []
    chip_copies = []
    for kind, (parts, pair_in, pair_sum, arrived_parts) in enumerate(vector_parts):
        for index, chip in enumerate(chips):
            place = 4 * kind + index
            pair_copies.append(
                push(
                    parts.at[across_many(me, chip + 1)],
                    pair_in.at[index],
                    pair_send.at[place],
                    pair_recv.at[place],
                    {"fsdp": across(me, 1)},
                )
            )
            if chip:
                place = 3 * kind + index - 1
                chip_copies.append(
                    push(
                        pair_sum.at[index - 1],
                        arrived_parts.at[index - 1],
                        chip_send.at[place],
                        chip_recv.at[place],
                        {"fsdp": across_many(me, chip)},
                    )
                )
    spread_lin = spread_copies(d_lin, lin_slots, lin_send, lin_recv, me)
    spread_query = spread_copies(d_query, query_slots, query_send, query_recv, me)
    spread_rest = spread_copies(d_rest, rest_slots, rest_send, rest_recv, me)
    for index in range(5):
        spread_lin[index].start()
    lin_slots[0] = d_lin[...]
    for index in range(8):
        gate_parts[index] = product_rows(residual[:, pl.ds(index * depth, depth)], d_vector[...]).astype(jnp.bfloat16)
    out_parts[...] = product_rows(gated_value[...], d_back[...]).reshape(out_parts.shape).astype(jnp.bfloat16)
    laurel_rows[...] = product_rows(middle[...], d_laurel[...])[0 : 8 * laurel_rows.shape[1]].reshape(laurel_rows.shape)
    for copy in pair_copies:
        copy.start()
    laurel_copies = [
        push(
            laurel_rows.at[across_many(me, distance)],
            laurel_arrived.at[distance],
            laurel_send.at[distance - 1],
            laurel_recv.at[distance - 1],
            {"fsdp": across_many(me, distance)},
        )
        for distance in range(1, 8)
    ]
    laurel_arrived[0] = laurel_rows[me]
    for slot in range(8):
        device = across_many(me, slot)
        ordered[pl.ds(slot * rows_of, rows_of), :] = features[
            pl.ds(pl.multiple_of(device * rows_of, rows_of), rows_of), :
        ]
    for index in range(8):
        loads[index].wait()
        d_attended[:, pl.ds(index * depth, depth)] = product_back(d_lin[...], outward[index % 2]).astype(jnp.bfloat16)
        if index + 2 < 8:
            loads[index + 2].start()

    allowed = window_mask(positions[...], rows_of, reach + 1)
    scale = HEAD_SIZE ** (-0.5)

    def one_head(index):
        group = index // per_group
        columns = pl.ds(index * HEAD_SIZE, HEAD_SIZE)
        keys = pl.ds(group * HEAD_SIZE, HEAD_SIZE)
        values = pl.ds(key_width + group * HEAD_SIZE, HEAD_SIZE)
        scores = product_back(query_low[:, columns], key_value[:, keys])
        scores = jnp.where(allowed, scores * scale, -1e30)
        grown = jnp.exp(scores - jnp.max(scores, axis=-1, keepdims=True))
        soft = grown / jnp.sum(grown, axis=-1, keepdims=True)
        d_soft = product_back(d_attended[:, columns], key_value[:, values])
        d_scores = (soft * (d_soft - jnp.sum(soft * d_soft, axis=-1, keepdims=True))).astype(jnp.bfloat16)
        upstream = scale * jnp.dot(d_scores, key_value[:, keys], preferred_element_type=jnp.float32)
        d_key = scale * product_rows(d_scores, query_low[:, columns])
        d_value = product_rows(soft.astype(jnp.bfloat16), d_attended[:, columns])
        if index % per_group == 0:
            d_key_value[:, keys] = d_key
            d_key_value[:, values] = d_value
        else:
            d_key_value[:, keys] += d_key
            d_key_value[:, values] += d_value
        d_head, grad_gain = turn_norm_grad(upstream, linear[:, columns], gains[6:7, 0:HEAD_SIZE], cosine[...], sine[...])
        d_query[:, columns] = d_head.astype(jnp.bfloat16)
        return grad_gain

    query_gain = one_head(0)
    for index in range(1, per_group):
        query_gain = query_gain + one_head(index)
    spread_lin[0].wait_recv()
    spread_lin[1].wait_recv()
    spread_lin[9].start()
    spread_lin[5].start()
    spread_lin[2].wait_recv()
    spread_lin[6].start()
    for index in range(per_group, QUERY_HEADS):
        query_gain = query_gain + one_head(index)
    parcel[...] = d_key_value[pl.ds(rows_of, reach * rows_of), :].astype(jnp.bfloat16)

    def return_copy(distance):
        span = pl.ds((distance - 1) * rows_of, rows_of)
        return push(
            parcel.at[span],
            arrived.at[span],
            kv_send.at[distance - 1],
            kv_recv.at[distance - 1],
            {"ctx": (block + others + 1 - distance) % (others + 1)},
        )

    for distance in range(1, reach + 1):
        copy = return_copy(distance)

        @pl.when(block >= distance)
        def _():
            copy.start()

        @pl.when(block + distance > others)
        def _():
            arrived[pl.ds((distance - 1) * rows_of, rows_of), :] = jnp.zeros((rows_of, 2 * key_width), jnp.bfloat16)

    for copy in near[2:]:
        copy.start()
    spread_lin[3].wait_recv()
    spread_lin[7].start()
    spread_lin[4].wait_recv()
    spread_lin[10].start()
    spread_lin[8].start()
    for index in range(5):
        spread_query[index].start()
    for copy in pair_copies:
        copy.wait_recv()
    for parts, pair_in, pair_sum, arrived_parts in vector_parts:
        for index, chip in enumerate(chips):
            if chip:
                pair_sum[index - 1] = (
                    parts[across_many(me, chip)].astype(jnp.float32) + pair_in[index].astype(jnp.float32)
                ).astype(jnp.bfloat16)
    for copy in chip_copies:
        copy.start()
    query_slots[0] = d_query[...]
    loads[8].wait()
    d_normed[...] = product_back(d_query[...], inward[:, pl.ds(0, query_width)])
    spread_lin[9].wait_recv()
    spread_lin[11].start()
    spread_lin[10].wait_recv()
    spread_lin[12].start()
    spread_query[0].wait_recv()
    spread_query[1].wait_recv()
    spread_query[9].start()
    spread_query[5].start()
    spread_query[2].wait_recv()
    spread_query[6].start()
    for index in (5, 6, 7, 8, 11, 12):
        spread_lin[index].wait_recv()
    grad_wide[:, pl.ds(inward.shape[1], width)] = product_rows(
        ordered[:, pl.ds(depth, depth)], lin_slots[...].reshape(8 * rows_of, width)
    ).astype(jnp.bfloat16)

    for distance in range(1, reach + 1):
        copy = return_copy(distance)

        @pl.when(block + distance <= others)
        def _():
            copy.wait_recv()

    total = d_key_value[pl.ds(0, rows_of), :]
    for distance in range(1, reach + 1):
        total = total + arrived[pl.ds((distance - 1) * rows_of, rows_of), :].astype(jnp.float32)
    for index in range(KEY_VALUE_HEADS):
        columns = pl.ds(index * HEAD_SIZE, HEAD_SIZE)
        d_head, grad_gain = turn_norm_grad(
            total[:, index * HEAD_SIZE : (index + 1) * HEAD_SIZE],
            linear[:, pl.ds(query_width + index * HEAD_SIZE, HEAD_SIZE)],
            gains[7:8, 0:HEAD_SIZE],
            cosine[...],
            sine[...],
        )
        d_rest[:, columns] = d_head.astype(jnp.bfloat16)
        key_gain = grad_gain if index == 0 else key_gain + grad_gain
    d_rest[:, pl.ds(key_width, key_width)] = total[:, key_width:].astype(jnp.bfloat16)
    d_rest[:, pl.ds(2 * key_width, d_middle.shape[1])] = d_middle[...]
    spread_query[3].wait_recv()
    spread_query[7].start()
    spread_query[4].wait_recv()
    spread_query[10].start()
    spread_query[8].start()
    for index in range(5):
        spread_rest[index].start()
    rest_slots[0] = d_rest[...]
    rest_width = d_rest.shape[1]
    d_normed[...] += product_back(d_rest[...], inward[:, pl.ds(query_width, rest_width)])
    value = source[...].astype(jnp.float32)
    factor = lax.rsqrt(jnp.mean(value * value, axis=-1, keepdims=True) + epsilon)
    unit = value * factor
    upstream = d_half[...] + d_normed[...]
    for index in range(8):
        columns = slice(index * depth, (index + 1) * depth)
        gain_parcel[index, 0:8, :] = gain_rows[0:8, columns]
        gain_parcel[index, 0:1, :] = jnp.sum(upstream[:, columns] * unit[:, columns], axis=0, keepdims=True)
        gain_parcel[index, 6:7, :] = query_gain
        gain_parcel[index, 7:8, :] = key_gain
    gain_copies = [
        push(
            gain_parcel.at[across_many(me, distance)],
            gain_arrived.at[distance],
            gain_send.at[distance - 1],
            gain_recv.at[distance - 1],
            {"fsdp": across_many(me, distance)},
        )
        for distance in range(1, 8)
    ]
    for copy in gain_copies + laurel_copies:
        copy.start()
    gain_arrived[0] = gain_parcel[me]
    upstream = upstream * gains[0:1, :]
    d_source[...] = d_half[...] + factor * (upstream - unit * jnp.mean(upstream * unit, axis=-1, keepdims=True))
    spread_rest[0].wait_recv()
    spread_rest[1].wait_recv()
    spread_rest[9].start()
    spread_rest[5].start()
    spread_rest[2].wait_recv()
    spread_rest[6].start()
    spread_query[9].wait_recv()
    spread_query[11].start()
    spread_query[10].wait_recv()
    spread_query[12].start()
    spread_rest[3].wait_recv()
    spread_rest[7].start()
    spread_rest[4].wait_recv()
    spread_rest[10].start()
    spread_rest[8].start()
    for index in (5, 6, 7, 8, 11, 12):
        spread_query[index].wait_recv()
    grad_wide[:, pl.ds(0, query_width)] = product_rows(
        ordered[:, pl.ds(0, depth)], query_slots[...].reshape(8 * rows_of, query_width)
    ).astype(jnp.bfloat16)
    spread_rest[9].wait_recv()
    spread_rest[11].start()
    spread_rest[10].wait_recv()
    spread_rest[12].start()
    for index in (5, 6, 7, 8, 11, 12):
        spread_rest[index].wait_recv()
    grad_wide[:, pl.ds(query_width, rest_width)] = product_rows(
        ordered[:, pl.ds(0, depth)], rest_slots[...].reshape(8 * rows_of, rest_width)
    ).astype(jnp.bfloat16)
    for copy, share in zip(near, near_share):
        copy.wait_recv()
        share.start()
    for copy in gain_copies + laurel_copies + chip_copies:
        copy.wait_recv()
    totals = []
    for parts, pair_in, pair_sum, arrived_parts in vector_parts:
        total = parts[me].astype(jnp.float32) + pair_in[0].astype(jnp.float32)
        for index in range(3):
            total = total + arrived_parts[index].astype(jnp.float32)
        totals.append(total.astype(jnp.bfloat16))
    grad_wide[:, pl.ds(inward.shape[1] + width, totals[0].shape[1])] = totals[0]
    laurel_size = laurel_rows.shape[1]
    tail = jnp.concatenate(
        [jnp.sum(laurel_arrived[...], axis=0), jnp.pad(jnp.sum(gain_arrived[...], axis=0), ((0, 0), (0, width - depth)))],
        axis=0,
    )
    out_size = totals[1].shape[0]
    grad_small[pl.ds(0, out_size), :] = totals[1]
    grad_small[pl.ds(out_size, laurel_size + 8), :] = tail.astype(jnp.bfloat16)
    for copy in near_share:
        copy.wait_recv()
    for copy in (
        spread_lin + spread_query + spread_rest + gain_copies + laurel_copies + near + near_share + pair_copies + chip_copies
    ):
        copy.wait_send()
    for distance in range(1, reach + 1):
        copy = return_copy(distance)

        @pl.when(block >= distance)
        def _():
            copy.wait_send()


def attend_back_call(
    reach, d_ffn_in, mixed, d_residual, laurel_lin, attn_lin, laurel, gain_part,
    query_low, key_value, linear, gains, positions, cosine, sine, middle, features,
    source, residual, d_vector, gated_value, d_back, outward_all, inward_all, d_rows,
):
    rows_of, width = source.shape
    others = lax.axis_size("ctx") - 1
    low, full = jnp.bfloat16, jnp.float32
    hbm = pl.BlockSpec(memory_space=pl.ANY)
    vmem = pl.BlockSpec(memory_space=pltpu.VMEM)
    dma = pltpu.SemaphoreType.DMA
    columns = inward_all.shape[1]
    query_width, key_width = QUERY_HEADS * HEAD_SIZE, KEY_VALUE_HEADS * HEAD_SIZE
    rest_width = columns - query_width
    depth = width // 8
    vector_width = d_vector.shape[1]
    part_shapes = ((depth, vector_width), (vector_width // 8, width))
    shapes = [
        jax.ShapeDtypeStruct((rows_of, width), full),
        jax.ShapeDtypeStruct((depth, columns + width + vector_width), low),
        jax.ShapeDtypeStruct((vector_width // 8 + 16, width), low),
        jax.ShapeDtypeStruct((4, 2 * rows_of, width), low),
    ]
    spans = max(reach, 1)
    return pl.pallas_call(
        functools.partial(attend_back_kernel, others, reach),
        out_shape=shapes,
        in_specs=[vmem] * 21 + [hbm] * 3,
        out_specs=[vmem] * 3 + [hbm],
        scratch_shapes=[
            pltpu.VMEM((rows_of, width), low),
            pltpu.VMEM((rows_of, width), full),
            pltpu.VMEM((rows_of, width), low),
            pltpu.VMEM(middle.shape, low),
            pltpu.VMEM((8, width), full),
            pltpu.VMEM((2, depth, width), low),
            pltpu.VMEM((width, columns), low),
            pltpu.VMEM((rows_of, query_width), low),
            pltpu.VMEM(((reach + 1) * rows_of, 2 * key_width), full),
            pltpu.VMEM((spans * rows_of, 2 * key_width), low),
            pltpu.VMEM((spans * rows_of, 2 * key_width), low),
            pltpu.VMEM((rows_of, query_width), low),
            pltpu.VMEM((rows_of, rest_width), low),
            pltpu.VMEM((8, rows_of, width), low),
            pltpu.VMEM((8, rows_of, query_width), low),
            pltpu.VMEM((8, rows_of, rest_width), low),
            pltpu.VMEM((8 * rows_of, 2 * depth), low),
            pltpu.VMEM((rows_of, width), full),
            pltpu.VMEM((8, 8, depth), full),
            pltpu.VMEM((8, 8, depth), full),
            pltpu.VMEM((8, 8, width), full),
            dma((9,)),
            dma((13,)),
            dma((13,)),
            dma((13,)),
            dma((13,)),
            dma((13,)),
            dma((13,)),
            dma((spans,)),
            dma((spans,)),
            dma((7,)),
            dma((7,)),
            dma((7,)),
            dma((7,)),
            dma((8,)),
            dma((8,)),
        ]
        + [
            pltpu.VMEM((count, *shape), low)
            for shape in part_shapes
            for count in (4, 3, 3)
        ]
        + [dma((8,)), dma((8,)), dma((6,)), dma((6,))]
        + [pltpu.VMEM((8, *shape), low) for shape in part_shapes]
        + [pltpu.VMEM((8, 8, width), full)],
        compiler_params=pltpu.CompilerParams(collective_id=4, has_side_effects=True, vmem_limit_bytes=60 * 2**20),
        cost_estimate=pl.CostEstimate(
            flops=40 * rows_of * width * columns, bytes_accessed=6 * width * columns, transcendentals=0
        ),
        name="attend_backward",
    )(
        d_ffn_in, mixed, d_residual, laurel_lin, attn_lin, laurel, gain_part,
        query_low, key_value, linear, gains, positions, cosine, sine, middle, features,
        source, residual, d_vector, gated_value, d_back, outward_all, inward_all, d_rows,
    )


def feed_call(forward, prelude, weights, kept=(), features=None, forward_rows=None, vectors=()):
    rows_of, width = prelude[0].shape
    hidden = weights[0].shape[0]
    all_rows = 8 * rows_of
    others = lax.axis_size("ctx") - 1
    low, full = jnp.bfloat16, jnp.float32
    count_made = 3 if forward else 2
    hbm = pl.BlockSpec(memory_space=pl.ANY)
    vmem = pl.BlockSpec(memory_space=pltpu.VMEM)
    half = rows_of // 2
    dma = pltpu.SemaphoreType.DMA

    def shape(columns, kind, rows=rows_of):
        return jax.ShapeDtypeStruct((rows, columns), kind)

    operands = (*prelude, *weights, *kept)
    operand_specs = [vmem] * len(prelude) + [hbm] * (3 + len(kept))
    shapes = [shape(width, full)]
    extra = []
    if forward:
        shapes += [shape(width, full)] * 2
        operands += (features, *vectors)
        operand_specs += [vmem] * 3
        extra = (
            [dma((7,)), dma((7,)), dma]
            + [pltpu.VMEM((8, *value.shape), low) for value in vectors]
            + [dma((13,))] * 4
            + [dma((8,))] * 2
        )
    else:
        vector_width = prelude[5].shape[1]
        shapes += [shape(width, low), shape(vector_width, full), shape(width, low), shape(vector_width, low)]
        shapes += [shape(vector_width, low), shape(width, low), shape(width, full), shape(width, full, 8)]
        operands += (forward_rows,)
        operand_specs += [hbm]
    count_vmem = len(shapes)
    shapes += [
        shape(width, low, all_rows),
        jax.ShapeDtypeStruct((2, rows_of, width), low),
        jax.ShapeDtypeStruct((2, 2 * rows_of, width), low),
    ]
    if forward:
        shapes += [jax.ShapeDtypeStruct((8, rows_of, features.shape[1] // 8), low)]
        shapes += [shape(value.shape[1], low, 8 * value.shape[0]) for value in vectors]
    shapes += [shape(hidden, low, all_rows)] * count_made
    return pl.pallas_call(
        functools.partial(feed_kernel, forward, rows_of, others),
        out_shape=shapes,
        in_specs=operand_specs,
        out_specs=[vmem] * count_vmem + [hbm] * (len(shapes) - count_vmem),
        scratch_shapes=[pltpu.VMEM((hidden, width), low)] * 3
        + [pltpu.VMEM((all_rows, hidden), low)] * (len(kept) + count_made)
        + [
            pltpu.VMEM((rows_of, width), low),
            pltpu.VMEM((4, 2 * rows_of, width), low),
            pltpu.VMEM((4, 2 * rows_of, width), low),
            pltpu.VMEM((4, rows_of, width), low),
            pltpu.VMEM((3, rows_of, width), low),
            pltpu.VMEM((2, half, width), low),
            pltpu.VMEM((2, half, width), low),
            pltpu.VMEM((4, half, width), low),
            dma((20,)),
            dma((20,)),
            dma((3 + len(kept),)),
            dma((4 * (1 + count_made),)),
            dma((2,)),
            dma((2,)),
            dma((4,)),
            dma((4,)),
        ]
        + extra,
        compiler_params=pltpu.CompilerParams(
            collective_id=1 if forward else 2,
            has_side_effects=True,
            vmem_limit_bytes=58 * 2**20,
        ),
        cost_estimate=pl.CostEstimate(
            flops=40 * all_rows * hidden * width // 2,
            bytes_accessed=6 * hidden * width + 8 * all_rows * width,
            transcendentals=0,
        ),
        name="feed_forward" if forward else "feed_backward",
    )(*operands)


def weight_grad_kernel(
    own_steps, near_steps, gate, up, down, rows, d_rows, hidden, d_gate, d_up,
    rows_near, rows_next, d_rows_near, rows_far, d_rows_far,
    grad_gate, grad_up, grad_down, hidden_tile, d_gate_tile, d_up_tile,
):
    step = pl.program_id(1)
    tile = 512
    hidden_size = gate.shape[0]
    chunk = rows.shape[1]

    @pl.when(step == 0)
    def _():
        grad_gate[...] = jnp.zeros_like(grad_gate)
        grad_up[...] = jnp.zeros_like(grad_up)
        grad_down[...] = jnp.zeros_like(grad_down)

    def accumulate(rows, d_rows):
        def body(index, carry):
            columns = pl.ds(pl.multiple_of(index * chunk, chunk), chunk)
            right, d_right = rows[:, columns], d_rows[:, columns]
            grad_gate[:, columns] += matrix_product(d_gate_tile[...], right)
            grad_up[:, columns] += matrix_product(d_up_tile[...], right)
            grad_down[:, columns] += matrix_product(hidden_tile[...], d_right)
            return carry
        lax.fori_loop(0, rows.shape[1] // chunk, body, 0)

    @pl.when(step < own_steps)
    def _():
        hidden_tile[...] = hidden[...].T
        d_gate_tile[...] = d_gate[...].T
        d_up_tile[...] = d_up[...].T
        accumulate(rows, d_rows)

    def other_rows(rows, d_rows):
        def body(index, carry):
            span = pl.ds(pl.multiple_of(index * tile, tile), tile)
            gate_value = product_back(gate[span, :], rows[...])
            up_value = product_back(up[span, :], rows[...])
            d_hidden = product_back(down[span, :], d_rows[...])
            value, slope = gelu_parts(gate_value)
            hidden_tile[span, :] = (value * up_value).astype(jnp.bfloat16)
            d_gate_tile[span, :] = (d_hidden * up_value * slope).astype(jnp.bfloat16)
            d_up_tile[span, :] = (d_hidden * value).astype(jnp.bfloat16)
            return carry

        lax.fori_loop(0, hidden_size // tile, body, 0)
        accumulate(rows, d_rows)

    @pl.when((step >= own_steps) & (step < own_steps + near_steps // 2))
    def _():
        other_rows(rows_near, d_rows_near)

    @pl.when((step >= own_steps + near_steps // 2) & (step < own_steps + near_steps))
    def _():
        other_rows(rows_next, d_rows_near)

    @pl.when(step >= own_steps + near_steps)
    def _():
        other_rows(rows_far, d_rows_far)


def weight_grad_call(
    gate, up, down, rows, d_rows, hidden, d_gate, d_up, rows_near, rows_next, d_rows_near, rows_far, d_rows_far,
    hid=1024, tok=256,
):
    size, width = gate.shape
    hid = min(hid, size)
    own_steps, near_steps, far_steps = [value.shape[0] // tok for value in (rows, d_rows_near, rows_far)]
    low = jnp.bfloat16

    def stream(first, steps, columns, across):
        def place(h, s):
            return jnp.clip(s - first, 0, steps - 1), h if across else 0

        return pl.BlockSpec((tok, columns), place)

    weight = pl.BlockSpec((hid, width), lambda h, s: (h, 0))
    own = stream(0, own_steps, width, False)
    own_mid = stream(0, own_steps, hid, True)
    near_one = stream(own_steps, near_steps // 2, width, False)
    near_two = stream(own_steps + near_steps // 2, near_steps // 2, width, False)
    near = stream(own_steps, near_steps, width, False)
    far = stream(own_steps + near_steps, far_steps, width, False)
    flops = 6 * size * width * (rows.shape[0] + 2 * d_rows_near.shape[0] + 2 * rows_far.shape[0])
    return pl.pallas_call(
        functools.partial(weight_grad_kernel, own_steps, near_steps),
        grid=(size // hid, own_steps + near_steps + far_steps),
        in_specs=[weight] * 3 + [own] * 2 + [own_mid] * 3 + [near_one, near_two, near] + [far] * 2,
        out_specs=[weight] * 3,
        out_shape=[jax.ShapeDtypeStruct((size, width), jnp.float32)] * 3,
        scratch_shapes=[pltpu.VMEM((hid, tok), low)] * 3,
        compiler_params=pltpu.CompilerParams(
            dimension_semantics=("arbitrary", "arbitrary"), vmem_limit_bytes=62 * 2**20
        ),
        cost_estimate=pl.CostEstimate(flops=flops, bytes_accessed=100 * 2**20, transcendentals=0),
        name="weight_grads",
    )(
        gate, up, down, rows, d_rows, hidden, d_gate, d_up, rows_near, rows_next, d_rows_near, rows_far, d_rows_far
    )


def finish_kernel(
    key_width, wide, small, result_in, d_vectors_in, d_source_in,
    result, d_source, d_vectors, query, key, value, output, down, up, gate, out,
    gain_one, gain_two, gain_three, gain_four, gain_five, gain_six, query_gain, key_gain,
):
    result[...] = result_in[...]
    d_vectors[...] = d_vectors_in[...]
    d_source[...] = d_source_in[...]
    query_width = query.shape[1]
    start = 0
    for target, columns in (
        (query, query_width),
        (key, key_width),
        (value, key_width),
        (down, down.shape[1]),
    ):
        target[...] = wide[:, start : start + columns].astype(jnp.float32)
        start += columns
    start += -start % 128
    output[...] = wide[:, start : start + output.shape[1]].astype(jnp.float32)
    start += output.shape[1]
    gate[...] = wide[:, start : start + gate.shape[1]].astype(jnp.float32)
    lines = small[...].astype(jnp.float32)
    first = out.shape[0]
    out[...] = lines[0:first]
    up[...] = lines[first : first + up.shape[0]]
    first += up.shape[0]
    for index, target in enumerate((gain_one, gain_two, gain_three, gain_four, gain_five, gain_six)):
        target[...] = lines[first + index : first + index + 1, 0 : target.shape[1]]
    me = lax.axis_index("fsdp")
    for index, target in enumerate((query_gain, key_gain)):
        size = target.shape[1]
        line = lines[first + 6 + index : first + 7 + index, 0 : 8 * size]
        total = jnp.zeros((1, size), jnp.float32)
        for device in range(8):
            total = total + jnp.where(me == device, line[:, device * size : (device + 1) * size], 0.0)
        target[...] = total


def finish_call(wide, small, result, d_vectors, d_source, shapes, key_width):
    vmem = pl.BlockSpec(memory_space=pltpu.VMEM)
    kinds = [jnp.bfloat16] + [jnp.float32] * (len(shapes) - 1)
    return pl.pallas_call(
        functools.partial(finish_kernel, key_width),
        out_shape=[jax.ShapeDtypeStruct(shape, kind) for shape, kind in zip(shapes, kinds)],
        in_specs=[vmem] * 5,
        out_specs=[vmem] * len(shapes),
        compiler_params=pltpu.CompilerParams(vmem_limit_bytes=40 * 2**20),
        name="finish",
    )(wide, small, result, d_vectors, d_source)


def per_device(
    tokens,
    per_layer,
    segments,
    positions,
    cotangent,
    query_weight,
    key_matrix,
    value_matrix,
    output_weight,
    laurel_down,
    laurel_up,
    vector_gate,
    vector_out,
    norm_input,
    norm_attention,
    norm_laurel,
    norm_before,
    norm_after,
    norm_vector,
    query_norm_gain,
    norm_key,
    hidden_gate,
    hidden_up,
    hidden_down,
):
    count_of_rows = tokens.shape[0]
    shards = lax.axis_size("fsdp")
    width = tokens.shape[1]
    heads_per_group = QUERY_HEADS // KEY_VALUE_HEADS
    reach_blocks = min((WINDOW + count_of_rows - 2) // count_of_rows, lax.axis_size("ctx") - 1)
    score_scale = HEAD_SIZE ** (-0.5)
    fused = shards == 8 and lax.axis_size("ctx") == 4
    query_width = query_weight.shape[1]
    key_width = key_matrix.shape[1]

    gain_shards = (
        norm_input,
        norm_attention,
        norm_laurel,
        norm_before,
        norm_after,
        norm_vector,
        query_norm_gain,
        norm_key,
    )
    gain_sizes = [gain.shape[0] for gain in gain_shards]
    gain_starts = [sum(gain_sizes[:index]) for index in range(len(gain_sizes))]
    source = tokens.astype(jnp.float32)
    vectors = per_layer.astype(jnp.float32)
    rank = laurel_down.shape[1]
    unused, allowed = window(positions, count_of_rows, reach_blocks)

    def head_facing(linear, gain):
        return rotary_apply(root_mean_norm(linear, gain), positions)

    if fused:
        me = lax.axis_index("fsdp")
        head_gains = jnp.stack([query_norm_gain, norm_key])
        place = jnp.arange(HEAD_SIZE) // head_gains.shape[1] == me
        head_gains = jnp.where(place[None, :], jnp.tile(head_gains, (1, shards)), 0).astype(jnp.bfloat16)
        cosine, sine_part = rotary_tables(positions, HEAD_SIZE)
        (
            normed,
            gains_all,
            linear,
            query_lowered,
            key_value,
            features,
            middle_low,
            attn_lin,
            full_laurel_up,
            full_inward,
            full_output,
        ) = attend_call(
            reach_blocks,
            tokens,
            [gain.reshape(-1, 128) for gain in gain_shards[:6]],
            head_gains,
            laurel_up,
            positions[:, None],
            cosine,
            sine_part,
            (query_weight, key_matrix, value_matrix, laurel_down),
            output_weight,
        )
    else:
        gain_line = jnp.concatenate(gain_shards)
        gain_line = jnp.pad(gain_line, (0, -gain_line.shape[0] % 2048)).reshape(-1, 128)
        gains_all = gather(gain_line, "fsdp").reshape(shards, -1)
        gains = [
            gains_all[:, start : start + size].reshape(-1).astype(jnp.float32)
            for start, size in zip(gain_starts, gain_sizes)
        ]
        inward_weight = jnp.concatenate([query_weight, key_matrix, value_matrix, laurel_down], axis=1)
        inward_weight = jnp.pad(inward_weight, ((0, 0), (0, -inward_weight.shape[1] % 128)))
        full_inward = gather(inward_weight, "fsdp")
        full_output, full_vector_gate, full_vector_out, full_laurel_up = [
            gather(value, "fsdp") for value in (output_weight, vector_gate, vector_out, laurel_up)
        ]
        normed = root_mean_norm(source, gains[0])
        lowered_normed = normed.astype(jnp.bfloat16)
        inward = matrix_product(lowered_normed, full_inward)
        linear = inward[:, : query_width + key_width]
        value_lowered = inward[:, query_width + key_width : query_width + 2 * key_width].astype(jnp.bfloat16)
        laurel_mid = inward[:, query_width + 2 * key_width :][:, :rank].astype(jnp.bfloat16)
        query_lowered = head_facing(
            linear[:, :query_width].reshape(count_of_rows, QUERY_HEADS, HEAD_SIZE), gains[6]
        ).astype(jnp.bfloat16)
        key_lowered = head_facing(
            linear[:, query_width:].reshape(count_of_rows, KEY_VALUE_HEADS, HEAD_SIZE), gains[7]
        ).astype(jnp.bfloat16)
        key_value = jnp.stack([key_lowered.reshape(count_of_rows, -1), value_lowered])
        pair_blocks = [key_value]
        for distance in range(1, reach_blocks + 1):
            pair_blocks.append(from_behind(key_value, "ctx", distance))
        window_couple = jnp.concatenate(pair_blocks, axis=1)
        window_keys, window_values = window_couple[0], window_couple[1]
    if fused:
        (
            feed_value,
            mixed,
            laurel_lin,
            rows_all,
            rows_far,
            rows_near,
            slices,
            full_vector_gate,
            full_vector_out,
            hidden_all,
            lift_all,
            bend_all,
        ) = feed_call(
            True,
            (tokens, normed, attn_lin, middle_low, full_laurel_up, gains_all),
            (hidden_gate, hidden_up, hidden_down),
            features=features,
            vectors=(vector_gate, vector_out),
        )
        slices = slices.reshape(shards * count_of_rows, -1)
        rows_far = gather(rows_far.reshape(-1, width), "fsdp")
        (
            d_ffn_in,
            result,
            d_vectors,
            residual_low,
            d_vector_lin_low,
            gated_low,
            d_vector_back_low,
            d_residual,
            gain_rows,
            d_rows_all,
            d_rows_far,
            rows_next,
            d_gate_low,
            d_up_low,
        ) = feed_call(
            False,
            (feed_value, mixed, gains_all, full_vector_gate, full_vector_out, per_layer, cotangent),
            (hidden_down, hidden_gate, hidden_up),
            (lift_all, bend_all),
            forward_rows=rows_all,
        )
        d_ffn_in, rows_far = lax.optimization_barrier((d_ffn_in, rows_far))
        d_rows_far = gather(d_rows_far.reshape(-1, width), "fsdp")
        d_source, grad_wide, grad_small, d_rows_near = attend_back_call(
            reach_blocks, d_ffn_in, mixed, d_residual, laurel_lin, attn_lin, full_laurel_up, gain_rows,
            query_lowered, key_value, linear, gains_all, positions[:, None], cosine, sine_part, middle_low, slices,
            tokens, residual_low, d_vector_lin_low, gated_low, d_vector_back_low, full_output, full_inward, d_rows_all,
        )
        grad_hidden_gate, grad_hidden_up, grad_hidden_down = weight_grad_call(
            hidden_gate,
            hidden_up,
            hidden_down,
            rows_all,
            d_rows_all,
            hidden_all,
            d_gate_low,
            d_up_low,
            rows_near.reshape(-1, width),
            rows_next.reshape(-1, width),
            d_rows_near.reshape(-1, width),
            rows_far,
            d_rows_far,
        )
    else:
        (
            gain_input,
            gain_attention,
            gain_laurel,
            gain_before,
            gain_after,
            gain_vector,
            gain_query,
            key_norm_gain,
        ) = gains
        query_linear = linear[:, :query_width].reshape(count_of_rows, QUERY_HEADS, HEAD_SIZE)
        key_linear = linear[:, query_width:].reshape(count_of_rows, KEY_VALUE_HEADS, HEAD_SIZE)
        query_lowered = query_lowered.reshape(count_of_rows, KEY_VALUE_HEADS, heads_per_group, HEAD_SIZE)
        window_keys = window_keys.reshape(-1, KEY_VALUE_HEADS, HEAD_SIZE)
        window_values = window_values.reshape(-1, KEY_VALUE_HEADS, HEAD_SIZE)

        def masked_scores():
            raw_scores = score_scale * jnp.einsum(
                "tgfd,kgd->gftk", query_lowered, window_keys, preferred_element_type=jnp.float32
            )
            return jnp.where(allowed, raw_scores, -1e30)

        scores_first = masked_scores()
        row_peak = jnp.max(scores_first, axis=-1, keepdims=True)
        exp_scores = jnp.exp(scores_first - row_peak)
        row_total = jnp.sum(exp_scores, axis=-1, keepdims=True)
        log_total = row_peak + jnp.log(row_total)
        soft_low = (exp_scores / row_total).astype(jnp.bfloat16)
        attended_low = (
            jnp.einsum("gftk,kgd->tgfd", soft_low, window_values, preferred_element_type=jnp.float32)
            .reshape(count_of_rows, QUERY_HEADS * HEAD_SIZE)
            .astype(jnp.bfloat16)
        )
        attn_lin = matrix_product(attended_low, full_output)
        residual_one = source + root_mean_norm(attn_lin, gain_attention)
        laurel_lin = matrix_product(laurel_mid, full_laurel_up)
        mixed = (residual_one + normed + root_mean_norm(laurel_lin, gain_laurel)) * inv_root
        ffn_in = root_mean_norm(mixed, gain_before).astype(jnp.bfloat16)
        normed_slices = feature_slices(lowered_normed)
        attended_slices = feature_slices(attended_low)
        rows_all = gather(ffn_in, "fsdp")
        gate_all = product_back(rows_all, hidden_gate)
        up_all = product_back(rows_all, hidden_up)
        hidden_all = gated(gate_all, up_all).astype(jnp.bfloat16)
        feed_value = scatter_sum(matrix_product(hidden_all, hidden_down))
        residual_two = mixed + root_mean_norm(feed_value, gain_after)
        residual_low = residual_two.astype(jnp.bfloat16)
        vector_lin = matrix_product(residual_low, full_vector_gate)
        gated_low = gated(vector_lin, vectors).astype(jnp.bfloat16)
        vector_back = matrix_product(gated_low, full_vector_out)
        result = residual_two + root_mean_norm(vector_back, gain_vector)
        upstream = cotangent.astype(jnp.float32)
        d_vector_back, grad_gain_vector = norm_grad(vector_back, gain_vector, upstream)
        d_vector_back_low = d_vector_back.astype(jnp.bfloat16)
        grad_vector_out = product_rows(gated_low, d_vector_back_low)
        d_gated = product_back(d_vector_back_low, full_vector_out)
        d_vector_lin, d_vectors = gated_grad(vector_lin, vectors, d_gated)
        d_vector_lin_low = d_vector_lin.astype(jnp.bfloat16)
        grad_vector_gate = product_rows(residual_low, d_vector_lin_low)
        d_residual = upstream + product_back(d_vector_lin_low, full_vector_gate)
        d_feed, grad_gain_after = norm_grad(feed_value, gain_after, d_residual)
        d_feed_low = d_feed.astype(jnp.bfloat16)
        d_rows_all = gather(d_feed_low, "fsdp")
        d_hidden = product_back(d_rows_all, hidden_down)
        d_gate_all, d_up_all = gated_grad(gate_all, up_all, d_hidden)
        d_gate_low = d_gate_all.astype(jnp.bfloat16)
        d_up_low = d_up_all.astype(jnp.bfloat16)
        d_ffn_in = scatter_sum(
            matrix_product(d_gate_low, hidden_gate) + matrix_product(d_up_low, hidden_up)
        )

        grad_hidden_gate, grad_hidden_up, grad_hidden_down = [
            lax.psum(grad.astype(jnp.bfloat16), "ctx").astype(jnp.float32)
            for grad in (
                product_rows(d_gate_low, rows_all),
                product_rows(d_up_low, rows_all),
                product_rows(hidden_all, d_rows_all),
            )
        ]

        d_mixed_part, grad_gain_before = norm_grad(mixed, gain_before, d_ffn_in)
        d_half = (d_residual + d_mixed_part) * inv_root
        d_laurel_lin, grad_gain_laurel = norm_grad(laurel_lin, gain_laurel, d_half)
        d_laurel_low = d_laurel_lin.astype(jnp.bfloat16)
        grad_laurel_up = product_rows(laurel_mid, d_laurel_low)
        d_laurel_mid = product_back(d_laurel_low, full_laurel_up).astype(jnp.bfloat16)
        d_attn_lin, grad_gain_attention = norm_grad(attn_lin, gain_attention, d_half)
        d_attn_low = d_attn_lin.astype(jnp.bfloat16)
        d_attended = (
            product_back(d_attn_low, full_output)
            .astype(jnp.bfloat16)
            .reshape(count_of_rows, KEY_VALUE_HEADS, heads_per_group, HEAD_SIZE)
        )
        soft_again = jnp.exp(masked_scores() - log_total)
        d_soft = jnp.einsum(
            "tgfd,kgd->gftk", d_attended, window_values, preferred_element_type=jnp.float32
        )
        d_scores = (
            soft_again * (d_soft - jnp.sum(soft_again * d_soft, axis=-1, keepdims=True))
        ).astype(jnp.bfloat16)
        d_query = score_scale * jnp.einsum(
            "gftk,kgd->tgfd", d_scores, window_keys, preferred_element_type=jnp.float32
        )
        grad_key_rows = score_scale * jnp.einsum(
            "gftk,tgfd->kgd", d_scores, query_lowered, preferred_element_type=jnp.float32
        )
        grad_value_rows = jnp.einsum(
            "gftk,tgfd->kgd",
            soft_again.astype(jnp.bfloat16),
            d_attended,
            preferred_element_type=jnp.float32,
        )
        grad_window_couple = jnp.stack(
            [
                grad_key_rows.reshape(-1, KEY_VALUE_HEADS * HEAD_SIZE),
                grad_value_rows.reshape(-1, KEY_VALUE_HEADS * HEAD_SIZE),
            ]
        )
        grad_own_part = grad_window_couple[:, :count_of_rows]
        for distance in range(1, reach_blocks + 1):
            grad_own_part = grad_own_part + from_behind(
                grad_window_couple[:, distance * count_of_rows : (distance + 1) * count_of_rows].astype(
                    jnp.bfloat16
                ),
                "ctx",
                -distance,
            ).astype(jnp.float32)
        unused, query_pull = jax.vjp(head_facing, query_linear, gain_query)
        d_query_lin, grad_gain_query = query_pull(
            d_query.reshape(count_of_rows, QUERY_HEADS, HEAD_SIZE)
        )
        unused, key_pullback_fn = jax.vjp(head_facing, key_linear, key_norm_gain)
        grad_key_linear, grad_key_norm_gain = key_pullback_fn(
            grad_own_part[0].reshape(count_of_rows, KEY_VALUE_HEADS, HEAD_SIZE)
        )
        d_inward = jnp.concatenate(
            [
                d_query_lin.reshape(count_of_rows, QUERY_HEADS * HEAD_SIZE).astype(jnp.bfloat16),
                grad_key_linear.reshape(count_of_rows, KEY_VALUE_HEADS * HEAD_SIZE).astype(
                    jnp.bfloat16
                ),
                grad_own_part[1].astype(jnp.bfloat16),
                d_laurel_mid,
                jnp.zeros((count_of_rows, full_inward.shape[1] - query_width - 2 * key_width - rank), jnp.bfloat16),
            ],
            axis=1,
        )
        grad_inward = product_rows(normed_slices, gather(d_inward, "fsdp")).astype(jnp.bfloat16)
        grad_output = product_rows(attended_slices, gather(d_attn_low, "fsdp")).astype(jnp.bfloat16)
        grad_wide = jnp.concatenate([grad_inward, grad_output], axis=1)
        small_rows = jnp.concatenate(
            [
                grad_vector_gate.reshape(shards, -1, width),
                grad_vector_out.reshape(shards, -1, width),
                grad_laurel_up.reshape(shards, -1, width),
            ],
            axis=1,
        ).astype(jnp.bfloat16)
        grad_small = lax.psum_scatter(small_rows, "fsdp", scatter_dimension=0, tiled=False)
        d_normed = d_half + product_back(d_inward, full_inward)
        d_source_part, grad_gain_input = norm_grad(source, gain_input, d_normed)
        d_source = d_half + d_source_part
        gain_lines = jnp.concatenate(
            [
                grad.reshape(shards, -1)
                for grad in (
                    grad_gain_input,
                    grad_gain_attention,
                    grad_gain_laurel,
                    grad_gain_before,
                    grad_gain_after,
                    grad_gain_vector,
                    grad_gain_query,
                    grad_key_norm_gain,
                )
            ],
            axis=1,
        )
        gain_share = lax.psum_scatter(gain_lines, "fsdp", scatter_dimension=0, tiled=False)
        gain_count = gain_share.shape[0]
        gain_share = jnp.pad(gain_share, (0, -gain_count % width)).astype(jnp.bfloat16)
        grad_small = jnp.concatenate([grad_small, gain_share.reshape(-1, width)], axis=0)

    grad_wide, grad_small = lax.psum((grad_wide, grad_small), "ctx")
    hidden_grads = (grad_hidden_gate, grad_hidden_up, grad_hidden_down)
    if fused:
        weights = (query_weight, key_matrix, value_matrix, output_weight, laurel_down, laurel_up, vector_gate, vector_out)
        shapes = [tokens.shape, tokens.shape, per_layer.shape] + [weight.shape for weight in weights]
        shapes += [(1, size) for size in gain_sizes]
        finished = finish_call(grad_wide, grad_small, result, d_vectors, d_source, shapes, key_width)
        gains_from = len(shapes) - len(gain_sizes)
        return tuple(finished[:gains_from]) + tuple(gain.reshape(-1) for gain in finished[gains_from:]) + hidden_grads
    grad_wide, grad_small = grad_wide.astype(jnp.float32), grad_small.astype(jnp.float32)
    inward_width = full_inward.shape[1]
    grad_inward = grad_wide[:, :inward_width]
    grad_output = grad_wide[:, inward_width:]
    out_rows, laurel_rows = vector_out.shape[0], laurel_up.shape[0]
    gate_rows = vector_gate.shape[0] * vector_gate.shape[1] // width
    share_vector_gate = grad_small[:gate_rows].reshape(vector_gate.shape)
    share_vector_out = grad_small[gate_rows : gate_rows + out_rows]
    gain_start = gate_rows + out_rows + laurel_rows
    share_laurel_up = grad_small[gate_rows + out_rows : gain_start]
    gain_share = grad_small[gain_start:].reshape(-1)
    gain_grads = tuple(gain_share[start : start + size] for start, size in zip(gain_starts, gain_sizes))
    value_start = query_width + key_width
    return (
        (
            result.astype(jnp.bfloat16),
            d_source,
            d_vectors,
            grad_inward[:, :query_width],
            grad_inward[:, query_width:value_start],
            grad_inward[:, value_start : value_start + key_width],
            grad_output,
            grad_inward[:, value_start + key_width : value_start + key_width + rank],
            share_laurel_up,
            share_vector_gate,
            share_vector_out,
        )
        + gain_grads
        + hidden_grads
    )


def solution(mesh):
    rows = P(("fsdp", "ctx"), None)
    line = P(("fsdp", "ctx"))
    weight = P("fsdp", None)
    gain = P("fsdp")
    return jax.shard_map(
        per_device,
        mesh=mesh,
        in_specs=(rows, rows, line, line, rows) + (weight,) * 8 + (gain,) * 8 + (weight,) * 3,
        out_specs=(rows,) * 3 + (weight,) * 8 + (gain,) * 8 + (weight,) * 3,
        check_vma=False,
    )
```

```python
import functools

import jax
import jax.numpy as jnp
from jax import lax
from jax.experimental import pallas as pl
from jax.experimental.pallas import tpu as pltpu
from jax.sharding import PartitionSpec as P

QUERY_HEADS = 8
KEY_VALUE_HEADS = 2
HEAD_SIZE = 256
WINDOW = 1024


epsilon = 1e-06
rope_base = 10000.0
inv_root = 0.7071067811865476
gelu_scale = 0.7978845608028654
gelu_cubic = 0.044715


def from_behind(value, axis, steps):
    count = lax.axis_size(axis)
    initial, last = (max(0, -steps), min(count, count - steps))
    return lax.ppermute(value, axis, [(source, source + steps) for source in range(initial, last)])


def other_blocks(value, axis):
    count = lax.axis_size(axis)
    return jnp.concatenate(
        [
            lax.ppermute(value, axis, [(source, (source + step) % count) for source in range(count)])
            for step in range(1, count)
        ],
        axis=0,
    )


def root_mean_norm(value, gain):
    factor = lax.rsqrt(jnp.mean(value * value, axis=-1, keepdims=True) + epsilon)
    return value * factor * gain


def gelu_tanh(value):
    return jax.nn.gelu(value, approximate=True)


def gated(gate_value, up_value):
    return gelu_tanh(gate_value) * up_value


def rotary_apply(value, token_position):
    half_size = value.shape[-1] // 2
    frequency = rope_base ** (-2.0 * jnp.arange(half_size, dtype=jnp.float32) / value.shape[-1])
    angle = token_position.astype(jnp.float32)[:, None] * frequency[None, :]
    cosine = jnp.cos(angle)[:, None, :]
    sine_part = jnp.sin(angle)[:, None, :]
    first_half = value[..., :half_size]
    second_half = value[..., half_size:]
    return jnp.concatenate(
        [
            first_half * cosine - second_half * sine_part,
            second_half * cosine + first_half * sine_part,
        ],
        axis=-1,
    )


def rotary_tables(token_position, size):
    half_size = size // 2
    frequency = rope_base ** (-2.0 * jnp.arange(half_size, dtype=jnp.float32) / size)
    angle = token_position.astype(jnp.float32)[:, None] * frequency[None, :]
    return jnp.cos(angle), jnp.sin(angle)


def window(positions, rows_of, reach):
    key_offset = jnp.concatenate(
        [distance * rows_of - jnp.arange(rows_of, dtype=jnp.int32) for distance in range(reach + 1)]
    )
    key_gap = jnp.arange(rows_of, dtype=jnp.int32)[:, None] + key_offset[None, :]
    return key_gap, (key_gap >= 0) & (key_gap <= positions[:, None]) & (key_gap < WINDOW)


def matrix_product(left, right):
    return jnp.dot(left, right, preferred_element_type=jnp.float32)


def product_back(left, right):
    return lax.dot_general(
        left, right, (((1,), (1,)), ((), ())), preferred_element_type=jnp.float32
    )


def product_rows(left, right):
    return lax.dot_general(
        left, right, (((0,), (0,)), ((), ())), preferred_element_type=jnp.float32
    )


def norm_grad(value, gain, upstream):
    unused, pullback = jax.vjp(root_mean_norm, value, gain)
    return pullback(upstream)


def gated_grad(gate_value, up_value, upstream):
    unused, pullback = jax.vjp(gated, gate_value, up_value)
    return pullback(upstream)


def gather(value, axis):
    return lax.all_gather(value, axis, axis=0, tiled=True)


def feature_slices(value):
    count = lax.axis_size("fsdp")
    rows = value.shape[0]
    return lax.all_to_all(
        value.reshape(rows, count, -1), "fsdp", split_axis=1, concat_axis=0, tiled=True
    ).reshape(count * rows, -1)


def scatter_sum(value):
    return lax.psum_scatter(
        value.astype(jnp.bfloat16), "fsdp", scatter_dimension=0, tiled=True
    ).astype(jnp.float32)


def gelu_parts(gate):
    square = gate * gate
    bend = jnp.tanh(gelu_scale * gate * (1.0 + gelu_cubic * square))
    half_up = 0.5 * (1.0 + bend)
    slope = half_up + 0.5 * gate * (1.0 - bend * bend) * (
        gelu_scale * (1.0 + 3.0 * gelu_cubic * square)
    )
    return gate * half_up, slope


def across(me, stride):
    return me + stride - 2 * stride * ((me // stride) % 2)


def across_many(me, bits):
    for stride in (1, 2, 4):
        if bits & stride:
            me = across(me, stride)
    return me


def feed_kernel(forward, rows_of, others, *refs):
    half = rows_of // 2
    if forward:
        (source, normed, attn_lin, middle, laurel, gains), refs = refs[:6], refs[6:]
        (gate_hbm, up_hbm, down_hbm, features, gate_own, out_own), refs = refs[:6], refs[6:]
        (total, mixed, laurel_lin, rows_hbm, far_hbm, near_hbm), refs = refs[:6], refs[6:]
        (slices_hbm, gate_all, out_all, hidden_hbm, lift_hbm, bend_hbm), rest = refs[:6], refs[6:]
        weights_hbm, kept_hbm, made_hbm = (gate_hbm, up_hbm, down_hbm), (), (hidden_hbm, lift_hbm, bend_hbm)
    else:
        (feed_value, mixed, gains, gate_all, out_all, vectors, cotangent), refs = refs[:7], refs[7:]
        (down_hbm, gate_hbm, up_hbm, lift_hbm, bend_hbm, forward_rows), refs = refs[:6], refs[6:]
        (total, result, d_vectors, residual_low, d_vector_low, gated_low, d_back_low, d_residual, gain_rows), refs = (
            refs[:9],
            refs[9:],
        )
        (rows_hbm, far_hbm, near_hbm, d_gate_hbm, d_up_hbm), rest = refs[:5], refs[5:]
        weights_hbm, kept_hbm, made_hbm = (down_hbm, gate_hbm, up_hbm), (lift_hbm, bend_hbm), (d_gate_hbm, d_up_hbm)
    count_kept, count_made = len(kept_hbm), len(made_hbm)
    weights = rest[:3]
    kept = rest[3 : 3 + count_kept]
    made = rest[3 + count_kept : 3 + count_kept + count_made]
    (own, rows, part, sib_in, chip_sum, relay_in, relay_sum, last_in, send_sem, recv_sem, in_sem, out_sem, far_send, far_recv, near_send, near_recv, *extra) = rest[
        3 + count_kept + count_made :
    ]
    hidden = weights[0].shape[0]
    width = weights[0].shape[1]
    me = lax.axis_index("fsdp")
    sibling, beside, above = across(me, 1), across(me, 2), across(me, 4)

    loads = [
        pltpu.make_async_copy(source, target, in_sem.at[index])
        for index, (source, target) in enumerate(zip(weights_hbm + kept_hbm, tuple(weights) + tuple(kept)))
    ]
    for load in loads:
        load.start()

    block = lax.axis_index("ctx")
    def before_feed():
        def unit(value):
            return value * lax.rsqrt(jnp.mean(value * value, axis=-1, keepdims=True) + epsilon)

        laurel_lin[...] = jnp.dot(middle[...], laurel[...].astype(jnp.bfloat16), preferred_element_type=jnp.float32)
        value = source[...].astype(jnp.float32) + unit(attn_lin[...]) * gains[1:2, :] + normed[...]
        value = (value + unit(laurel_lin[...]) * gains[2:3, :]) * inv_root
        mixed[...] = value
        own[...] = (unit(value) * gains[3:4, :]).astype(jnp.bfloat16)

    def after_feed():
        def unit(value):
            return value * lax.rsqrt(jnp.mean(value * value, axis=-1, keepdims=True) + epsilon)

        residual = mixed[...] + unit(feed_value[...]) * gains[4:5, :]
        residual_low[...] = residual.astype(jnp.bfloat16)
        vector_lin = jnp.dot(residual_low[...], gate_all[...], preferred_element_type=jnp.float32)
        value, slope = gelu_parts(vector_lin)
        per_token = vectors[...].astype(jnp.float32)
        gated_low[...] = (value * per_token).astype(jnp.bfloat16)
        vector_back = jnp.dot(gated_low[...], out_all[...], preferred_element_type=jnp.float32)
        result[...] = (residual + unit(vector_back) * gains[5:6, :]).astype(jnp.bfloat16)
        upstream = cotangent[...].astype(jnp.float32)
        d_back, grad_vector_gain = norm_rows_grad(vector_back, gains[5:6, :], upstream)
        d_back_low[...] = d_back.astype(jnp.bfloat16)
        d_gated = product_back(d_back_low[...], out_all[...])
        d_vectors[...] = d_gated * value
        d_vector_low[...] = (d_gated * per_token * slope).astype(jnp.bfloat16)
        d_residual[...] = upstream + product_back(d_vector_low[...], gate_all[...])
        d_feed, grad_after_gain = norm_rows_grad(feed_value[...], gains[4:5, :], d_residual[...])
        own[...] = d_feed.astype(jnp.bfloat16)
        gain_rows[...] = jnp.zeros_like(gain_rows)
        gain_rows[4:5, :] = grad_after_gain
        gain_rows[5:6, :] = grad_vector_gain

    greet(me, range(1, 8) if forward else (1, 2, 4), block, others, before_feed if forward else after_feed)

    def send(index, source, target, partner):
        return pltpu.make_async_remote_copy(
            src_ref=source,
            dst_ref=target,
            send_sem=send_sem.at[index],
            recv_sem=recv_sem.at[index],
            device_id={"fsdp": partner},
            device_id_type=pl.DeviceIdType.MESH,
        )

    low, high = pl.ds(0, half), pl.ds(half, half)
    mine, theirs = pl.ds(0, rows_of), pl.ds(rows_of, rows_of)
    copies = [
        send(0, own, rows.at[0, theirs], sibling),
        send(1, own.at[low], rows.at[1, low], beside),
        send(2, own.at[low], rows.at[1, high], above),
        send(3, own.at[high], rows.at[2, low], beside),
        send(4, own.at[high], rows.at[2, high], above),
        send(5, rows.at[1, mine], rows.at[1, theirs], sibling),
        send(6, rows.at[2, mine], rows.at[2, theirs], sibling),
        send(7, rows.at[1, low], rows.at[3, low], above),
        send(8, rows.at[2, high], rows.at[3, high], beside),
        send(9, rows.at[3, mine], rows.at[3, theirs], sibling),
        send(10, part.at[0, theirs], sib_in.at[0], sibling),
        send(11, part.at[1, theirs], sib_in.at[1], sibling),
        send(12, part.at[2, theirs], sib_in.at[2], sibling),
        send(13, part.at[3, theirs], sib_in.at[3], sibling),
        send(14, chip_sum.at[0, high], last_in.at[2], above),
        send(15, chip_sum.at[1, low], last_in.at[1], beside),
        send(16, chip_sum.at[2, low], relay_in.at[0], above),
        send(17, chip_sum.at[2, high], relay_in.at[1], beside),
        send(18, relay_sum.at[0], last_in.at[0], beside),
        send(19, relay_sum.at[1], last_in.at[3], above),
    ]
    outs = []

    def write_out(source, target):
        copy = pltpu.make_async_copy(source, target, out_sem.at[len(outs)])
        copy.start()
        outs.append(copy)

    for index in range(5):
        copies[index].start()
    spreads = []
    if forward:
        gate_slots, out_slots, gate_send, gate_recv, vec_send, vec_recv, gate_out, vec_out = extra[3:]
        spreads = [
            spread_copies(gate_own, gate_slots, gate_send, gate_recv, me),
            spread_copies(out_own, out_slots, vec_send, vec_recv, me),
        ]
        for spread in spreads:
            for index in range(5):
                spread[index].start()
        gate_slots[0] = gate_own[...]
        out_slots[0] = out_own[...]
    far = [
        push(own, far_hbm.at[index], far_send.at[index], far_recv.at[index], {"ctx": across_many(block, 2 + index)})
        for index in range(2)
    ]
    for copy in far:
        copy.start()
    def near_source(index):
        if forward:
            return rows.at[1, mine] if index else own
        return forward_rows.at[pl.ds((2 + index) * 2 * rows_of, rows_of)]

    near = [
        push(near_source(index), near_hbm.at[index, mine], near_send.at[index], near_recv.at[index], {"ctx": across(block, 1)})
        for index in range(2)
    ]
    near_share = [
        push(
            near_hbm.at[index, mine],
            near_hbm.at[index, theirs],
            near_send.at[2 + index],
            near_recv.at[2 + index],
            {"fsdp": sibling},
        )
        for index in range(2)
    ]
    near[0].start()
    if not forward:
        near[1].start()
    rows[0, mine] = own[...]
    slices = []
    if forward:
        share = features.shape[1] // 8

        def share_of(device):
            return features.at[:, pl.ds(pl.multiple_of(device * share, share), share)]

        own_slice = pltpu.make_async_copy(share_of(me), slices_hbm.at[me], extra[2])
        own_slice.start()
        slices = [
            pltpu.make_async_remote_copy(
                src_ref=share_of(across_many(me, distance)),
                dst_ref=slices_hbm.at[me],
                send_sem=extra[0].at[distance - 1],
                recv_sem=extra[1].at[distance - 1],
                device_id={"fsdp": across_many(me, distance)},
                device_id_type=pl.DeviceIdType.MESH,
            )
            for distance in range(1, 8)
        ]

    tile = min(hidden, 1024)
    wide = min(width, 1024)

    def first_stage(group):
        span = pl.ds(group * 2 * rows_of, 2 * rows_of)

        def step(index, carry):
            columns = pl.ds(pl.multiple_of(index * tile, tile), tile)
            left = rows[group]

            def back(weight):
                return lax.dot_general(
                    left, weight[columns, :], (((1,), (1,)), ((), ())), preferred_element_type=jnp.float32
                )

            if forward:
                gate, up = back(weights[0]), back(weights[1])
                value, slope = gelu_parts(gate)
                made[0][span, columns] = (value * up).astype(jnp.bfloat16)
                made[1][span, columns] = value.astype(jnp.bfloat16)
                made[2][span, columns] = (slope * up).astype(jnp.bfloat16)
            else:
                d_hidden = back(weights[0])
                made[0][span, columns] = (d_hidden * kept[1][span, columns].astype(jnp.float32)).astype(jnp.bfloat16)
                made[1][span, columns] = (d_hidden * kept[0][span, columns].astype(jnp.float32)).astype(jnp.bfloat16)
            return carry

        lax.fori_loop(0, hidden // tile, step, 0)

    def second_stage(group):
        span = pl.ds(group * 2 * rows_of, 2 * rows_of)

        def step(index, carry):
            columns = pl.ds(pl.multiple_of(index * wide, wide), wide)
            if forward:
                value = jnp.dot(made[0][span, :], weights[2][:, columns], preferred_element_type=jnp.float32)
            else:
                value = jnp.dot(made[0][span, :], weights[1][:, columns], preferred_element_type=jnp.float32)
                value = value + jnp.dot(made[1][span, :], weights[2][:, columns], preferred_element_type=jnp.float32)
            part[group, :, columns] = value.astype(jnp.bfloat16)
            return carry

        lax.fori_loop(0, width // wide, step, 0)

    def keep_out(group):
        span = pl.ds(group * 2 * rows_of, 2 * rows_of)
        write_out(rows.at[group], rows_hbm.at[span])
        for source, target in zip(made, made_hbm):
            write_out(source.at[span], target.at[span])

    def add_chip(group):
        chip_sum[group - 1] = (
            part[group, mine].astype(jnp.float32) + sib_in[group].astype(jnp.float32)
        ).astype(jnp.bfloat16)

    copies[0].wait_recv()
    loads[0].wait()
    if forward:
        loads[1].wait()
    else:
        loads[3].wait()
        loads[4].wait()
    first_stage(0)
    if forward:
        loads[2].wait()
    else:
        loads[1].wait()
        loads[2].wait()
    second_stage(0)
    copies[10].start()
    keep_out(0)
    copies[1].wait_recv()
    copies[7].start()
    copies[2].wait_recv()
    copies[5].start()
    if forward:
        near[1].start()
    copies[5].wait_recv()
    first_stage(1)
    second_stage(1)
    copies[11].start()
    keep_out(1)
    copies[3].wait_recv()
    copies[4].wait_recv()
    copies[8].start()
    copies[6].start()
    copies[11].wait_recv()
    add_chip(1)
    copies[14].start()
    copies[6].wait_recv()
    first_stage(2)
    second_stage(2)
    copies[12].start()
    keep_out(2)
    for copy in slices:
        copy.start()
    for spread in spreads:
        for index in range(1, 5):
            spread[index].wait_recv()
        for index in range(5, 11):
            spread[index].start()
    copies[7].wait_recv()
    copies[8].wait_recv()
    copies[9].start()
    copies[12].wait_recv()
    add_chip(2)
    copies[15].start()
    copies[9].wait_recv()
    first_stage(3)
    second_stage(3)
    copies[13].start()
    keep_out(3)
    copies[13].wait_recv()
    add_chip(3)
    copies[16].start()
    copies[17].start()
    for spread in spreads:
        for index in (9, 10):
            spread[index].wait_recv()
        for index in (11, 12):
            spread[index].start()
    copies[10].wait_recv()
    total[...] = part[0, mine].astype(jnp.float32) + sib_in[0].astype(jnp.float32)
    copies[16].wait_recv()
    relay_sum[0] = (chip_sum[0, low].astype(jnp.float32) + relay_in[0].astype(jnp.float32)).astype(jnp.bfloat16)
    copies[18].start()
    copies[17].wait_recv()
    relay_sum[1] = (chip_sum[1, high].astype(jnp.float32) + relay_in[1].astype(jnp.float32)).astype(jnp.bfloat16)
    copies[19].start()
    copies[14].wait_recv()
    total[low] = total[low] + last_in[2].astype(jnp.float32)
    copies[15].wait_recv()
    total[high] = total[high] + last_in[1].astype(jnp.float32)
    for index in range(2):
        near[index].wait_recv()
        near_share[index].start()
    copies[18].wait_recv()
    total[low] = total[low] + last_in[0].astype(jnp.float32)
    copies[19].wait_recv()
    total[high] = total[high] + last_in[3].astype(jnp.float32)
    if forward:
        for spread, slots, target, sems in (
            (spreads[0], gate_slots, gate_all, gate_out),
            (spreads[1], out_slots, out_all, vec_out),
        ):
            for index in (0, 5, 6, 7, 8, 11, 12):
                spread[index].wait_recv()
            size = slots.shape[1]
            for slot in range(8):
                place = pl.ds(pl.multiple_of(across_many(me, slot) * size, size), size)
                copy = pltpu.make_async_copy(slots.at[slot], target.at[place], sems.at[slot])
                copy.start()
                outs.append(copy)
            for copy in spread:
                copy.wait_send()
    for copy in copies:
        copy.wait_send()
    for copy in outs:
        copy.wait()
    for copy in far + slices:
        copy.wait()
    for index in range(2):
        near[index].wait_send()
        near_share[index].wait()
    if forward:
        own_slice.wait()


def turn(value, cosine, sine, direction=1.0):
    middle = value.shape[1] // 2
    first, second = value[:, :middle], value[:, middle:]
    sine = sine * direction
    return jnp.concatenate([first * cosine - second * sine, second * cosine + first * sine], axis=1)


def window_mask(positions, rows_of, blocks):
    query_row = lax.broadcasted_iota(jnp.int32, (rows_of, blocks * rows_of), 0)
    column = lax.broadcasted_iota(jnp.int32, (rows_of, blocks * rows_of), 1)
    behind = column // rows_of
    gap = query_row + 2 * behind * rows_of - column
    return (gap >= 0) & (gap <= positions) & (gap < WINDOW)


def norm_rows_grad(value, gain, upstream):
    factor = lax.rsqrt(jnp.mean(value * value, axis=-1, keepdims=True) + epsilon)
    unit = value * factor
    grad_gain = jnp.sum(upstream * unit, axis=0, keepdims=True)
    back = upstream * gain
    return factor * (back - unit * jnp.mean(back * unit, axis=-1, keepdims=True)), grad_gain


def greet(me, partners, block, others, work=None):
    barrier = pltpu.get_barrier_semaphore()
    for distance in partners:
        pl.semaphore_signal(
            barrier, inc=1, device_id={"fsdp": across_many(me, distance)}, device_id_type=pl.DeviceIdType.MESH
        )
    for distance in range(1, others + 1):
        pl.semaphore_signal(
            barrier,
            inc=1,
            device_id={"ctx": (block + distance) % (others + 1)},
            device_id_type=pl.DeviceIdType.MESH,
        )
    if work is not None:
        work()
    pl.semaphore_wait(barrier, len(partners) + others)


def push(source, target, send_sem, recv_sem, place):
    return pltpu.make_async_remote_copy(
        src_ref=source,
        dst_ref=target,
        send_sem=send_sem,
        recv_sem=recv_sem,
        device_id=place,
        device_id_type=pl.DeviceIdType.MESH,
    )


def spread_copies(own, slots, send_sem, recv_sem, me):
    half = own.shape[0] // 2
    low, high = pl.ds(0, half), pl.ds(half, half)
    sibling, beside, above = across(me, 1), across(me, 2), across(me, 4)
    plan = [
        (own, slots.at[1], sibling),
        (own.at[low], slots.at[2, low], beside),
        (own.at[low], slots.at[4, low], above),
        (own.at[high], slots.at[2, high], beside),
        (own.at[high], slots.at[4, high], above),
        (slots.at[2, low], slots.at[3, low], sibling),
        (slots.at[4, low], slots.at[5, low], sibling),
        (slots.at[2, high], slots.at[3, high], sibling),
        (slots.at[4, high], slots.at[5, high], sibling),
        (slots.at[2, low], slots.at[6, low], above),
        (slots.at[4, high], slots.at[6, high], beside),
        (slots.at[6, low], slots.at[7, low], sibling),
        (slots.at[6, high], slots.at[7, high], sibling),
    ]
    return [
        push(source, target, send_sem.at[index], recv_sem.at[index], {"fsdp": partner})
        for index, (source, target, partner) in enumerate(plan)
    ]


def attend_kernel(
    others, reach, source, gain_one, gain_two, gain_three, gain_four, gain_five, gain_six, head_gains, laurel_own,
    positions, cosine, sine, query_own, key_own, value_own, down_own, outward_own,
    normed, gains, linear, query_low, key_value, features, middle, attn_lin, laurel_all, inward_all, outward_all,
    gain_share, gain_slots, inward_slots, outward_slots, normed_low, attended, inward, lin_sum,
    gain_send, gain_recv, in_send, in_recv, out_send, out_recv, kv_send, kv_recv, in_copy, out_copy,
):
    rows_of, width = source.shape
    me, block = lax.axis_index("fsdp"), lax.axis_index("ctx")
    inward_own = inward_slots.at[0]
    gain_lines = gain_slots.at[0]

    def own_shares():
        start = 0
        for piece in (query_own, key_own, value_own, down_own):
            inward_slots[0, :, pl.ds(start, piece.shape[1])] = piece[...]
            start += piece.shape[1]
        inward_slots[0, :, pl.ds(start, inward_slots.shape[2] - start)] = jnp.zeros(
            (inward_slots.shape[1], inward_slots.shape[2] - start), jnp.bfloat16
        )
        gain_share[...] = jnp.zeros_like(gain_share)
        for index, gain in enumerate((gain_one, gain_two, gain_three, gain_four, gain_five, gain_six)):
            pieces = gain[...].astype(jnp.float32)
            size = pieces.shape[0] * 128
            for row in range(pieces.shape[0]):
                place = pl.ds(pl.multiple_of(me * size + row * 128, 128), 128)
                gain_share[index : index + 1, place] = pieces[row : row + 1, :]
        gain_share[6:8, 0:HEAD_SIZE] = head_gains[...].astype(jnp.float32)
        gain_share[8:16, :] = laurel_own[...].astype(jnp.float32)
        gain_slots[0] = gain_share[...].astype(jnp.bfloat16)

    greet(me, range(1, 8), block, others, own_shares)
    gain_copies = [
        push(gain_lines, gain_slots.at[distance], gain_send.at[distance - 1], gain_recv.at[distance - 1],
             {"fsdp": across_many(me, distance)})
        for distance in range(1, 8)
    ]
    for copy in gain_copies:
        copy.start()
    spread_in = spread_copies(inward_own, inward_slots, in_send, in_recv, me)
    spread_out = spread_copies(outward_own, outward_slots, out_send, out_recv, me)
    for index in range(5):
        spread_in[index].start()
    outward_slots[0] = outward_own[...]

    value = source[...].astype(jnp.float32)
    factor = lax.rsqrt(jnp.mean(value * value, axis=-1, keepdims=True) + epsilon)
    for copy in gain_copies:
        copy.wait_recv()
    lines = gain_slots[...].astype(jnp.float32)
    gains[...] = jnp.sum(lines, axis=0)[0:8]
    laurel_size = 8
    laurel_all[...] = jnp.zeros_like(laurel_all)
    for slot in range(8):
        device = across_many(me, slot)
        laurel_all[pl.ds(pl.multiple_of(device * laurel_size, laurel_size), laurel_size), :] = lines[slot, 8:16]
    value = value * factor * gains[0:1, :]
    normed[...] = value
    normed_low[...] = value.astype(jnp.bfloat16)
    share = width // 8
    for index in range(8):
        features[:, pl.ds(2 * index * share, share)] = normed_low[:, pl.ds(index * share, share)]

    depth = inward_own.shape[0]
    head_rows = width // 8
    written = []

    def add_inward(slot):
        device = across_many(me, slot)
        part = normed_low[:, pl.ds(pl.multiple_of(device * depth, depth), depth)]
        for start in range(0, inward.shape[1], 640):
            span = pl.ds(start, 640)
            product = jnp.dot(part, inward_slots[slot, :, span], preferred_element_type=jnp.float32)
            inward[:, span] = product if slot == 0 else inward[:, span] + product
        copy = pltpu.make_async_copy(
            inward_slots.at[slot], inward_all.at[pl.ds(pl.multiple_of(device * depth, depth), depth)], in_copy.at[slot]
        )
        copy.start()
        written.append(copy)

    def add_outward(slot):
        device = across_many(me, slot)
        part = attended[:, pl.ds(pl.multiple_of(device * head_rows, head_rows), head_rows)]
        for start in range(0, width, 512):
            span = pl.ds(start, 512)
            product = jnp.dot(part, outward_slots[slot, pl.ds(0, head_rows), span], preferred_element_type=jnp.float32)
            lin_sum[:, span] = product if slot == 0 else lin_sum[:, span] + product

    def write_outward(slot):
        device = across_many(me, slot)
        rows = pl.ds(pl.multiple_of(device * head_rows, head_rows), head_rows)
        copy = pltpu.make_async_copy(outward_slots.at[slot], outward_all.at[rows], out_copy.at[slot])
        copy.start()
        written.append(copy)

    add_inward(0)
    spread_in[0].wait_recv()
    add_inward(1)
    spread_in[1].wait_recv()
    spread_in[9].start()
    spread_in[5].start()
    spread_in[2].wait_recv()
    spread_in[6].start()
    spread_in[3].wait_recv()
    spread_in[7].start()
    spread_in[4].wait_recv()
    spread_in[10].start()
    spread_in[8].start()
    add_inward(2)
    add_inward(4)
    spread_in[5].wait_recv()
    spread_in[7].wait_recv()
    add_inward(3)
    spread_in[6].wait_recv()
    spread_in[8].wait_recv()
    add_inward(5)
    spread_in[9].wait_recv()
    spread_in[11].start()
    spread_in[10].wait_recv()
    spread_in[12].start()
    for index in range(5):
        spread_out[index].start()
    add_inward(6)
    spread_in[11].wait_recv()
    spread_in[12].wait_recv()
    add_inward(7)

    query_width, key_width = QUERY_HEADS * HEAD_SIZE, KEY_VALUE_HEADS * HEAD_SIZE
    own_rows = pl.ds(0, rows_of)

    def head(start, gain):
        lane = inward[:, pl.ds(start, HEAD_SIZE)]
        scale = lax.rsqrt(jnp.mean(lane * lane, axis=-1, keepdims=True) + epsilon)
        return turn(lane * scale * gain, cosine[...], sine[...]).astype(jnp.bfloat16)

    for index in range(KEY_VALUE_HEADS):
        key_value[own_rows, pl.ds(index * HEAD_SIZE, HEAD_SIZE)] = head(
            query_width + index * HEAD_SIZE, gains[7:8, 0:HEAD_SIZE]
        )
    key_value[own_rows, pl.ds(key_width, key_width)] = inward[:, pl.ds(query_width + key_width, key_width)].astype(
        jnp.bfloat16
    )
    for distance in range(1, reach + 1):
        copy = push(
            key_value.at[own_rows],
            key_value.at[pl.ds(distance * rows_of, rows_of)],
            kv_send.at[distance - 1],
            kv_recv.at[distance - 1],
            {"ctx": (block + distance) % (others + 1)},
        )

        @pl.when(block + distance <= others)
        def _():
            copy.start()

        @pl.when(block < distance)
        def _():
            key_value[pl.ds(distance * rows_of, rows_of), :] = jnp.zeros((rows_of, 2 * key_width), jnp.bfloat16)

    for index in range(QUERY_HEADS):
        query_low[:, pl.ds(index * HEAD_SIZE, HEAD_SIZE)] = head(index * HEAD_SIZE, gains[6:7, 0:HEAD_SIZE])
    linear[...] = inward[:, pl.ds(0, query_width + key_width)]
    middle[...] = inward[:, pl.ds(query_width + 2 * key_width, middle.shape[1])].astype(jnp.bfloat16)

    spread_out[0].wait_recv()
    spread_out[1].wait_recv()
    spread_out[9].start()
    spread_out[5].start()
    spread_out[2].wait_recv()
    spread_out[6].start()
    for distance in range(1, reach + 1):
        copy = push(
            key_value.at[own_rows],
            key_value.at[pl.ds(distance * rows_of, rows_of)],
            kv_send.at[distance - 1],
            kv_recv.at[distance - 1],
            {"ctx": (block + distance) % (others + 1)},
        )

        @pl.when(block >= distance)
        def _():
            copy.wait_recv()

    allowed = window_mask(positions[...], rows_of, reach + 1)
    per_group = QUERY_HEADS // KEY_VALUE_HEADS
    for index in range(QUERY_HEADS):
        group = index // per_group
        columns = pl.ds(index * HEAD_SIZE, HEAD_SIZE)
        scores = product_back(query_low[:, columns], key_value[:, pl.ds(group * HEAD_SIZE, HEAD_SIZE)])
        scores = jnp.where(allowed, scores * HEAD_SIZE ** (-0.5), -1e30)
        grown = jnp.exp(scores - jnp.max(scores, axis=-1, keepdims=True))
        soft = (grown / jnp.sum(grown, axis=-1, keepdims=True)).astype(jnp.bfloat16)
        attended[:, columns] = jnp.dot(
            soft, key_value[:, pl.ds(key_width + group * HEAD_SIZE, HEAD_SIZE)], preferred_element_type=jnp.float32
        ).astype(jnp.bfloat16)

    for index in range(8):
        features[:, pl.ds((2 * index + 1) * share, share)] = attended[:, pl.ds(index * share, share)]
    add_outward(0)
    add_outward(1)
    write_outward(0)
    write_outward(1)
    spread_out[3].wait_recv()
    spread_out[7].start()
    spread_out[4].wait_recv()
    spread_out[10].start()
    spread_out[8].start()
    add_outward(2)
    add_outward(4)
    spread_out[5].wait_recv()
    spread_out[7].wait_recv()
    add_outward(3)
    spread_out[6].wait_recv()
    spread_out[8].wait_recv()
    add_outward(5)
    for slot in range(2, 6):
        write_outward(slot)
    spread_out[9].wait_recv()
    spread_out[11].start()
    spread_out[10].wait_recv()
    spread_out[12].start()
    add_outward(6)
    write_outward(6)
    spread_out[11].wait_recv()
    spread_out[12].wait_recv()
    add_outward(7)
    write_outward(7)
    attn_lin[...] = lin_sum[...]
    for copy in gain_copies + spread_in + spread_out:
        copy.wait_send()
    for copy in written:
        copy.wait()
    for distance in range(1, reach + 1):
        copy = push(
            key_value.at[own_rows],
            key_value.at[pl.ds(distance * rows_of, rows_of)],
            kv_send.at[distance - 1],
            kv_recv.at[distance - 1],
            {"ctx": (block + distance) % (others + 1)},
        )

        @pl.when(block + distance <= others)
        def _():
            copy.wait_send()


def attend_call(reach, source, gains, head_gains, laurel_own, positions, cosine, sine, inward_own, outward_own):
    rows_of, width = source.shape
    others = lax.axis_size("ctx") - 1
    low, full = jnp.bfloat16, jnp.float32
    hbm = pl.BlockSpec(memory_space=pl.ANY)
    vmem = pl.BlockSpec(memory_space=pltpu.VMEM)
    dma = pltpu.SemaphoreType.DMA
    depth = inward_own[0].shape[0]
    columns = sum(piece.shape[1] for piece in inward_own)
    columns += -columns % 128
    gain_shape = (16, width)
    query_width, key_width = QUERY_HEADS * HEAD_SIZE, KEY_VALUE_HEADS * HEAD_SIZE
    tail = columns - query_width - 2 * key_width
    shapes = [
        jax.ShapeDtypeStruct((rows_of, width), full),
        jax.ShapeDtypeStruct((8, width), full),
        jax.ShapeDtypeStruct((rows_of, query_width + key_width), full),
        jax.ShapeDtypeStruct((rows_of, query_width), low),
        jax.ShapeDtypeStruct(((reach + 1) * rows_of, 2 * key_width), low),
        jax.ShapeDtypeStruct((rows_of, 2 * width), low),
        jax.ShapeDtypeStruct((rows_of, tail), low),
        jax.ShapeDtypeStruct((rows_of, width), full),
        jax.ShapeDtypeStruct((tail, width), full),
        jax.ShapeDtypeStruct((8 * depth, columns), low),
        jax.ShapeDtypeStruct((8 * outward_own.shape[0], width), low),
    ]
    return pl.pallas_call(
        functools.partial(attend_kernel, others, reach),
        out_shape=shapes,
        in_specs=[vmem] * 17,
        out_specs=[vmem] * 9 + [hbm] * 2,
        scratch_shapes=[
            pltpu.VMEM(gain_shape, full),
            pltpu.VMEM((8, *gain_shape), low),
            pltpu.VMEM((8, depth, columns), low),
            pltpu.VMEM((8, *outward_own.shape), low),
            pltpu.VMEM((rows_of, width), low),
            pltpu.VMEM((rows_of, query_width), low),
            pltpu.VMEM((rows_of, columns), full),
            pltpu.VMEM((rows_of, width), full),
            dma((7,)),
            dma((7,)),
            dma((13,)),
            dma((13,)),
            dma((13,)),
            dma((13,)),
            dma((max(reach, 1),)),
            dma((max(reach, 1),)),
            dma((8,)),
            dma((8,)),
        ],
        compiler_params=pltpu.CompilerParams(collective_id=3, has_side_effects=True, vmem_limit_bytes=56 * 2**20),
        cost_estimate=pl.CostEstimate(
            flops=60 * rows_of * width * columns, bytes_accessed=20 * depth * columns, transcendentals=0
        ),
        name="attend_forward",
    )(source, *gains, head_gains, laurel_own, positions, cosine, sine, *inward_own, outward_own)


def turn_norm_grad(upstream, linear, gain, cosine, sine):
    scale = lax.rsqrt(jnp.mean(linear * linear, axis=-1, keepdims=True) + epsilon)
    unit = linear * scale
    back = turn(upstream, cosine, sine, -1.0)
    grad_gain = jnp.sum(back * unit, axis=0, keepdims=True)
    back = back * gain
    return scale * (back - unit * jnp.mean(back * unit, axis=-1, keepdims=True)), grad_gain


def attend_back_kernel(
    others, reach, d_ffn_in, mixed, d_residual, laurel_lin, attn_lin, laurel, gain_part,
    query_low, key_value, linear, gains, positions, cosine, sine, middle, features,
    source, residual, d_vector, gated_value, d_back, outward_all, inward_all, d_rows,
    d_source, grad_wide, grad_small, near_hbm,
    d_lin, d_half, d_laurel, d_middle, gain_rows,
    outward, inward, d_attended, d_key_value, parcel, arrived, d_query, d_rest, lin_slots, query_slots, rest_slots,
    ordered, d_normed, gain_parcel, gain_arrived, laurel_arrived, load_sem, lin_send, lin_recv, query_send, query_recv, rest_send, rest_recv, kv_send, kv_recv, gain_send, gain_recv, laurel_send, laurel_recv, near_send, near_recv,
    gate_in, gate_sum, gate_arrived, out_in, out_sum, out_arrived, pair_send, pair_recv, chip_send, chip_recv,
    gate_parts, out_parts, laurel_rows,
):
    rows_of, width = source.shape
    me, block = lax.axis_index("fsdp"), lax.axis_index("ctx")
    query_width, key_width = QUERY_HEADS * HEAD_SIZE, KEY_VALUE_HEADS * HEAD_SIZE
    per_group = QUERY_HEADS // KEY_VALUE_HEADS
    depth = width // 8
    loads = [
        pltpu.make_async_copy(outward_all.at[pl.ds(index * depth, depth)], outward.at[index % 2], load_sem.at[index])
        for index in range(8)
    ]
    loads.append(pltpu.make_async_copy(inward_all, inward, load_sem.at[8]))
    for index in (0, 1, 8):
        loads[index].start()

    def before_attention():
        d_mixed, grad_before = norm_rows_grad(mixed[...], gains[3:4, :], d_ffn_in[...])
        d_half[...] = (d_residual[...] + d_mixed) * inv_root
        d_branch, grad_laurel_gain = norm_rows_grad(laurel_lin[...], gains[2:3, :], d_half[...])
        d_laurel[...] = d_branch.astype(jnp.bfloat16)
        d_middle[...] = product_back(d_laurel[...], laurel[...].astype(jnp.bfloat16)).astype(jnp.bfloat16)
        d_branch, grad_attention = norm_rows_grad(attn_lin[...], gains[1:2, :], d_half[...])
        d_lin[...] = d_branch.astype(jnp.bfloat16)
        gain_rows[...] = gain_part[...]
        gain_rows[1:2, :] = grad_attention
        gain_rows[2:3, :] = grad_laurel_gain
        gain_rows[3:4, :] = grad_before

    greet(me, range(1, 8), block, others, before_attention)
    mine, theirs = pl.ds(0, rows_of), pl.ds(rows_of, rows_of)
    near = [
        push(
            d_rows.at[pl.ds(group * 2 * rows_of, rows_of)],
            near_hbm.at[group, mine],
            near_send.at[group],
            near_recv.at[group],
            {"ctx": across(block, 1)},
        )
        for group in range(4)
    ]
    near_share = [
        push(
            near_hbm.at[group, mine],
            near_hbm.at[group, theirs],
            near_send.at[4 + group],
            near_recv.at[4 + group],
            {"fsdp": across(me, 1)},
        )
        for group in range(4)
    ]
    for copy in near[:2]:
        copy.start()
    vector_parts = ((gate_parts, gate_in, gate_sum, gate_arrived), (out_parts, out_in, out_sum, out_arrived))
    chips = (0, 2, 4, 6)
    pair_copies = []
    chip_copies = []
    for kind, (parts, pair_in, pair_sum, arrived_parts) in enumerate(vector_parts):
        for index, chip in enumerate(chips):
            place = 4 * kind + index
            pair_copies.append(
                push(
                    parts.at[across_many(me, chip + 1)],
                    pair_in.at[index],
                    pair_send.at[place],
                    pair_recv.at[place],
                    {"fsdp": across(me, 1)},
                )
            )
            if chip:
                place = 3 * kind + index - 1
                chip_copies.append(
                    push(
                        pair_sum.at[index - 1],
                        arrived_parts.at[index - 1],
                        chip_send.at[place],
                        chip_recv.at[place],
                        {"fsdp": across_many(me, chip)},
                    )
                )
    spread_lin = spread_copies(d_lin, lin_slots, lin_send, lin_recv, me)
    spread_query = spread_copies(d_query, query_slots, query_send, query_recv, me)
    spread_rest = spread_copies(d_rest, rest_slots, rest_send, rest_recv, me)
    for index in range(5):
        spread_lin[index].start()
    lin_slots[0] = d_lin[...]
    for index in range(8):
        gate_parts[index] = product_rows(residual[:, pl.ds(index * depth, depth)], d_vector[...]).astype(jnp.bfloat16)
    out_parts[...] = product_rows(gated_value[...], d_back[...]).reshape(out_parts.shape).astype(jnp.bfloat16)
    laurel_rows[...] = product_rows(middle[...], d_laurel[...])[0 : 8 * laurel_rows.shape[1]].reshape(laurel_rows.shape)
    for copy in pair_copies:
        copy.start()
    laurel_copies = [
        push(
            laurel_rows.at[across_many(me, distance)],
            laurel_arrived.at[distance],
            laurel_send.at[distance - 1],
            laurel_recv.at[distance - 1],
            {"fsdp": across_many(me, distance)},
        )
        for distance in range(1, 8)
    ]
    laurel_arrived[0] = laurel_rows[me]
    for slot in range(8):
        device = across_many(me, slot)
        ordered[pl.ds(slot * rows_of, rows_of), :] = features[
            pl.ds(pl.multiple_of(device * rows_of, rows_of), rows_of), :
        ]
    for index in range(8):
        loads[index].wait()
        d_attended[:, pl.ds(index * depth, depth)] = product_back(d_lin[...], outward[index % 2]).astype(jnp.bfloat16)
        if index + 2 < 8:
            loads[index + 2].start()

    allowed = window_mask(positions[...], rows_of, reach + 1)
    scale = HEAD_SIZE ** (-0.5)

    def one_head(index):
        group = index // per_group
        columns = pl.ds(index * HEAD_SIZE, HEAD_SIZE)
        keys = pl.ds(group * HEAD_SIZE, HEAD_SIZE)
        values = pl.ds(key_width + group * HEAD_SIZE, HEAD_SIZE)
        scores = product_back(query_low[:, columns], key_value[:, keys])
        scores = jnp.where(allowed, scores * scale, -1e30)
        grown = jnp.exp(scores - jnp.max(scores, axis=-1, keepdims=True))
        soft = grown / jnp.sum(grown, axis=-1, keepdims=True)
        d_soft = product_back(d_attended[:, columns], key_value[:, values])
        d_scores = (soft * (d_soft - jnp.sum(soft * d_soft, axis=-1, keepdims=True))).astype(jnp.bfloat16)
        upstream = scale * jnp.dot(d_scores, key_value[:, keys], preferred_element_type=jnp.float32)
        d_key = scale * product_rows(d_scores, query_low[:, columns])
        d_value = product_rows(soft.astype(jnp.bfloat16), d_attended[:, columns])
        if index % per_group == 0:
            d_key_value[:, keys] = d_key
            d_key_value[:, values] = d_value
        else:
            d_key_value[:, keys] += d_key
            d_key_value[:, values] += d_value
        d_head, grad_gain = turn_norm_grad(upstream, linear[:, columns], gains[6:7, 0:HEAD_SIZE], cosine[...], sine[...])
        d_query[:, columns] = d_head.astype(jnp.bfloat16)
        return grad_gain

    query_gain = one_head(0)
    for index in range(1, per_group):
        query_gain = query_gain + one_head(index)
    spread_lin[0].wait_recv()
    spread_lin[1].wait_recv()
    spread_lin[9].start()
    spread_lin[5].start()
    spread_lin[2].wait_recv()
    spread_lin[6].start()
    for index in range(per_group, QUERY_HEADS):
        query_gain = query_gain + one_head(index)
    parcel[...] = d_key_value[pl.ds(rows_of, reach * rows_of), :].astype(jnp.bfloat16)

    def return_copy(distance):
        span = pl.ds((distance - 1) * rows_of, rows_of)
        return push(
            parcel.at[span],
            arrived.at[span],
            kv_send.at[distance - 1],
            kv_recv.at[distance - 1],
            {"ctx": (block + others + 1 - distance) % (others + 1)},
        )

    for distance in range(1, reach + 1):
        copy = return_copy(distance)

        @pl.when(block >= distance)
        def _():
            copy.start()

        @pl.when(block + distance > others)
        def _():
            arrived[pl.ds((distance - 1) * rows_of, rows_of), :] = jnp.zeros((rows_of, 2 * key_width), jnp.bfloat16)

    for copy in near[2:]:
        copy.start()
    spread_lin[3].wait_recv()
    spread_lin[7].start()
    spread_lin[4].wait_recv()
    spread_lin[10].start()
    spread_lin[8].start()
    for index in range(5):
        spread_query[index].start()
    for copy in pair_copies:
        copy.wait_recv()
    for parts, pair_in, pair_sum, arrived_parts in vector_parts:
        for index, chip in enumerate(chips):
            if chip:
                pair_sum[index - 1] = (
                    parts[across_many(me, chip)].astype(jnp.float32) + pair_in[index].astype(jnp.float32)
                ).astype(jnp.bfloat16)
    for copy in chip_copies:
        copy.start()
    query_slots[0] = d_query[...]
    loads[8].wait()
    d_normed[...] = product_back(d_query[...], inward[:, pl.ds(0, query_width)])
    spread_lin[9].wait_recv()
    spread_lin[11].start()
    spread_lin[10].wait_recv()
    spread_lin[12].start()
    spread_query[0].wait_recv()
    spread_query[1].wait_recv()
    spread_query[9].start()
    spread_query[5].start()
    spread_query[2].wait_recv()
    spread_query[6].start()
    for index in (5, 6, 7, 8, 11, 12):
        spread_lin[index].wait_recv()
    grad_wide[:, pl.ds(inward.shape[1], width)] = product_rows(
        ordered[:, pl.ds(depth, depth)], lin_slots[...].reshape(8 * rows_of, width)
    ).astype(jnp.bfloat16)

    for distance in range(1, reach + 1):
        copy = return_copy(distance)

        @pl.when(block + distance <= others)
        def _():
            copy.wait_recv()

    total = d_key_value[pl.ds(0, rows_of), :]
    for distance in range(1, reach + 1):
        total = total + arrived[pl.ds((distance - 1) * rows_of, rows_of), :].astype(jnp.float32)
    for index in range(KEY_VALUE_HEADS):
        columns = pl.ds(index * HEAD_SIZE, HEAD_SIZE)
        d_head, grad_gain = turn_norm_grad(
            total[:, index * HEAD_SIZE : (index + 1) * HEAD_SIZE],
            linear[:, pl.ds(query_width + index * HEAD_SIZE, HEAD_SIZE)],
            gains[7:8, 0:HEAD_SIZE],
            cosine[...],
            sine[...],
        )
        d_rest[:, columns] = d_head.astype(jnp.bfloat16)
        key_gain = grad_gain if index == 0 else key_gain + grad_gain
    d_rest[:, pl.ds(key_width, key_width)] = total[:, key_width:].astype(jnp.bfloat16)
    d_rest[:, pl.ds(2 * key_width, d_middle.shape[1])] = d_middle[...]
    spread_query[3].wait_recv()
    spread_query[7].start()
    spread_query[4].wait_recv()
    spread_query[10].start()
    spread_query[8].start()
    for index in range(5):
        spread_rest[index].start()
    rest_slots[0] = d_rest[...]
    rest_width = d_rest.shape[1]
    d_normed[...] += product_back(d_rest[...], inward[:, pl.ds(query_width, rest_width)])
    value = source[...].astype(jnp.float32)
    factor = lax.rsqrt(jnp.mean(value * value, axis=-1, keepdims=True) + epsilon)
    unit = value * factor
    upstream = d_half[...] + d_normed[...]
    for index in range(8):
        columns = slice(index * depth, (index + 1) * depth)
        gain_parcel[index, 0:8, :] = gain_rows[0:8, columns]
        gain_parcel[index, 0:1, :] = jnp.sum(upstream[:, columns] * unit[:, columns], axis=0, keepdims=True)
        gain_parcel[index, 6:7, :] = query_gain
        gain_parcel[index, 7:8, :] = key_gain
    gain_copies = [
        push(
            gain_parcel.at[across_many(me, distance)],
            gain_arrived.at[distance],
            gain_send.at[distance - 1],
            gain_recv.at[distance - 1],
            {"fsdp": across_many(me, distance)},
        )
        for distance in range(1, 8)
    ]
    for copy in gain_copies + laurel_copies:
        copy.start()
    gain_arrived[0] = gain_parcel[me]
    upstream = upstream * gains[0:1, :]
    d_source[...] = d_half[...] + factor * (upstream - unit * jnp.mean(upstream * unit, axis=-1, keepdims=True))
    spread_rest[0].wait_recv()
    spread_rest[1].wait_recv()
    spread_rest[9].start()
    spread_rest[5].start()
    spread_rest[2].wait_recv()
    spread_rest[6].start()
    spread_query[9].wait_recv()
    spread_query[11].start()
    spread_query[10].wait_recv()
    spread_query[12].start()
    spread_rest[3].wait_recv()
    spread_rest[7].start()
    spread_rest[4].wait_recv()
    spread_rest[10].start()
    spread_rest[8].start()
    for index in (5, 6, 7, 8, 11, 12):
        spread_query[index].wait_recv()
    grad_wide[:, pl.ds(0, query_width)] = product_rows(
        ordered[:, pl.ds(0, depth)], query_slots[...].reshape(8 * rows_of, query_width)
    ).astype(jnp.bfloat16)
    spread_rest[9].wait_recv()
    spread_rest[11].start()
    spread_rest[10].wait_recv()
    spread_rest[12].start()
    for index in (5, 6, 7, 8, 11, 12):
        spread_rest[index].wait_recv()
    grad_wide[:, pl.ds(query_width, rest_width)] = product_rows(
        ordered[:, pl.ds(0, depth)], rest_slots[...].reshape(8 * rows_of, rest_width)
    ).astype(jnp.bfloat16)
    for copy, share in zip(near, near_share):
        copy.wait_recv()
        share.start()
    for copy in gain_copies + laurel_copies + chip_copies:
        copy.wait_recv()
    totals = []
    for parts, pair_in, pair_sum, arrived_parts in vector_parts:
        total = parts[me].astype(jnp.float32) + pair_in[0].astype(jnp.float32)
        for index in range(3):
            total = total + arrived_parts[index].astype(jnp.float32)
        totals.append(total.astype(jnp.bfloat16))
    grad_wide[:, pl.ds(inward.shape[1] + width, totals[0].shape[1])] = totals[0]
    laurel_size = laurel_rows.shape[1]
    tail = jnp.concatenate(
        [jnp.sum(laurel_arrived[...], axis=0), jnp.pad(jnp.sum(gain_arrived[...], axis=0), ((0, 0), (0, width - depth)))],
        axis=0,
    )
    out_size = totals[1].shape[0]
    grad_small[pl.ds(0, out_size), :] = totals[1]
    grad_small[pl.ds(out_size, laurel_size + 8), :] = tail.astype(jnp.bfloat16)
    for copy in near_share:
        copy.wait_recv()
    for copy in (
        spread_lin + spread_query + spread_rest + gain_copies + laurel_copies + near + near_share + pair_copies + chip_copies
    ):
        copy.wait_send()
    for distance in range(1, reach + 1):
        copy = return_copy(distance)

        @pl.when(block >= distance)
        def _():
            copy.wait_send()


def attend_back_call(
    reach, d_ffn_in, mixed, d_residual, laurel_lin, attn_lin, laurel, gain_part,
    query_low, key_value, linear, gains, positions, cosine, sine, middle, features,
    source, residual, d_vector, gated_value, d_back, outward_all, inward_all, d_rows,
):
    rows_of, width = source.shape
    others = lax.axis_size("ctx") - 1
    low, full = jnp.bfloat16, jnp.float32
    hbm = pl.BlockSpec(memory_space=pl.ANY)
    vmem = pl.BlockSpec(memory_space=pltpu.VMEM)
    dma = pltpu.SemaphoreType.DMA
    columns = inward_all.shape[1]
    query_width, key_width = QUERY_HEADS * HEAD_SIZE, KEY_VALUE_HEADS * HEAD_SIZE
    rest_width = columns - query_width
    depth = width // 8
    vector_width = d_vector.shape[1]
    part_shapes = ((depth, vector_width), (vector_width // 8, width))
    shapes = [
        jax.ShapeDtypeStruct((rows_of, width), full),
        jax.ShapeDtypeStruct((depth, columns + width + vector_width), low),
        jax.ShapeDtypeStruct((vector_width // 8 + 16, width), low),
        jax.ShapeDtypeStruct((4, 2 * rows_of, width), low),
    ]
    spans = max(reach, 1)
    return pl.pallas_call(
        functools.partial(attend_back_kernel, others, reach),
        out_shape=shapes,
        in_specs=[vmem] * 21 + [hbm] * 3,
        out_specs=[vmem] * 3 + [hbm],
        scratch_shapes=[
            pltpu.VMEM((rows_of, width), low),
            pltpu.VMEM((rows_of, width), full),
            pltpu.VMEM((rows_of, width), low),
            pltpu.VMEM(middle.shape, low),
            pltpu.VMEM((8, width), full),
            pltpu.VMEM((2, depth, width), low),
            pltpu.VMEM((width, columns), low),
            pltpu.VMEM((rows_of, query_width), low),
            pltpu.VMEM(((reach + 1) * rows_of, 2 * key_width), full),
            pltpu.VMEM((spans * rows_of, 2 * key_width), low),
            pltpu.VMEM((spans * rows_of, 2 * key_width), low),
            pltpu.VMEM((rows_of, query_width), low),
            pltpu.VMEM((rows_of, rest_width), low),
            pltpu.VMEM((8, rows_of, width), low),
            pltpu.VMEM((8, rows_of, query_width), low),
            pltpu.VMEM((8, rows_of, rest_width), low),
            pltpu.VMEM((8 * rows_of, 2 * depth), low),
            pltpu.VMEM((rows_of, width), full),
            pltpu.VMEM((8, 8, depth), full),
            pltpu.VMEM((8, 8, depth), full),
            pltpu.VMEM((8, 8, width), full),
            dma((9,)),
            dma((13,)),
            dma((13,)),
            dma((13,)),
            dma((13,)),
            dma((13,)),
            dma((13,)),
            dma((spans,)),
            dma((spans,)),
            dma((7,)),
            dma((7,)),
            dma((7,)),
            dma((7,)),
            dma((8,)),
            dma((8,)),
        ]
        + [
            pltpu.VMEM((count, *shape), low)
            for shape in part_shapes
            for count in (4, 3, 3)
        ]
        + [dma((8,)), dma((8,)), dma((6,)), dma((6,))]
        + [pltpu.VMEM((8, *shape), low) for shape in part_shapes]
        + [pltpu.VMEM((8, 8, width), full)],
        compiler_params=pltpu.CompilerParams(collective_id=4, has_side_effects=True, vmem_limit_bytes=60 * 2**20),
        cost_estimate=pl.CostEstimate(
            flops=40 * rows_of * width * columns, bytes_accessed=6 * width * columns, transcendentals=0
        ),
        name="attend_backward",
    )(
        d_ffn_in, mixed, d_residual, laurel_lin, attn_lin, laurel, gain_part,
        query_low, key_value, linear, gains, positions, cosine, sine, middle, features,
        source, residual, d_vector, gated_value, d_back, outward_all, inward_all, d_rows,
    )


def feed_call(forward, prelude, weights, kept=(), features=None, forward_rows=None, vectors=()):
    rows_of, width = prelude[0].shape
    hidden = weights[0].shape[0]
    all_rows = 8 * rows_of
    others = lax.axis_size("ctx") - 1
    low, full = jnp.bfloat16, jnp.float32
    count_made = 3 if forward else 2
    hbm = pl.BlockSpec(memory_space=pl.ANY)
    vmem = pl.BlockSpec(memory_space=pltpu.VMEM)
    half = rows_of // 2
    dma = pltpu.SemaphoreType.DMA

    def shape(columns, kind, rows=rows_of):
        return jax.ShapeDtypeStruct((rows, columns), kind)

    operands = (*prelude, *weights, *kept)
    operand_specs = [vmem] * len(prelude) + [hbm] * (3 + len(kept))
    shapes = [shape(width, full)]
    extra = []
    if forward:
        shapes += [shape(width, full)] * 2
        operands += (features, *vectors)
        operand_specs += [vmem] * 3
        extra = (
            [dma((7,)), dma((7,)), dma]
            + [pltpu.VMEM((8, *value.shape), low) for value in vectors]
            + [dma((13,))] * 4
            + [dma((8,))] * 2
        )
    else:
        vector_width = prelude[5].shape[1]
        shapes += [shape(width, low), shape(vector_width, full), shape(width, low), shape(vector_width, low)]
        shapes += [shape(vector_width, low), shape(width, low), shape(width, full), shape(width, full, 8)]
        operands += (forward_rows,)
        operand_specs += [hbm]
    count_vmem = len(shapes)
    shapes += [
        shape(width, low, all_rows),
        jax.ShapeDtypeStruct((2, rows_of, width), low),
        jax.ShapeDtypeStruct((2, 2 * rows_of, width), low),
    ]
    if forward:
        shapes += [jax.ShapeDtypeStruct((8, rows_of, features.shape[1] // 8), low)]
        shapes += [shape(value.shape[1], low, 8 * value.shape[0]) for value in vectors]
    shapes += [shape(hidden, low, all_rows)] * count_made
    return pl.pallas_call(
        functools.partial(feed_kernel, forward, rows_of, others),
        out_shape=shapes,
        in_specs=operand_specs,
        out_specs=[vmem] * count_vmem + [hbm] * (len(shapes) - count_vmem),
        scratch_shapes=[pltpu.VMEM((hidden, width), low)] * 3
        + [pltpu.VMEM((all_rows, hidden), low)] * (len(kept) + count_made)
        + [
            pltpu.VMEM((rows_of, width), low),
            pltpu.VMEM((4, 2 * rows_of, width), low),
            pltpu.VMEM((4, 2 * rows_of, width), low),
            pltpu.VMEM((4, rows_of, width), low),
            pltpu.VMEM((3, rows_of, width), low),
            pltpu.VMEM((2, half, width), low),
            pltpu.VMEM((2, half, width), low),
            pltpu.VMEM((4, half, width), low),
            dma((20,)),
            dma((20,)),
            dma((3 + len(kept),)),
            dma((4 * (1 + count_made),)),
            dma((2,)),
            dma((2,)),
            dma((4,)),
            dma((4,)),
        ]
        + extra,
        compiler_params=pltpu.CompilerParams(
            collective_id=1 if forward else 2,
            has_side_effects=True,
            vmem_limit_bytes=58 * 2**20,
        ),
        cost_estimate=pl.CostEstimate(
            flops=40 * all_rows * hidden * width // 2,
            bytes_accessed=6 * hidden * width + 8 * all_rows * width,
            transcendentals=0,
        ),
        name="feed_forward" if forward else "feed_backward",
    )(*operands)


def other_rows(rows, d_rows, gate, up, down, hidden_tile, d_gate_tile, d_up_tile):
    tile = min(512, gate.shape[0])

    def body(index, carry):
        span = pl.ds(pl.multiple_of(index * tile, tile), tile)
        gate_value = product_back(gate[span, :], rows[...])
        up_value = product_back(up[span, :], rows[...])
        d_hidden = product_back(down[span, :], d_rows[...])
        value, slope = gelu_parts(gate_value)
        hidden_tile[span, :] = (value * up_value).astype(jnp.bfloat16)
        d_gate_tile[span, :] = (d_hidden * up_value * slope).astype(jnp.bfloat16)
        d_up_tile[span, :] = (d_hidden * value).astype(jnp.bfloat16)
        return carry

    lax.fori_loop(0, gate.shape[0] // tile, body, 0)


def add_weight_grads(grads, tiles, rows, d_rows, first=False):
    hidden_tile, d_gate_tile, d_up_tile = tiles
    for grad, tile, right in zip(grads, (d_gate_tile, d_up_tile, hidden_tile), (rows, rows, d_rows)):
        product = matrix_product(tile[...], right[...])
        if first:
            grad[...] = product
        else:
            grad[...] += product


def weight_part_kernel(
    own_steps, near_steps, gate, up, down, rows, d_rows, hidden, d_gate, d_up, rows_near, rows_next, d_rows_near,
    far_own,
    grad_gate, grad_up, grad_down, far_all,
    hidden_tile, d_gate_tile, d_up_tile, send_sem, recv_sem, own_sem,
):
    step = pl.program_id(0)
    last = own_steps + near_steps - 1
    me = lax.axis_index("fsdp")
    grads = (grad_gate, grad_up, grad_down)
    tiles = (hidden_tile, d_gate_tile, d_up_tile)

    sibling, beside, above = across(me, 1), across(me, 2), across(me, 4)
    diagonal = across(beside, 4)
    plan = [(far_own, far_all.at[me], sibling)]
    for part in range(2):
        plan += [(far_own.at[part], far_all.at[me, part], beside), (far_own.at[part], far_all.at[me, part], above)]
    for part in range(2):
        plan += [(far_all.at[device, part], far_all.at[device, part], sibling) for device in (beside, above)]
    plan.append((far_all.at[beside, 0], far_all.at[beside, 0], above))
    plan.append((far_all.at[above, 1], far_all.at[above, 1], beside))
    plan += [(far_all.at[diagonal, part], far_all.at[diagonal, part], sibling) for part in range(2)]
    copies = [
        push(source, target, send_sem.at[index], recv_sem.at[index], {"fsdp": partner})
        for index, (source, target, partner) in enumerate(plan)
    ]
    own_copy = pltpu.make_async_copy(far_own, far_all.at[me], own_sem)

    @pl.when(step == 0)
    def _():
        greet(me, (1, 2, 4), 0, 0)
        own_copy.start()
        for index in range(5):
            copies[index].start()

    @pl.when(step == own_steps - 1)
    def _():
        copies[0].wait_recv()
        copies[1].wait_recv()
        copies[9].start()
        copies[5].start()
        copies[2].wait_recv()
        copies[6].start()

    @pl.when(step == own_steps + 1)
    def _():
        copies[3].wait_recv()
        copies[7].start()
        copies[4].wait_recv()
        copies[10].start()
        copies[8].start()

    @pl.when(step == last)
    def _():
        copies[9].wait_recv()
        copies[11].start()
        copies[10].wait_recv()
        copies[12].start()

    @pl.when(step < own_steps)
    def _():
        hidden_tile[...] = hidden[...].T
        d_gate_tile[...] = d_gate[...].T
        d_up_tile[...] = d_up[...].T

    @pl.when(step == 0)
    def _():
        add_weight_grads(grads, tiles, rows, d_rows, True)

    @pl.when((step > 0) & (step < own_steps))
    def _():
        add_weight_grads(grads, tiles, rows, d_rows)

    @pl.when((step >= own_steps) & (step < own_steps + near_steps // 2))
    def _():
        other_rows(rows_near, d_rows_near, gate, up, down, *tiles)
        add_weight_grads(grads, tiles, rows_near, d_rows_near)

    @pl.when(step >= own_steps + near_steps // 2)
    def _():
        other_rows(rows_next, d_rows_near, gate, up, down, *tiles)
        add_weight_grads(grads, tiles, rows_next, d_rows_near)

    @pl.when(step == last)
    def _():
        for index in (5, 6, 7, 8, 11, 12):
            copies[index].wait_recv()
        own_copy.wait()
        for copy in copies:
            copy.wait_send()


def weight_rest_kernel(
    gate, up, down, rows, d_rows, gate_part, up_part, down_part,
    grad_gate, grad_up, grad_down, hidden_tile, d_gate_tile, d_up_tile, part_sem,
):
    step = pl.program_id(0)
    grads = (grad_gate, grad_up, grad_down)
    tiles = (hidden_tile, d_gate_tile, d_up_tile)
    loads = [
        pltpu.make_async_copy(source, target, part_sem.at[index])
        for index, (source, target) in enumerate(zip((gate_part, up_part, down_part), grads))
    ]

    @pl.when(step == 0)
    def _():
        for load in loads:
            load.start()

    other_rows(rows, d_rows, gate, up, down, *tiles)

    @pl.when(step == 0)
    def _():
        for load in loads:
            load.wait()

    add_weight_grads(grads, tiles, rows, d_rows)


def weight_grad_calls(
    gate, up, down, rows, d_rows, hidden, d_gate, d_up, rows_near, rows_next, d_rows_near, rows_far, far_own,
    tok=256, far_tok=512,
):
    size, width = gate.shape
    low = jnp.bfloat16
    own_steps = near_steps = rows.shape[0] // tok
    hbm = pl.BlockSpec(memory_space=pl.ANY)
    dma = pltpu.SemaphoreType.DMA

    def stream(first, steps, columns):
        return pl.BlockSpec((tok, columns), lambda s: (jnp.clip(s - first, 0, steps - 1), 0))

    weight = pl.BlockSpec((size, width), lambda s: (0, 0))
    own, own_mid = stream(0, own_steps, width), stream(0, own_steps, size)
    near_one = stream(own_steps, near_steps // 2, width)
    near_two = stream(own_steps + near_steps // 2, near_steps // 2, width)
    near = stream(own_steps, near_steps, width)
    grad = jax.ShapeDtypeStruct((size, width), jnp.float32)
    *parts, far_all = pl.pallas_call(
        functools.partial(weight_part_kernel, own_steps, near_steps),
        grid=(own_steps + near_steps,),
        in_specs=[weight] * 3 + [own] * 2 + [own_mid] * 3 + [near_one, near_two, near, hbm],
        out_specs=[weight] * 3 + [hbm],
        out_shape=[grad] * 3 + [jax.ShapeDtypeStruct((8, *far_own.shape), low)],
        scratch_shapes=[pltpu.VMEM((size, tok), low)] * 3 + [dma((13,)), dma((13,)), dma],
        compiler_params=pltpu.CompilerParams(
            dimension_semantics=("arbitrary",), vmem_limit_bytes=62 * 2**20, collective_id=5, has_side_effects=True
        ),
        cost_estimate=pl.CostEstimate(
            flops=18 * size * width * rows.shape[0], bytes_accessed=80 * 2**20, transcendentals=0
        ),
        name="weight_grads_part",
    )(gate, up, down, rows, d_rows, hidden, d_gate, d_up, rows_near, rows_next, d_rows_near, far_own)
    far = pl.BlockSpec((far_tok, width), lambda s: (s, 0))
    return pl.pallas_call(
        weight_rest_kernel,
        grid=(rows_far.shape[0] // far_tok,),
        in_specs=[weight] * 3 + [far] * 2 + [hbm] * 3,
        out_specs=[weight] * 3,
        out_shape=[grad] * 3,
        scratch_shapes=[pltpu.VMEM((size, far_tok), low)] * 3 + [dma((3,))],
        compiler_params=pltpu.CompilerParams(dimension_semantics=("arbitrary",), vmem_limit_bytes=62 * 2**20),
        cost_estimate=pl.CostEstimate(
            flops=12 * size * width * rows_far.shape[0], bytes_accessed=80 * 2**20, transcendentals=0
        ),
        name="weight_grads_rest",
    )(gate, up, down, rows_far, far_all.reshape(-1, width), *parts)


def finish_kernel(
    key_width, wide, small, result_in, d_vectors_in, d_source_in,
    result, d_source, d_vectors, query, key, value, output, down, up, gate, out,
    gain_one, gain_two, gain_three, gain_four, gain_five, gain_six, query_gain, key_gain,
):
    result[...] = result_in[...]
    d_vectors[...] = d_vectors_in[...]
    d_source[...] = d_source_in[...]
    query_width = query.shape[1]
    start = 0
    for target, columns in (
        (query, query_width),
        (key, key_width),
        (value, key_width),
        (down, down.shape[1]),
    ):
        target[...] = wide[:, start : start + columns].astype(jnp.float32)
        start += columns
    start += -start % 128
    output[...] = wide[:, start : start + output.shape[1]].astype(jnp.float32)
    start += output.shape[1]
    gate[...] = wide[:, start : start + gate.shape[1]].astype(jnp.float32)
    lines = small[...].astype(jnp.float32)
    first = out.shape[0]
    out[...] = lines[0:first]
    up[...] = lines[first : first + up.shape[0]]
    first += up.shape[0]
    for index, target in enumerate((gain_one, gain_two, gain_three, gain_four, gain_five, gain_six)):
        target[...] = lines[first + index : first + index + 1, 0 : target.shape[1]]
    me = lax.axis_index("fsdp")
    for index, target in enumerate((query_gain, key_gain)):
        size = target.shape[1]
        line = lines[first + 6 + index : first + 7 + index, 0 : 8 * size]
        total = jnp.zeros((1, size), jnp.float32)
        for device in range(8):
            total = total + jnp.where(me == device, line[:, device * size : (device + 1) * size], 0.0)
        target[...] = total


def finish_call(wide, small, result, d_vectors, d_source, shapes, key_width):
    vmem = pl.BlockSpec(memory_space=pltpu.VMEM)
    kinds = [jnp.bfloat16] + [jnp.float32] * (len(shapes) - 1)
    return pl.pallas_call(
        functools.partial(finish_kernel, key_width),
        out_shape=[jax.ShapeDtypeStruct(shape, kind) for shape, kind in zip(shapes, kinds)],
        in_specs=[vmem] * 5,
        out_specs=[vmem] * len(shapes),
        compiler_params=pltpu.CompilerParams(vmem_limit_bytes=40 * 2**20),
        name="finish",
    )(wide, small, result, d_vectors, d_source)


def per_device(
    tokens,
    per_layer,
    segments,
    positions,
    cotangent,
    query_weight,
    key_matrix,
    value_matrix,
    output_weight,
    laurel_down,
    laurel_up,
    vector_gate,
    vector_out,
    norm_input,
    norm_attention,
    norm_laurel,
    norm_before,
    norm_after,
    norm_vector,
    query_norm_gain,
    norm_key,
    hidden_gate,
    hidden_up,
    hidden_down,
):
    count_of_rows = tokens.shape[0]
    shards = lax.axis_size("fsdp")
    width = tokens.shape[1]
    heads_per_group = QUERY_HEADS // KEY_VALUE_HEADS
    reach_blocks = min((WINDOW + count_of_rows - 2) // count_of_rows, lax.axis_size("ctx") - 1)
    score_scale = HEAD_SIZE ** (-0.5)
    fused = shards == 8 and lax.axis_size("ctx") == 4
    query_width = query_weight.shape[1]
    key_width = key_matrix.shape[1]

    gain_shards = (
        norm_input,
        norm_attention,
        norm_laurel,
        norm_before,
        norm_after,
        norm_vector,
        query_norm_gain,
        norm_key,
    )
    gain_sizes = [gain.shape[0] for gain in gain_shards]
    gain_starts = [sum(gain_sizes[:index]) for index in range(len(gain_sizes))]
    source = tokens.astype(jnp.float32)
    vectors = per_layer.astype(jnp.float32)
    rank = laurel_down.shape[1]
    unused, allowed = window(positions, count_of_rows, reach_blocks)

    def head_facing(linear, gain):
        return rotary_apply(root_mean_norm(linear, gain), positions)

    if fused:
        me = lax.axis_index("fsdp")
        head_gains = jnp.stack([query_norm_gain, norm_key])
        place = jnp.arange(HEAD_SIZE) // head_gains.shape[1] == me
        head_gains = jnp.where(place[None, :], jnp.tile(head_gains, (1, shards)), 0).astype(jnp.bfloat16)
        cosine, sine_part = rotary_tables(positions, HEAD_SIZE)
        (
            normed,
            gains_all,
            linear,
            query_lowered,
            key_value,
            features,
            middle_low,
            attn_lin,
            full_laurel_up,
            full_inward,
            full_output,
        ) = attend_call(
            reach_blocks,
            tokens,
            [gain.reshape(-1, 128) for gain in gain_shards[:6]],
            head_gains,
            laurel_up,
            positions[:, None],
            cosine,
            sine_part,
            (query_weight, key_matrix, value_matrix, laurel_down),
            output_weight,
        )
    else:
        gain_line = jnp.concatenate(gain_shards)
        gain_line = jnp.pad(gain_line, (0, -gain_line.shape[0] % 2048)).reshape(-1, 128)
        gains_all = gather(gain_line, "fsdp").reshape(shards, -1)
        gains = [
            gains_all[:, start : start + size].reshape(-1).astype(jnp.float32)
            for start, size in zip(gain_starts, gain_sizes)
        ]
        inward_weight = jnp.concatenate([query_weight, key_matrix, value_matrix, laurel_down], axis=1)
        inward_weight = jnp.pad(inward_weight, ((0, 0), (0, -inward_weight.shape[1] % 128)))
        full_inward = gather(inward_weight, "fsdp")
        full_output, full_vector_gate, full_vector_out, full_laurel_up = [
            gather(value, "fsdp") for value in (output_weight, vector_gate, vector_out, laurel_up)
        ]
        normed = root_mean_norm(source, gains[0])
        lowered_normed = normed.astype(jnp.bfloat16)
        inward = matrix_product(lowered_normed, full_inward)
        linear = inward[:, : query_width + key_width]
        value_lowered = inward[:, query_width + key_width : query_width + 2 * key_width].astype(jnp.bfloat16)
        laurel_mid = inward[:, query_width + 2 * key_width :][:, :rank].astype(jnp.bfloat16)
        query_lowered = head_facing(
            linear[:, :query_width].reshape(count_of_rows, QUERY_HEADS, HEAD_SIZE), gains[6]
        ).astype(jnp.bfloat16)
        key_lowered = head_facing(
            linear[:, query_width:].reshape(count_of_rows, KEY_VALUE_HEADS, HEAD_SIZE), gains[7]
        ).astype(jnp.bfloat16)
        key_value = jnp.stack([key_lowered.reshape(count_of_rows, -1), value_lowered])
        pair_blocks = [key_value]
        for distance in range(1, reach_blocks + 1):
            pair_blocks.append(from_behind(key_value, "ctx", distance))
        window_couple = jnp.concatenate(pair_blocks, axis=1)
        window_keys, window_values = window_couple[0], window_couple[1]
    if fused:
        (
            feed_value,
            mixed,
            laurel_lin,
            rows_all,
            rows_far,
            rows_near,
            slices,
            full_vector_gate,
            full_vector_out,
            hidden_all,
            lift_all,
            bend_all,
        ) = feed_call(
            True,
            (tokens, normed, attn_lin, middle_low, full_laurel_up, gains_all),
            (hidden_gate, hidden_up, hidden_down),
            features=features,
            vectors=(vector_gate, vector_out),
        )
        slices = slices.reshape(shards * count_of_rows, -1)
        rows_far = gather(rows_far.reshape(-1, width), "fsdp")
        (
            d_ffn_in,
            result,
            d_vectors,
            residual_low,
            d_vector_lin_low,
            gated_low,
            d_vector_back_low,
            d_residual,
            gain_rows,
            d_rows_all,
            d_rows_far,
            rows_next,
            d_gate_low,
            d_up_low,
        ) = feed_call(
            False,
            (feed_value, mixed, gains_all, full_vector_gate, full_vector_out, per_layer, cotangent),
            (hidden_down, hidden_gate, hidden_up),
            (lift_all, bend_all),
            forward_rows=rows_all,
        )
        d_ffn_in, rows_far = lax.optimization_barrier((d_ffn_in, rows_far))
        d_source, grad_wide, grad_small, d_rows_near = attend_back_call(
            reach_blocks, d_ffn_in, mixed, d_residual, laurel_lin, attn_lin, full_laurel_up, gain_rows,
            query_lowered, key_value, linear, gains_all, positions[:, None], cosine, sine_part, middle_low, slices,
            tokens, residual_low, d_vector_lin_low, gated_low, d_vector_back_low, full_output, full_inward, d_rows_all,
        )
        grad_hidden_gate, grad_hidden_up, grad_hidden_down = weight_grad_calls(
            hidden_gate,
            hidden_up,
            hidden_down,
            rows_all,
            d_rows_all,
            hidden_all,
            d_gate_low,
            d_up_low,
            rows_near.reshape(-1, width),
            rows_next.reshape(-1, width),
            d_rows_near.reshape(-1, width),
            rows_far,
            d_rows_far,
        )
    else:
        (
            gain_input,
            gain_attention,
            gain_laurel,
            gain_before,
            gain_after,
            gain_vector,
            gain_query,
            key_norm_gain,
        ) = gains
        query_linear = linear[:, :query_width].reshape(count_of_rows, QUERY_HEADS, HEAD_SIZE)
        key_linear = linear[:, query_width:].reshape(count_of_rows, KEY_VALUE_HEADS, HEAD_SIZE)
        query_lowered = query_lowered.reshape(count_of_rows, KEY_VALUE_HEADS, heads_per_group, HEAD_SIZE)
        window_keys = window_keys.reshape(-1, KEY_VALUE_HEADS, HEAD_SIZE)
        window_values = window_values.reshape(-1, KEY_VALUE_HEADS, HEAD_SIZE)

        def masked_scores():
            raw_scores = score_scale * jnp.einsum(
                "tgfd,kgd->gftk", query_lowered, window_keys, preferred_element_type=jnp.float32
            )
            return jnp.where(allowed, raw_scores, -1e30)

        scores_first = masked_scores()
        row_peak = jnp.max(scores_first, axis=-1, keepdims=True)
        exp_scores = jnp.exp(scores_first - row_peak)
        row_total = jnp.sum(exp_scores, axis=-1, keepdims=True)
        log_total = row_peak + jnp.log(row_total)
        soft_low = (exp_scores / row_total).astype(jnp.bfloat16)
        attended_low = (
            jnp.einsum("gftk,kgd->tgfd", soft_low, window_values, preferred_element_type=jnp.float32)
            .reshape(count_of_rows, QUERY_HEADS * HEAD_SIZE)
            .astype(jnp.bfloat16)
        )
        attn_lin = matrix_product(attended_low, full_output)
        residual_one = source + root_mean_norm(attn_lin, gain_attention)
        laurel_lin = matrix_product(laurel_mid, full_laurel_up)
        mixed = (residual_one + normed + root_mean_norm(laurel_lin, gain_laurel)) * inv_root
        ffn_in = root_mean_norm(mixed, gain_before).astype(jnp.bfloat16)
        normed_slices = feature_slices(lowered_normed)
        attended_slices = feature_slices(attended_low)
        rows_all = gather(ffn_in, "fsdp")
        gate_all = product_back(rows_all, hidden_gate)
        up_all = product_back(rows_all, hidden_up)
        hidden_all = gated(gate_all, up_all).astype(jnp.bfloat16)
        feed_value = scatter_sum(matrix_product(hidden_all, hidden_down))
        residual_two = mixed + root_mean_norm(feed_value, gain_after)
        residual_low = residual_two.astype(jnp.bfloat16)
        vector_lin = matrix_product(residual_low, full_vector_gate)
        gated_low = gated(vector_lin, vectors).astype(jnp.bfloat16)
        vector_back = matrix_product(gated_low, full_vector_out)
        result = residual_two + root_mean_norm(vector_back, gain_vector)
        upstream = cotangent.astype(jnp.float32)
        d_vector_back, grad_gain_vector = norm_grad(vector_back, gain_vector, upstream)
        d_vector_back_low = d_vector_back.astype(jnp.bfloat16)
        grad_vector_out = product_rows(gated_low, d_vector_back_low)
        d_gated = product_back(d_vector_back_low, full_vector_out)
        d_vector_lin, d_vectors = gated_grad(vector_lin, vectors, d_gated)
        d_vector_lin_low = d_vector_lin.astype(jnp.bfloat16)
        grad_vector_gate = product_rows(residual_low, d_vector_lin_low)
        d_residual = upstream + product_back(d_vector_lin_low, full_vector_gate)
        d_feed, grad_gain_after = norm_grad(feed_value, gain_after, d_residual)
        d_feed_low = d_feed.astype(jnp.bfloat16)
        d_rows_all = gather(d_feed_low, "fsdp")
        d_hidden = product_back(d_rows_all, hidden_down)
        d_gate_all, d_up_all = gated_grad(gate_all, up_all, d_hidden)
        d_gate_low = d_gate_all.astype(jnp.bfloat16)
        d_up_low = d_up_all.astype(jnp.bfloat16)
        d_ffn_in = scatter_sum(
            matrix_product(d_gate_low, hidden_gate) + matrix_product(d_up_low, hidden_up)
        )

        grad_hidden_gate, grad_hidden_up, grad_hidden_down = [
            lax.psum(grad.astype(jnp.bfloat16), "ctx").astype(jnp.float32)
            for grad in (
                product_rows(d_gate_low, rows_all),
                product_rows(d_up_low, rows_all),
                product_rows(hidden_all, d_rows_all),
            )
        ]

        d_mixed_part, grad_gain_before = norm_grad(mixed, gain_before, d_ffn_in)
        d_half = (d_residual + d_mixed_part) * inv_root
        d_laurel_lin, grad_gain_laurel = norm_grad(laurel_lin, gain_laurel, d_half)
        d_laurel_low = d_laurel_lin.astype(jnp.bfloat16)
        grad_laurel_up = product_rows(laurel_mid, d_laurel_low)
        d_laurel_mid = product_back(d_laurel_low, full_laurel_up).astype(jnp.bfloat16)
        d_attn_lin, grad_gain_attention = norm_grad(attn_lin, gain_attention, d_half)
        d_attn_low = d_attn_lin.astype(jnp.bfloat16)
        d_attended = (
            product_back(d_attn_low, full_output)
            .astype(jnp.bfloat16)
            .reshape(count_of_rows, KEY_VALUE_HEADS, heads_per_group, HEAD_SIZE)
        )
        soft_again = jnp.exp(masked_scores() - log_total)
        d_soft = jnp.einsum(
            "tgfd,kgd->gftk", d_attended, window_values, preferred_element_type=jnp.float32
        )
        d_scores = (
            soft_again * (d_soft - jnp.sum(soft_again * d_soft, axis=-1, keepdims=True))
        ).astype(jnp.bfloat16)
        d_query = score_scale * jnp.einsum(
            "gftk,kgd->tgfd", d_scores, window_keys, preferred_element_type=jnp.float32
        )
        grad_key_rows = score_scale * jnp.einsum(
            "gftk,tgfd->kgd", d_scores, query_lowered, preferred_element_type=jnp.float32
        )
        grad_value_rows = jnp.einsum(
            "gftk,tgfd->kgd",
            soft_again.astype(jnp.bfloat16),
            d_attended,
            preferred_element_type=jnp.float32,
        )
        grad_window_couple = jnp.stack(
            [
                grad_key_rows.reshape(-1, KEY_VALUE_HEADS * HEAD_SIZE),
                grad_value_rows.reshape(-1, KEY_VALUE_HEADS * HEAD_SIZE),
            ]
        )
        grad_own_part = grad_window_couple[:, :count_of_rows]
        for distance in range(1, reach_blocks + 1):
            grad_own_part = grad_own_part + from_behind(
                grad_window_couple[:, distance * count_of_rows : (distance + 1) * count_of_rows].astype(
                    jnp.bfloat16
                ),
                "ctx",
                -distance,
            ).astype(jnp.float32)
        unused, query_pull = jax.vjp(head_facing, query_linear, gain_query)
        d_query_lin, grad_gain_query = query_pull(
            d_query.reshape(count_of_rows, QUERY_HEADS, HEAD_SIZE)
        )
        unused, key_pullback_fn = jax.vjp(head_facing, key_linear, key_norm_gain)
        grad_key_linear, grad_key_norm_gain = key_pullback_fn(
            grad_own_part[0].reshape(count_of_rows, KEY_VALUE_HEADS, HEAD_SIZE)
        )
        d_inward = jnp.concatenate(
            [
                d_query_lin.reshape(count_of_rows, QUERY_HEADS * HEAD_SIZE).astype(jnp.bfloat16),
                grad_key_linear.reshape(count_of_rows, KEY_VALUE_HEADS * HEAD_SIZE).astype(
                    jnp.bfloat16
                ),
                grad_own_part[1].astype(jnp.bfloat16),
                d_laurel_mid,
                jnp.zeros((count_of_rows, full_inward.shape[1] - query_width - 2 * key_width - rank), jnp.bfloat16),
            ],
            axis=1,
        )
        grad_inward = product_rows(normed_slices, gather(d_inward, "fsdp")).astype(jnp.bfloat16)
        grad_output = product_rows(attended_slices, gather(d_attn_low, "fsdp")).astype(jnp.bfloat16)
        grad_wide = jnp.concatenate([grad_inward, grad_output], axis=1)
        small_rows = jnp.concatenate(
            [
                grad_vector_gate.reshape(shards, -1, width),
                grad_vector_out.reshape(shards, -1, width),
                grad_laurel_up.reshape(shards, -1, width),
            ],
            axis=1,
        ).astype(jnp.bfloat16)
        grad_small = lax.psum_scatter(small_rows, "fsdp", scatter_dimension=0, tiled=False)
        d_normed = d_half + product_back(d_inward, full_inward)
        d_source_part, grad_gain_input = norm_grad(source, gain_input, d_normed)
        d_source = d_half + d_source_part
        gain_lines = jnp.concatenate(
            [
                grad.reshape(shards, -1)
                for grad in (
                    grad_gain_input,
                    grad_gain_attention,
                    grad_gain_laurel,
                    grad_gain_before,
                    grad_gain_after,
                    grad_gain_vector,
                    grad_gain_query,
                    grad_key_norm_gain,
                )
            ],
            axis=1,
        )
        gain_share = lax.psum_scatter(gain_lines, "fsdp", scatter_dimension=0, tiled=False)
        gain_count = gain_share.shape[0]
        gain_share = jnp.pad(gain_share, (0, -gain_count % width)).astype(jnp.bfloat16)
        grad_small = jnp.concatenate([grad_small, gain_share.reshape(-1, width)], axis=0)

    grad_wide, grad_small = lax.psum((grad_wide, grad_small), "ctx")
    hidden_grads = (grad_hidden_gate, grad_hidden_up, grad_hidden_down)
    if fused:
        weights = (query_weight, key_matrix, value_matrix, output_weight, laurel_down, laurel_up, vector_gate, vector_out)
        shapes = [tokens.shape, tokens.shape, per_layer.shape] + [weight.shape for weight in weights]
        shapes += [(1, size) for size in gain_sizes]
        finished = finish_call(grad_wide, grad_small, result, d_vectors, d_source, shapes, key_width)
        gains_from = len(shapes) - len(gain_sizes)
        return tuple(finished[:gains_from]) + tuple(gain.reshape(-1) for gain in finished[gains_from:]) + hidden_grads
    grad_wide, grad_small = grad_wide.astype(jnp.float32), grad_small.astype(jnp.float32)
    inward_width = full_inward.shape[1]
    grad_inward = grad_wide[:, :inward_width]
    grad_output = grad_wide[:, inward_width:]
    out_rows, laurel_rows = vector_out.shape[0], laurel_up.shape[0]
    gate_rows = vector_gate.shape[0] * vector_gate.shape[1] // width
    share_vector_gate = grad_small[:gate_rows].reshape(vector_gate.shape)
    share_vector_out = grad_small[gate_rows : gate_rows + out_rows]
    gain_start = gate_rows + out_rows + laurel_rows
    share_laurel_up = grad_small[gate_rows + out_rows : gain_start]
    gain_share = grad_small[gain_start:].reshape(-1)
    gain_grads = tuple(gain_share[start : start + size] for start, size in zip(gain_starts, gain_sizes))
    value_start = query_width + key_width
    return (
        (
            result.astype(jnp.bfloat16),
            d_source,
            d_vectors,
            grad_inward[:, :query_width],
            grad_inward[:, query_width:value_start],
            grad_inward[:, value_start : value_start + key_width],
            grad_output,
            grad_inward[:, value_start + key_width : value_start + key_width + rank],
            share_laurel_up,
            share_vector_gate,
            share_vector_out,
        )
        + gain_grads
        + hidden_grads
    )


def solution(mesh):
    rows = P(("fsdp", "ctx"), None)
    line = P(("fsdp", "ctx"))
    weight = P("fsdp", None)
    gain = P("fsdp")
    return jax.shard_map(
        per_device,
        mesh=mesh,
        in_specs=(rows, rows, line, line, rows) + (weight,) * 8 + (gain,) * 8 + (weight,) * 3,
        out_specs=(rows,) * 3 + (weight,) * 8 + (gain,) * 8 + (weight,) * 3,
        check_vma=False,
    )
```

```python
import functools

import jax
import jax.numpy as jnp
from jax import lax
from jax.experimental import pallas as pl
from jax.experimental.pallas import tpu as pltpu
from jax.sharding import PartitionSpec as P

QUERY_HEADS = 8
KEY_VALUE_HEADS = 2
HEAD_SIZE = 256
WINDOW = 1024


epsilon = 1e-06
rope_base = 10000.0
inv_root = 0.7071067811865476
gelu_scale = 0.7978845608028654
gelu_cubic = 0.044715


def from_behind(value, axis, steps):
    count = lax.axis_size(axis)
    initial, last = (max(0, -steps), min(count, count - steps))
    return lax.ppermute(value, axis, [(source, source + steps) for source in range(initial, last)])


def other_blocks(value, axis):
    count = lax.axis_size(axis)
    return jnp.concatenate(
        [
            lax.ppermute(value, axis, [(source, (source + step) % count) for source in range(count)])
            for step in range(1, count)
        ],
        axis=0,
    )


def root_mean_norm(value, gain):
    factor = lax.rsqrt(jnp.mean(value * value, axis=-1, keepdims=True) + epsilon)
    return value * factor * gain


def gelu_tanh(value):
    return jax.nn.gelu(value, approximate=True)


def gated(gate_value, up_value):
    return gelu_tanh(gate_value) * up_value


def rotary_apply(value, token_position):
    half_size = value.shape[-1] // 2
    frequency = rope_base ** (-2.0 * jnp.arange(half_size, dtype=jnp.float32) / value.shape[-1])
    angle = token_position.astype(jnp.float32)[:, None] * frequency[None, :]
    cosine = jnp.cos(angle)[:, None, :]
    sine_part = jnp.sin(angle)[:, None, :]
    first_half = value[..., :half_size]
    second_half = value[..., half_size:]
    return jnp.concatenate(
        [
            first_half * cosine - second_half * sine_part,
            second_half * cosine + first_half * sine_part,
        ],
        axis=-1,
    )


def rotary_tables(token_position, size):
    half_size = size // 2
    frequency = rope_base ** (-2.0 * jnp.arange(half_size, dtype=jnp.float32) / size)
    angle = token_position.astype(jnp.float32)[:, None] * frequency[None, :]
    return jnp.cos(angle), jnp.sin(angle)


def window(positions, rows_of, reach):
    key_offset = jnp.concatenate(
        [distance * rows_of - jnp.arange(rows_of, dtype=jnp.int32) for distance in range(reach + 1)]
    )
    key_gap = jnp.arange(rows_of, dtype=jnp.int32)[:, None] + key_offset[None, :]
    return key_gap, (key_gap >= 0) & (key_gap <= positions[:, None]) & (key_gap < WINDOW)


def matrix_product(left, right):
    return jnp.dot(left, right, preferred_element_type=jnp.float32)


def product_back(left, right):
    return lax.dot_general(
        left, right, (((1,), (1,)), ((), ())), preferred_element_type=jnp.float32
    )


def product_rows(left, right):
    return lax.dot_general(
        left, right, (((0,), (0,)), ((), ())), preferred_element_type=jnp.float32
    )


def norm_grad(value, gain, upstream):
    unused, pullback = jax.vjp(root_mean_norm, value, gain)
    return pullback(upstream)


def gated_grad(gate_value, up_value, upstream):
    unused, pullback = jax.vjp(gated, gate_value, up_value)
    return pullback(upstream)


def gather(value, axis):
    return lax.all_gather(value, axis, axis=0, tiled=True)


def feature_slices(value):
    count = lax.axis_size("fsdp")
    rows = value.shape[0]
    return lax.all_to_all(
        value.reshape(rows, count, -1), "fsdp", split_axis=1, concat_axis=0, tiled=True
    ).reshape(count * rows, -1)


def scatter_sum(value):
    return lax.psum_scatter(
        value.astype(jnp.bfloat16), "fsdp", scatter_dimension=0, tiled=True
    ).astype(jnp.float32)


def gelu_parts(gate):
    square = gate * gate
    bend = jnp.tanh(gelu_scale * gate * (1.0 + gelu_cubic * square))
    half_up = 0.5 * (1.0 + bend)
    slope = half_up + 0.5 * gate * (1.0 - bend * bend) * (
        gelu_scale * (1.0 + 3.0 * gelu_cubic * square)
    )
    return gate * half_up, slope


def across(me, stride):
    return me + stride - 2 * stride * ((me // stride) % 2)


def across_many(me, bits):
    for stride in (1, 2, 4):
        if bits & stride:
            me = across(me, stride)
    return me


def feed_kernel(forward, rows_of, others, *refs):
    half = rows_of // 2
    if forward:
        (source, normed, attn_lin, middle, laurel, gains), refs = refs[:6], refs[6:]
        (gate_hbm, up_hbm, down_hbm, features, gate_own, out_own), refs = refs[:6], refs[6:]
        (total, mixed, laurel_lin, rows_hbm, far_hbm, near_hbm), refs = refs[:6], refs[6:]
        (slices_hbm, gate_all, out_all, hidden_hbm, lift_hbm, bend_hbm), rest = refs[:6], refs[6:]
        weights_hbm, kept_hbm, made_hbm = (gate_hbm, up_hbm, down_hbm), (), (hidden_hbm, lift_hbm, bend_hbm)
    else:
        (feed_value, mixed, gains, gate_all, out_all, vectors, cotangent), refs = refs[:7], refs[7:]
        (down_hbm, gate_hbm, up_hbm, lift_hbm, bend_hbm, forward_rows, hidden_in), refs = refs[:7], refs[7:]
        (total, result, d_vectors, residual_low, d_vector_low, gated_low, d_back_low, d_residual, gain_rows), refs = (
            refs[:9],
            refs[9:],
        )
        (rows_hbm, far_hbm, near_hbm, *part_hbm, d_gate_hbm, d_up_hbm), rest = refs[:8], refs[8:]
        weights_hbm, kept_hbm, made_hbm = (down_hbm, gate_hbm, up_hbm), (lift_hbm, bend_hbm), (d_gate_hbm, d_up_hbm)
    count_kept, count_made = len(kept_hbm), len(made_hbm)
    weights = rest[:3]
    kept = rest[3 : 3 + count_kept]
    made = rest[3 + count_kept : 3 + count_kept + count_made]
    (own, rows, part, sib_in, chip_sum, relay_in, relay_sum, last_in, send_sem, recv_sem, in_sem, out_sem, far_send, far_recv, near_send, near_recv, *extra) = rest[
        3 + count_kept + count_made :
    ]
    hidden = weights[0].shape[0]
    width = weights[0].shape[1]
    me = lax.axis_index("fsdp")
    sibling, beside, above = across(me, 1), across(me, 2), across(me, 4)

    loads = [
        pltpu.make_async_copy(source, target, in_sem.at[index])
        for index, (source, target) in enumerate(zip(weights_hbm + kept_hbm, tuple(weights) + tuple(kept)))
    ]
    for load in loads:
        load.start()

    block = lax.axis_index("ctx")
    def before_feed():
        def unit(value):
            return value * lax.rsqrt(jnp.mean(value * value, axis=-1, keepdims=True) + epsilon)

        laurel_lin[...] = jnp.dot(middle[...], laurel[...].astype(jnp.bfloat16), preferred_element_type=jnp.float32)
        value = source[...].astype(jnp.float32) + unit(attn_lin[...]) * gains[1:2, :] + normed[...]
        value = (value + unit(laurel_lin[...]) * gains[2:3, :]) * inv_root
        mixed[...] = value
        own[...] = (unit(value) * gains[3:4, :]).astype(jnp.bfloat16)

    def after_feed():
        def unit(value):
            return value * lax.rsqrt(jnp.mean(value * value, axis=-1, keepdims=True) + epsilon)

        residual = mixed[...] + unit(feed_value[...]) * gains[4:5, :]
        residual_low[...] = residual.astype(jnp.bfloat16)
        vector_lin = jnp.dot(residual_low[...], gate_all[...], preferred_element_type=jnp.float32)
        value, slope = gelu_parts(vector_lin)
        per_token = vectors[...].astype(jnp.float32)
        gated_low[...] = (value * per_token).astype(jnp.bfloat16)
        vector_back = jnp.dot(gated_low[...], out_all[...], preferred_element_type=jnp.float32)
        result[...] = (residual + unit(vector_back) * gains[5:6, :]).astype(jnp.bfloat16)
        upstream = cotangent[...].astype(jnp.float32)
        d_back, grad_vector_gain = norm_rows_grad(vector_back, gains[5:6, :], upstream)
        d_back_low[...] = d_back.astype(jnp.bfloat16)
        d_gated = product_back(d_back_low[...], out_all[...])
        d_vectors[...] = d_gated * value
        d_vector_low[...] = (d_gated * per_token * slope).astype(jnp.bfloat16)
        d_residual[...] = upstream + product_back(d_vector_low[...], gate_all[...])
        d_feed, grad_after_gain = norm_rows_grad(feed_value[...], gains[4:5, :], d_residual[...])
        own[...] = d_feed.astype(jnp.bfloat16)
        gain_rows[...] = jnp.zeros_like(gain_rows)
        gain_rows[4:5, :] = grad_after_gain
        gain_rows[5:6, :] = grad_vector_gain

    greet(me, range(1, 8) if forward else (1, 2, 4), block, others, before_feed if forward else after_feed)

    def send(index, source, target, partner):
        return pltpu.make_async_remote_copy(
            src_ref=source,
            dst_ref=target,
            send_sem=send_sem.at[index],
            recv_sem=recv_sem.at[index],
            device_id={"fsdp": partner},
            device_id_type=pl.DeviceIdType.MESH,
        )

    low, high = pl.ds(0, half), pl.ds(half, half)
    mine, theirs = pl.ds(0, rows_of), pl.ds(rows_of, rows_of)
    copies = [
        send(0, own, rows.at[0, theirs], sibling),
        send(1, own.at[low], rows.at[1, low], beside),
        send(2, own.at[low], rows.at[1, high], above),
        send(3, own.at[high], rows.at[2, low], beside),
        send(4, own.at[high], rows.at[2, high], above),
        send(5, rows.at[1, mine], rows.at[1, theirs], sibling),
        send(6, rows.at[2, mine], rows.at[2, theirs], sibling),
        send(7, rows.at[1, low], rows.at[3, low], above),
        send(8, rows.at[2, high], rows.at[3, high], beside),
        send(9, rows.at[3, mine], rows.at[3, theirs], sibling),
        send(10, part.at[0, theirs], sib_in.at[0], sibling),
        send(11, part.at[1, theirs], sib_in.at[1], sibling),
        send(12, part.at[2, theirs], sib_in.at[2], sibling),
        send(13, part.at[3, theirs], sib_in.at[3], sibling),
        send(14, chip_sum.at[0, high], last_in.at[2], above),
        send(15, chip_sum.at[1, low], last_in.at[1], beside),
        send(16, chip_sum.at[2, low], relay_in.at[0], above),
        send(17, chip_sum.at[2, high], relay_in.at[1], beside),
        send(18, relay_sum.at[0], last_in.at[0], beside),
        send(19, relay_sum.at[1], last_in.at[3], above),
    ]
    outs = []

    def write_out(source, target):
        copy = pltpu.make_async_copy(source, target, out_sem.at[len(outs)])
        copy.start()
        outs.append(copy)

    for index in range(5):
        copies[index].start()
    spreads = []
    if forward:
        gate_slots, out_slots, gate_send, gate_recv, vec_send, vec_recv, gate_out, vec_out = extra[3:]
        spreads = [
            spread_copies(gate_own, gate_slots, gate_send, gate_recv, me),
            spread_copies(out_own, out_slots, vec_send, vec_recv, me),
        ]
        for spread in spreads:
            for index in range(5):
                spread[index].start()
        gate_slots[0] = gate_own[...]
        out_slots[0] = out_own[...]
    far = [
        push(own, far_hbm.at[index], far_send.at[index], far_recv.at[index], {"ctx": across_many(block, 2 + index)})
        for index in range(2)
    ]
    for copy in far:
        copy.start()
    def near_source(index):
        if forward:
            return rows.at[1, mine] if index else own
        return forward_rows.at[pl.ds((2 + index) * 2 * rows_of, rows_of)]

    near = [
        push(near_source(index), near_hbm.at[index, mine], near_send.at[index], near_recv.at[index], {"ctx": across(block, 1)})
        for index in range(2)
    ]
    near_share = [
        push(
            near_hbm.at[index, mine],
            near_hbm.at[index, theirs],
            near_send.at[2 + index],
            near_recv.at[2 + index],
            {"fsdp": sibling},
        )
        for index in range(2)
    ]
    near[0].start()
    if not forward:
        near[1].start()
    rows[0, mine] = own[...]
    slices = []
    if forward:
        share = features.shape[1] // 8

        def share_of(device):
            return features.at[:, pl.ds(pl.multiple_of(device * share, share), share)]

        own_slice = pltpu.make_async_copy(share_of(me), slices_hbm.at[me], extra[2])
        own_slice.start()
        slices = [
            pltpu.make_async_remote_copy(
                src_ref=share_of(across_many(me, distance)),
                dst_ref=slices_hbm.at[me],
                send_sem=extra[0].at[distance - 1],
                recv_sem=extra[1].at[distance - 1],
                device_id={"fsdp": across_many(me, distance)},
                device_id_type=pl.DeviceIdType.MESH,
            )
            for distance in range(1, 8)
        ]

    tile = min(hidden, 1024)
    wide = min(width, 1024)

    def first_stage(group):
        span = pl.ds(group * 2 * rows_of, 2 * rows_of)

        def step(index, carry):
            columns = pl.ds(pl.multiple_of(index * tile, tile), tile)
            left = rows[group]

            def back(weight):
                return lax.dot_general(
                    left, weight[columns, :], (((1,), (1,)), ((), ())), preferred_element_type=jnp.float32
                )

            if forward:
                gate, up = back(weights[0]), back(weights[1])
                value, slope = gelu_parts(gate)
                made[0][span, columns] = (value * up).astype(jnp.bfloat16)
                made[1][span, columns] = value.astype(jnp.bfloat16)
                made[2][span, columns] = (slope * up).astype(jnp.bfloat16)
            else:
                d_hidden = back(weights[0])
                made[0][span, columns] = (d_hidden * kept[1][span, columns].astype(jnp.float32)).astype(jnp.bfloat16)
                made[1][span, columns] = (d_hidden * kept[0][span, columns].astype(jnp.float32)).astype(jnp.bfloat16)
            return carry

        lax.fori_loop(0, hidden // tile, step, 0)

    def second_stage(group):
        span = pl.ds(group * 2 * rows_of, 2 * rows_of)

        def step(index, carry):
            columns = pl.ds(pl.multiple_of(index * wide, wide), wide)
            if forward:
                value = jnp.dot(made[0][span, :], weights[2][:, columns], preferred_element_type=jnp.float32)
            else:
                value = jnp.dot(made[0][span, :], weights[1][:, columns], preferred_element_type=jnp.float32)
                value = value + jnp.dot(made[1][span, :], weights[2][:, columns], preferred_element_type=jnp.float32)
            part[group, :, columns] = value.astype(jnp.bfloat16)
            return carry

        lax.fori_loop(0, width // wide, step, 0)

    fillers = []
    if not forward:
        hidden_rows, forward_all, tiles, hidden_sem, forward_sem, tile_sem = extra
        side_loads = [
            pltpu.make_async_copy(hidden_in, hidden_rows, hidden_sem),
            pltpu.make_async_copy(forward_rows, forward_all, forward_sem),
        ]
        tile_width = tiles.shape[2]
        tiles_each = width // tile_width
        tile_copies = [
            pltpu.make_async_copy(
                tiles.at[index % 2],
                part_hbm[index // tiles_each].at[:, pl.ds((index % tiles_each) * tile_width, tile_width)],
                tile_sem.at[index],
            )
            for index in range(3 * tiles_each)
        ]

        def weight_tile(index):
            kind, columns = index // tiles_each, pl.ds((index % tiles_each) * tile_width, tile_width)
            if index >= 2:
                tile_copies[index - 2].wait()
            if kind == 2:
                right = rows[:, :, columns].reshape(8 * rows_of, tile_width)
                tiles[index % 2] = product_rows(hidden_rows[...], right)
            else:
                tiles[index % 2] = product_rows(made[kind][...], forward_all[:, columns])
            tile_copies[index].start()

        fillers = [functools.partial(weight_tile, index) for index in range(3 * tiles_each)]

    def fill(count):
        for unused in range(min(count, len(fillers))):
            fillers.pop(0)()

    def keep_out(group):
        span = pl.ds(group * 2 * rows_of, 2 * rows_of)
        write_out(rows.at[group], rows_hbm.at[span])
        for source, target in zip(made, made_hbm):
            write_out(source.at[span], target.at[span])

    def add_chip(group):
        chip_sum[group - 1] = (
            part[group, mine].astype(jnp.float32) + sib_in[group].astype(jnp.float32)
        ).astype(jnp.bfloat16)

    if not forward:
        for load in side_loads:
            load.start()
    copies[0].wait_recv()
    loads[0].wait()
    if forward:
        loads[1].wait()
    else:
        loads[3].wait()
        loads[4].wait()
    first_stage(0)
    if forward:
        loads[2].wait()
    else:
        loads[1].wait()
        loads[2].wait()
    second_stage(0)
    copies[10].start()
    keep_out(0)
    copies[1].wait_recv()
    copies[7].start()
    copies[2].wait_recv()
    copies[5].start()
    if forward:
        near[1].start()
    copies[5].wait_recv()
    first_stage(1)
    second_stage(1)
    copies[11].start()
    keep_out(1)
    copies[3].wait_recv()
    copies[4].wait_recv()
    copies[8].start()
    copies[6].start()
    copies[11].wait_recv()
    add_chip(1)
    copies[14].start()
    copies[6].wait_recv()
    first_stage(2)
    second_stage(2)
    copies[12].start()
    keep_out(2)
    for copy in slices:
        copy.start()
    for spread in spreads:
        for index in range(1, 5):
            spread[index].wait_recv()
        for index in range(5, 11):
            spread[index].start()
    copies[7].wait_recv()
    copies[8].wait_recv()
    copies[9].start()
    copies[12].wait_recv()
    add_chip(2)
    copies[15].start()
    copies[9].wait_recv()
    first_stage(3)
    second_stage(3)
    copies[13].start()
    keep_out(3)
    if not forward:
        for load in side_loads:
            load.wait()
    fill(1)
    copies[13].wait_recv()
    add_chip(3)
    copies[16].start()
    copies[17].start()
    for spread in spreads:
        for index in (9, 10):
            spread[index].wait_recv()
        for index in (11, 12):
            spread[index].start()
    fill(4)
    copies[10].wait_recv()
    total[...] = part[0, mine].astype(jnp.float32) + sib_in[0].astype(jnp.float32)
    copies[16].wait_recv()
    relay_sum[0] = (chip_sum[0, low].astype(jnp.float32) + relay_in[0].astype(jnp.float32)).astype(jnp.bfloat16)
    copies[18].start()
    copies[17].wait_recv()
    relay_sum[1] = (chip_sum[1, high].astype(jnp.float32) + relay_in[1].astype(jnp.float32)).astype(jnp.bfloat16)
    copies[19].start()
    fill(4)
    copies[14].wait_recv()
    total[low] = total[low] + last_in[2].astype(jnp.float32)
    copies[15].wait_recv()
    total[high] = total[high] + last_in[1].astype(jnp.float32)
    for index in range(2):
        near[index].wait_recv()
        near_share[index].start()
    copies[18].wait_recv()
    total[low] = total[low] + last_in[0].astype(jnp.float32)
    fill(len(fillers))
    copies[19].wait_recv()
    total[high] = total[high] + last_in[3].astype(jnp.float32)
    if not forward:
        for copy in tile_copies[-2:]:
            copy.wait()
    if forward:
        for spread, slots, target, sems in (
            (spreads[0], gate_slots, gate_all, gate_out),
            (spreads[1], out_slots, out_all, vec_out),
        ):
            for index in (0, 5, 6, 7, 8, 11, 12):
                spread[index].wait_recv()
            size = slots.shape[1]
            for slot in range(8):
                place = pl.ds(pl.multiple_of(across_many(me, slot) * size, size), size)
                copy = pltpu.make_async_copy(slots.at[slot], target.at[place], sems.at[slot])
                copy.start()
                outs.append(copy)
            for copy in spread:
                copy.wait_send()
    for copy in copies:
        copy.wait_send()
    for copy in outs:
        copy.wait()
    for copy in far + slices:
        copy.wait()
    for index in range(2):
        near[index].wait_send()
        near_share[index].wait()
    if forward:
        own_slice.wait()


def turn(value, cosine, sine, direction=1.0):
    middle = value.shape[1] // 2
    first, second = value[:, :middle], value[:, middle:]
    sine = sine * direction
    return jnp.concatenate([first * cosine - second * sine, second * cosine + first * sine], axis=1)


def window_mask(positions, rows_of, blocks):
    query_row = lax.broadcasted_iota(jnp.int32, (rows_of, blocks * rows_of), 0)
    column = lax.broadcasted_iota(jnp.int32, (rows_of, blocks * rows_of), 1)
    behind = column // rows_of
    gap = query_row + 2 * behind * rows_of - column
    return (gap >= 0) & (gap <= positions) & (gap < WINDOW)


def norm_rows_grad(value, gain, upstream):
    factor = lax.rsqrt(jnp.mean(value * value, axis=-1, keepdims=True) + epsilon)
    unit = value * factor
    grad_gain = jnp.sum(upstream * unit, axis=0, keepdims=True)
    back = upstream * gain
    return factor * (back - unit * jnp.mean(back * unit, axis=-1, keepdims=True)), grad_gain


def greet(me, partners, block, others, work=None):
    barrier = pltpu.get_barrier_semaphore()
    for distance in partners:
        pl.semaphore_signal(
            barrier, inc=1, device_id={"fsdp": across_many(me, distance)}, device_id_type=pl.DeviceIdType.MESH
        )
    for distance in range(1, others + 1):
        pl.semaphore_signal(
            barrier,
            inc=1,
            device_id={"ctx": (block + distance) % (others + 1)},
            device_id_type=pl.DeviceIdType.MESH,
        )
    if work is not None:
        work()
    pl.semaphore_wait(barrier, len(partners) + others)


def push(source, target, send_sem, recv_sem, place):
    return pltpu.make_async_remote_copy(
        src_ref=source,
        dst_ref=target,
        send_sem=send_sem,
        recv_sem=recv_sem,
        device_id=place,
        device_id_type=pl.DeviceIdType.MESH,
    )


def spread_copies(own, slots, send_sem, recv_sem, me):
    half = own.shape[0] // 2
    low, high = pl.ds(0, half), pl.ds(half, half)
    sibling, beside, above = across(me, 1), across(me, 2), across(me, 4)
    plan = [
        (own, slots.at[1], sibling),
        (own.at[low], slots.at[2, low], beside),
        (own.at[low], slots.at[4, low], above),
        (own.at[high], slots.at[2, high], beside),
        (own.at[high], slots.at[4, high], above),
        (slots.at[2, low], slots.at[3, low], sibling),
        (slots.at[4, low], slots.at[5, low], sibling),
        (slots.at[2, high], slots.at[3, high], sibling),
        (slots.at[4, high], slots.at[5, high], sibling),
        (slots.at[2, low], slots.at[6, low], above),
        (slots.at[4, high], slots.at[6, high], beside),
        (slots.at[6, low], slots.at[7, low], sibling),
        (slots.at[6, high], slots.at[7, high], sibling),
    ]
    return [
        push(source, target, send_sem.at[index], recv_sem.at[index], {"fsdp": partner})
        for index, (source, target, partner) in enumerate(plan)
    ]


def attend_kernel(
    others, reach, source, gain_one, gain_two, gain_three, gain_four, gain_five, gain_six, head_gains, laurel_own,
    positions, cosine, sine, query_own, key_own, value_own, down_own, outward_own,
    normed, gains, linear, query_low, key_value, features, middle, attn_lin, laurel_all, inward_all, outward_all,
    gain_share, gain_slots, inward_slots, outward_slots, normed_low, attended, inward, lin_sum,
    gain_send, gain_recv, in_send, in_recv, out_send, out_recv, kv_send, kv_recv, in_copy, out_copy,
):
    rows_of, width = source.shape
    me, block = lax.axis_index("fsdp"), lax.axis_index("ctx")
    inward_own = inward_slots.at[0]
    gain_lines = gain_slots.at[0]

    def own_shares():
        start = 0
        for piece in (query_own, key_own, value_own, down_own):
            inward_slots[0, :, pl.ds(start, piece.shape[1])] = piece[...]
            start += piece.shape[1]
        inward_slots[0, :, pl.ds(start, inward_slots.shape[2] - start)] = jnp.zeros(
            (inward_slots.shape[1], inward_slots.shape[2] - start), jnp.bfloat16
        )
        gain_share[...] = jnp.zeros_like(gain_share)
        for index, gain in enumerate((gain_one, gain_two, gain_three, gain_four, gain_five, gain_six)):
            pieces = gain[...].astype(jnp.float32)
            size = pieces.shape[0] * 128
            for row in range(pieces.shape[0]):
                place = pl.ds(pl.multiple_of(me * size + row * 128, 128), 128)
                gain_share[index : index + 1, place] = pieces[row : row + 1, :]
        gain_share[6:8, 0:HEAD_SIZE] = head_gains[...].astype(jnp.float32)
        gain_share[8:16, :] = laurel_own[...].astype(jnp.float32)
        gain_slots[0] = gain_share[...].astype(jnp.bfloat16)

    greet(me, range(1, 8), block, others, own_shares)
    gain_copies = [
        push(gain_lines, gain_slots.at[distance], gain_send.at[distance - 1], gain_recv.at[distance - 1],
             {"fsdp": across_many(me, distance)})
        for distance in range(1, 8)
    ]
    for copy in gain_copies:
        copy.start()
    spread_in = spread_copies(inward_own, inward_slots, in_send, in_recv, me)
    spread_out = spread_copies(outward_own, outward_slots, out_send, out_recv, me)
    for index in range(5):
        spread_in[index].start()
    outward_slots[0] = outward_own[...]

    value = source[...].astype(jnp.float32)
    factor = lax.rsqrt(jnp.mean(value * value, axis=-1, keepdims=True) + epsilon)
    for copy in gain_copies:
        copy.wait_recv()
    lines = gain_slots[...].astype(jnp.float32)
    gains[...] = jnp.sum(lines, axis=0)[0:8]
    laurel_size = 8
    laurel_all[...] = jnp.zeros_like(laurel_all)
    for slot in range(8):
        device = across_many(me, slot)
        laurel_all[pl.ds(pl.multiple_of(device * laurel_size, laurel_size), laurel_size), :] = lines[slot, 8:16]
    value = value * factor * gains[0:1, :]
    normed[...] = value
    normed_low[...] = value.astype(jnp.bfloat16)
    share = width // 8
    for index in range(8):
        features[:, pl.ds(2 * index * share, share)] = normed_low[:, pl.ds(index * share, share)]

    depth = inward_own.shape[0]
    head_rows = width // 8
    written = []

    def add_inward(slot):
        device = across_many(me, slot)
        part = normed_low[:, pl.ds(pl.multiple_of(device * depth, depth), depth)]
        for start in range(0, inward.shape[1], 640):
            span = pl.ds(start, 640)
            product = jnp.dot(part, inward_slots[slot, :, span], preferred_element_type=jnp.float32)
            inward[:, span] = product if slot == 0 else inward[:, span] + product
        copy = pltpu.make_async_copy(
            inward_slots.at[slot], inward_all.at[pl.ds(pl.multiple_of(device * depth, depth), depth)], in_copy.at[slot]
        )
        copy.start()
        written.append(copy)

    def add_outward(slot):
        device = across_many(me, slot)
        part = attended[:, pl.ds(pl.multiple_of(device * head_rows, head_rows), head_rows)]
        for start in range(0, width, 512):
            span = pl.ds(start, 512)
            product = jnp.dot(part, outward_slots[slot, pl.ds(0, head_rows), span], preferred_element_type=jnp.float32)
            lin_sum[:, span] = product if slot == 0 else lin_sum[:, span] + product

    def write_outward(slot):
        device = across_many(me, slot)
        rows = pl.ds(pl.multiple_of(device * head_rows, head_rows), head_rows)
        copy = pltpu.make_async_copy(outward_slots.at[slot], outward_all.at[rows], out_copy.at[slot])
        copy.start()
        written.append(copy)

    add_inward(0)
    spread_in[0].wait_recv()
    add_inward(1)
    spread_in[1].wait_recv()
    spread_in[9].start()
    spread_in[5].start()
    spread_in[2].wait_recv()
    spread_in[6].start()
    spread_in[3].wait_recv()
    spread_in[7].start()
    spread_in[4].wait_recv()
    spread_in[10].start()
    spread_in[8].start()
    add_inward(2)
    add_inward(4)
    spread_in[5].wait_recv()
    spread_in[7].wait_recv()
    add_inward(3)
    spread_in[6].wait_recv()
    spread_in[8].wait_recv()
    add_inward(5)
    spread_in[9].wait_recv()
    spread_in[11].start()
    spread_in[10].wait_recv()
    spread_in[12].start()
    for index in range(5):
        spread_out[index].start()
    add_inward(6)
    spread_in[11].wait_recv()
    spread_in[12].wait_recv()
    add_inward(7)

    query_width, key_width = QUERY_HEADS * HEAD_SIZE, KEY_VALUE_HEADS * HEAD_SIZE
    own_rows = pl.ds(0, rows_of)

    def head(start, gain):
        lane = inward[:, pl.ds(start, HEAD_SIZE)]
        scale = lax.rsqrt(jnp.mean(lane * lane, axis=-1, keepdims=True) + epsilon)
        return turn(lane * scale * gain, cosine[...], sine[...]).astype(jnp.bfloat16)

    for index in range(KEY_VALUE_HEADS):
        key_value[own_rows, pl.ds(index * HEAD_SIZE, HEAD_SIZE)] = head(
            query_width + index * HEAD_SIZE, gains[7:8, 0:HEAD_SIZE]
        )
    key_value[own_rows, pl.ds(key_width, key_width)] = inward[:, pl.ds(query_width + key_width, key_width)].astype(
        jnp.bfloat16
    )
    for distance in range(1, reach + 1):
        copy = push(
            key_value.at[own_rows],
            key_value.at[pl.ds(distance * rows_of, rows_of)],
            kv_send.at[distance - 1],
            kv_recv.at[distance - 1],
            {"ctx": (block + distance) % (others + 1)},
        )

        @pl.when(block + distance <= others)
        def _():
            copy.start()

        @pl.when(block < distance)
        def _():
            key_value[pl.ds(distance * rows_of, rows_of), :] = jnp.zeros((rows_of, 2 * key_width), jnp.bfloat16)

    for index in range(QUERY_HEADS):
        query_low[:, pl.ds(index * HEAD_SIZE, HEAD_SIZE)] = head(index * HEAD_SIZE, gains[6:7, 0:HEAD_SIZE])
    linear[...] = inward[:, pl.ds(0, query_width + key_width)]
    middle[...] = inward[:, pl.ds(query_width + 2 * key_width, middle.shape[1])].astype(jnp.bfloat16)

    spread_out[0].wait_recv()
    spread_out[1].wait_recv()
    spread_out[9].start()
    spread_out[5].start()
    spread_out[2].wait_recv()
    spread_out[6].start()
    for distance in range(1, reach + 1):
        copy = push(
            key_value.at[own_rows],
            key_value.at[pl.ds(distance * rows_of, rows_of)],
            kv_send.at[distance - 1],
            kv_recv.at[distance - 1],
            {"ctx": (block + distance) % (others + 1)},
        )

        @pl.when(block >= distance)
        def _():
            copy.wait_recv()

    allowed = window_mask(positions[...], rows_of, reach + 1)
    per_group = QUERY_HEADS // KEY_VALUE_HEADS
    for index in range(QUERY_HEADS):
        group = index // per_group
        columns = pl.ds(index * HEAD_SIZE, HEAD_SIZE)
        scores = product_back(query_low[:, columns], key_value[:, pl.ds(group * HEAD_SIZE, HEAD_SIZE)])
        scores = jnp.where(allowed, scores * HEAD_SIZE ** (-0.5), -1e30)
        grown = jnp.exp(scores - jnp.max(scores, axis=-1, keepdims=True))
        soft = (grown / jnp.sum(grown, axis=-1, keepdims=True)).astype(jnp.bfloat16)
        attended[:, columns] = jnp.dot(
            soft, key_value[:, pl.ds(key_width + group * HEAD_SIZE, HEAD_SIZE)], preferred_element_type=jnp.float32
        ).astype(jnp.bfloat16)

    for index in range(8):
        features[:, pl.ds((2 * index + 1) * share, share)] = attended[:, pl.ds(index * share, share)]
    add_outward(0)
    add_outward(1)
    write_outward(0)
    write_outward(1)
    spread_out[3].wait_recv()
    spread_out[7].start()
    spread_out[4].wait_recv()
    spread_out[10].start()
    spread_out[8].start()
    add_outward(2)
    add_outward(4)
    spread_out[5].wait_recv()
    spread_out[7].wait_recv()
    add_outward(3)
    spread_out[6].wait_recv()
    spread_out[8].wait_recv()
    add_outward(5)
    for slot in range(2, 6):
        write_outward(slot)
    spread_out[9].wait_recv()
    spread_out[11].start()
    spread_out[10].wait_recv()
    spread_out[12].start()
    add_outward(6)
    write_outward(6)
    spread_out[11].wait_recv()
    spread_out[12].wait_recv()
    add_outward(7)
    write_outward(7)
    attn_lin[...] = lin_sum[...]
    for copy in gain_copies + spread_in + spread_out:
        copy.wait_send()
    for copy in written:
        copy.wait()
    for distance in range(1, reach + 1):
        copy = push(
            key_value.at[own_rows],
            key_value.at[pl.ds(distance * rows_of, rows_of)],
            kv_send.at[distance - 1],
            kv_recv.at[distance - 1],
            {"ctx": (block + distance) % (others + 1)},
        )

        @pl.when(block + distance <= others)
        def _():
            copy.wait_send()


def attend_call(reach, source, gains, head_gains, laurel_own, positions, cosine, sine, inward_own, outward_own):
    rows_of, width = source.shape
    others = lax.axis_size("ctx") - 1
    low, full = jnp.bfloat16, jnp.float32
    hbm = pl.BlockSpec(memory_space=pl.ANY)
    vmem = pl.BlockSpec(memory_space=pltpu.VMEM)
    dma = pltpu.SemaphoreType.DMA
    depth = inward_own[0].shape[0]
    columns = sum(piece.shape[1] for piece in inward_own)
    columns += -columns % 128
    gain_shape = (16, width)
    query_width, key_width = QUERY_HEADS * HEAD_SIZE, KEY_VALUE_HEADS * HEAD_SIZE
    tail = columns - query_width - 2 * key_width
    shapes = [
        jax.ShapeDtypeStruct((rows_of, width), full),
        jax.ShapeDtypeStruct((8, width), full),
        jax.ShapeDtypeStruct((rows_of, query_width + key_width), full),
        jax.ShapeDtypeStruct((rows_of, query_width), low),
        jax.ShapeDtypeStruct(((reach + 1) * rows_of, 2 * key_width), low),
        jax.ShapeDtypeStruct((rows_of, 2 * width), low),
        jax.ShapeDtypeStruct((rows_of, tail), low),
        jax.ShapeDtypeStruct((rows_of, width), full),
        jax.ShapeDtypeStruct((tail, width), full),
        jax.ShapeDtypeStruct((8 * depth, columns), low),
        jax.ShapeDtypeStruct((8 * outward_own.shape[0], width), low),
    ]
    return pl.pallas_call(
        functools.partial(attend_kernel, others, reach),
        out_shape=shapes,
        in_specs=[vmem] * 17,
        out_specs=[vmem] * 9 + [hbm] * 2,
        scratch_shapes=[
            pltpu.VMEM(gain_shape, full),
            pltpu.VMEM((8, *gain_shape), low),
            pltpu.VMEM((8, depth, columns), low),
            pltpu.VMEM((8, *outward_own.shape), low),
            pltpu.VMEM((rows_of, width), low),
            pltpu.VMEM((rows_of, query_width), low),
            pltpu.VMEM((rows_of, columns), full),
            pltpu.VMEM((rows_of, width), full),
            dma((7,)),
            dma((7,)),
            dma((13,)),
            dma((13,)),
            dma((13,)),
            dma((13,)),
            dma((max(reach, 1),)),
            dma((max(reach, 1),)),
            dma((8,)),
            dma((8,)),
        ],
        compiler_params=pltpu.CompilerParams(collective_id=3, has_side_effects=True, vmem_limit_bytes=56 * 2**20),
        cost_estimate=pl.CostEstimate(
            flops=60 * rows_of * width * columns, bytes_accessed=20 * depth * columns, transcendentals=0
        ),
        name="attend_forward",
    )(source, *gains, head_gains, laurel_own, positions, cosine, sine, *inward_own, outward_own)


def turn_norm_grad(upstream, linear, gain, cosine, sine):
    scale = lax.rsqrt(jnp.mean(linear * linear, axis=-1, keepdims=True) + epsilon)
    unit = linear * scale
    back = turn(upstream, cosine, sine, -1.0)
    grad_gain = jnp.sum(back * unit, axis=0, keepdims=True)
    back = back * gain
    return scale * (back - unit * jnp.mean(back * unit, axis=-1, keepdims=True)), grad_gain


def attend_back_kernel(
    others, reach, d_ffn_in, mixed, d_residual, laurel_lin, attn_lin, laurel, gain_part,
    query_low, key_value, linear, gains, positions, cosine, sine, middle, features,
    source, residual, d_vector, gated_value, d_back, outward_all, inward_all, d_rows,
    d_source, grad_wide, grad_small, near_hbm,
    d_lin, d_half, d_laurel, d_middle, gain_rows,
    outward, inward, d_attended, d_key_value, parcel, arrived, d_query, d_rest, lin_slots, query_slots, rest_slots,
    ordered, d_normed, gain_parcel, gain_arrived, laurel_arrived, load_sem, lin_send, lin_recv, query_send, query_recv, rest_send, rest_recv, kv_send, kv_recv, gain_send, gain_recv, laurel_send, laurel_recv, near_send, near_recv,
    gate_in, gate_sum, gate_arrived, out_in, out_sum, out_arrived, pair_send, pair_recv, chip_send, chip_recv,
    gate_parts, out_parts, laurel_rows,
):
    rows_of, width = source.shape
    me, block = lax.axis_index("fsdp"), lax.axis_index("ctx")
    query_width, key_width = QUERY_HEADS * HEAD_SIZE, KEY_VALUE_HEADS * HEAD_SIZE
    per_group = QUERY_HEADS // KEY_VALUE_HEADS
    depth = width // 8
    loads = [
        pltpu.make_async_copy(outward_all.at[pl.ds(index * depth, depth)], outward.at[index % 2], load_sem.at[index])
        for index in range(8)
    ]
    loads.append(pltpu.make_async_copy(inward_all, inward, load_sem.at[8]))
    for index in (0, 1, 8):
        loads[index].start()

    def before_attention():
        d_mixed, grad_before = norm_rows_grad(mixed[...], gains[3:4, :], d_ffn_in[...])
        d_half[...] = (d_residual[...] + d_mixed) * inv_root
        d_branch, grad_laurel_gain = norm_rows_grad(laurel_lin[...], gains[2:3, :], d_half[...])
        d_laurel[...] = d_branch.astype(jnp.bfloat16)
        d_middle[...] = product_back(d_laurel[...], laurel[...].astype(jnp.bfloat16)).astype(jnp.bfloat16)
        d_branch, grad_attention = norm_rows_grad(attn_lin[...], gains[1:2, :], d_half[...])
        d_lin[...] = d_branch.astype(jnp.bfloat16)
        gain_rows[...] = gain_part[...]
        gain_rows[1:2, :] = grad_attention
        gain_rows[2:3, :] = grad_laurel_gain
        gain_rows[3:4, :] = grad_before

    greet(me, range(1, 8), block, others, before_attention)
    mine, theirs = pl.ds(0, rows_of), pl.ds(rows_of, rows_of)
    near = [
        push(
            d_rows.at[pl.ds(group * 2 * rows_of, rows_of)],
            near_hbm.at[group, mine],
            near_send.at[group],
            near_recv.at[group],
            {"ctx": across(block, 1)},
        )
        for group in range(4)
    ]
    near_share = [
        push(
            near_hbm.at[group, mine],
            near_hbm.at[group, theirs],
            near_send.at[4 + group],
            near_recv.at[4 + group],
            {"fsdp": across(me, 1)},
        )
        for group in range(4)
    ]
    for copy in near[:2]:
        copy.start()
    vector_parts = ((gate_parts, gate_in, gate_sum, gate_arrived), (out_parts, out_in, out_sum, out_arrived))
    chips = (0, 2, 4, 6)
    pair_copies = []
    chip_copies = []
    for kind, (parts, pair_in, pair_sum, arrived_parts) in enumerate(vector_parts):
        for index, chip in enumerate(chips):
            place = 4 * kind + index
            pair_copies.append(
                push(
                    parts.at[across_many(me, chip + 1)],
                    pair_in.at[index],
                    pair_send.at[place],
                    pair_recv.at[place],
                    {"fsdp": across(me, 1)},
                )
            )
            if chip:
                place = 3 * kind + index - 1
                chip_copies.append(
                    push(
                        pair_sum.at[index - 1],
                        arrived_parts.at[index - 1],
                        chip_send.at[place],
                        chip_recv.at[place],
                        {"fsdp": across_many(me, chip)},
                    )
                )
    spread_lin = spread_copies(d_lin, lin_slots, lin_send, lin_recv, me)
    spread_query = spread_copies(d_query, query_slots, query_send, query_recv, me)
    spread_rest = spread_copies(d_rest, rest_slots, rest_send, rest_recv, me)
    for index in range(5):
        spread_lin[index].start()
    lin_slots[0] = d_lin[...]
    for index in range(8):
        gate_parts[index] = product_rows(residual[:, pl.ds(index * depth, depth)], d_vector[...]).astype(jnp.bfloat16)
    out_parts[...] = product_rows(gated_value[...], d_back[...]).reshape(out_parts.shape).astype(jnp.bfloat16)
    laurel_rows[...] = product_rows(middle[...], d_laurel[...])[0 : 8 * laurel_rows.shape[1]].reshape(laurel_rows.shape)
    for copy in pair_copies:
        copy.start()
    laurel_copies = [
        push(
            laurel_rows.at[across_many(me, distance)],
            laurel_arrived.at[distance],
            laurel_send.at[distance - 1],
            laurel_recv.at[distance - 1],
            {"fsdp": across_many(me, distance)},
        )
        for distance in range(1, 8)
    ]
    laurel_arrived[0] = laurel_rows[me]
    for slot in range(8):
        device = across_many(me, slot)
        ordered[pl.ds(slot * rows_of, rows_of), :] = features[
            pl.ds(pl.multiple_of(device * rows_of, rows_of), rows_of), :
        ]
    for index in range(8):
        loads[index].wait()
        d_attended[:, pl.ds(index * depth, depth)] = product_back(d_lin[...], outward[index % 2]).astype(jnp.bfloat16)
        if index + 2 < 8:
            loads[index + 2].start()

    allowed = window_mask(positions[...], rows_of, reach + 1)
    scale = HEAD_SIZE ** (-0.5)

    def one_head(index):
        group = index // per_group
        columns = pl.ds(index * HEAD_SIZE, HEAD_SIZE)
        keys = pl.ds(group * HEAD_SIZE, HEAD_SIZE)
        values = pl.ds(key_width + group * HEAD_SIZE, HEAD_SIZE)
        scores = product_back(query_low[:, columns], key_value[:, keys])
        scores = jnp.where(allowed, scores * scale, -1e30)
        grown = jnp.exp(scores - jnp.max(scores, axis=-1, keepdims=True))
        soft = grown / jnp.sum(grown, axis=-1, keepdims=True)
        d_soft = product_back(d_attended[:, columns], key_value[:, values])
        d_scores = (soft * (d_soft - jnp.sum(soft * d_soft, axis=-1, keepdims=True))).astype(jnp.bfloat16)
        upstream = scale * jnp.dot(d_scores, key_value[:, keys], preferred_element_type=jnp.float32)
        d_key = scale * product_rows(d_scores, query_low[:, columns])
        d_value = product_rows(soft.astype(jnp.bfloat16), d_attended[:, columns])
        if index % per_group == 0:
            d_key_value[:, keys] = d_key
            d_key_value[:, values] = d_value
        else:
            d_key_value[:, keys] += d_key
            d_key_value[:, values] += d_value
        d_head, grad_gain = turn_norm_grad(upstream, linear[:, columns], gains[6:7, 0:HEAD_SIZE], cosine[...], sine[...])
        d_query[:, columns] = d_head.astype(jnp.bfloat16)
        return grad_gain

    query_gain = one_head(0)
    for index in range(1, per_group):
        query_gain = query_gain + one_head(index)
    spread_lin[0].wait_recv()
    spread_lin[1].wait_recv()
    spread_lin[9].start()
    spread_lin[5].start()
    spread_lin[2].wait_recv()
    spread_lin[6].start()
    for index in range(per_group, QUERY_HEADS):
        query_gain = query_gain + one_head(index)
    parcel[...] = d_key_value[pl.ds(rows_of, reach * rows_of), :].astype(jnp.bfloat16)

    def return_copy(distance):
        span = pl.ds((distance - 1) * rows_of, rows_of)
        return push(
            parcel.at[span],
            arrived.at[span],
            kv_send.at[distance - 1],
            kv_recv.at[distance - 1],
            {"ctx": (block + others + 1 - distance) % (others + 1)},
        )

    for distance in range(1, reach + 1):
        copy = return_copy(distance)

        @pl.when(block >= distance)
        def _():
            copy.start()

        @pl.when(block + distance > others)
        def _():
            arrived[pl.ds((distance - 1) * rows_of, rows_of), :] = jnp.zeros((rows_of, 2 * key_width), jnp.bfloat16)

    for copy in near[2:]:
        copy.start()
    spread_lin[3].wait_recv()
    spread_lin[7].start()
    spread_lin[4].wait_recv()
    spread_lin[10].start()
    spread_lin[8].start()
    for index in range(5):
        spread_query[index].start()
    for copy in pair_copies:
        copy.wait_recv()
    for parts, pair_in, pair_sum, arrived_parts in vector_parts:
        for index, chip in enumerate(chips):
            if chip:
                pair_sum[index - 1] = (
                    parts[across_many(me, chip)].astype(jnp.float32) + pair_in[index].astype(jnp.float32)
                ).astype(jnp.bfloat16)
    for copy in chip_copies:
        copy.start()
    query_slots[0] = d_query[...]
    loads[8].wait()
    d_normed[...] = product_back(d_query[...], inward[:, pl.ds(0, query_width)])
    spread_lin[9].wait_recv()
    spread_lin[11].start()
    spread_lin[10].wait_recv()
    spread_lin[12].start()
    spread_query[0].wait_recv()
    spread_query[1].wait_recv()
    spread_query[9].start()
    spread_query[5].start()
    spread_query[2].wait_recv()
    spread_query[6].start()
    for index in (5, 6, 7, 8, 11, 12):
        spread_lin[index].wait_recv()
    grad_wide[:, pl.ds(inward.shape[1], width)] = product_rows(
        ordered[:, pl.ds(depth, depth)], lin_slots[...].reshape(8 * rows_of, width)
    ).astype(jnp.bfloat16)

    for distance in range(1, reach + 1):
        copy = return_copy(distance)

        @pl.when(block + distance <= others)
        def _():
            copy.wait_recv()

    total = d_key_value[pl.ds(0, rows_of), :]
    for distance in range(1, reach + 1):
        total = total + arrived[pl.ds((distance - 1) * rows_of, rows_of), :].astype(jnp.float32)
    for index in range(KEY_VALUE_HEADS):
        columns = pl.ds(index * HEAD_SIZE, HEAD_SIZE)
        d_head, grad_gain = turn_norm_grad(
            total[:, index * HEAD_SIZE : (index + 1) * HEAD_SIZE],
            linear[:, pl.ds(query_width + index * HEAD_SIZE, HEAD_SIZE)],
            gains[7:8, 0:HEAD_SIZE],
            cosine[...],
            sine[...],
        )
        d_rest[:, columns] = d_head.astype(jnp.bfloat16)
        key_gain = grad_gain if index == 0 else key_gain + grad_gain
    d_rest[:, pl.ds(key_width, key_width)] = total[:, key_width:].astype(jnp.bfloat16)
    d_rest[:, pl.ds(2 * key_width, d_middle.shape[1])] = d_middle[...]
    spread_query[3].wait_recv()
    spread_query[7].start()
    spread_query[4].wait_recv()
    spread_query[10].start()
    spread_query[8].start()
    for index in range(5):
        spread_rest[index].start()
    rest_slots[0] = d_rest[...]
    rest_width = d_rest.shape[1]
    d_normed[...] += product_back(d_rest[...], inward[:, pl.ds(query_width, rest_width)])
    value = source[...].astype(jnp.float32)
    factor = lax.rsqrt(jnp.mean(value * value, axis=-1, keepdims=True) + epsilon)
    unit = value * factor
    upstream = d_half[...] + d_normed[...]
    for index in range(8):
        columns = slice(index * depth, (index + 1) * depth)
        gain_parcel[index, 0:8, :] = gain_rows[0:8, columns]
        gain_parcel[index, 0:1, :] = jnp.sum(upstream[:, columns] * unit[:, columns], axis=0, keepdims=True)
        gain_parcel[index, 6:7, :] = query_gain
        gain_parcel[index, 7:8, :] = key_gain
    gain_copies = [
        push(
            gain_parcel.at[across_many(me, distance)],
            gain_arrived.at[distance],
            gain_send.at[distance - 1],
            gain_recv.at[distance - 1],
            {"fsdp": across_many(me, distance)},
        )
        for distance in range(1, 8)
    ]
    for copy in gain_copies + laurel_copies:
        copy.start()
    gain_arrived[0] = gain_parcel[me]
    upstream = upstream * gains[0:1, :]
    d_source[...] = d_half[...] + factor * (upstream - unit * jnp.mean(upstream * unit, axis=-1, keepdims=True))
    spread_rest[0].wait_recv()
    spread_rest[1].wait_recv()
    spread_rest[9].start()
    spread_rest[5].start()
    spread_rest[2].wait_recv()
    spread_rest[6].start()
    spread_query[9].wait_recv()
    spread_query[11].start()
    spread_query[10].wait_recv()
    spread_query[12].start()
    spread_rest[3].wait_recv()
    spread_rest[7].start()
    spread_rest[4].wait_recv()
    spread_rest[10].start()
    spread_rest[8].start()
    for index in (5, 6, 7, 8, 11, 12):
        spread_query[index].wait_recv()
    grad_wide[:, pl.ds(0, query_width)] = product_rows(
        ordered[:, pl.ds(0, depth)], query_slots[...].reshape(8 * rows_of, query_width)
    ).astype(jnp.bfloat16)
    spread_rest[9].wait_recv()
    spread_rest[11].start()
    spread_rest[10].wait_recv()
    spread_rest[12].start()
    for index in (5, 6, 7, 8, 11, 12):
        spread_rest[index].wait_recv()
    grad_wide[:, pl.ds(query_width, rest_width)] = product_rows(
        ordered[:, pl.ds(0, depth)], rest_slots[...].reshape(8 * rows_of, rest_width)
    ).astype(jnp.bfloat16)
    for copy, share in zip(near, near_share):
        copy.wait_recv()
        share.start()
    for copy in gain_copies + laurel_copies + chip_copies:
        copy.wait_recv()
    totals = []
    for parts, pair_in, pair_sum, arrived_parts in vector_parts:
        total = parts[me].astype(jnp.float32) + pair_in[0].astype(jnp.float32)
        for index in range(3):
            total = total + arrived_parts[index].astype(jnp.float32)
        totals.append(total.astype(jnp.bfloat16))
    grad_wide[:, pl.ds(inward.shape[1] + width, totals[0].shape[1])] = totals[0]
    laurel_size = laurel_rows.shape[1]
    tail = jnp.concatenate(
        [jnp.sum(laurel_arrived[...], axis=0), jnp.pad(jnp.sum(gain_arrived[...], axis=0), ((0, 0), (0, width - depth)))],
        axis=0,
    )
    out_size = totals[1].shape[0]
    grad_small[pl.ds(0, out_size), :] = totals[1]
    grad_small[pl.ds(out_size, laurel_size + 8), :] = tail.astype(jnp.bfloat16)
    for copy in near_share:
        copy.wait_recv()
    for copy in (
        spread_lin + spread_query + spread_rest + gain_copies + laurel_copies + near + near_share + pair_copies + chip_copies
    ):
        copy.wait_send()
    for distance in range(1, reach + 1):
        copy = return_copy(distance)

        @pl.when(block >= distance)
        def _():
            copy.wait_send()


def attend_back_call(
    reach, d_ffn_in, mixed, d_residual, laurel_lin, attn_lin, laurel, gain_part,
    query_low, key_value, linear, gains, positions, cosine, sine, middle, features,
    source, residual, d_vector, gated_value, d_back, outward_all, inward_all, d_rows,
):
    rows_of, width = source.shape
    others = lax.axis_size("ctx") - 1
    low, full = jnp.bfloat16, jnp.float32
    hbm = pl.BlockSpec(memory_space=pl.ANY)
    vmem = pl.BlockSpec(memory_space=pltpu.VMEM)
    dma = pltpu.SemaphoreType.DMA
    columns = inward_all.shape[1]
    query_width, key_width = QUERY_HEADS * HEAD_SIZE, KEY_VALUE_HEADS * HEAD_SIZE
    rest_width = columns - query_width
    depth = width // 8
    vector_width = d_vector.shape[1]
    part_shapes = ((depth, vector_width), (vector_width // 8, width))
    shapes = [
        jax.ShapeDtypeStruct((rows_of, width), full),
        jax.ShapeDtypeStruct((depth, columns + width + vector_width), low),
        jax.ShapeDtypeStruct((vector_width // 8 + 16, width), low),
        jax.ShapeDtypeStruct((4, 2 * rows_of, width), low),
    ]
    spans = max(reach, 1)
    return pl.pallas_call(
        functools.partial(attend_back_kernel, others, reach),
        out_shape=shapes,
        in_specs=[vmem] * 21 + [hbm] * 3,
        out_specs=[vmem] * 3 + [hbm],
        scratch_shapes=[
            pltpu.VMEM((rows_of, width), low),
            pltpu.VMEM((rows_of, width), full),
            pltpu.VMEM((rows_of, width), low),
            pltpu.VMEM(middle.shape, low),
            pltpu.VMEM((8, width), full),
            pltpu.VMEM((2, depth, width), low),
            pltpu.VMEM((width, columns), low),
            pltpu.VMEM((rows_of, query_width), low),
            pltpu.VMEM(((reach + 1) * rows_of, 2 * key_width), full),
            pltpu.VMEM((spans * rows_of, 2 * key_width), low),
            pltpu.VMEM((spans * rows_of, 2 * key_width), low),
            pltpu.VMEM((rows_of, query_width), low),
            pltpu.VMEM((rows_of, rest_width), low),
            pltpu.VMEM((8, rows_of, width), low),
            pltpu.VMEM((8, rows_of, query_width), low),
            pltpu.VMEM((8, rows_of, rest_width), low),
            pltpu.VMEM((8 * rows_of, 2 * depth), low),
            pltpu.VMEM((rows_of, width), full),
            pltpu.VMEM((8, 8, depth), full),
            pltpu.VMEM((8, 8, depth), full),
            pltpu.VMEM((8, 8, width), full),
            dma((9,)),
            dma((13,)),
            dma((13,)),
            dma((13,)),
            dma((13,)),
            dma((13,)),
            dma((13,)),
            dma((spans,)),
            dma((spans,)),
            dma((7,)),
            dma((7,)),
            dma((7,)),
            dma((7,)),
            dma((8,)),
            dma((8,)),
        ]
        + [
            pltpu.VMEM((count, *shape), low)
            for shape in part_shapes
            for count in (4, 3, 3)
        ]
        + [dma((8,)), dma((8,)), dma((6,)), dma((6,))]
        + [pltpu.VMEM((8, *shape), low) for shape in part_shapes]
        + [pltpu.VMEM((8, 8, width), full)],
        compiler_params=pltpu.CompilerParams(collective_id=4, has_side_effects=True, vmem_limit_bytes=60 * 2**20),
        cost_estimate=pl.CostEstimate(
            flops=40 * rows_of * width * columns, bytes_accessed=6 * width * columns, transcendentals=0
        ),
        name="attend_backward",
    )(
        d_ffn_in, mixed, d_residual, laurel_lin, attn_lin, laurel, gain_part,
        query_low, key_value, linear, gains, positions, cosine, sine, middle, features,
        source, residual, d_vector, gated_value, d_back, outward_all, inward_all, d_rows,
    )


def feed_call(forward, prelude, weights, kept=(), features=None, forward_rows=None, hidden_rows=None, vectors=()):
    rows_of, width = prelude[0].shape
    hidden = weights[0].shape[0]
    all_rows = 8 * rows_of
    others = lax.axis_size("ctx") - 1
    low, full = jnp.bfloat16, jnp.float32
    count_made = 3 if forward else 2
    hbm = pl.BlockSpec(memory_space=pl.ANY)
    vmem = pl.BlockSpec(memory_space=pltpu.VMEM)
    half = rows_of // 2
    dma = pltpu.SemaphoreType.DMA

    def shape(columns, kind, rows=rows_of):
        return jax.ShapeDtypeStruct((rows, columns), kind)

    operands = (*prelude, *weights, *kept)
    operand_specs = [vmem] * len(prelude) + [hbm] * (3 + len(kept))
    shapes = [shape(width, full)]
    extra = []
    if forward:
        shapes += [shape(width, full)] * 2
        operands += (features, *vectors)
        operand_specs += [vmem] * 3
        extra = (
            [dma((7,)), dma((7,)), dma]
            + [pltpu.VMEM((8, *value.shape), low) for value in vectors]
            + [dma((13,))] * 4
            + [dma((8,))] * 2
        )
    else:
        vector_width = prelude[5].shape[1]
        shapes += [shape(width, low), shape(vector_width, full), shape(width, low), shape(vector_width, low)]
        shapes += [shape(vector_width, low), shape(width, low), shape(width, full), shape(width, full, 8)]
        operands += (forward_rows, hidden_rows)
        operand_specs += [hbm] * 2
        extra = [
            pltpu.VMEM((all_rows, hidden), low),
            pltpu.VMEM((all_rows, width), low),
            pltpu.VMEM((2, hidden, 512), full),
            dma,
            dma,
            dma((3 * (width // 512),)),
        ]
    count_vmem = len(shapes)
    shapes += [
        shape(width, low, all_rows),
        jax.ShapeDtypeStruct((2, rows_of, width), low),
        jax.ShapeDtypeStruct((2, 2 * rows_of, width), low),
    ]
    if forward:
        shapes += [jax.ShapeDtypeStruct((8, rows_of, features.shape[1] // 8), low)]
        shapes += [shape(value.shape[1], low, 8 * value.shape[0]) for value in vectors]
    else:
        shapes += [shape(width, full, hidden)] * 3
    shapes += [shape(hidden, low, all_rows)] * count_made
    return pl.pallas_call(
        functools.partial(feed_kernel, forward, rows_of, others),
        out_shape=shapes,
        in_specs=operand_specs,
        out_specs=[vmem] * count_vmem + [hbm] * (len(shapes) - count_vmem),
        scratch_shapes=[pltpu.VMEM((hidden, width), low)] * 3
        + [pltpu.VMEM((all_rows, hidden), low)] * (len(kept) + count_made)
        + [
            pltpu.VMEM((rows_of, width), low),
            pltpu.VMEM((4, 2 * rows_of, width), low),
            pltpu.VMEM((4, 2 * rows_of, width), low),
            pltpu.VMEM((4, rows_of, width), low),
            pltpu.VMEM((3, rows_of, width), low),
            pltpu.VMEM((2, half, width), low),
            pltpu.VMEM((2, half, width), low),
            pltpu.VMEM((4, half, width), low),
            dma((20,)),
            dma((20,)),
            dma((3 + len(kept),)),
            dma((4 * (1 + count_made),)),
            dma((2,)),
            dma((2,)),
            dma((4,)),
            dma((4,)),
        ]
        + extra,
        compiler_params=pltpu.CompilerParams(
            collective_id=1 if forward else 2,
            has_side_effects=True,
            vmem_limit_bytes=62 * 2**20,
        ),
        cost_estimate=pl.CostEstimate(
            flops=40 * all_rows * hidden * width // 2,
            bytes_accessed=6 * hidden * width + 8 * all_rows * width,
            transcendentals=0,
        ),
        name="feed_forward" if forward else "feed_backward",
    )(*operands)


def other_rows(rows, d_rows, weights, tiles, arrive):
    gate, up, down = weights
    hidden_tile, d_gate_tile, d_up_tile = tiles
    tile = min(512, gate.shape[0])
    for index in range(3):
        arrive(index)

    def body(index, carry):
        span = pl.ds(pl.multiple_of(index * tile, tile), tile)
        gate_value = product_back(gate[span, :], rows[...])
        up_value = product_back(up[span, :], rows[...])
        d_hidden = product_back(down[span, :], d_rows[...])
        value, slope = gelu_parts(gate_value)
        hidden_tile[span, :] = (value * up_value).astype(jnp.bfloat16)
        d_gate_tile[span, :] = (d_hidden * up_value * slope).astype(jnp.bfloat16)
        d_up_tile[span, :] = (d_hidden * value).astype(jnp.bfloat16)
        return carry

    lax.fori_loop(0, gate.shape[0] // tile, body, 0)


def add_weight_grads(grads, tiles, rows, d_rows, last, done):
    hidden_tile, d_gate_tile, d_up_tile = tiles
    terms = list(zip(grads, (d_gate_tile, d_up_tile, hidden_tile), (rows, rows, d_rows)))

    @pl.when(jnp.logical_not(last))
    def _():
        for grad, tile, right in terms:
            grad[...] += matrix_product(tile[...], right[...])

    @pl.when(last)
    def _():
        for index, (grad, tile, right) in enumerate(terms):
            grad[...] += matrix_product(tile[...], right[...])
            done(index)


def weight_moves(step, last, weights_hbm, weights, parts_hbm, grads, grads_hbm, weight_sem, part_sem, out_sem):
    weight_loads, part_loads, out_copies = [
        [pltpu.make_async_copy(source, target, sem.at[index]) for index, (source, target) in enumerate(zip(sources, targets))]
        for sources, targets, sem in (
            (weights_hbm, weights, weight_sem),
            (parts_hbm, grads, part_sem),
            (grads, grads_hbm, out_sem),
        )
    ]

    @pl.when(step == 0)
    def _():
        for load in weight_loads + part_loads:
            load.start()

    def arrive(index):
        @pl.when(step == 0)
        def _():
            weight_loads[index].wait()

    def begin_sums():
        @pl.when(step == 0)
        def _():
            for load in part_loads:
                load.wait()

    def done(index):
        out_copies[index].start()

    def finish():
        @pl.when(step == last)
        def _():
            for copy in out_copies:
                copy.wait()

    return arrive, begin_sums, done, finish


def weight_part_kernel(
    near_steps, gate_hbm, up_hbm, down_hbm, rows_near, rows_next, d_rows_near, gate_part, up_part, down_part, far_own,
    gate_out, up_out, down_out, far_all,
    gate, up, down, grad_gate, grad_up, grad_down, hidden_tile, d_gate_tile, d_up_tile,
    send_sem, recv_sem, own_sem, weight_sem, part_sem, out_sem,
):
    step = pl.program_id(0)
    last = near_steps - 1
    me = lax.axis_index("fsdp")
    grads = (grad_gate, grad_up, grad_down)
    tiles = (hidden_tile, d_gate_tile, d_up_tile)

    sibling, beside, above = across(me, 1), across(me, 2), across(me, 4)
    diagonal = across(beside, 4)
    plan = [(far_own, far_all.at[me], sibling)]
    for part in range(2):
        plan += [(far_own.at[part], far_all.at[me, part], beside), (far_own.at[part], far_all.at[me, part], above)]
    for part in range(2):
        plan += [(far_all.at[device, part], far_all.at[device, part], sibling) for device in (beside, above)]
    plan.append((far_all.at[beside, 0], far_all.at[beside, 0], above))
    plan.append((far_all.at[above, 1], far_all.at[above, 1], beside))
    plan += [(far_all.at[diagonal, part], far_all.at[diagonal, part], sibling) for part in range(2)]
    copies = [
        push(source, target, send_sem.at[index], recv_sem.at[index], {"fsdp": partner})
        for index, (source, target, partner) in enumerate(plan)
    ]
    own_copy = pltpu.make_async_copy(far_own, far_all.at[me], own_sem)

    arrive, begin_sums, done, finish = weight_moves(
        step, last, (gate_hbm, up_hbm, down_hbm), (gate, up, down), (gate_part, up_part, down_part), grads,
        (gate_out, up_out, down_out), weight_sem, part_sem, out_sem,
    )

    @pl.when(step == 0)
    def _():
        greet(me, (1, 2, 4), 0, 0)
        own_copy.start()
        for index in range(5):
            copies[index].start()

    @pl.when(step == last - 1)
    def _():
        copies[0].wait_recv()
        copies[1].wait_recv()
        copies[9].start()
        copies[5].start()
        copies[2].wait_recv()
        copies[6].start()

    @pl.when(step == last)
    def _():
        copies[3].wait_recv()
        copies[7].start()
        copies[4].wait_recv()
        copies[10].start()
        copies[8].start()

    weights = (gate, up, down)

    @pl.when(step < near_steps // 2)
    def _():
        other_rows(rows_near, d_rows_near, weights, tiles, arrive)
        begin_sums()
        add_weight_grads(grads, tiles, rows_near, d_rows_near, step == last, done)

    @pl.when(step >= near_steps // 2)
    def _():
        other_rows(rows_next, d_rows_near, weights, tiles, arrive)
        add_weight_grads(grads, tiles, rows_next, d_rows_near, step == last, done)

    @pl.when(step == last)
    def _():
        copies[9].wait_recv()
        copies[11].start()
        copies[10].wait_recv()
        copies[12].start()

    @pl.when(step == last)
    def _():
        for index in (5, 6, 7, 8, 11, 12):
            copies[index].wait_recv()
        own_copy.wait()
        for copy in copies:
            copy.wait_send()

    finish()


def weight_rest_kernel(
    steps, gate_hbm, up_hbm, down_hbm, rows, d_rows, gate_part, up_part, down_part,
    gate_out, up_out, down_out,
    gate, up, down, grad_gate, grad_up, grad_down, hidden_tile, d_gate_tile, d_up_tile, weight_sem, part_sem, out_sem,
):
    grads = (grad_gate, grad_up, grad_down)
    tiles = (hidden_tile, d_gate_tile, d_up_tile)
    arrive, begin_sums, done, finish = weight_moves(
        pl.program_id(0), steps - 1, (gate_hbm, up_hbm, down_hbm), (gate, up, down), (gate_part, up_part, down_part),
        grads, (gate_out, up_out, down_out), weight_sem, part_sem, out_sem,
    )
    other_rows(rows, d_rows, (gate, up, down), tiles, arrive)
    begin_sums()
    add_weight_grads(grads, tiles, rows, d_rows, pl.program_id(0) == steps - 1, done)
    finish()


def weight_grad_calls(
    gate, up, down, own_parts, rows_near, rows_next, d_rows_near, rows_far, far_own, tok=256, far_tok=512
):
    size, width = gate.shape
    low = jnp.bfloat16
    near_steps = d_rows_near.shape[0] // tok
    hbm = pl.BlockSpec(memory_space=pl.ANY)
    dma = pltpu.SemaphoreType.DMA

    def stream(first, steps):
        return pl.BlockSpec((tok, width), lambda s: (jnp.clip(s - first, 0, steps - 1), 0))

    buffers = [pltpu.VMEM((size, width), low)] * 3 + [pltpu.VMEM((size, width), jnp.float32)] * 3
    near_one, near_two = stream(0, near_steps // 2), stream(near_steps // 2, near_steps // 2)
    near = stream(0, near_steps)
    grad = jax.ShapeDtypeStruct((size, width), jnp.float32)
    *parts, far_all = pl.pallas_call(
        functools.partial(weight_part_kernel, near_steps),
        grid=(near_steps,),
        in_specs=[hbm] * 3 + [near_one, near_two, near] + [hbm] * 4,
        out_specs=[hbm] * 4,
        out_shape=[grad] * 3 + [jax.ShapeDtypeStruct((8, *far_own.shape), low)],
        scratch_shapes=buffers
        + [pltpu.VMEM((size, tok), low)] * 3
        + [dma((13,)), dma((13,)), dma, dma((3,)), dma((3,)), dma((3,))],
        compiler_params=pltpu.CompilerParams(
            dimension_semantics=("arbitrary",), vmem_limit_bytes=62 * 2**20, collective_id=5, has_side_effects=True
        ),
        cost_estimate=pl.CostEstimate(
            flops=12 * size * width * d_rows_near.shape[0], bytes_accessed=80 * 2**20, transcendentals=0
        ),
        name="weight_grads_part",
    )(gate, up, down, rows_near, rows_next, d_rows_near, *own_parts, far_own)
    far = pl.BlockSpec((far_tok, width), lambda s: (s, 0))
    return pl.pallas_call(
        functools.partial(weight_rest_kernel, rows_far.shape[0] // far_tok),
        grid=(rows_far.shape[0] // far_tok,),
        in_specs=[hbm] * 3 + [far] * 2 + [hbm] * 3,
        out_specs=[hbm] * 3,
        out_shape=[grad] * 3,
        scratch_shapes=buffers + [pltpu.VMEM((size, far_tok), low)] * 3 + [dma((3,)), dma((3,)), dma((3,))],
        compiler_params=pltpu.CompilerParams(dimension_semantics=("arbitrary",), vmem_limit_bytes=62 * 2**20),
        cost_estimate=pl.CostEstimate(
            flops=12 * size * width * rows_far.shape[0], bytes_accessed=80 * 2**20, transcendentals=0
        ),
        name="weight_grads_rest",
    )(gate, up, down, rows_far, far_all.reshape(-1, width), *parts)


def finish_kernel(
    key_width, wide, small, result_in, d_vectors_in, d_source_in,
    result, d_source, d_vectors, query, key, value, output, down, up, gate, out,
    gain_one, gain_two, gain_three, gain_four, gain_five, gain_six, query_gain, key_gain,
):
    result[...] = result_in[...]
    d_vectors[...] = d_vectors_in[...]
    d_source[...] = d_source_in[...]
    query_width = query.shape[1]
    start = 0
    for target, columns in (
        (query, query_width),
        (key, key_width),
        (value, key_width),
        (down, down.shape[1]),
    ):
        target[...] = wide[:, start : start + columns].astype(jnp.float32)
        start += columns
    start += -start % 128
    output[...] = wide[:, start : start + output.shape[1]].astype(jnp.float32)
    start += output.shape[1]
    gate[...] = wide[:, start : start + gate.shape[1]].astype(jnp.float32)
    lines = small[...].astype(jnp.float32)
    first = out.shape[0]
    out[...] = lines[0:first]
    up[...] = lines[first : first + up.shape[0]]
    first += up.shape[0]
    for index, target in enumerate((gain_one, gain_two, gain_three, gain_four, gain_five, gain_six)):
        target[...] = lines[first + index : first + index + 1, 0 : target.shape[1]]
    me = lax.axis_index("fsdp")
    for index, target in enumerate((query_gain, key_gain)):
        size = target.shape[1]
        line = lines[first + 6 + index : first + 7 + index, 0 : 8 * size]
        total = jnp.zeros((1, size), jnp.float32)
        for device in range(8):
            total = total + jnp.where(me == device, line[:, device * size : (device + 1) * size], 0.0)
        target[...] = total


def finish_call(wide, small, result, d_vectors, d_source, shapes, key_width):
    vmem = pl.BlockSpec(memory_space=pltpu.VMEM)
    kinds = [jnp.bfloat16] + [jnp.float32] * (len(shapes) - 1)
    return pl.pallas_call(
        functools.partial(finish_kernel, key_width),
        out_shape=[jax.ShapeDtypeStruct(shape, kind) for shape, kind in zip(shapes, kinds)],
        in_specs=[vmem] * 5,
        out_specs=[vmem] * len(shapes),
        compiler_params=pltpu.CompilerParams(vmem_limit_bytes=40 * 2**20),
        name="finish",
    )(wide, small, result, d_vectors, d_source)


def per_device(
    tokens,
    per_layer,
    segments,
    positions,
    cotangent,
    query_weight,
    key_matrix,
    value_matrix,
    output_weight,
    laurel_down,
    laurel_up,
    vector_gate,
    vector_out,
    norm_input,
    norm_attention,
    norm_laurel,
    norm_before,
    norm_after,
    norm_vector,
    query_norm_gain,
    norm_key,
    hidden_gate,
    hidden_up,
    hidden_down,
):
    count_of_rows = tokens.shape[0]
    shards = lax.axis_size("fsdp")
    width = tokens.shape[1]
    heads_per_group = QUERY_HEADS // KEY_VALUE_HEADS
    reach_blocks = min((WINDOW + count_of_rows - 2) // count_of_rows, lax.axis_size("ctx") - 1)
    score_scale = HEAD_SIZE ** (-0.5)
    fused = shards == 8 and lax.axis_size("ctx") == 4
    query_width = query_weight.shape[1]
    key_width = key_matrix.shape[1]

    gain_shards = (
        norm_input,
        norm_attention,
        norm_laurel,
        norm_before,
        norm_after,
        norm_vector,
        query_norm_gain,
        norm_key,
    )
    gain_sizes = [gain.shape[0] for gain in gain_shards]
    gain_starts = [sum(gain_sizes[:index]) for index in range(len(gain_sizes))]
    source = tokens.astype(jnp.float32)
    vectors = per_layer.astype(jnp.float32)
    rank = laurel_down.shape[1]
    unused, allowed = window(positions, count_of_rows, reach_blocks)

    def head_facing(linear, gain):
        return rotary_apply(root_mean_norm(linear, gain), positions)

    if fused:
        me = lax.axis_index("fsdp")
        head_gains = jnp.stack([query_norm_gain, norm_key])
        place = jnp.arange(HEAD_SIZE) // head_gains.shape[1] == me
        head_gains = jnp.where(place[None, :], jnp.tile(head_gains, (1, shards)), 0).astype(jnp.bfloat16)
        cosine, sine_part = rotary_tables(positions, HEAD_SIZE)
        (
            normed,
            gains_all,
            linear,
            query_lowered,
            key_value,
            features,
            middle_low,
            attn_lin,
            full_laurel_up,
            full_inward,
            full_output,
        ) = attend_call(
            reach_blocks,
            tokens,
            [gain.reshape(-1, 128) for gain in gain_shards[:6]],
            head_gains,
            laurel_up,
            positions[:, None],
            cosine,
            sine_part,
            (query_weight, key_matrix, value_matrix, laurel_down),
            output_weight,
        )
    else:
        gain_line = jnp.concatenate(gain_shards)
        gain_line = jnp.pad(gain_line, (0, -gain_line.shape[0] % 2048)).reshape(-1, 128)
        gains_all = gather(gain_line, "fsdp").reshape(shards, -1)
        gains = [
            gains_all[:, start : start + size].reshape(-1).astype(jnp.float32)
            for start, size in zip(gain_starts, gain_sizes)
        ]
        inward_weight = jnp.concatenate([query_weight, key_matrix, value_matrix, laurel_down], axis=1)
        inward_weight = jnp.pad(inward_weight, ((0, 0), (0, -inward_weight.shape[1] % 128)))
        full_inward = gather(inward_weight, "fsdp")
        full_output, full_vector_gate, full_vector_out, full_laurel_up = [
            gather(value, "fsdp") for value in (output_weight, vector_gate, vector_out, laurel_up)
        ]
        normed = root_mean_norm(source, gains[0])
        lowered_normed = normed.astype(jnp.bfloat16)
        inward = matrix_product(lowered_normed, full_inward)
        linear = inward[:, : query_width + key_width]
        value_lowered = inward[:, query_width + key_width : query_width + 2 * key_width].astype(jnp.bfloat16)
        laurel_mid = inward[:, query_width + 2 * key_width :][:, :rank].astype(jnp.bfloat16)
        query_lowered = head_facing(
            linear[:, :query_width].reshape(count_of_rows, QUERY_HEADS, HEAD_SIZE), gains[6]
        ).astype(jnp.bfloat16)
        key_lowered = head_facing(
            linear[:, query_width:].reshape(count_of_rows, KEY_VALUE_HEADS, HEAD_SIZE), gains[7]
        ).astype(jnp.bfloat16)
        key_value = jnp.stack([key_lowered.reshape(count_of_rows, -1), value_lowered])
        pair_blocks = [key_value]
        for distance in range(1, reach_blocks + 1):
            pair_blocks.append(from_behind(key_value, "ctx", distance))
        window_couple = jnp.concatenate(pair_blocks, axis=1)
        window_keys, window_values = window_couple[0], window_couple[1]
    if fused:
        (
            feed_value,
            mixed,
            laurel_lin,
            rows_all,
            rows_far,
            rows_near,
            slices,
            full_vector_gate,
            full_vector_out,
            hidden_all,
            lift_all,
            bend_all,
        ) = feed_call(
            True,
            (tokens, normed, attn_lin, middle_low, full_laurel_up, gains_all),
            (hidden_gate, hidden_up, hidden_down),
            features=features,
            vectors=(vector_gate, vector_out),
        )
        slices = slices.reshape(shards * count_of_rows, -1)
        rows_far = gather(rows_far.reshape(-1, width), "fsdp")
        (
            d_ffn_in,
            result,
            d_vectors,
            residual_low,
            d_vector_lin_low,
            gated_low,
            d_vector_back_low,
            d_residual,
            gain_rows,
            d_rows_all,
            d_rows_far,
            rows_next,
            *own_parts,
            unused,
            unused,
        ) = feed_call(
            False,
            (feed_value, mixed, gains_all, full_vector_gate, full_vector_out, per_layer, cotangent),
            (hidden_down, hidden_gate, hidden_up),
            (lift_all, bend_all),
            forward_rows=rows_all,
            hidden_rows=hidden_all,
        )
        d_ffn_in, rows_far = lax.optimization_barrier((d_ffn_in, rows_far))
        d_source, grad_wide, grad_small, d_rows_near = attend_back_call(
            reach_blocks, d_ffn_in, mixed, d_residual, laurel_lin, attn_lin, full_laurel_up, gain_rows,
            query_lowered, key_value, linear, gains_all, positions[:, None], cosine, sine_part, middle_low, slices,
            tokens, residual_low, d_vector_lin_low, gated_low, d_vector_back_low, full_output, full_inward, d_rows_all,
        )
        grad_hidden_gate, grad_hidden_up, grad_hidden_down = weight_grad_calls(
            hidden_gate,
            hidden_up,
            hidden_down,
            own_parts,
            rows_near.reshape(-1, width),
            rows_next.reshape(-1, width),
            d_rows_near.reshape(-1, width),
            rows_far,
            d_rows_far,
        )
    else:
        (
            gain_input,
            gain_attention,
            gain_laurel,
            gain_before,
            gain_after,
            gain_vector,
            gain_query,
            key_norm_gain,
        ) = gains
        query_linear = linear[:, :query_width].reshape(count_of_rows, QUERY_HEADS, HEAD_SIZE)
        key_linear = linear[:, query_width:].reshape(count_of_rows, KEY_VALUE_HEADS, HEAD_SIZE)
        query_lowered = query_lowered.reshape(count_of_rows, KEY_VALUE_HEADS, heads_per_group, HEAD_SIZE)
        window_keys = window_keys.reshape(-1, KEY_VALUE_HEADS, HEAD_SIZE)
        window_values = window_values.reshape(-1, KEY_VALUE_HEADS, HEAD_SIZE)

        def masked_scores():
            raw_scores = score_scale * jnp.einsum(
                "tgfd,kgd->gftk", query_lowered, window_keys, preferred_element_type=jnp.float32
            )
            return jnp.where(allowed, raw_scores, -1e30)

        scores_first = masked_scores()
        row_peak = jnp.max(scores_first, axis=-1, keepdims=True)
        exp_scores = jnp.exp(scores_first - row_peak)
        row_total = jnp.sum(exp_scores, axis=-1, keepdims=True)
        log_total = row_peak + jnp.log(row_total)
        soft_low = (exp_scores / row_total).astype(jnp.bfloat16)
        attended_low = (
            jnp.einsum("gftk,kgd->tgfd", soft_low, window_values, preferred_element_type=jnp.float32)
            .reshape(count_of_rows, QUERY_HEADS * HEAD_SIZE)
            .astype(jnp.bfloat16)
        )
        attn_lin = matrix_product(attended_low, full_output)
        residual_one = source + root_mean_norm(attn_lin, gain_attention)
        laurel_lin = matrix_product(laurel_mid, full_laurel_up)
        mixed = (residual_one + normed + root_mean_norm(laurel_lin, gain_laurel)) * inv_root
        ffn_in = root_mean_norm(mixed, gain_before).astype(jnp.bfloat16)
        normed_slices = feature_slices(lowered_normed)
        attended_slices = feature_slices(attended_low)
        rows_all = gather(ffn_in, "fsdp")
        gate_all = product_back(rows_all, hidden_gate)
        up_all = product_back(rows_all, hidden_up)
        hidden_all = gated(gate_all, up_all).astype(jnp.bfloat16)
        feed_value = scatter_sum(matrix_product(hidden_all, hidden_down))
        residual_two = mixed + root_mean_norm(feed_value, gain_after)
        residual_low = residual_two.astype(jnp.bfloat16)
        vector_lin = matrix_product(residual_low, full_vector_gate)
        gated_low = gated(vector_lin, vectors).astype(jnp.bfloat16)
        vector_back = matrix_product(gated_low, full_vector_out)
        result = residual_two + root_mean_norm(vector_back, gain_vector)
        upstream = cotangent.astype(jnp.float32)
        d_vector_back, grad_gain_vector = norm_grad(vector_back, gain_vector, upstream)
        d_vector_back_low = d_vector_back.astype(jnp.bfloat16)
        grad_vector_out = product_rows(gated_low, d_vector_back_low)
        d_gated = product_back(d_vector_back_low, full_vector_out)
        d_vector_lin, d_vectors = gated_grad(vector_lin, vectors, d_gated)
        d_vector_lin_low = d_vector_lin.astype(jnp.bfloat16)
        grad_vector_gate = product_rows(residual_low, d_vector_lin_low)
        d_residual = upstream + product_back(d_vector_lin_low, full_vector_gate)
        d_feed, grad_gain_after = norm_grad(feed_value, gain_after, d_residual)
        d_feed_low = d_feed.astype(jnp.bfloat16)
        d_rows_all = gather(d_feed_low, "fsdp")
        d_hidden = product_back(d_rows_all, hidden_down)
        d_gate_all, d_up_all = gated_grad(gate_all, up_all, d_hidden)
        d_gate_low = d_gate_all.astype(jnp.bfloat16)
        d_up_low = d_up_all.astype(jnp.bfloat16)
        d_ffn_in = scatter_sum(
            matrix_product(d_gate_low, hidden_gate) + matrix_product(d_up_low, hidden_up)
        )

        grad_hidden_gate, grad_hidden_up, grad_hidden_down = [
            lax.psum(grad.astype(jnp.bfloat16), "ctx").astype(jnp.float32)
            for grad in (
                product_rows(d_gate_low, rows_all),
                product_rows(d_up_low, rows_all),
                product_rows(hidden_all, d_rows_all),
            )
        ]

        d_mixed_part, grad_gain_before = norm_grad(mixed, gain_before, d_ffn_in)
        d_half = (d_residual + d_mixed_part) * inv_root
        d_laurel_lin, grad_gain_laurel = norm_grad(laurel_lin, gain_laurel, d_half)
        d_laurel_low = d_laurel_lin.astype(jnp.bfloat16)
        grad_laurel_up = product_rows(laurel_mid, d_laurel_low)
        d_laurel_mid = product_back(d_laurel_low, full_laurel_up).astype(jnp.bfloat16)
        d_attn_lin, grad_gain_attention = norm_grad(attn_lin, gain_attention, d_half)
        d_attn_low = d_attn_lin.astype(jnp.bfloat16)
        d_attended = (
            product_back(d_attn_low, full_output)
            .astype(jnp.bfloat16)
            .reshape(count_of_rows, KEY_VALUE_HEADS, heads_per_group, HEAD_SIZE)
        )
        soft_again = jnp.exp(masked_scores() - log_total)
        d_soft = jnp.einsum(
            "tgfd,kgd->gftk", d_attended, window_values, preferred_element_type=jnp.float32
        )
        d_scores = (
            soft_again * (d_soft - jnp.sum(soft_again * d_soft, axis=-1, keepdims=True))
        ).astype(jnp.bfloat16)
        d_query = score_scale * jnp.einsum(
            "gftk,kgd->tgfd", d_scores, window_keys, preferred_element_type=jnp.float32
        )
        grad_key_rows = score_scale * jnp.einsum(
            "gftk,tgfd->kgd", d_scores, query_lowered, preferred_element_type=jnp.float32
        )
        grad_value_rows = jnp.einsum(
            "gftk,tgfd->kgd",
            soft_again.astype(jnp.bfloat16),
            d_attended,
            preferred_element_type=jnp.float32,
        )
        grad_window_couple = jnp.stack(
            [
                grad_key_rows.reshape(-1, KEY_VALUE_HEADS * HEAD_SIZE),
                grad_value_rows.reshape(-1, KEY_VALUE_HEADS * HEAD_SIZE),
            ]
        )
        grad_own_part = grad_window_couple[:, :count_of_rows]
        for distance in range(1, reach_blocks + 1):
            grad_own_part = grad_own_part + from_behind(
                grad_window_couple[:, distance * count_of_rows : (distance + 1) * count_of_rows].astype(
                    jnp.bfloat16
                ),
                "ctx",
                -distance,
            ).astype(jnp.float32)
        unused, query_pull = jax.vjp(head_facing, query_linear, gain_query)
        d_query_lin, grad_gain_query = query_pull(
            d_query.reshape(count_of_rows, QUERY_HEADS, HEAD_SIZE)
        )
        unused, key_pullback_fn = jax.vjp(head_facing, key_linear, key_norm_gain)
        grad_key_linear, grad_key_norm_gain = key_pullback_fn(
            grad_own_part[0].reshape(count_of_rows, KEY_VALUE_HEADS, HEAD_SIZE)
        )
        d_inward = jnp.concatenate(
            [
                d_query_lin.reshape(count_of_rows, QUERY_HEADS * HEAD_SIZE).astype(jnp.bfloat16),
                grad_key_linear.reshape(count_of_rows, KEY_VALUE_HEADS * HEAD_SIZE).astype(
                    jnp.bfloat16
                ),
                grad_own_part[1].astype(jnp.bfloat16),
                d_laurel_mid,
                jnp.zeros((count_of_rows, full_inward.shape[1] - query_width - 2 * key_width - rank), jnp.bfloat16),
            ],
            axis=1,
        )
        grad_inward = product_rows(normed_slices, gather(d_inward, "fsdp")).astype(jnp.bfloat16)
        grad_output = product_rows(attended_slices, gather(d_attn_low, "fsdp")).astype(jnp.bfloat16)
        grad_wide = jnp.concatenate([grad_inward, grad_output], axis=1)
        small_rows = jnp.concatenate(
            [
                grad_vector_gate.reshape(shards, -1, width),
                grad_vector_out.reshape(shards, -1, width),
                grad_laurel_up.reshape(shards, -1, width),
            ],
            axis=1,
        ).astype(jnp.bfloat16)
        grad_small = lax.psum_scatter(small_rows, "fsdp", scatter_dimension=0, tiled=False)
        d_normed = d_half + product_back(d_inward, full_inward)
        d_source_part, grad_gain_input = norm_grad(source, gain_input, d_normed)
        d_source = d_half + d_source_part
        gain_lines = jnp.concatenate(
            [
                grad.reshape(shards, -1)
                for grad in (
                    grad_gain_input,
                    grad_gain_attention,
                    grad_gain_laurel,
                    grad_gain_before,
                    grad_gain_after,
                    grad_gain_vector,
                    grad_gain_query,
                    grad_key_norm_gain,
                )
            ],
            axis=1,
        )
        gain_share = lax.psum_scatter(gain_lines, "fsdp", scatter_dimension=0, tiled=False)
        gain_count = gain_share.shape[0]
        gain_share = jnp.pad(gain_share, (0, -gain_count % width)).astype(jnp.bfloat16)
        grad_small = jnp.concatenate([grad_small, gain_share.reshape(-1, width)], axis=0)

    grad_wide, grad_small = lax.psum((grad_wide, grad_small), "ctx")
    hidden_grads = (grad_hidden_gate, grad_hidden_up, grad_hidden_down)
    if fused:
        weights = (query_weight, key_matrix, value_matrix, output_weight, laurel_down, laurel_up, vector_gate, vector_out)
        shapes = [tokens.shape, tokens.shape, per_layer.shape] + [weight.shape for weight in weights]
        shapes += [(1, size) for size in gain_sizes]
        finished = finish_call(grad_wide, grad_small, result, d_vectors, d_source, shapes, key_width)
        gains_from = len(shapes) - len(gain_sizes)
        return tuple(finished[:gains_from]) + tuple(gain.reshape(-1) for gain in finished[gains_from:]) + hidden_grads
    grad_wide, grad_small = grad_wide.astype(jnp.float32), grad_small.astype(jnp.float32)
    inward_width = full_inward.shape[1]
    grad_inward = grad_wide[:, :inward_width]
    grad_output = grad_wide[:, inward_width:]
    out_rows, laurel_rows = vector_out.shape[0], laurel_up.shape[0]
    gate_rows = vector_gate.shape[0] * vector_gate.shape[1] // width
    share_vector_gate = grad_small[:gate_rows].reshape(vector_gate.shape)
    share_vector_out = grad_small[gate_rows : gate_rows + out_rows]
    gain_start = gate_rows + out_rows + laurel_rows
    share_laurel_up = grad_small[gate_rows + out_rows : gain_start]
    gain_share = grad_small[gain_start:].reshape(-1)
    gain_grads = tuple(gain_share[start : start + size] for start, size in zip(gain_starts, gain_sizes))
    value_start = query_width + key_width
    return (
        (
            result.astype(jnp.bfloat16),
            d_source,
            d_vectors,
            grad_inward[:, :query_width],
            grad_inward[:, query_width:value_start],
            grad_inward[:, value_start : value_start + key_width],
            grad_output,
            grad_inward[:, value_start + key_width : value_start + key_width + rank],
            share_laurel_up,
            share_vector_gate,
            share_vector_out,
        )
        + gain_grads
        + hidden_grads
    )


def solution(mesh):
    rows = P(("fsdp", "ctx"), None)
    line = P(("fsdp", "ctx"))
    weight = P("fsdp", None)
    gain = P("fsdp")
    return jax.shard_map(
        per_device,
        mesh=mesh,
        in_specs=(rows, rows, line, line, rows) + (weight,) * 8 + (gain,) * 8 + (weight,) * 3,
        out_specs=(rows,) * 3 + (weight,) * 8 + (gain,) * 8 + (weight,) * 3,
        check_vma=False,
    )
```

```python
import functools

import jax
import jax.numpy as jnp
from jax import lax
from jax.experimental import pallas as pl
from jax.experimental.pallas import tpu as pltpu
from jax.sharding import PartitionSpec as P

QUERY_HEADS = 8
KEY_VALUE_HEADS = 2
HEAD_SIZE = 256
WINDOW = 1024


epsilon = 1e-06
rope_base = 10000.0
inv_root = 0.7071067811865476
gelu_scale = 0.7978845608028654
gelu_cubic = 0.044715


def from_behind(value, axis, steps):
    count = lax.axis_size(axis)
    initial, last = (max(0, -steps), min(count, count - steps))
    return lax.ppermute(value, axis, [(source, source + steps) for source in range(initial, last)])


def other_blocks(value, axis):
    count = lax.axis_size(axis)
    return jnp.concatenate(
        [
            lax.ppermute(value, axis, [(source, (source + step) % count) for source in range(count)])
            for step in range(1, count)
        ],
        axis=0,
    )


def root_mean_norm(value, gain):
    factor = lax.rsqrt(jnp.mean(value * value, axis=-1, keepdims=True) + epsilon)
    return value * factor * gain


def gelu_tanh(value):
    return jax.nn.gelu(value, approximate=True)


def gated(gate_value, up_value):
    return gelu_tanh(gate_value) * up_value


def rotary_apply(value, token_position):
    half_size = value.shape[-1] // 2
    frequency = rope_base ** (-2.0 * jnp.arange(half_size, dtype=jnp.float32) / value.shape[-1])
    angle = token_position.astype(jnp.float32)[:, None] * frequency[None, :]
    cosine = jnp.cos(angle)[:, None, :]
    sine_part = jnp.sin(angle)[:, None, :]
    first_half = value[..., :half_size]
    second_half = value[..., half_size:]
    return jnp.concatenate(
        [
            first_half * cosine - second_half * sine_part,
            second_half * cosine + first_half * sine_part,
        ],
        axis=-1,
    )


def rotary_tables(token_position, size):
    half_size = size // 2
    frequency = rope_base ** (-2.0 * jnp.arange(half_size, dtype=jnp.float32) / size)
    angle = token_position.astype(jnp.float32)[:, None] * frequency[None, :]
    return jnp.cos(angle), jnp.sin(angle)


def window(positions, rows_of, reach):
    key_offset = jnp.concatenate(
        [distance * rows_of - jnp.arange(rows_of, dtype=jnp.int32) for distance in range(reach + 1)]
    )
    key_gap = jnp.arange(rows_of, dtype=jnp.int32)[:, None] + key_offset[None, :]
    return key_gap, (key_gap >= 0) & (key_gap <= positions[:, None]) & (key_gap < WINDOW)


def matrix_product(left, right):
    return jnp.dot(left, right, preferred_element_type=jnp.float32)


def product_back(left, right):
    return lax.dot_general(
        left, right, (((1,), (1,)), ((), ())), preferred_element_type=jnp.float32
    )


def product_rows(left, right):
    return lax.dot_general(
        left, right, (((0,), (0,)), ((), ())), preferred_element_type=jnp.float32
    )


def norm_grad(value, gain, upstream):
    unused, pullback = jax.vjp(root_mean_norm, value, gain)
    return pullback(upstream)


def gated_grad(gate_value, up_value, upstream):
    unused, pullback = jax.vjp(gated, gate_value, up_value)
    return pullback(upstream)


def gather(value, axis):
    return lax.all_gather(value, axis, axis=0, tiled=True)


def feature_slices(value):
    count = lax.axis_size("fsdp")
    rows = value.shape[0]
    return lax.all_to_all(
        value.reshape(rows, count, -1), "fsdp", split_axis=1, concat_axis=0, tiled=True
    ).reshape(count * rows, -1)


def scatter_sum(value):
    return lax.psum_scatter(
        value.astype(jnp.bfloat16), "fsdp", scatter_dimension=0, tiled=True
    ).astype(jnp.float32)


def gelu_parts(gate):
    square = gate * gate
    bend = jnp.tanh(gelu_scale * gate * (1.0 + gelu_cubic * square))
    half_up = 0.5 * (1.0 + bend)
    slope = half_up + 0.5 * gate * (1.0 - bend * bend) * (
        gelu_scale * (1.0 + 3.0 * gelu_cubic * square)
    )
    return gate * half_up, slope


def across(me, stride):
    return me + stride - 2 * stride * ((me // stride) % 2)


def across_many(me, bits):
    for stride in (1, 2, 4):
        if bits & stride:
            me = across(me, stride)
    return me


def feed_kernel(forward, rows_of, others, *refs):
    half = rows_of // 2
    if forward:
        (source, normed, attn_lin, middle, laurel, gains), refs = refs[:6], refs[6:]
        (gate_hbm, up_hbm, down_hbm, features, gate_own, out_own), refs = refs[:6], refs[6:]
        (total, mixed, laurel_lin, rows_hbm, far_hbm, near_hbm), refs = refs[:6], refs[6:]
        (slices_hbm, gate_all, out_all, hidden_hbm, lift_hbm, bend_hbm), rest = refs[:6], refs[6:]
        weights_hbm, kept_hbm, made_hbm = (gate_hbm, up_hbm, down_hbm), (), (hidden_hbm, lift_hbm, bend_hbm)
    else:
        (feed_value, mixed, gains, gate_all, out_all, vectors, cotangent), refs = refs[:7], refs[7:]
        (down_hbm, gate_hbm, up_hbm, lift_hbm, bend_hbm, forward_rows, hidden_in), refs = refs[:7], refs[7:]
        (total, result, d_vectors, residual_low, d_vector_low, gated_low, d_back_low, d_residual, gain_rows), refs = (
            refs[:9],
            refs[9:],
        )
        (rows_hbm, far_hbm, near_hbm, *part_hbm, d_gate_hbm, d_up_hbm), rest = refs[:8], refs[8:]
        weights_hbm, kept_hbm, made_hbm = (down_hbm, gate_hbm, up_hbm), (lift_hbm, bend_hbm), (d_gate_hbm, d_up_hbm)
    count_kept, count_made = len(kept_hbm), len(made_hbm)
    weights = rest[:3]
    kept = rest[3 : 3 + count_kept]
    made = rest[3 + count_kept : 3 + count_kept + count_made]
    (own, rows, part, sib_in, chip_sum, relay_in, relay_sum, last_in, send_sem, recv_sem, in_sem, out_sem, far_send, far_recv, near_send, near_recv, *extra) = rest[
        3 + count_kept + count_made :
    ]
    hidden = weights[0].shape[0]
    width = weights[0].shape[1]
    me = lax.axis_index("fsdp")
    sibling, beside, above = across(me, 1), across(me, 2), across(me, 4)

    loads = [
        pltpu.make_async_copy(source, target, in_sem.at[index])
        for index, (source, target) in enumerate(zip(weights_hbm + kept_hbm, tuple(weights) + tuple(kept)))
    ]
    for load in loads:
        load.start()

    block = lax.axis_index("ctx")
    def before_feed():
        def unit(value):
            return value * lax.rsqrt(jnp.mean(value * value, axis=-1, keepdims=True) + epsilon)

        laurel_lin[...] = jnp.dot(middle[...], laurel[...].astype(jnp.bfloat16), preferred_element_type=jnp.float32)
        value = source[...].astype(jnp.float32) + unit(attn_lin[...]) * gains[1:2, :] + normed[...]
        value = (value + unit(laurel_lin[...]) * gains[2:3, :]) * inv_root
        mixed[...] = value
        own[...] = (unit(value) * gains[3:4, :]).astype(jnp.bfloat16)

    def after_feed():
        def unit(value):
            return value * lax.rsqrt(jnp.mean(value * value, axis=-1, keepdims=True) + epsilon)

        residual = mixed[...] + unit(feed_value[...]) * gains[4:5, :]
        residual_low[...] = residual.astype(jnp.bfloat16)
        vector_lin = jnp.dot(residual_low[...], gate_all[...], preferred_element_type=jnp.float32)
        value, slope = gelu_parts(vector_lin)
        per_token = vectors[...].astype(jnp.float32)
        gated_low[...] = (value * per_token).astype(jnp.bfloat16)
        vector_back = jnp.dot(gated_low[...], out_all[...], preferred_element_type=jnp.float32)
        result[...] = (residual + unit(vector_back) * gains[5:6, :]).astype(jnp.bfloat16)
        upstream = cotangent[...].astype(jnp.float32)
        d_back, grad_vector_gain = norm_rows_grad(vector_back, gains[5:6, :], upstream)
        d_back_low[...] = d_back.astype(jnp.bfloat16)
        d_gated = product_back(d_back_low[...], out_all[...])
        d_vectors[...] = d_gated * value
        d_vector_low[...] = (d_gated * per_token * slope).astype(jnp.bfloat16)
        d_residual[...] = upstream + product_back(d_vector_low[...], gate_all[...])
        d_feed, grad_after_gain = norm_rows_grad(feed_value[...], gains[4:5, :], d_residual[...])
        own[...] = d_feed.astype(jnp.bfloat16)
        gain_rows[...] = jnp.zeros_like(gain_rows)
        gain_rows[4:5, :] = grad_after_gain
        gain_rows[5:6, :] = grad_vector_gain

    greet(me, range(1, 8) if forward else (1, 2, 4), block, others, before_feed if forward else after_feed)

    def send(index, source, target, partner):
        return pltpu.make_async_remote_copy(
            src_ref=source,
            dst_ref=target,
            send_sem=send_sem.at[index],
            recv_sem=recv_sem.at[index],
            device_id={"fsdp": partner},
            device_id_type=pl.DeviceIdType.MESH,
        )

    low, high = pl.ds(0, half), pl.ds(half, half)
    mine, theirs = pl.ds(0, rows_of), pl.ds(rows_of, rows_of)
    copies = [
        send(0, own, rows.at[0, theirs], sibling),
        send(1, own.at[low], rows.at[1, low], beside),
        send(2, own.at[low], rows.at[1, high], above),
        send(3, own.at[high], rows.at[2, low], beside),
        send(4, own.at[high], rows.at[2, high], above),
        send(5, rows.at[1, mine], rows.at[1, theirs], sibling),
        send(6, rows.at[2, mine], rows.at[2, theirs], sibling),
        send(7, rows.at[1, low], rows.at[3, low], above),
        send(8, rows.at[2, high], rows.at[3, high], beside),
        send(9, rows.at[3, mine], rows.at[3, theirs], sibling),
        send(10, part.at[0, theirs], sib_in.at[0], sibling),
        send(11, part.at[1, theirs], sib_in.at[1], sibling),
        send(12, part.at[2, theirs], sib_in.at[2], sibling),
        send(13, part.at[3, theirs], sib_in.at[3], sibling),
        send(14, chip_sum.at[0, high], last_in.at[2], above),
        send(15, chip_sum.at[1, low], last_in.at[1], beside),
        send(16, chip_sum.at[2, low], relay_in.at[0], above),
        send(17, chip_sum.at[2, high], relay_in.at[1], beside),
        send(18, relay_sum.at[0], last_in.at[0], beside),
        send(19, relay_sum.at[1], last_in.at[3], above),
    ]
    outs = []

    def write_out(source, target):
        copy = pltpu.make_async_copy(source, target, out_sem.at[len(outs)])
        copy.start()
        outs.append(copy)

    for index in range(5):
        copies[index].start()
    spreads = []
    if forward:
        gate_slots, out_slots, gate_send, gate_recv, vec_send, vec_recv, gate_out, vec_out = extra[3:]
        spreads = [
            spread_copies(gate_own, gate_slots, gate_send, gate_recv, me),
            spread_copies(out_own, out_slots, vec_send, vec_recv, me),
        ]
        for spread in spreads:
            for index in range(5):
                spread[index].start()
        gate_slots[0] = gate_own[...]
        out_slots[0] = out_own[...]
    far = [
        push(own, far_hbm.at[index], far_send.at[index], far_recv.at[index], {"ctx": across_many(block, 2 + index)})
        for index in range(2)
    ]
    for copy in far:
        copy.start()
    def near_source(index):
        if forward:
            return rows.at[1, mine] if index else own
        return forward_rows.at[pl.ds((2 + index) * 2 * rows_of, rows_of)]

    near = [
        push(near_source(index), near_hbm.at[index, mine], near_send.at[index], near_recv.at[index], {"ctx": across(block, 1)})
        for index in range(2)
    ]
    near_share = [
        push(
            near_hbm.at[index, mine],
            near_hbm.at[index, theirs],
            near_send.at[2 + index],
            near_recv.at[2 + index],
            {"fsdp": sibling},
        )
        for index in range(2)
    ]
    near[0].start()
    if not forward:
        near[1].start()
    rows[0, mine] = own[...]
    slices = []
    if forward:
        share = features.shape[1] // 8

        def share_of(device):
            return features.at[:, pl.ds(pl.multiple_of(device * share, share), share)]

        own_slice = pltpu.make_async_copy(share_of(me), slices_hbm.at[me], extra[2])
        own_slice.start()
        slices = [
            pltpu.make_async_remote_copy(
                src_ref=share_of(across_many(me, distance)),
                dst_ref=slices_hbm.at[me],
                send_sem=extra[0].at[distance - 1],
                recv_sem=extra[1].at[distance - 1],
                device_id={"fsdp": across_many(me, distance)},
                device_id_type=pl.DeviceIdType.MESH,
            )
            for distance in range(1, 8)
        ]

    tile = min(hidden, 1024)
    wide = min(width, 1024)

    def first_stage(group):
        span = pl.ds(group * 2 * rows_of, 2 * rows_of)

        def step(index, carry):
            columns = pl.ds(pl.multiple_of(index * tile, tile), tile)
            left = rows[group]

            def back(weight):
                return lax.dot_general(
                    left, weight[columns, :], (((1,), (1,)), ((), ())), preferred_element_type=jnp.float32
                )

            if forward:
                gate, up = back(weights[0]), back(weights[1])
                value, slope = gelu_parts(gate)
                made[0][span, columns] = (value * up).astype(jnp.bfloat16)
                made[1][span, columns] = value.astype(jnp.bfloat16)
                made[2][span, columns] = (slope * up).astype(jnp.bfloat16)
            else:
                d_hidden = back(weights[0])
                made[0][span, columns] = (d_hidden * kept[1][span, columns].astype(jnp.float32)).astype(jnp.bfloat16)
                made[1][span, columns] = (d_hidden * kept[0][span, columns].astype(jnp.float32)).astype(jnp.bfloat16)
            return carry

        lax.fori_loop(0, hidden // tile, step, 0)

    def second_stage(group):
        span = pl.ds(group * 2 * rows_of, 2 * rows_of)

        def step(index, carry):
            columns = pl.ds(pl.multiple_of(index * wide, wide), wide)
            if forward:
                value = jnp.dot(made[0][span, :], weights[2][:, columns], preferred_element_type=jnp.float32)
            else:
                value = jnp.dot(made[0][span, :], weights[1][:, columns], preferred_element_type=jnp.float32)
                value = value + jnp.dot(made[1][span, :], weights[2][:, columns], preferred_element_type=jnp.float32)
            part[group, :, columns] = value.astype(jnp.bfloat16)
            return carry

        lax.fori_loop(0, width // wide, step, 0)

    fillers = []
    if not forward:
        hidden_rows, forward_all, tiles, hidden_sem, forward_sem, tile_sem = extra
        side_loads = [
            pltpu.make_async_copy(hidden_in, hidden_rows, hidden_sem),
            pltpu.make_async_copy(forward_rows, forward_all, forward_sem),
        ]
        tile_width = tiles.shape[2]
        tiles_each = width // tile_width
        tile_copies = [
            pltpu.make_async_copy(
                tiles.at[index % 2],
                part_hbm[index // tiles_each].at[:, pl.ds((index % tiles_each) * tile_width, tile_width)],
                tile_sem.at[index],
            )
            for index in range(3 * tiles_each)
        ]

        def weight_tile(index):
            kind, columns = index // tiles_each, pl.ds((index % tiles_each) * tile_width, tile_width)
            if index >= 2:
                tile_copies[index - 2].wait()
            if kind == 2:
                right = rows[:, :, columns].reshape(8 * rows_of, tile_width)
                tiles[index % 2] = product_rows(hidden_rows[...], right)
            else:
                tiles[index % 2] = product_rows(made[kind][...], forward_all[:, columns])
            tile_copies[index].start()

        fillers = [functools.partial(weight_tile, index) for index in range(3 * tiles_each)]

    def fill(count):
        for unused in range(min(count, len(fillers))):
            fillers.pop(0)()

    def keep_out(group):
        span = pl.ds(group * 2 * rows_of, 2 * rows_of)
        write_out(rows.at[group], rows_hbm.at[span])
        for source, target in zip(made, made_hbm):
            write_out(source.at[span], target.at[span])

    def add_chip(group):
        chip_sum[group - 1] = (
            part[group, mine].astype(jnp.float32) + sib_in[group].astype(jnp.float32)
        ).astype(jnp.bfloat16)

    if not forward:
        for load in side_loads:
            load.start()
    copies[0].wait_recv()
    loads[0].wait()
    if forward:
        loads[1].wait()
    else:
        loads[3].wait()
        loads[4].wait()
    first_stage(0)
    if forward:
        loads[2].wait()
    else:
        loads[1].wait()
        loads[2].wait()
    second_stage(0)
    copies[10].start()
    keep_out(0)
    copies[1].wait_recv()
    copies[7].start()
    copies[2].wait_recv()
    copies[5].start()
    if forward:
        near[1].start()
    copies[5].wait_recv()
    first_stage(1)
    second_stage(1)
    copies[11].start()
    keep_out(1)
    copies[3].wait_recv()
    copies[4].wait_recv()
    copies[8].start()
    copies[6].start()
    copies[11].wait_recv()
    add_chip(1)
    copies[14].start()
    copies[6].wait_recv()
    first_stage(2)
    second_stage(2)
    copies[12].start()
    keep_out(2)
    for copy in slices:
        copy.start()
    for spread in spreads:
        for index in range(1, 5):
            spread[index].wait_recv()
        for index in range(5, 11):
            spread[index].start()
    copies[7].wait_recv()
    copies[8].wait_recv()
    copies[9].start()
    copies[12].wait_recv()
    add_chip(2)
    copies[15].start()
    copies[9].wait_recv()
    first_stage(3)
    second_stage(3)
    copies[13].start()
    keep_out(3)
    if not forward:
        for load in side_loads:
            load.wait()
    fill(1)
    copies[13].wait_recv()
    add_chip(3)
    copies[16].start()
    copies[17].start()
    for spread in spreads:
        for index in (9, 10):
            spread[index].wait_recv()
        for index in (11, 12):
            spread[index].start()
    fill(4)
    copies[10].wait_recv()
    total[...] = part[0, mine].astype(jnp.float32) + sib_in[0].astype(jnp.float32)
    copies[16].wait_recv()
    relay_sum[0] = (chip_sum[0, low].astype(jnp.float32) + relay_in[0].astype(jnp.float32)).astype(jnp.bfloat16)
    copies[18].start()
    copies[17].wait_recv()
    relay_sum[1] = (chip_sum[1, high].astype(jnp.float32) + relay_in[1].astype(jnp.float32)).astype(jnp.bfloat16)
    copies[19].start()
    fill(4)
    copies[14].wait_recv()
    total[low] = total[low] + last_in[2].astype(jnp.float32)
    copies[15].wait_recv()
    total[high] = total[high] + last_in[1].astype(jnp.float32)
    for index in range(2):
        near[index].wait_recv()
        near_share[index].start()
    copies[18].wait_recv()
    total[low] = total[low] + last_in[0].astype(jnp.float32)
    fill(len(fillers))
    copies[19].wait_recv()
    total[high] = total[high] + last_in[3].astype(jnp.float32)
    if not forward:
        for copy in tile_copies[-2:]:
            copy.wait()
    if forward:
        for spread, slots, target, sems in (
            (spreads[0], gate_slots, gate_all, gate_out),
            (spreads[1], out_slots, out_all, vec_out),
        ):
            for index in (0, 5, 6, 7, 8, 11, 12):
                spread[index].wait_recv()
            size = slots.shape[1]
            for slot in range(8):
                place = pl.ds(pl.multiple_of(across_many(me, slot) * size, size), size)
                copy = pltpu.make_async_copy(slots.at[slot], target.at[place], sems.at[slot])
                copy.start()
                outs.append(copy)
            for copy in spread:
                copy.wait_send()
    for copy in copies:
        copy.wait_send()
    for copy in outs:
        copy.wait()
    for copy in far + slices:
        copy.wait()
    for index in range(2):
        near[index].wait_send()
        near_share[index].wait()
    if forward:
        own_slice.wait()


def turn(value, cosine, sine, direction=1.0):
    middle = value.shape[1] // 2
    first, second = value[:, :middle], value[:, middle:]
    sine = sine * direction
    return jnp.concatenate([first * cosine - second * sine, second * cosine + first * sine], axis=1)


def window_mask(positions, rows_of, blocks):
    row = lax.broadcasted_iota(jnp.int32, (rows_of, rows_of), 0)
    column = lax.broadcasted_iota(jnp.int32, (rows_of, rows_of), 1)
    positions = jnp.sum(jnp.where(row == column, positions, 0), axis=1, keepdims=True)
    query_row = lax.broadcasted_iota(jnp.int32, (rows_of, blocks * rows_of), 0)
    column = lax.broadcasted_iota(jnp.int32, (rows_of, blocks * rows_of), 1)
    behind = column // rows_of
    gap = query_row + 2 * behind * rows_of - column
    return (gap >= 0) & (gap <= positions) & (gap < WINDOW)


def norm_rows_grad(value, gain, upstream):
    factor = lax.rsqrt(jnp.mean(value * value, axis=-1, keepdims=True) + epsilon)
    unit = value * factor
    grad_gain = jnp.sum(upstream * unit, axis=0, keepdims=True)
    back = upstream * gain
    return factor * (back - unit * jnp.mean(back * unit, axis=-1, keepdims=True)), grad_gain


def greet(me, partners, block, others, work=None):
    barrier = pltpu.get_barrier_semaphore()
    for distance in partners:
        pl.semaphore_signal(
            barrier, inc=1, device_id={"fsdp": across_many(me, distance)}, device_id_type=pl.DeviceIdType.MESH
        )
    for distance in range(1, others + 1):
        pl.semaphore_signal(
            barrier,
            inc=1,
            device_id={"ctx": (block + distance) % (others + 1)},
            device_id_type=pl.DeviceIdType.MESH,
        )
    if work is not None:
        work()
    pl.semaphore_wait(barrier, len(partners) + others)


def push(source, target, send_sem, recv_sem, place):
    return pltpu.make_async_remote_copy(
        src_ref=source,
        dst_ref=target,
        send_sem=send_sem,
        recv_sem=recv_sem,
        device_id=place,
        device_id_type=pl.DeviceIdType.MESH,
    )


def spread_copies(own, slots, send_sem, recv_sem, me):
    half = own.shape[0] // 2
    low, high = pl.ds(0, half), pl.ds(half, half)
    sibling, beside, above = across(me, 1), across(me, 2), across(me, 4)
    plan = [
        (own, slots.at[1], sibling),
        (own.at[low], slots.at[2, low], beside),
        (own.at[low], slots.at[4, low], above),
        (own.at[high], slots.at[2, high], beside),
        (own.at[high], slots.at[4, high], above),
        (slots.at[2, low], slots.at[3, low], sibling),
        (slots.at[4, low], slots.at[5, low], sibling),
        (slots.at[2, high], slots.at[3, high], sibling),
        (slots.at[4, high], slots.at[5, high], sibling),
        (slots.at[2, low], slots.at[6, low], above),
        (slots.at[4, high], slots.at[6, high], beside),
        (slots.at[6, low], slots.at[7, low], sibling),
        (slots.at[6, high], slots.at[7, high], sibling),
    ]
    return [
        push(source, target, send_sem.at[index], recv_sem.at[index], {"fsdp": partner})
        for index, (source, target, partner) in enumerate(plan)
    ]


def attend_kernel(
    others, reach, source, gain_one, gain_two, gain_three, gain_four, gain_five, gain_six, head_gains, laurel_own,
    positions, cosine, sine, query_own, key_own, value_own, down_own, outward_own,
    normed, gains, linear, query_low, key_value, features, middle, attn_lin, laurel_all, inward_all, outward_all,
    gain_share, gain_slots, inward_slots, outward_slots, normed_low, attended, inward, lin_sum,
    gain_send, gain_recv, in_send, in_recv, out_send, out_recv, kv_send, kv_recv, in_copy, out_copy,
):
    rows_of, width = source.shape
    me, block = lax.axis_index("fsdp"), lax.axis_index("ctx")
    inward_own = inward_slots.at[0]
    gain_lines = gain_slots.at[0]

    def own_shares():
        start = 0
        for piece in (query_own, key_own, value_own, down_own):
            value = piece[...] if piece is not down_own else down_own[...].astype(jnp.float32).T.astype(jnp.bfloat16)
            inward_slots[0, :, pl.ds(start, value.shape[1])] = value
            start += value.shape[1]
        inward_slots[0, :, pl.ds(start, inward_slots.shape[2] - start)] = jnp.zeros(
            (inward_slots.shape[1], inward_slots.shape[2] - start), jnp.bfloat16
        )
        gain_share[...] = jnp.zeros_like(gain_share)
        for index, gain in enumerate((gain_one, gain_two, gain_three, gain_four, gain_five, gain_six)):
            pieces = gain[...].astype(jnp.float32)
            size = pieces.shape[0] * 128
            for row in range(pieces.shape[0]):
                place = pl.ds(pl.multiple_of(me * size + row * 128, 128), 128)
                gain_share[index : index + 1, place] = pieces[row : row + 1, :]
        gain_share[6:8, 0:HEAD_SIZE] = head_gains[...].astype(jnp.float32)
        gain_share[8:16, :] = laurel_own[...].astype(jnp.float32)
        gain_slots[0] = gain_share[...].astype(jnp.bfloat16)

    greet(me, range(1, 8), block, others, own_shares)
    gain_copies = [
        push(gain_lines, gain_slots.at[distance], gain_send.at[distance - 1], gain_recv.at[distance - 1],
             {"fsdp": across_many(me, distance)})
        for distance in range(1, 8)
    ]
    for copy in gain_copies:
        copy.start()
    spread_in = spread_copies(inward_own, inward_slots, in_send, in_recv, me)
    spread_out = spread_copies(outward_own, outward_slots, out_send, out_recv, me)
    for index in range(5):
        spread_in[index].start()
    outward_slots[0] = outward_own[...]

    value = source[...].astype(jnp.float32)
    factor = lax.rsqrt(jnp.mean(value * value, axis=-1, keepdims=True) + epsilon)
    for copy in gain_copies:
        copy.wait_recv()
    lines = gain_slots[...].astype(jnp.float32)
    gains[...] = jnp.sum(lines, axis=0)[0:8]
    laurel_size = 8
    laurel_all[...] = jnp.zeros_like(laurel_all)
    for slot in range(8):
        device = across_many(me, slot)
        laurel_all[pl.ds(pl.multiple_of(device * laurel_size, laurel_size), laurel_size), :] = lines[slot, 8:16]
    value = value * factor * gains[0:1, :]
    normed[...] = value
    normed_low[...] = value.astype(jnp.bfloat16)
    share = width // 8
    for index in range(8):
        features[:, pl.ds(2 * index * share, share)] = normed_low[:, pl.ds(index * share, share)]

    depth = inward_own.shape[0]
    head_rows = width // 8
    written = []

    def add_inward(slot):
        device = across_many(me, slot)
        part = normed_low[:, pl.ds(pl.multiple_of(device * depth, depth), depth)]
        for start in range(0, inward.shape[1], 640):
            span = pl.ds(start, 640)
            product = jnp.dot(part, inward_slots[slot, :, span], preferred_element_type=jnp.float32)
            inward[:, span] = product if slot == 0 else inward[:, span] + product
        copy = pltpu.make_async_copy(
            inward_slots.at[slot], inward_all.at[pl.ds(pl.multiple_of(device * depth, depth), depth)], in_copy.at[slot]
        )
        copy.start()
        written.append(copy)

    def add_outward(slot):
        device = across_many(me, slot)
        part = attended[:, pl.ds(pl.multiple_of(device * head_rows, head_rows), head_rows)]
        for start in range(0, width, 512):
            span = pl.ds(start, 512)
            product = jnp.dot(part, outward_slots[slot, pl.ds(0, head_rows), span], preferred_element_type=jnp.float32)
            lin_sum[:, span] = product if slot == 0 else lin_sum[:, span] + product

    def write_outward(slot):
        device = across_many(me, slot)
        rows = pl.ds(pl.multiple_of(device * head_rows, head_rows), head_rows)
        copy = pltpu.make_async_copy(outward_slots.at[slot], outward_all.at[rows], out_copy.at[slot])
        copy.start()
        written.append(copy)

    add_inward(0)
    spread_in[0].wait_recv()
    add_inward(1)
    spread_in[1].wait_recv()
    spread_in[9].start()
    spread_in[5].start()
    spread_in[2].wait_recv()
    spread_in[6].start()
    spread_in[3].wait_recv()
    spread_in[7].start()
    spread_in[4].wait_recv()
    spread_in[10].start()
    spread_in[8].start()
    for index in range(5):
        spread_out[index].start()
    add_inward(2)
    add_inward(4)
    spread_in[5].wait_recv()
    spread_in[7].wait_recv()
    add_inward(3)
    spread_in[6].wait_recv()
    spread_in[8].wait_recv()
    add_inward(5)
    spread_in[9].wait_recv()
    spread_in[11].start()
    spread_in[10].wait_recv()
    spread_in[12].start()
    add_inward(6)
    spread_in[11].wait_recv()
    spread_in[12].wait_recv()
    add_inward(7)

    query_width, key_width = QUERY_HEADS * HEAD_SIZE, KEY_VALUE_HEADS * HEAD_SIZE
    own_rows = pl.ds(0, rows_of)

    def head(start, gain):
        lane = inward[:, pl.ds(start, HEAD_SIZE)]
        scale = lax.rsqrt(jnp.mean(lane * lane, axis=-1, keepdims=True) + epsilon)
        return turn(lane * scale * gain, cosine[...], sine[...]).astype(jnp.bfloat16)

    for index in range(KEY_VALUE_HEADS):
        key_value[own_rows, pl.ds(index * HEAD_SIZE, HEAD_SIZE)] = head(
            query_width + index * HEAD_SIZE, gains[7:8, 0:HEAD_SIZE]
        )
    key_value[own_rows, pl.ds(key_width, key_width)] = inward[:, pl.ds(query_width + key_width, key_width)].astype(
        jnp.bfloat16
    )
    for distance in range(1, reach + 1):
        copy = push(
            key_value.at[own_rows],
            key_value.at[pl.ds(distance * rows_of, rows_of)],
            kv_send.at[distance - 1],
            kv_recv.at[distance - 1],
            {"ctx": (block + distance) % (others + 1)},
        )

        @pl.when(block + distance <= others)
        def _():
            copy.start()

        @pl.when(block < distance)
        def _():
            key_value[pl.ds(distance * rows_of, rows_of), :] = jnp.zeros((rows_of, 2 * key_width), jnp.bfloat16)

    for index in range(QUERY_HEADS):
        query_low[:, pl.ds(index * HEAD_SIZE, HEAD_SIZE)] = head(index * HEAD_SIZE, gains[6:7, 0:HEAD_SIZE])
    linear[...] = inward[:, pl.ds(0, query_width + key_width)]
    middle[...] = inward[:, pl.ds(query_width + 2 * key_width, middle.shape[1])].astype(jnp.bfloat16)

    spread_out[0].wait_recv()
    spread_out[1].wait_recv()
    spread_out[9].start()
    spread_out[5].start()
    spread_out[2].wait_recv()
    spread_out[6].start()
    for distance in range(1, reach + 1):
        copy = push(
            key_value.at[own_rows],
            key_value.at[pl.ds(distance * rows_of, rows_of)],
            kv_send.at[distance - 1],
            kv_recv.at[distance - 1],
            {"ctx": (block + distance) % (others + 1)},
        )

        @pl.when(block >= distance)
        def _():
            copy.wait_recv()

    allowed = window_mask(positions[...], rows_of, reach + 1)
    per_group = QUERY_HEADS // KEY_VALUE_HEADS
    for index in range(QUERY_HEADS):
        group = index // per_group
        columns = pl.ds(index * HEAD_SIZE, HEAD_SIZE)
        scores = product_back(query_low[:, columns], key_value[:, pl.ds(group * HEAD_SIZE, HEAD_SIZE)])
        scores = jnp.where(allowed, scores * HEAD_SIZE ** (-0.5), -1e30)
        grown = jnp.exp(scores - jnp.max(scores, axis=-1, keepdims=True))
        soft = (grown / jnp.sum(grown, axis=-1, keepdims=True)).astype(jnp.bfloat16)
        attended[:, columns] = jnp.dot(
            soft, key_value[:, pl.ds(key_width + group * HEAD_SIZE, HEAD_SIZE)], preferred_element_type=jnp.float32
        ).astype(jnp.bfloat16)

    for index in range(8):
        features[:, pl.ds((2 * index + 1) * share, share)] = attended[:, pl.ds(index * share, share)]
    add_outward(0)
    add_outward(1)
    write_outward(0)
    write_outward(1)
    spread_out[3].wait_recv()
    spread_out[7].start()
    spread_out[4].wait_recv()
    spread_out[10].start()
    spread_out[8].start()
    add_outward(2)
    add_outward(4)
    spread_out[5].wait_recv()
    spread_out[7].wait_recv()
    add_outward(3)
    spread_out[6].wait_recv()
    spread_out[8].wait_recv()
    add_outward(5)
    for slot in range(2, 6):
        write_outward(slot)
    spread_out[9].wait_recv()
    spread_out[11].start()
    spread_out[10].wait_recv()
    spread_out[12].start()
    add_outward(6)
    write_outward(6)
    spread_out[11].wait_recv()
    spread_out[12].wait_recv()
    add_outward(7)
    write_outward(7)
    attn_lin[...] = lin_sum[...]
    for copy in gain_copies + spread_in + spread_out:
        copy.wait_send()
    for copy in written:
        copy.wait()
    for distance in range(1, reach + 1):
        copy = push(
            key_value.at[own_rows],
            key_value.at[pl.ds(distance * rows_of, rows_of)],
            kv_send.at[distance - 1],
            kv_recv.at[distance - 1],
            {"ctx": (block + distance) % (others + 1)},
        )

        @pl.when(block + distance <= others)
        def _():
            copy.wait_send()


def attend_call(reach, source, gains, head_gains, laurel_own, positions, cosine, sine, inward_own, outward_own):
    rows_of, width = source.shape
    others = lax.axis_size("ctx") - 1
    low, full = jnp.bfloat16, jnp.float32
    hbm = pl.BlockSpec(memory_space=pl.ANY)
    vmem = pl.BlockSpec(memory_space=pltpu.VMEM)
    dma = pltpu.SemaphoreType.DMA
    depth = inward_own[0].shape[0]
    columns = sum(piece.shape[1] for piece in inward_own[:3]) + inward_own[3].shape[0]
    columns += -columns % 128
    gain_shape = (16, width)
    query_width, key_width = QUERY_HEADS * HEAD_SIZE, KEY_VALUE_HEADS * HEAD_SIZE
    tail = columns - query_width - 2 * key_width
    shapes = [
        jax.ShapeDtypeStruct((rows_of, width), full),
        jax.ShapeDtypeStruct((8, width), full),
        jax.ShapeDtypeStruct((rows_of, query_width + key_width), full),
        jax.ShapeDtypeStruct((rows_of, query_width), low),
        jax.ShapeDtypeStruct(((reach + 1) * rows_of, 2 * key_width), low),
        jax.ShapeDtypeStruct((rows_of, 2 * width), low),
        jax.ShapeDtypeStruct((rows_of, tail), low),
        jax.ShapeDtypeStruct((rows_of, width), full),
        jax.ShapeDtypeStruct((tail, width), full),
        jax.ShapeDtypeStruct((8 * depth, columns), low),
        jax.ShapeDtypeStruct((8 * outward_own.shape[0], width), low),
    ]
    return pl.pallas_call(
        functools.partial(attend_kernel, others, reach),
        out_shape=shapes,
        in_specs=[vmem] * 17,
        out_specs=[vmem] * 9 + [hbm] * 2,
        scratch_shapes=[
            pltpu.VMEM(gain_shape, full),
            pltpu.VMEM((8, *gain_shape), low),
            pltpu.VMEM((8, depth, columns), low),
            pltpu.VMEM((8, *outward_own.shape), low),
            pltpu.VMEM((rows_of, width), low),
            pltpu.VMEM((rows_of, query_width), low),
            pltpu.VMEM((rows_of, columns), full),
            pltpu.VMEM((rows_of, width), full),
            dma((7,)),
            dma((7,)),
            dma((13,)),
            dma((13,)),
            dma((13,)),
            dma((13,)),
            dma((max(reach, 1),)),
            dma((max(reach, 1),)),
            dma((8,)),
            dma((8,)),
        ],
        compiler_params=pltpu.CompilerParams(collective_id=3, has_side_effects=True, vmem_limit_bytes=56 * 2**20),
        cost_estimate=pl.CostEstimate(
            flops=60 * rows_of * width * columns, bytes_accessed=20 * depth * columns, transcendentals=0
        ),
        name="attend_forward",
    )(source, *gains, head_gains, laurel_own, positions, cosine, sine, *inward_own, outward_own)


def turn_norm_grad(upstream, linear, gain, cosine, sine):
    scale = lax.rsqrt(jnp.mean(linear * linear, axis=-1, keepdims=True) + epsilon)
    unit = linear * scale
    back = turn(upstream, cosine, sine, -1.0)
    grad_gain = jnp.sum(back * unit, axis=0, keepdims=True)
    back = back * gain
    return scale * (back - unit * jnp.mean(back * unit, axis=-1, keepdims=True)), grad_gain


def attend_back_kernel(
    others, reach, d_ffn_in, mixed, d_residual, laurel_lin, attn_lin, laurel, gain_part,
    query_low, key_value, linear, gains, positions, cosine, sine, middle, features,
    source, residual, d_vector, gated_value, d_back, outward_all, inward_all, d_rows,
    d_source, grad_wide, grad_small, near_hbm,
    d_lin, d_half, d_laurel, d_middle, gain_rows,
    outward, inward, d_attended, d_key_value, parcel, arrived, d_query, d_rest, lin_slots, query_slots, rest_slots,
    ordered, d_normed, gain_parcel, gain_arrived, laurel_arrived, load_sem, lin_send, lin_recv, query_send, query_recv, rest_send, rest_recv, kv_send, kv_recv, gain_send, gain_recv, laurel_send, laurel_recv, near_send, near_recv,
    gate_in, gate_sum, gate_arrived, out_in, out_sum, out_arrived, pair_send, pair_recv, chip_send, chip_recv,
    gate_parts, out_parts, laurel_rows,
):
    rows_of, width = source.shape
    me, block = lax.axis_index("fsdp"), lax.axis_index("ctx")
    query_width, key_width = QUERY_HEADS * HEAD_SIZE, KEY_VALUE_HEADS * HEAD_SIZE
    per_group = QUERY_HEADS // KEY_VALUE_HEADS
    depth = width // 8
    loads = [
        pltpu.make_async_copy(outward_all.at[pl.ds(index * depth, depth)], outward.at[index % 2], load_sem.at[index])
        for index in range(8)
    ]
    loads.append(pltpu.make_async_copy(inward_all, inward, load_sem.at[8]))
    for index in (0, 1, 8):
        loads[index].start()

    def before_attention():
        d_mixed, grad_before = norm_rows_grad(mixed[...], gains[3:4, :], d_ffn_in[...])
        d_half[...] = (d_residual[...] + d_mixed) * inv_root
        d_branch, grad_laurel_gain = norm_rows_grad(laurel_lin[...], gains[2:3, :], d_half[...])
        d_laurel[...] = d_branch.astype(jnp.bfloat16)
        d_middle[...] = product_back(d_laurel[...], laurel[...].astype(jnp.bfloat16)).astype(jnp.bfloat16)
        d_branch, grad_attention = norm_rows_grad(attn_lin[...], gains[1:2, :], d_half[...])
        d_lin[...] = d_branch.astype(jnp.bfloat16)
        gain_rows[...] = gain_part[...]
        gain_rows[1:2, :] = grad_attention
        gain_rows[2:3, :] = grad_laurel_gain
        gain_rows[3:4, :] = grad_before

    greet(me, range(1, 8), block, others, before_attention)
    mine, theirs = pl.ds(0, rows_of), pl.ds(rows_of, rows_of)
    near = [
        push(
            d_rows.at[pl.ds(group * 2 * rows_of, rows_of)],
            near_hbm.at[group, mine],
            near_send.at[group],
            near_recv.at[group],
            {"ctx": across(block, 1)},
        )
        for group in range(4)
    ]
    near_share = [
        push(
            near_hbm.at[group, mine],
            near_hbm.at[group, theirs],
            near_send.at[4 + group],
            near_recv.at[4 + group],
            {"fsdp": across(me, 1)},
        )
        for group in range(4)
    ]
    for copy in near[:2]:
        copy.start()
    vector_parts = ((gate_parts, gate_in, gate_sum, gate_arrived), (out_parts, out_in, out_sum, out_arrived))
    chips = (0, 2, 4, 6)
    pair_copies = []
    chip_copies = []
    for kind, (parts, pair_in, pair_sum, arrived_parts) in enumerate(vector_parts):
        for index, chip in enumerate(chips):
            place = 4 * kind + index
            pair_copies.append(
                push(
                    parts.at[across_many(me, chip + 1)],
                    pair_in.at[index],
                    pair_send.at[place],
                    pair_recv.at[place],
                    {"fsdp": across(me, 1)},
                )
            )
            if chip:
                place = 3 * kind + index - 1
                chip_copies.append(
                    push(
                        pair_sum.at[index - 1],
                        arrived_parts.at[index - 1],
                        chip_send.at[place],
                        chip_recv.at[place],
                        {"fsdp": across_many(me, chip)},
                    )
                )
    spread_lin = spread_copies(d_lin, lin_slots, lin_send, lin_recv, me)
    spread_query = spread_copies(d_query, query_slots, query_send, query_recv, me)
    spread_rest = spread_copies(d_rest, rest_slots, rest_send, rest_recv, me)
    for index in range(5):
        spread_lin[index].start()
    lin_slots[0] = d_lin[...]
    for index in range(8):
        gate_parts[index] = product_rows(residual[:, pl.ds(index * depth, depth)], d_vector[...]).astype(jnp.bfloat16)
    out_parts[...] = product_rows(gated_value[...], d_back[...]).reshape(out_parts.shape).astype(jnp.bfloat16)
    laurel_rows[...] = product_rows(middle[...], d_laurel[...])[0 : 8 * laurel_rows.shape[1]].reshape(laurel_rows.shape)
    for copy in pair_copies:
        copy.start()
    laurel_copies = [
        push(
            laurel_rows.at[across_many(me, distance)],
            laurel_arrived.at[distance],
            laurel_send.at[distance - 1],
            laurel_recv.at[distance - 1],
            {"fsdp": across_many(me, distance)},
        )
        for distance in range(1, 8)
    ]
    laurel_arrived[0] = laurel_rows[me]
    for slot in range(8):
        device = across_many(me, slot)
        ordered[pl.ds(slot * rows_of, rows_of), :] = features[
            pl.ds(pl.multiple_of(device * rows_of, rows_of), rows_of), :
        ]
    for index in range(8):
        loads[index].wait()
        d_attended[:, pl.ds(index * depth, depth)] = product_back(d_lin[...], outward[index % 2]).astype(jnp.bfloat16)
        if index + 2 < 8:
            loads[index + 2].start()

    allowed = window_mask(positions[...], rows_of, reach + 1)
    scale = HEAD_SIZE ** (-0.5)

    def one_head(index):
        group = index // per_group
        columns = pl.ds(index * HEAD_SIZE, HEAD_SIZE)
        keys = pl.ds(group * HEAD_SIZE, HEAD_SIZE)
        values = pl.ds(key_width + group * HEAD_SIZE, HEAD_SIZE)
        scores = product_back(query_low[:, columns], key_value[:, keys])
        scores = jnp.where(allowed, scores * scale, -1e30)
        grown = jnp.exp(scores - jnp.max(scores, axis=-1, keepdims=True))
        soft = grown / jnp.sum(grown, axis=-1, keepdims=True)
        d_soft = product_back(d_attended[:, columns], key_value[:, values])
        d_scores = (soft * (d_soft - jnp.sum(soft * d_soft, axis=-1, keepdims=True))).astype(jnp.bfloat16)
        upstream = scale * jnp.dot(d_scores, key_value[:, keys], preferred_element_type=jnp.float32)
        d_key = scale * product_rows(d_scores, query_low[:, columns])
        d_value = product_rows(soft.astype(jnp.bfloat16), d_attended[:, columns])
        if index % per_group == 0:
            d_key_value[:, keys] = d_key
            d_key_value[:, values] = d_value
        else:
            d_key_value[:, keys] += d_key
            d_key_value[:, values] += d_value
        d_head, grad_gain = turn_norm_grad(upstream, linear[:, columns], gains[6:7, 0:HEAD_SIZE], cosine[...], sine[...])
        d_query[:, columns] = d_head.astype(jnp.bfloat16)
        return grad_gain

    query_gain = one_head(0)
    for index in range(1, per_group):
        query_gain = query_gain + one_head(index)
    spread_lin[0].wait_recv()
    spread_lin[1].wait_recv()
    spread_lin[9].start()
    spread_lin[5].start()
    spread_lin[2].wait_recv()
    spread_lin[6].start()
    for index in range(per_group, QUERY_HEADS):
        query_gain = query_gain + one_head(index)
    parcel[...] = d_key_value[pl.ds(rows_of, reach * rows_of), :].astype(jnp.bfloat16)

    def return_copy(distance):
        span = pl.ds((distance - 1) * rows_of, rows_of)
        return push(
            parcel.at[span],
            arrived.at[span],
            kv_send.at[distance - 1],
            kv_recv.at[distance - 1],
            {"ctx": (block + others + 1 - distance) % (others + 1)},
        )

    for distance in range(1, reach + 1):
        copy = return_copy(distance)

        @pl.when(block >= distance)
        def _():
            copy.start()

        @pl.when(block + distance > others)
        def _():
            arrived[pl.ds((distance - 1) * rows_of, rows_of), :] = jnp.zeros((rows_of, 2 * key_width), jnp.bfloat16)

    for copy in near[2:]:
        copy.start()
    spread_lin[3].wait_recv()
    spread_lin[7].start()
    spread_lin[4].wait_recv()
    spread_lin[10].start()
    spread_lin[8].start()
    for index in range(5):
        spread_query[index].start()
    for copy in pair_copies:
        copy.wait_recv()
    for parts, pair_in, pair_sum, arrived_parts in vector_parts:
        for index, chip in enumerate(chips):
            if chip:
                pair_sum[index - 1] = (
                    parts[across_many(me, chip)].astype(jnp.float32) + pair_in[index].astype(jnp.float32)
                ).astype(jnp.bfloat16)
    for copy in chip_copies:
        copy.start()
    query_slots[0] = d_query[...]
    loads[8].wait()
    d_normed[...] = product_back(d_query[...], inward[:, pl.ds(0, query_width)])
    spread_lin[9].wait_recv()
    spread_lin[11].start()
    spread_lin[10].wait_recv()
    spread_lin[12].start()
    spread_query[0].wait_recv()
    spread_query[1].wait_recv()
    spread_query[9].start()
    spread_query[5].start()
    spread_query[2].wait_recv()
    spread_query[6].start()
    for index in (5, 6, 7, 8, 11, 12):
        spread_lin[index].wait_recv()
    grad_wide[:, pl.ds(inward.shape[1], width)] = product_rows(
        ordered[:, pl.ds(depth, depth)], lin_slots[...].reshape(8 * rows_of, width)
    ).astype(jnp.bfloat16)

    for distance in range(1, reach + 1):
        copy = return_copy(distance)

        @pl.when(block + distance <= others)
        def _():
            copy.wait_recv()

    total = d_key_value[pl.ds(0, rows_of), :]
    for distance in range(1, reach + 1):
        total = total + arrived[pl.ds((distance - 1) * rows_of, rows_of), :].astype(jnp.float32)
    for index in range(KEY_VALUE_HEADS):
        columns = pl.ds(index * HEAD_SIZE, HEAD_SIZE)
        d_head, grad_gain = turn_norm_grad(
            total[:, index * HEAD_SIZE : (index + 1) * HEAD_SIZE],
            linear[:, pl.ds(query_width + index * HEAD_SIZE, HEAD_SIZE)],
            gains[7:8, 0:HEAD_SIZE],
            cosine[...],
            sine[...],
        )
        d_rest[:, columns] = d_head.astype(jnp.bfloat16)
        key_gain = grad_gain if index == 0 else key_gain + grad_gain
    d_rest[:, pl.ds(key_width, key_width)] = total[:, key_width:].astype(jnp.bfloat16)
    d_rest[:, pl.ds(2 * key_width, d_middle.shape[1])] = d_middle[...]
    spread_query[3].wait_recv()
    spread_query[7].start()
    spread_query[4].wait_recv()
    spread_query[10].start()
    spread_query[8].start()
    for index in range(5):
        spread_rest[index].start()
    rest_slots[0] = d_rest[...]
    rest_width = d_rest.shape[1]
    d_normed[...] += product_back(d_rest[...], inward[:, pl.ds(query_width, rest_width)])
    value = source[...].astype(jnp.float32)
    factor = lax.rsqrt(jnp.mean(value * value, axis=-1, keepdims=True) + epsilon)
    unit = value * factor
    upstream = d_half[...] + d_normed[...]
    for index in range(8):
        columns = slice(index * depth, (index + 1) * depth)
        gain_parcel[index, 0:8, :] = gain_rows[0:8, columns]
        gain_parcel[index, 0:1, :] = jnp.sum(upstream[:, columns] * unit[:, columns], axis=0, keepdims=True)
        gain_parcel[index, 6:7, :] = query_gain
        gain_parcel[index, 7:8, :] = key_gain
    gain_copies = [
        push(
            gain_parcel.at[across_many(me, distance)],
            gain_arrived.at[distance],
            gain_send.at[distance - 1],
            gain_recv.at[distance - 1],
            {"fsdp": across_many(me, distance)},
        )
        for distance in range(1, 8)
    ]
    for copy in gain_copies + laurel_copies:
        copy.start()
    gain_arrived[0] = gain_parcel[me]
    upstream = upstream * gains[0:1, :]
    d_source[...] = d_half[...] + factor * (upstream - unit * jnp.mean(upstream * unit, axis=-1, keepdims=True))
    spread_rest[0].wait_recv()
    spread_rest[1].wait_recv()
    spread_rest[9].start()
    spread_rest[5].start()
    spread_rest[2].wait_recv()
    spread_rest[6].start()
    spread_query[9].wait_recv()
    spread_query[11].start()
    spread_query[10].wait_recv()
    spread_query[12].start()
    spread_rest[3].wait_recv()
    spread_rest[7].start()
    spread_rest[4].wait_recv()
    spread_rest[10].start()
    spread_rest[8].start()
    for index in (5, 6, 7, 8, 11, 12):
        spread_query[index].wait_recv()
    grad_wide[:, pl.ds(0, query_width)] = product_rows(
        ordered[:, pl.ds(0, depth)], query_slots[...].reshape(8 * rows_of, query_width)
    ).astype(jnp.bfloat16)
    spread_rest[9].wait_recv()
    spread_rest[11].start()
    spread_rest[10].wait_recv()
    spread_rest[12].start()
    for index in (5, 6, 7, 8, 11, 12):
        spread_rest[index].wait_recv()
    grad_wide[:, pl.ds(query_width, rest_width)] = product_rows(
        ordered[:, pl.ds(0, depth)], rest_slots[...].reshape(8 * rows_of, rest_width)
    ).astype(jnp.bfloat16)
    for copy, share in zip(near, near_share):
        copy.wait_recv()
        share.start()
    for copy in gain_copies + laurel_copies + chip_copies:
        copy.wait_recv()
    totals = []
    for parts, pair_in, pair_sum, arrived_parts in vector_parts:
        total = parts[me].astype(jnp.float32) + pair_in[0].astype(jnp.float32)
        for index in range(3):
            total = total + arrived_parts[index].astype(jnp.float32)
        totals.append(total.astype(jnp.bfloat16))
    grad_wide[:, pl.ds(inward.shape[1] + width, totals[0].shape[1])] = totals[0]
    laurel_size = laurel_rows.shape[1]
    tail = jnp.concatenate(
        [jnp.sum(laurel_arrived[...], axis=0), jnp.pad(jnp.sum(gain_arrived[...], axis=0), ((0, 0), (0, width - depth)))],
        axis=0,
    )
    out_size = totals[1].shape[0]
    grad_small[pl.ds(0, out_size), :] = totals[1]
    grad_small[pl.ds(out_size, laurel_size + 8), :] = tail.astype(jnp.bfloat16)
    for copy in near_share:
        copy.wait_recv()
    for copy in (
        spread_lin + spread_query + spread_rest + gain_copies + laurel_copies + near + near_share + pair_copies + chip_copies
    ):
        copy.wait_send()
    for distance in range(1, reach + 1):
        copy = return_copy(distance)

        @pl.when(block >= distance)
        def _():
            copy.wait_send()


def attend_back_call(
    reach, d_ffn_in, mixed, d_residual, laurel_lin, attn_lin, laurel, gain_part,
    query_low, key_value, linear, gains, positions, cosine, sine, middle, features,
    source, residual, d_vector, gated_value, d_back, outward_all, inward_all, d_rows,
):
    rows_of, width = source.shape
    others = lax.axis_size("ctx") - 1
    low, full = jnp.bfloat16, jnp.float32
    hbm = pl.BlockSpec(memory_space=pl.ANY)
    vmem = pl.BlockSpec(memory_space=pltpu.VMEM)
    dma = pltpu.SemaphoreType.DMA
    columns = inward_all.shape[1]
    query_width, key_width = QUERY_HEADS * HEAD_SIZE, KEY_VALUE_HEADS * HEAD_SIZE
    rest_width = columns - query_width
    depth = width // 8
    vector_width = d_vector.shape[1]
    part_shapes = ((depth, vector_width), (vector_width // 8, width))
    shapes = [
        jax.ShapeDtypeStruct((rows_of, width), full),
        jax.ShapeDtypeStruct((depth, columns + width + vector_width), low),
        jax.ShapeDtypeStruct((vector_width // 8 + 16, width), low),
        jax.ShapeDtypeStruct((4, 2 * rows_of, width), low),
    ]
    spans = max(reach, 1)
    return pl.pallas_call(
        functools.partial(attend_back_kernel, others, reach),
        out_shape=shapes,
        in_specs=[vmem] * 21 + [hbm] * 3,
        out_specs=[vmem] * 3 + [hbm],
        scratch_shapes=[
            pltpu.VMEM((rows_of, width), low),
            pltpu.VMEM((rows_of, width), full),
            pltpu.VMEM((rows_of, width), low),
            pltpu.VMEM(middle.shape, low),
            pltpu.VMEM((8, width), full),
            pltpu.VMEM((2, depth, width), low),
            pltpu.VMEM((width, columns), low),
            pltpu.VMEM((rows_of, query_width), low),
            pltpu.VMEM(((reach + 1) * rows_of, 2 * key_width), full),
            pltpu.VMEM((spans * rows_of, 2 * key_width), low),
            pltpu.VMEM((spans * rows_of, 2 * key_width), low),
            pltpu.VMEM((rows_of, query_width), low),
            pltpu.VMEM((rows_of, rest_width), low),
            pltpu.VMEM((8, rows_of, width), low),
            pltpu.VMEM((8, rows_of, query_width), low),
            pltpu.VMEM((8, rows_of, rest_width), low),
            pltpu.VMEM((8 * rows_of, 2 * depth), low),
            pltpu.VMEM((rows_of, width), full),
            pltpu.VMEM((8, 8, depth), full),
            pltpu.VMEM((8, 8, depth), full),
            pltpu.VMEM((8, 8, width), full),
            dma((9,)),
            dma((13,)),
            dma((13,)),
            dma((13,)),
            dma((13,)),
            dma((13,)),
            dma((13,)),
            dma((spans,)),
            dma((spans,)),
            dma((7,)),
            dma((7,)),
            dma((7,)),
            dma((7,)),
            dma((8,)),
            dma((8,)),
        ]
        + [
            pltpu.VMEM((count, *shape), low)
            for shape in part_shapes
            for count in (4, 3, 3)
        ]
        + [dma((8,)), dma((8,)), dma((6,)), dma((6,))]
        + [pltpu.VMEM((8, *shape), low) for shape in part_shapes]
        + [pltpu.VMEM((8, 8, width), full)],
        compiler_params=pltpu.CompilerParams(collective_id=4, has_side_effects=True, vmem_limit_bytes=60 * 2**20),
        cost_estimate=pl.CostEstimate(
            flops=40 * rows_of * width * columns, bytes_accessed=6 * width * columns, transcendentals=0
        ),
        name="attend_backward",
    )(
        d_ffn_in, mixed, d_residual, laurel_lin, attn_lin, laurel, gain_part,
        query_low, key_value, linear, gains, positions, cosine, sine, middle, features,
        source, residual, d_vector, gated_value, d_back, outward_all, inward_all, d_rows,
    )


def feed_call(forward, prelude, weights, kept=(), features=None, forward_rows=None, hidden_rows=None, vectors=()):
    rows_of, width = prelude[0].shape
    hidden = weights[0].shape[0]
    all_rows = 8 * rows_of
    others = lax.axis_size("ctx") - 1
    low, full = jnp.bfloat16, jnp.float32
    count_made = 3 if forward else 2
    hbm = pl.BlockSpec(memory_space=pl.ANY)
    vmem = pl.BlockSpec(memory_space=pltpu.VMEM)
    half = rows_of // 2
    dma = pltpu.SemaphoreType.DMA

    def shape(columns, kind, rows=rows_of):
        return jax.ShapeDtypeStruct((rows, columns), kind)

    operands = (*prelude, *weights, *kept)
    operand_specs = [vmem] * len(prelude) + [hbm] * (3 + len(kept))
    shapes = [shape(width, full)]
    extra = []
    if forward:
        shapes += [shape(width, full)] * 2
        operands += (features, *vectors)
        operand_specs += [vmem] * 3
        extra = (
            [dma((7,)), dma((7,)), dma]
            + [pltpu.VMEM((8, *value.shape), low) for value in vectors]
            + [dma((13,))] * 4
            + [dma((8,))] * 2
        )
    else:
        vector_width = prelude[5].shape[1]
        shapes += [shape(width, low), shape(vector_width, full), shape(width, low), shape(vector_width, low)]
        shapes += [shape(vector_width, low), shape(width, low), shape(width, full), shape(width, full, 8)]
        operands += (forward_rows, hidden_rows)
        operand_specs += [hbm] * 2
        extra = [
            pltpu.VMEM((all_rows, hidden), low),
            pltpu.VMEM((all_rows, width), low),
            pltpu.VMEM((2, hidden, 512), full),
            dma,
            dma,
            dma((3 * (width // 512),)),
        ]
    count_vmem = len(shapes)
    shapes += [
        shape(width, low, all_rows),
        jax.ShapeDtypeStruct((2, rows_of, width), low),
        jax.ShapeDtypeStruct((2, 2 * rows_of, width), low),
    ]
    if forward:
        shapes += [jax.ShapeDtypeStruct((8, rows_of, features.shape[1] // 8), low)]
        shapes += [shape(value.shape[1], low, 8 * value.shape[0]) for value in vectors]
    else:
        shapes += [shape(width, full, hidden)] * 3
    shapes += [shape(hidden, low, all_rows)] * count_made
    return pl.pallas_call(
        functools.partial(feed_kernel, forward, rows_of, others),
        out_shape=shapes,
        in_specs=operand_specs,
        out_specs=[vmem] * count_vmem + [hbm] * (len(shapes) - count_vmem),
        scratch_shapes=[pltpu.VMEM((hidden, width), low)] * 3
        + [pltpu.VMEM((all_rows, hidden), low)] * (len(kept) + count_made)
        + [
            pltpu.VMEM((rows_of, width), low),
            pltpu.VMEM((4, 2 * rows_of, width), low),
            pltpu.VMEM((4, 2 * rows_of, width), low),
            pltpu.VMEM((4, rows_of, width), low),
            pltpu.VMEM((3, rows_of, width), low),
            pltpu.VMEM((2, half, width), low),
            pltpu.VMEM((2, half, width), low),
            pltpu.VMEM((4, half, width), low),
            dma((20,)),
            dma((20,)),
            dma((3 + len(kept),)),
            dma((4 * (1 + count_made),)),
            dma((2,)),
            dma((2,)),
            dma((4,)),
            dma((4,)),
        ]
        + extra,
        compiler_params=pltpu.CompilerParams(
            collective_id=1 if forward else 2,
            has_side_effects=True,
            vmem_limit_bytes=62 * 2**20,
        ),
        cost_estimate=pl.CostEstimate(
            flops=40 * all_rows * hidden * width // 2,
            bytes_accessed=6 * hidden * width + 8 * all_rows * width,
            transcendentals=0,
        ),
        name="feed_forward" if forward else "feed_backward",
    )(*operands)


def other_rows(rows, d_rows, weights, tiles, arrive):
    gate, up, down = weights
    hidden_tile, d_gate_tile, d_up_tile = tiles
    tile = min(512, gate.shape[0])
    for index in range(3):
        arrive(index)

    def body(index, carry):
        span = pl.ds(pl.multiple_of(index * tile, tile), tile)
        gate_value = product_back(gate[span, :], rows[...])
        up_value = product_back(up[span, :], rows[...])
        d_hidden = product_back(down[span, :], d_rows[...])
        value, slope = gelu_parts(gate_value)
        hidden_tile[span, :] = (value * up_value).astype(jnp.bfloat16)
        d_gate_tile[span, :] = (d_hidden * up_value * slope).astype(jnp.bfloat16)
        d_up_tile[span, :] = (d_hidden * value).astype(jnp.bfloat16)
        return carry

    lax.fori_loop(0, gate.shape[0] // tile, body, 0)


def add_weight_grads(grads, tiles, rows, d_rows, last, done):
    hidden_tile, d_gate_tile, d_up_tile = tiles
    terms = list(zip(grads, (d_gate_tile, d_up_tile, hidden_tile), (rows, rows, d_rows)))

    @pl.when(jnp.logical_not(last))
    def _():
        for grad, tile, right in terms:
            grad[...] += matrix_product(tile[...], right[...])

    @pl.when(last)
    def _():
        for index, (grad, tile, right) in enumerate(terms):
            grad[...] += matrix_product(tile[...], right[...])
            done(index)


def weight_moves(step, last, weights_hbm, weights, parts_hbm, grads, grads_hbm, weight_sem, part_sem, out_sem):
    weight_loads, part_loads, out_copies = [
        [pltpu.make_async_copy(source, target, sem.at[index]) for index, (source, target) in enumerate(zip(sources, targets))]
        for sources, targets, sem in (
            (weights_hbm, weights, weight_sem),
            (parts_hbm, grads, part_sem),
            (grads, grads_hbm, out_sem),
        )
    ]

    @pl.when(step == 0)
    def _():
        for load in weight_loads + part_loads:
            load.start()

    def arrive(index):
        @pl.when(step == 0)
        def _():
            weight_loads[index].wait()

    def begin_sums():
        @pl.when(step == 0)
        def _():
            for load in part_loads:
                load.wait()

    def done(index):
        out_copies[index].start()

    def finish():
        @pl.when(step == last)
        def _():
            for copy in out_copies:
                copy.wait()

    return arrive, begin_sums, done, finish


def weight_part_kernel(
    near_steps, gate_hbm, up_hbm, down_hbm, rows_near, rows_next, d_rows_near, gate_part, up_part, down_part, far_own,
    gate_out, up_out, down_out, far_all,
    gate, up, down, grad_gate, grad_up, grad_down, hidden_tile, d_gate_tile, d_up_tile,
    send_sem, recv_sem, own_sem, weight_sem, part_sem, out_sem,
):
    step = pl.program_id(0)
    last = near_steps - 1
    me = lax.axis_index("fsdp")
    grads = (grad_gate, grad_up, grad_down)
    tiles = (hidden_tile, d_gate_tile, d_up_tile)

    sibling, beside, above = across(me, 1), across(me, 2), across(me, 4)
    diagonal = across(beside, 4)
    plan = [(far_own, far_all.at[me], sibling)]
    for part in range(2):
        plan += [(far_own.at[part], far_all.at[me, part], beside), (far_own.at[part], far_all.at[me, part], above)]
    for part in range(2):
        plan += [(far_all.at[device, part], far_all.at[device, part], sibling) for device in (beside, above)]
    plan.append((far_all.at[beside, 0], far_all.at[beside, 0], above))
    plan.append((far_all.at[above, 1], far_all.at[above, 1], beside))
    plan += [(far_all.at[diagonal, part], far_all.at[diagonal, part], sibling) for part in range(2)]
    copies = [
        push(source, target, send_sem.at[index], recv_sem.at[index], {"fsdp": partner})
        for index, (source, target, partner) in enumerate(plan)
    ]
    own_copy = pltpu.make_async_copy(far_own, far_all.at[me], own_sem)

    arrive, begin_sums, done, finish = weight_moves(
        step, last, (gate_hbm, up_hbm, down_hbm), (gate, up, down), (gate_part, up_part, down_part), grads,
        (gate_out, up_out, down_out), weight_sem, part_sem, out_sem,
    )

    @pl.when(step == 0)
    def _():
        greet(me, (1, 2, 4), 0, 0)
        own_copy.start()
        for index in range(5):
            copies[index].start()

    @pl.when(step == last - 1)
    def _():
        copies[0].wait_recv()
        copies[1].wait_recv()
        copies[9].start()
        copies[5].start()
        copies[2].wait_recv()
        copies[6].start()

    @pl.when(step == last)
    def _():
        copies[3].wait_recv()
        copies[7].start()
        copies[4].wait_recv()
        copies[10].start()
        copies[8].start()

    weights = (gate, up, down)

    @pl.when(step < near_steps // 2)
    def _():
        other_rows(rows_near, d_rows_near, weights, tiles, arrive)
        begin_sums()
        add_weight_grads(grads, tiles, rows_near, d_rows_near, step == last, done)

    @pl.when(step >= near_steps // 2)
    def _():
        other_rows(rows_next, d_rows_near, weights, tiles, arrive)
        add_weight_grads(grads, tiles, rows_next, d_rows_near, step == last, done)

    @pl.when(step == last)
    def _():
        copies[9].wait_recv()
        copies[11].start()
        copies[10].wait_recv()
        copies[12].start()

    @pl.when(step == last)
    def _():
        for index in (5, 6, 7, 8, 11, 12):
            copies[index].wait_recv()
        own_copy.wait()
        for copy in copies:
            copy.wait_send()

    finish()


def weight_rest_kernel(
    steps, gate_hbm, up_hbm, down_hbm, rows, d_rows, gate_part, up_part, down_part,
    gate_out, up_out, down_out,
    gate, up, down, grad_gate, grad_up, grad_down, hidden_tile, d_gate_tile, d_up_tile, weight_sem, part_sem, out_sem,
):
    grads = (grad_gate, grad_up, grad_down)
    tiles = (hidden_tile, d_gate_tile, d_up_tile)
    arrive, begin_sums, done, finish = weight_moves(
        pl.program_id(0), steps - 1, (gate_hbm, up_hbm, down_hbm), (gate, up, down), (gate_part, up_part, down_part),
        grads, (gate_out, up_out, down_out), weight_sem, part_sem, out_sem,
    )
    other_rows(rows, d_rows, (gate, up, down), tiles, arrive)
    begin_sums()
    add_weight_grads(grads, tiles, rows, d_rows, pl.program_id(0) == steps - 1, done)
    finish()


def weight_grad_calls(
    gate, up, down, own_parts, rows_near, rows_next, d_rows_near, rows_far, far_own, tok=256, far_tok=512
):
    size, width = gate.shape
    low = jnp.bfloat16
    near_steps = d_rows_near.shape[0] // tok
    hbm = pl.BlockSpec(memory_space=pl.ANY)
    dma = pltpu.SemaphoreType.DMA

    def stream(first, steps):
        return pl.BlockSpec((tok, width), lambda s: (jnp.clip(s - first, 0, steps - 1), 0))

    buffers = [pltpu.VMEM((size, width), low)] * 3 + [pltpu.VMEM((size, width), jnp.float32)] * 3
    near_one, near_two = stream(0, near_steps // 2), stream(near_steps // 2, near_steps // 2)
    near = stream(0, near_steps)
    grad = jax.ShapeDtypeStruct((size, width), jnp.float32)
    *parts, far_all = pl.pallas_call(
        functools.partial(weight_part_kernel, near_steps),
        grid=(near_steps,),
        in_specs=[hbm] * 3 + [near_one, near_two, near] + [hbm] * 4,
        out_specs=[hbm] * 4,
        out_shape=[grad] * 3 + [jax.ShapeDtypeStruct((8, *far_own.shape), low)],
        scratch_shapes=buffers
        + [pltpu.VMEM((size, tok), low)] * 3
        + [dma((13,)), dma((13,)), dma, dma((3,)), dma((3,)), dma((3,))],
        compiler_params=pltpu.CompilerParams(
            dimension_semantics=("arbitrary",), vmem_limit_bytes=62 * 2**20, collective_id=5, has_side_effects=True
        ),
        cost_estimate=pl.CostEstimate(
            flops=12 * size * width * d_rows_near.shape[0], bytes_accessed=80 * 2**20, transcendentals=0
        ),
        name="weight_grads_part",
    )(gate, up, down, rows_near, rows_next, d_rows_near, *own_parts, far_own)
    far = pl.BlockSpec((far_tok, width), lambda s: (s, 0))
    return pl.pallas_call(
        functools.partial(weight_rest_kernel, rows_far.shape[0] // far_tok),
        grid=(rows_far.shape[0] // far_tok,),
        in_specs=[hbm] * 3 + [far] * 2 + [hbm] * 3,
        out_specs=[hbm] * 3,
        out_shape=[grad] * 3,
        scratch_shapes=buffers + [pltpu.VMEM((size, far_tok), low)] * 3 + [dma((3,)), dma((3,)), dma((3,))],
        compiler_params=pltpu.CompilerParams(dimension_semantics=("arbitrary",), vmem_limit_bytes=62 * 2**20),
        cost_estimate=pl.CostEstimate(
            flops=12 * size * width * rows_far.shape[0], bytes_accessed=80 * 2**20, transcendentals=0
        ),
        name="weight_grads_rest",
    )(gate, up, down, rows_far, far_all.reshape(-1, width), *parts)


def finish_kernel(
    key_width, wide, small, result_in, d_vectors_in, d_source_in,
    result, d_source, d_vectors, query, key, value, output, down, up, gate, out,
    gain_one, gain_two, gain_three, gain_four, gain_five, gain_six, query_gain, key_gain,
):
    result[...] = result_in[...]
    d_vectors[...] = d_vectors_in[...]
    d_source[...] = d_source_in[...]
    query_width = query.shape[1]
    start = 0
    for target, columns in (
        (query, query_width),
        (key, key_width),
        (value, key_width),
        (down, down.shape[1]),
    ):
        target[...] = wide[:, start : start + columns].astype(jnp.float32)
        start += columns
    start += -start % 128
    output[...] = wide[:, start : start + output.shape[1]].astype(jnp.float32)
    start += output.shape[1]
    gate[...] = wide[:, start : start + gate.shape[1]].astype(jnp.float32)
    lines = small[...].astype(jnp.float32)
    first = out.shape[0]
    out[...] = lines[0:first]
    up[...] = lines[first : first + up.shape[0]]
    first += up.shape[0]
    for index, target in enumerate((gain_one, gain_two, gain_three, gain_four, gain_five, gain_six)):
        target[...] = lines[first + index : first + index + 1, 0 : target.shape[1]]
    me = lax.axis_index("fsdp")
    for index, target in enumerate((query_gain, key_gain)):
        size = target.shape[1]
        line = lines[first + 6 + index : first + 7 + index, 0 : 8 * size]
        total = jnp.zeros((1, size), jnp.float32)
        for device in range(8):
            total = total + jnp.where(me == device, line[:, device * size : (device + 1) * size], 0.0)
        target[...] = total


def finish_call(wide, small, result, d_vectors, d_source, shapes, key_width):
    vmem = pl.BlockSpec(memory_space=pltpu.VMEM)
    kinds = [jnp.bfloat16] + [jnp.float32] * (len(shapes) - 1)
    return pl.pallas_call(
        functools.partial(finish_kernel, key_width),
        out_shape=[jax.ShapeDtypeStruct(shape, kind) for shape, kind in zip(shapes, kinds)],
        in_specs=[vmem] * 5,
        out_specs=[vmem] * len(shapes),
        compiler_params=pltpu.CompilerParams(vmem_limit_bytes=40 * 2**20),
        name="finish",
    )(wide, small, result, d_vectors, d_source)


def per_device(
    tokens,
    per_layer,
    segments,
    positions,
    cotangent,
    query_weight,
    key_matrix,
    value_matrix,
    output_weight,
    laurel_down,
    laurel_up,
    vector_gate,
    vector_out,
    norm_input,
    norm_attention,
    norm_laurel,
    norm_before,
    norm_after,
    norm_vector,
    query_norm_gain,
    norm_key,
    hidden_gate,
    hidden_up,
    hidden_down,
):
    count_of_rows = tokens.shape[0]
    shards = lax.axis_size("fsdp")
    width = tokens.shape[1]
    heads_per_group = QUERY_HEADS // KEY_VALUE_HEADS
    reach_blocks = min((WINDOW + count_of_rows - 2) // count_of_rows, lax.axis_size("ctx") - 1)
    score_scale = HEAD_SIZE ** (-0.5)
    fused = shards == 8 and lax.axis_size("ctx") == 4
    query_width = query_weight.shape[1]
    key_width = key_matrix.shape[1]

    gain_shards = (
        norm_input,
        norm_attention,
        norm_laurel,
        norm_before,
        norm_after,
        norm_vector,
        query_norm_gain,
        norm_key,
    )
    gain_sizes = [gain.shape[0] for gain in gain_shards]
    gain_starts = [sum(gain_sizes[:index]) for index in range(len(gain_sizes))]
    source = tokens.astype(jnp.float32)
    vectors = per_layer.astype(jnp.float32)
    rank = laurel_down.shape[1]
    unused, allowed = window(positions, count_of_rows, reach_blocks)

    def head_facing(linear, gain):
        return rotary_apply(root_mean_norm(linear, gain), positions)

    if fused:
        me = lax.axis_index("fsdp")
        head_gains = jnp.stack([query_norm_gain, norm_key])
        place = jnp.arange(HEAD_SIZE) // head_gains.shape[1] == me
        head_gains = jnp.where(place[None, :], jnp.tile(head_gains, (1, shards)), 0).astype(jnp.bfloat16)
        cosine, sine_part = rotary_tables(positions, HEAD_SIZE)
        (
            normed,
            gains_all,
            linear,
            query_lowered,
            key_value,
            features,
            middle_low,
            attn_lin,
            full_laurel_up,
            full_inward,
            full_output,
        ) = attend_call(
            reach_blocks,
            tokens,
            [gain.reshape(-1, 128) for gain in gain_shards[:6]],
            head_gains,
            laurel_up,
            positions[None, :],
            cosine,
            sine_part,
            (query_weight, key_matrix, value_matrix, laurel_down.T),
            output_weight,
        )
    else:
        gain_line = jnp.concatenate(gain_shards)
        gain_line = jnp.pad(gain_line, (0, -gain_line.shape[0] % 2048)).reshape(-1, 128)
        gains_all = gather(gain_line, "fsdp").reshape(shards, -1)
        gains = [
            gains_all[:, start : start + size].reshape(-1).astype(jnp.float32)
            for start, size in zip(gain_starts, gain_sizes)
        ]
        inward_weight = jnp.concatenate([query_weight, key_matrix, value_matrix, laurel_down], axis=1)
        inward_weight = jnp.pad(inward_weight, ((0, 0), (0, -inward_weight.shape[1] % 128)))
        full_inward = gather(inward_weight, "fsdp")
        full_output, full_vector_gate, full_vector_out, full_laurel_up = [
            gather(value, "fsdp") for value in (output_weight, vector_gate, vector_out, laurel_up)
        ]
        normed = root_mean_norm(source, gains[0])
        lowered_normed = normed.astype(jnp.bfloat16)
        inward = matrix_product(lowered_normed, full_inward)
        linear = inward[:, : query_width + key_width]
        value_lowered = inward[:, query_width + key_width : query_width + 2 * key_width].astype(jnp.bfloat16)
        laurel_mid = inward[:, query_width + 2 * key_width :][:, :rank].astype(jnp.bfloat16)
        query_lowered = head_facing(
            linear[:, :query_width].reshape(count_of_rows, QUERY_HEADS, HEAD_SIZE), gains[6]
        ).astype(jnp.bfloat16)
        key_lowered = head_facing(
            linear[:, query_width:].reshape(count_of_rows, KEY_VALUE_HEADS, HEAD_SIZE), gains[7]
        ).astype(jnp.bfloat16)
        key_value = jnp.stack([key_lowered.reshape(count_of_rows, -1), value_lowered])
        pair_blocks = [key_value]
        for distance in range(1, reach_blocks + 1):
            pair_blocks.append(from_behind(key_value, "ctx", distance))
        window_couple = jnp.concatenate(pair_blocks, axis=1)
        window_keys, window_values = window_couple[0], window_couple[1]
    if fused:
        (
            feed_value,
            mixed,
            laurel_lin,
            rows_all,
            rows_far,
            rows_near,
            slices,
            full_vector_gate,
            full_vector_out,
            hidden_all,
            lift_all,
            bend_all,
        ) = feed_call(
            True,
            (tokens, normed, attn_lin, middle_low, full_laurel_up, gains_all),
            (hidden_gate, hidden_up, hidden_down),
            features=features,
            vectors=(vector_gate, vector_out),
        )
        slices = slices.reshape(shards * count_of_rows, -1)
        rows_far = gather(rows_far.reshape(-1, width), "fsdp")
        (
            d_ffn_in,
            result,
            d_vectors,
            residual_low,
            d_vector_lin_low,
            gated_low,
            d_vector_back_low,
            d_residual,
            gain_rows,
            d_rows_all,
            d_rows_far,
            rows_next,
            *own_parts,
            unused,
            unused,
        ) = feed_call(
            False,
            (feed_value, mixed, gains_all, full_vector_gate, full_vector_out, per_layer, cotangent),
            (hidden_down, hidden_gate, hidden_up),
            (lift_all, bend_all),
            forward_rows=rows_all,
            hidden_rows=hidden_all,
        )
        d_ffn_in, rows_far = lax.optimization_barrier((d_ffn_in, rows_far))
        d_source, grad_wide, grad_small, d_rows_near = attend_back_call(
            reach_blocks, d_ffn_in, mixed, d_residual, laurel_lin, attn_lin, full_laurel_up, gain_rows,
            query_lowered, key_value, linear, gains_all, positions[None, :], cosine, sine_part, middle_low, slices,
            tokens, residual_low, d_vector_lin_low, gated_low, d_vector_back_low, full_output, full_inward, d_rows_all,
        )
        grad_hidden_gate, grad_hidden_up, grad_hidden_down = weight_grad_calls(
            hidden_gate,
            hidden_up,
            hidden_down,
            own_parts,
            rows_near.reshape(-1, width),
            rows_next.reshape(-1, width),
            d_rows_near.reshape(-1, width),
            rows_far,
            d_rows_far,
        )
    else:
        (
            gain_input,
            gain_attention,
            gain_laurel,
            gain_before,
            gain_after,
            gain_vector,
            gain_query,
            key_norm_gain,
        ) = gains
        query_linear = linear[:, :query_width].reshape(count_of_rows, QUERY_HEADS, HEAD_SIZE)
        key_linear = linear[:, query_width:].reshape(count_of_rows, KEY_VALUE_HEADS, HEAD_SIZE)
        query_lowered = query_lowered.reshape(count_of_rows, KEY_VALUE_HEADS, heads_per_group, HEAD_SIZE)
        window_keys = window_keys.reshape(-1, KEY_VALUE_HEADS, HEAD_SIZE)
        window_values = window_values.reshape(-1, KEY_VALUE_HEADS, HEAD_SIZE)

        def masked_scores():
            raw_scores = score_scale * jnp.einsum(
                "tgfd,kgd->gftk", query_lowered, window_keys, preferred_element_type=jnp.float32
            )
            return jnp.where(allowed, raw_scores, -1e30)

        scores_first = masked_scores()
        row_peak = jnp.max(scores_first, axis=-1, keepdims=True)
        exp_scores = jnp.exp(scores_first - row_peak)
        row_total = jnp.sum(exp_scores, axis=-1, keepdims=True)
        log_total = row_peak + jnp.log(row_total)
        soft_low = (exp_scores / row_total).astype(jnp.bfloat16)
        attended_low = (
            jnp.einsum("gftk,kgd->tgfd", soft_low, window_values, preferred_element_type=jnp.float32)
            .reshape(count_of_rows, QUERY_HEADS * HEAD_SIZE)
            .astype(jnp.bfloat16)
        )
        attn_lin = matrix_product(attended_low, full_output)
        residual_one = source + root_mean_norm(attn_lin, gain_attention)
        laurel_lin = matrix_product(laurel_mid, full_laurel_up)
        mixed = (residual_one + normed + root_mean_norm(laurel_lin, gain_laurel)) * inv_root
        ffn_in = root_mean_norm(mixed, gain_before).astype(jnp.bfloat16)
        normed_slices = feature_slices(lowered_normed)
        attended_slices = feature_slices(attended_low)
        rows_all = gather(ffn_in, "fsdp")
        gate_all = product_back(rows_all, hidden_gate)
        up_all = product_back(rows_all, hidden_up)
        hidden_all = gated(gate_all, up_all).astype(jnp.bfloat16)
        feed_value = scatter_sum(matrix_product(hidden_all, hidden_down))
        residual_two = mixed + root_mean_norm(feed_value, gain_after)
        residual_low = residual_two.astype(jnp.bfloat16)
        vector_lin = matrix_product(residual_low, full_vector_gate)
        gated_low = gated(vector_lin, vectors).astype(jnp.bfloat16)
        vector_back = matrix_product(gated_low, full_vector_out)
        result = residual_two + root_mean_norm(vector_back, gain_vector)
        upstream = cotangent.astype(jnp.float32)
        d_vector_back, grad_gain_vector = norm_grad(vector_back, gain_vector, upstream)
        d_vector_back_low = d_vector_back.astype(jnp.bfloat16)
        grad_vector_out = product_rows(gated_low, d_vector_back_low)
        d_gated = product_back(d_vector_back_low, full_vector_out)
        d_vector_lin, d_vectors = gated_grad(vector_lin, vectors, d_gated)
        d_vector_lin_low = d_vector_lin.astype(jnp.bfloat16)
        grad_vector_gate = product_rows(residual_low, d_vector_lin_low)
        d_residual = upstream + product_back(d_vector_lin_low, full_vector_gate)
        d_feed, grad_gain_after = norm_grad(feed_value, gain_after, d_residual)
        d_feed_low = d_feed.astype(jnp.bfloat16)
        d_rows_all = gather(d_feed_low, "fsdp")
        d_hidden = product_back(d_rows_all, hidden_down)
        d_gate_all, d_up_all = gated_grad(gate_all, up_all, d_hidden)
        d_gate_low = d_gate_all.astype(jnp.bfloat16)
        d_up_low = d_up_all.astype(jnp.bfloat16)
        d_ffn_in = scatter_sum(
            matrix_product(d_gate_low, hidden_gate) + matrix_product(d_up_low, hidden_up)
        )

        grad_hidden_gate, grad_hidden_up, grad_hidden_down = [
            lax.psum(grad.astype(jnp.bfloat16), "ctx").astype(jnp.float32)
            for grad in (
                product_rows(d_gate_low, rows_all),
                product_rows(d_up_low, rows_all),
                product_rows(hidden_all, d_rows_all),
            )
        ]

        d_mixed_part, grad_gain_before = norm_grad(mixed, gain_before, d_ffn_in)
        d_half = (d_residual + d_mixed_part) * inv_root
        d_laurel_lin, grad_gain_laurel = norm_grad(laurel_lin, gain_laurel, d_half)
        d_laurel_low = d_laurel_lin.astype(jnp.bfloat16)
        grad_laurel_up = product_rows(laurel_mid, d_laurel_low)
        d_laurel_mid = product_back(d_laurel_low, full_laurel_up).astype(jnp.bfloat16)
        d_attn_lin, grad_gain_attention = norm_grad(attn_lin, gain_attention, d_half)
        d_attn_low = d_attn_lin.astype(jnp.bfloat16)
        d_attended = (
            product_back(d_attn_low, full_output)
            .astype(jnp.bfloat16)
            .reshape(count_of_rows, KEY_VALUE_HEADS, heads_per_group, HEAD_SIZE)
        )
        soft_again = jnp.exp(masked_scores() - log_total)
        d_soft = jnp.einsum(
            "tgfd,kgd->gftk", d_attended, window_values, preferred_element_type=jnp.float32
        )
        d_scores = (
            soft_again * (d_soft - jnp.sum(soft_again * d_soft, axis=-1, keepdims=True))
        ).astype(jnp.bfloat16)
        d_query = score_scale * jnp.einsum(
            "gftk,kgd->tgfd", d_scores, window_keys, preferred_element_type=jnp.float32
        )
        grad_key_rows = score_scale * jnp.einsum(
            "gftk,tgfd->kgd", d_scores, query_lowered, preferred_element_type=jnp.float32
        )
        grad_value_rows = jnp.einsum(
            "gftk,tgfd->kgd",
            soft_again.astype(jnp.bfloat16),
            d_attended,
            preferred_element_type=jnp.float32,
        )
        grad_window_couple = jnp.stack(
            [
                grad_key_rows.reshape(-1, KEY_VALUE_HEADS * HEAD_SIZE),
                grad_value_rows.reshape(-1, KEY_VALUE_HEADS * HEAD_SIZE),
            ]
        )
        grad_own_part = grad_window_couple[:, :count_of_rows]
        for distance in range(1, reach_blocks + 1):
            grad_own_part = grad_own_part + from_behind(
                grad_window_couple[:, distance * count_of_rows : (distance + 1) * count_of_rows].astype(
                    jnp.bfloat16
                ),
                "ctx",
                -distance,
            ).astype(jnp.float32)
        unused, query_pull = jax.vjp(head_facing, query_linear, gain_query)
        d_query_lin, grad_gain_query = query_pull(
            d_query.reshape(count_of_rows, QUERY_HEADS, HEAD_SIZE)
        )
        unused, key_pullback_fn = jax.vjp(head_facing, key_linear, key_norm_gain)
        grad_key_linear, grad_key_norm_gain = key_pullback_fn(
            grad_own_part[0].reshape(count_of_rows, KEY_VALUE_HEADS, HEAD_SIZE)
        )
        d_inward = jnp.concatenate(
            [
                d_query_lin.reshape(count_of_rows, QUERY_HEADS * HEAD_SIZE).astype(jnp.bfloat16),
                grad_key_linear.reshape(count_of_rows, KEY_VALUE_HEADS * HEAD_SIZE).astype(
                    jnp.bfloat16
                ),
                grad_own_part[1].astype(jnp.bfloat16),
                d_laurel_mid,
                jnp.zeros((count_of_rows, full_inward.shape[1] - query_width - 2 * key_width - rank), jnp.bfloat16),
            ],
            axis=1,
        )
        grad_inward = product_rows(normed_slices, gather(d_inward, "fsdp")).astype(jnp.bfloat16)
        grad_output = product_rows(attended_slices, gather(d_attn_low, "fsdp")).astype(jnp.bfloat16)
        grad_wide = jnp.concatenate([grad_inward, grad_output], axis=1)
        small_rows = jnp.concatenate(
            [
                grad_vector_gate.reshape(shards, -1, width),
                grad_vector_out.reshape(shards, -1, width),
                grad_laurel_up.reshape(shards, -1, width),
            ],
            axis=1,
        ).astype(jnp.bfloat16)
        grad_small = lax.psum_scatter(small_rows, "fsdp", scatter_dimension=0, tiled=False)
        d_normed = d_half + product_back(d_inward, full_inward)
        d_source_part, grad_gain_input = norm_grad(source, gain_input, d_normed)
        d_source = d_half + d_source_part
        gain_lines = jnp.concatenate(
            [
                grad.reshape(shards, -1)
                for grad in (
                    grad_gain_input,
                    grad_gain_attention,
                    grad_gain_laurel,
                    grad_gain_before,
                    grad_gain_after,
                    grad_gain_vector,
                    grad_gain_query,
                    grad_key_norm_gain,
                )
            ],
            axis=1,
        )
        gain_share = lax.psum_scatter(gain_lines, "fsdp", scatter_dimension=0, tiled=False)
        gain_count = gain_share.shape[0]
        gain_share = jnp.pad(gain_share, (0, -gain_count % width)).astype(jnp.bfloat16)
        grad_small = jnp.concatenate([grad_small, gain_share.reshape(-1, width)], axis=0)

    grad_wide, grad_small = lax.psum((grad_wide, grad_small), "ctx")
    hidden_grads = (grad_hidden_gate, grad_hidden_up, grad_hidden_down)
    if fused:
        weights = (query_weight, key_matrix, value_matrix, output_weight, laurel_down, laurel_up, vector_gate, vector_out)
        shapes = [tokens.shape, tokens.shape, per_layer.shape] + [weight.shape for weight in weights]
        shapes += [(1, size) for size in gain_sizes]
        finished = finish_call(grad_wide, grad_small, result, d_vectors, d_source, shapes, key_width)
        gains_from = len(shapes) - len(gain_sizes)
        return tuple(finished[:gains_from]) + tuple(gain.reshape(-1) for gain in finished[gains_from:]) + hidden_grads
    grad_wide, grad_small = grad_wide.astype(jnp.float32), grad_small.astype(jnp.float32)
    inward_width = full_inward.shape[1]
    grad_inward = grad_wide[:, :inward_width]
    grad_output = grad_wide[:, inward_width:]
    out_rows, laurel_rows = vector_out.shape[0], laurel_up.shape[0]
    gate_rows = vector_gate.shape[0] * vector_gate.shape[1] // width
    share_vector_gate = grad_small[:gate_rows].reshape(vector_gate.shape)
    share_vector_out = grad_small[gate_rows : gate_rows + out_rows]
    gain_start = gate_rows + out_rows + laurel_rows
    share_laurel_up = grad_small[gate_rows + out_rows : gain_start]
    gain_share = grad_small[gain_start:].reshape(-1)
    gain_grads = tuple(gain_share[start : start + size] for start, size in zip(gain_starts, gain_sizes))
    value_start = query_width + key_width
    return (
        (
            result.astype(jnp.bfloat16),
            d_source,
            d_vectors,
            grad_inward[:, :query_width],
            grad_inward[:, query_width:value_start],
            grad_inward[:, value_start : value_start + key_width],
            grad_output,
            grad_inward[:, value_start + key_width : value_start + key_width + rank],
            share_laurel_up,
            share_vector_gate,
            share_vector_out,
        )
        + gain_grads
        + hidden_grads
    )


def solution(mesh):
    rows = P(("fsdp", "ctx"), None)
    line = P(("fsdp", "ctx"))
    weight = P("fsdp", None)
    gain = P("fsdp")
    return jax.shard_map(
        per_device,
        mesh=mesh,
        in_specs=(rows, rows, line, line, rows) + (weight,) * 8 + (gain,) * 8 + (weight,) * 3,
        out_specs=(rows,) * 3 + (weight,) * 8 + (gain,) * 8 + (weight,) * 3,
        check_vma=False,
    )
```

```python
import functools

import jax
import jax.numpy as jnp
from jax import lax
from jax.experimental import pallas as pl
from jax.experimental.pallas import tpu as pltpu
from jax.sharding import PartitionSpec as P

QUERY_HEADS = 8
KEY_VALUE_HEADS = 2
HEAD_SIZE = 256
WINDOW = 1024


epsilon = 1e-06
rope_base = 10000.0
inv_root = 0.7071067811865476
gelu_scale = 0.7978845608028654
gelu_cubic = 0.044715


def from_behind(value, axis, steps):
    count = lax.axis_size(axis)
    initial, last = (max(0, -steps), min(count, count - steps))
    return lax.ppermute(value, axis, [(source, source + steps) for source in range(initial, last)])


def other_blocks(value, axis):
    count = lax.axis_size(axis)
    return jnp.concatenate(
        [
            lax.ppermute(value, axis, [(source, (source + step) % count) for source in range(count)])
            for step in range(1, count)
        ],
        axis=0,
    )


def root_mean_norm(value, gain):
    factor = lax.rsqrt(jnp.mean(value * value, axis=-1, keepdims=True) + epsilon)
    return value * factor * gain


def gelu_tanh(value):
    return jax.nn.gelu(value, approximate=True)


def gated(gate_value, up_value):
    return gelu_tanh(gate_value) * up_value


def rotary_apply(value, token_position):
    half_size = value.shape[-1] // 2
    frequency = rope_base ** (-2.0 * jnp.arange(half_size, dtype=jnp.float32) / value.shape[-1])
    angle = token_position.astype(jnp.float32)[:, None] * frequency[None, :]
    cosine = jnp.cos(angle)[:, None, :]
    sine_part = jnp.sin(angle)[:, None, :]
    first_half = value[..., :half_size]
    second_half = value[..., half_size:]
    return jnp.concatenate(
        [
            first_half * cosine - second_half * sine_part,
            second_half * cosine + first_half * sine_part,
        ],
        axis=-1,
    )


def rotary_tables(token_position, size):
    half_size = size // 2
    frequency = rope_base ** (-2.0 * jnp.arange(half_size, dtype=jnp.float32) / size)
    angle = token_position.astype(jnp.float32)[:, None] * frequency[None, :]
    return jnp.cos(angle), jnp.sin(angle)


def window(positions, rows_of, reach):
    key_offset = jnp.concatenate(
        [distance * rows_of - jnp.arange(rows_of, dtype=jnp.int32) for distance in range(reach + 1)]
    )
    key_gap = jnp.arange(rows_of, dtype=jnp.int32)[:, None] + key_offset[None, :]
    return key_gap, (key_gap >= 0) & (key_gap <= positions[:, None]) & (key_gap < WINDOW)


def matrix_product(left, right):
    return jnp.dot(left, right, preferred_element_type=jnp.float32)


def product_back(left, right):
    return lax.dot_general(
        left, right, (((1,), (1,)), ((), ())), preferred_element_type=jnp.float32
    )


def product_rows(left, right):
    return lax.dot_general(
        left, right, (((0,), (0,)), ((), ())), preferred_element_type=jnp.float32
    )


def norm_grad(value, gain, upstream):
    unused, pullback = jax.vjp(root_mean_norm, value, gain)
    return pullback(upstream)


def gated_grad(gate_value, up_value, upstream):
    unused, pullback = jax.vjp(gated, gate_value, up_value)
    return pullback(upstream)


def gather(value, axis):
    return lax.all_gather(value, axis, axis=0, tiled=True)


def feature_slices(value):
    count = lax.axis_size("fsdp")
    rows = value.shape[0]
    return lax.all_to_all(
        value.reshape(rows, count, -1), "fsdp", split_axis=1, concat_axis=0, tiled=True
    ).reshape(count * rows, -1)


def scatter_sum(value):
    return lax.psum_scatter(
        value.astype(jnp.bfloat16), "fsdp", scatter_dimension=0, tiled=True
    ).astype(jnp.float32)


def gelu_parts(gate):
    square = gate * gate
    bend = jnp.tanh(gelu_scale * gate * (1.0 + gelu_cubic * square))
    half_up = 0.5 * (1.0 + bend)
    slope = half_up + 0.5 * gate * (1.0 - bend * bend) * (
        gelu_scale * (1.0 + 3.0 * gelu_cubic * square)
    )
    return gate * half_up, slope


def across(me, stride):
    return me + stride - 2 * stride * ((me // stride) % 2)


def across_many(me, bits):
    for stride in (1, 2, 4):
        if bits & stride:
            me = across(me, stride)
    return me


def feed_kernel(forward, rows_of, others, *refs):
    half = rows_of // 2
    if forward:
        (source, normed, attn_lin, middle, laurel, gains), refs = refs[:6], refs[6:]
        (gate_hbm, up_hbm, down_hbm, features, gate_own, out_own), refs = refs[:6], refs[6:]
        (total, mixed, laurel_lin, rows_hbm, far_hbm, near_hbm), refs = refs[:6], refs[6:]
        (slices_hbm, gate_all, out_all, hidden_hbm, lift_hbm, bend_hbm), rest = refs[:6], refs[6:]
        weights_hbm, kept_hbm, made_hbm = (gate_hbm, up_hbm, down_hbm), (), (hidden_hbm, lift_hbm, bend_hbm)
    else:
        (feed_value, mixed, gains, gate_all, out_all, vectors, cotangent), refs = refs[:7], refs[7:]
        (down_hbm, gate_hbm, up_hbm, lift_hbm, bend_hbm, forward_rows, hidden_in), refs = refs[:7], refs[7:]
        (total, result, d_vectors, residual_low, d_vector_low, gated_low, d_back_low, d_residual, gain_rows), refs = (
            refs[:9],
            refs[9:],
        )
        (rows_hbm, far_hbm, near_hbm, *part_hbm, d_gate_hbm, d_up_hbm), rest = refs[:8], refs[8:]
        weights_hbm, kept_hbm, made_hbm = (down_hbm, gate_hbm, up_hbm), (lift_hbm, bend_hbm), (d_gate_hbm, d_up_hbm)
    count_kept, count_made = len(kept_hbm), len(made_hbm)
    weights = rest[:3]
    kept = rest[3 : 3 + count_kept]
    made = rest[3 + count_kept : 3 + count_kept + count_made]
    (own, rows, part, sib_in, chip_sum, relay_in, relay_sum, last_in, send_sem, recv_sem, in_sem, out_sem, far_send, far_recv, near_send, near_recv, *extra) = rest[
        3 + count_kept + count_made :
    ]
    hidden = weights[0].shape[0]
    width = weights[0].shape[1]
    me = lax.axis_index("fsdp")
    sibling, beside, above = across(me, 1), across(me, 2), across(me, 4)

    loads = [
        pltpu.make_async_copy(source, target, in_sem.at[index])
        for index, (source, target) in enumerate(zip(weights_hbm + kept_hbm, tuple(weights) + tuple(kept)))
    ]
    for load in loads:
        load.start()

    block = lax.axis_index("ctx")
    def before_feed():
        def unit(value):
            return value * lax.rsqrt(jnp.mean(value * value, axis=-1, keepdims=True) + epsilon)

        laurel_lin[...] = jnp.dot(middle[...], laurel[...].astype(jnp.bfloat16), preferred_element_type=jnp.float32)
        value = source[...].astype(jnp.float32) + unit(attn_lin[...]) * gains[1:2, :] + normed[...]
        value = (value + unit(laurel_lin[...]) * gains[2:3, :]) * inv_root
        mixed[...] = value
        own[...] = (unit(value) * gains[3:4, :]).astype(jnp.bfloat16)

    def after_feed():
        def unit(value):
            return value * lax.rsqrt(jnp.mean(value * value, axis=-1, keepdims=True) + epsilon)

        residual = mixed[...] + unit(feed_value[...]) * gains[4:5, :]
        residual_low[...] = residual.astype(jnp.bfloat16)
        vector_lin = jnp.dot(residual_low[...], gate_all[...], preferred_element_type=jnp.float32)
        value, slope = gelu_parts(vector_lin)
        per_token = vectors[...].astype(jnp.float32)
        gated_low[...] = (value * per_token).astype(jnp.bfloat16)
        vector_back = jnp.dot(gated_low[...], out_all[...], preferred_element_type=jnp.float32)
        result[...] = (residual + unit(vector_back) * gains[5:6, :]).astype(jnp.bfloat16)
        upstream = cotangent[...].astype(jnp.float32)
        d_back, grad_vector_gain = norm_rows_grad(vector_back, gains[5:6, :], upstream)
        d_back_low[...] = d_back.astype(jnp.bfloat16)
        d_gated = product_back(d_back_low[...], out_all[...])
        d_vectors[...] = d_gated * value
        d_vector_low[...] = (d_gated * per_token * slope).astype(jnp.bfloat16)
        d_residual[...] = upstream + product_back(d_vector_low[...], gate_all[...])
        d_feed, grad_after_gain = norm_rows_grad(feed_value[...], gains[4:5, :], d_residual[...])
        own[...] = d_feed.astype(jnp.bfloat16)
        gain_rows[...] = jnp.zeros_like(gain_rows)
        gain_rows[4:5, :] = grad_after_gain
        gain_rows[5:6, :] = grad_vector_gain

    greet(me, range(1, 8) if forward else (1, 2, 4), block, others, before_feed if forward else after_feed)

    def send(index, source, target, partner):
        return pltpu.make_async_remote_copy(
            src_ref=source,
            dst_ref=target,
            send_sem=send_sem.at[index],
            recv_sem=recv_sem.at[index],
            device_id={"fsdp": partner},
            device_id_type=pl.DeviceIdType.MESH,
        )

    low, high = pl.ds(0, half), pl.ds(half, half)
    mine, theirs = pl.ds(0, rows_of), pl.ds(rows_of, rows_of)
    copies = [
        send(0, own, rows.at[0, theirs], sibling),
        send(1, own.at[low], rows.at[1, low], beside),
        send(2, own.at[low], rows.at[1, high], above),
        send(3, own.at[high], rows.at[2, low], beside),
        send(4, own.at[high], rows.at[2, high], above),
        send(5, rows.at[1, mine], rows.at[1, theirs], sibling),
        send(6, rows.at[2, mine], rows.at[2, theirs], sibling),
        send(7, rows.at[1, low], rows.at[3, low], above),
        send(8, rows.at[2, high], rows.at[3, high], beside),
        send(9, rows.at[3, mine], rows.at[3, theirs], sibling),
        send(10, part.at[0, theirs], sib_in.at[0], sibling),
        send(11, part.at[1, theirs], sib_in.at[1], sibling),
        send(12, part.at[2, theirs], sib_in.at[2], sibling),
        send(13, part.at[3, theirs], sib_in.at[3], sibling),
        send(14, chip_sum.at[0, high], last_in.at[2], above),
        send(15, chip_sum.at[1, low], last_in.at[1], beside),
        send(16, chip_sum.at[2, low], relay_in.at[0], above),
        send(17, chip_sum.at[2, high], relay_in.at[1], beside),
        send(18, relay_sum.at[0], last_in.at[0], beside),
        send(19, relay_sum.at[1], last_in.at[3], above),
    ]
    outs = []

    def write_out(source, target):
        copy = pltpu.make_async_copy(source, target, out_sem.at[len(outs)])
        copy.start()
        outs.append(copy)

    for index in range(5):
        copies[index].start()
    spreads = []
    if forward:
        gate_slots, out_slots, gate_send, gate_recv, vec_send, vec_recv, gate_out, vec_out = extra[3:]
        spreads = [
            spread_copies(gate_own, gate_slots, gate_send, gate_recv, me),
            spread_copies(out_own, out_slots, vec_send, vec_recv, me),
        ]
        for spread in spreads:
            for index in range(5):
                spread[index].start()
        gate_slots[0] = gate_own[...]
        out_slots[0] = out_own[...]
    far = [
        push(own, far_hbm.at[index], far_send.at[index], far_recv.at[index], {"ctx": across_many(block, 2 + index)})
        for index in range(2)
    ]
    for copy in far:
        copy.start()
    def near_source(index):
        if forward:
            return rows.at[1, mine] if index else own
        return forward_rows.at[pl.ds((2 + index) * 2 * rows_of, rows_of)]

    near = [
        push(near_source(index), near_hbm.at[index, mine], near_send.at[index], near_recv.at[index], {"ctx": across(block, 1)})
        for index in range(2)
    ]
    near_share = [
        push(
            near_hbm.at[index, mine],
            near_hbm.at[index, theirs],
            near_send.at[2 + index],
            near_recv.at[2 + index],
            {"fsdp": sibling},
        )
        for index in range(2)
    ]
    near[0].start()
    if not forward:
        near[1].start()
    rows[0, mine] = own[...]
    slices = []
    if forward:
        share = features.shape[1] // 8

        def share_of(device):
            return features.at[:, pl.ds(pl.multiple_of(device * share, share), share)]

        own_slice = pltpu.make_async_copy(share_of(me), slices_hbm.at[me], extra[2])
        own_slice.start()
        slices = [
            pltpu.make_async_remote_copy(
                src_ref=share_of(across_many(me, distance)),
                dst_ref=slices_hbm.at[me],
                send_sem=extra[0].at[distance - 1],
                recv_sem=extra[1].at[distance - 1],
                device_id={"fsdp": across_many(me, distance)},
                device_id_type=pl.DeviceIdType.MESH,
            )
            for distance in range(1, 8)
        ]

    tile = min(hidden, 1024)
    wide = min(width, 1024)

    def first_stage(group):
        span = pl.ds(group * 2 * rows_of, 2 * rows_of)

        def step(index, carry):
            columns = pl.ds(pl.multiple_of(index * tile, tile), tile)
            left = rows[group]

            def back(weight):
                return lax.dot_general(
                    left, weight[columns, :], (((1,), (1,)), ((), ())), preferred_element_type=jnp.float32
                )

            if forward:
                gate, up = back(weights[0]), back(weights[1])
                value, slope = gelu_parts(gate)
                made[0][span, columns] = (value * up).astype(jnp.bfloat16)
                made[1][span, columns] = value.astype(jnp.bfloat16)
                made[2][span, columns] = (slope * up).astype(jnp.bfloat16)
            else:
                d_hidden = back(weights[0])
                made[0][span, columns] = (d_hidden * kept[1][span, columns].astype(jnp.float32)).astype(jnp.bfloat16)
                made[1][span, columns] = (d_hidden * kept[0][span, columns].astype(jnp.float32)).astype(jnp.bfloat16)
            return carry

        lax.fori_loop(0, hidden // tile, step, 0)

    def second_stage(group):
        span = pl.ds(group * 2 * rows_of, 2 * rows_of)

        def step(index, carry):
            columns = pl.ds(pl.multiple_of(index * wide, wide), wide)
            if forward:
                value = jnp.dot(made[0][span, :], weights[2][:, columns], preferred_element_type=jnp.float32)
            else:
                value = jnp.dot(made[0][span, :], weights[1][:, columns], preferred_element_type=jnp.float32)
                value = value + jnp.dot(made[1][span, :], weights[2][:, columns], preferred_element_type=jnp.float32)
            part[group, :, columns] = value.astype(jnp.bfloat16)
            return carry

        lax.fori_loop(0, width // wide, step, 0)

    fillers = []
    if not forward:
        hidden_rows, forward_all, tiles, hidden_sem, forward_sem, tile_sem = extra
        side_loads = [
            pltpu.make_async_copy(hidden_in, hidden_rows, hidden_sem),
            pltpu.make_async_copy(forward_rows, forward_all, forward_sem),
        ]
        tile_width = tiles.shape[2]
        tiles_each = width // tile_width
        tile_copies = [
            pltpu.make_async_copy(
                tiles.at[index % 2],
                part_hbm[index // tiles_each].at[:, pl.ds((index % tiles_each) * tile_width, tile_width)],
                tile_sem.at[index],
            )
            for index in range(3 * tiles_each)
        ]

        def weight_tile(index):
            kind, columns = index // tiles_each, pl.ds((index % tiles_each) * tile_width, tile_width)
            if index >= 2:
                tile_copies[index - 2].wait()
            if kind == 2:
                right = rows[:, :, columns].reshape(8 * rows_of, tile_width)
                tiles[index % 2] = product_rows(hidden_rows[...], right)
            else:
                tiles[index % 2] = product_rows(made[kind][...], forward_all[:, columns])
            tile_copies[index].start()

        fillers = [functools.partial(weight_tile, index) for index in range(3 * tiles_each)]

    def fill(count):
        for unused in range(min(count, len(fillers))):
            fillers.pop(0)()

    def keep_out(group):
        span = pl.ds(group * 2 * rows_of, 2 * rows_of)
        write_out(rows.at[group], rows_hbm.at[span])
        for source, target in zip(made, made_hbm):
            write_out(source.at[span], target.at[span])

    def add_chip(group):
        chip_sum[group - 1] = (
            part[group, mine].astype(jnp.float32) + sib_in[group].astype(jnp.float32)
        ).astype(jnp.bfloat16)

    if not forward:
        for load in side_loads:
            load.start()
    copies[0].wait_recv()
    loads[0].wait()
    if forward:
        loads[1].wait()
    else:
        loads[3].wait()
        loads[4].wait()
    first_stage(0)
    if forward:
        loads[2].wait()
    else:
        loads[1].wait()
        loads[2].wait()
    second_stage(0)
    copies[10].start()
    keep_out(0)
    copies[1].wait_recv()
    copies[7].start()
    copies[2].wait_recv()
    copies[5].start()
    if forward:
        near[1].start()
    copies[5].wait_recv()
    first_stage(1)
    second_stage(1)
    copies[11].start()
    keep_out(1)
    copies[3].wait_recv()
    copies[4].wait_recv()
    copies[8].start()
    copies[6].start()
    copies[11].wait_recv()
    add_chip(1)
    copies[14].start()
    copies[6].wait_recv()
    first_stage(2)
    second_stage(2)
    copies[12].start()
    keep_out(2)
    for copy in slices:
        copy.start()
    for spread in spreads:
        for index in range(1, 5):
            spread[index].wait_recv()
        for index in range(5, 11):
            spread[index].start()
    copies[7].wait_recv()
    copies[8].wait_recv()
    copies[9].start()
    copies[12].wait_recv()
    add_chip(2)
    copies[15].start()
    copies[9].wait_recv()
    first_stage(3)
    second_stage(3)
    copies[13].start()
    keep_out(3)
    if not forward:
        for load in side_loads:
            load.wait()
    fill(1)
    copies[13].wait_recv()
    add_chip(3)
    copies[16].start()
    copies[17].start()
    for spread in spreads:
        for index in (9, 10):
            spread[index].wait_recv()
        for index in (11, 12):
            spread[index].start()
    fill(4)
    copies[10].wait_recv()
    total[...] = part[0, mine].astype(jnp.float32) + sib_in[0].astype(jnp.float32)
    copies[16].wait_recv()
    relay_sum[0] = (chip_sum[0, low].astype(jnp.float32) + relay_in[0].astype(jnp.float32)).astype(jnp.bfloat16)
    copies[18].start()
    copies[17].wait_recv()
    relay_sum[1] = (chip_sum[1, high].astype(jnp.float32) + relay_in[1].astype(jnp.float32)).astype(jnp.bfloat16)
    copies[19].start()
    fill(4)
    copies[14].wait_recv()
    total[low] = total[low] + last_in[2].astype(jnp.float32)
    copies[15].wait_recv()
    total[high] = total[high] + last_in[1].astype(jnp.float32)
    for index in range(2):
        near[index].wait_recv()
        near_share[index].start()
    copies[18].wait_recv()
    total[low] = total[low] + last_in[0].astype(jnp.float32)
    fill(len(fillers))
    copies[19].wait_recv()
    total[high] = total[high] + last_in[3].astype(jnp.float32)
    if not forward:
        for copy in tile_copies[-2:]:
            copy.wait()
    if forward:
        for spread, slots, target, sems in (
            (spreads[0], gate_slots, gate_all, gate_out),
            (spreads[1], out_slots, out_all, vec_out),
        ):
            for index in (0, 5, 6, 7, 8, 11, 12):
                spread[index].wait_recv()
            size = slots.shape[1]
            for slot in range(8):
                place = pl.ds(pl.multiple_of(across_many(me, slot) * size, size), size)
                copy = pltpu.make_async_copy(slots.at[slot], target.at[place], sems.at[slot])
                copy.start()
                outs.append(copy)
            for copy in spread:
                copy.wait_send()
    for copy in copies:
        copy.wait_send()
    for copy in outs:
        copy.wait()
    for copy in far + slices:
        copy.wait()
    for index in range(2):
        near[index].wait_send()
        near_share[index].wait()
    if forward:
        own_slice.wait()


def turn(value, cosine, sine, direction=1.0):
    middle = value.shape[1] // 2
    first, second = value[:, :middle], value[:, middle:]
    sine = sine * direction
    return jnp.concatenate([first * cosine - second * sine, second * cosine + first * sine], axis=1)


def window_mask(positions, rows_of, blocks):
    row = lax.broadcasted_iota(jnp.int32, (rows_of, rows_of), 0)
    column = lax.broadcasted_iota(jnp.int32, (rows_of, rows_of), 1)
    positions = jnp.sum(jnp.where(row == column, positions, 0), axis=1, keepdims=True)
    query_row = lax.broadcasted_iota(jnp.int32, (rows_of, blocks * rows_of), 0)
    column = lax.broadcasted_iota(jnp.int32, (rows_of, blocks * rows_of), 1)
    behind = column // rows_of
    gap = query_row + 2 * behind * rows_of - column
    return (gap >= 0) & (gap <= positions) & (gap < WINDOW)


def norm_rows_grad(value, gain, upstream):
    factor = lax.rsqrt(jnp.mean(value * value, axis=-1, keepdims=True) + epsilon)
    unit = value * factor
    grad_gain = jnp.sum(upstream * unit, axis=0, keepdims=True)
    back = upstream * gain
    return factor * (back - unit * jnp.mean(back * unit, axis=-1, keepdims=True)), grad_gain


def greet(me, partners, block, others, work=None):
    barrier = pltpu.get_barrier_semaphore()
    for distance in partners:
        pl.semaphore_signal(
            barrier, inc=1, device_id={"fsdp": across_many(me, distance)}, device_id_type=pl.DeviceIdType.MESH
        )
    for distance in range(1, others + 1):
        pl.semaphore_signal(
            barrier,
            inc=1,
            device_id={"ctx": (block + distance) % (others + 1)},
            device_id_type=pl.DeviceIdType.MESH,
        )
    if work is not None:
        work()
    pl.semaphore_wait(barrier, len(partners) + others)


def push(source, target, send_sem, recv_sem, place):
    return pltpu.make_async_remote_copy(
        src_ref=source,
        dst_ref=target,
        send_sem=send_sem,
        recv_sem=recv_sem,
        device_id=place,
        device_id_type=pl.DeviceIdType.MESH,
    )


def spread_copies(own, slots, send_sem, recv_sem, me):
    half = own.shape[0] // 2
    low, high = pl.ds(0, half), pl.ds(half, half)
    sibling, beside, above = across(me, 1), across(me, 2), across(me, 4)
    plan = [
        (own, slots.at[1], sibling),
        (own.at[low], slots.at[2, low], beside),
        (own.at[low], slots.at[4, low], above),
        (own.at[high], slots.at[2, high], beside),
        (own.at[high], slots.at[4, high], above),
        (slots.at[2, low], slots.at[3, low], sibling),
        (slots.at[4, low], slots.at[5, low], sibling),
        (slots.at[2, high], slots.at[3, high], sibling),
        (slots.at[4, high], slots.at[5, high], sibling),
        (slots.at[2, low], slots.at[6, low], above),
        (slots.at[4, high], slots.at[6, high], beside),
        (slots.at[6, low], slots.at[7, low], sibling),
        (slots.at[6, high], slots.at[7, high], sibling),
    ]
    return [
        push(source, target, send_sem.at[index], recv_sem.at[index], {"fsdp": partner})
        for index, (source, target, partner) in enumerate(plan)
    ]


def attend_kernel(
    others, reach, source, gain_one, gain_two, gain_three, gain_four, gain_five, gain_six, head_gains, laurel_own,
    positions, cosine, sine, query_own, key_own, value_own, down_own, outward_own,
    normed, gains, linear, query_low, key_value, features, middle, attn_lin, laurel_all, inward_all, outward_all,
    gain_share, gain_slots, inward_slots, outward_slots, normed_low, attended, inward, lin_sum,
    gain_send, gain_recv, in_send, in_recv, out_send, out_recv, kv_send, kv_recv, in_copy, out_copy,
):
    rows_of, width = source.shape
    me, block = lax.axis_index("fsdp"), lax.axis_index("ctx")
    inward_own = inward_slots.at[0]
    gain_lines = gain_slots.at[0]

    def own_shares():
        start = 0
        for piece in (query_own, key_own, value_own, down_own):
            value = piece[...] if piece is not down_own else down_own[...].astype(jnp.float32).T.astype(jnp.bfloat16)
            inward_slots[0, :, pl.ds(start, value.shape[1])] = value
            start += value.shape[1]
        inward_slots[0, :, pl.ds(start, inward_slots.shape[2] - start)] = jnp.zeros(
            (inward_slots.shape[1], inward_slots.shape[2] - start), jnp.bfloat16
        )
        gain_share[...] = jnp.zeros_like(gain_share)
        for index, gain in enumerate((gain_one, gain_two, gain_three, gain_four, gain_five, gain_six)):
            pieces = gain[...].astype(jnp.float32)
            size = pieces.shape[0] * 128
            for row in range(pieces.shape[0]):
                place = pl.ds(pl.multiple_of(me * size + row * 128, 128), 128)
                gain_share[index : index + 1, place] = pieces[row : row + 1, :]
        gain_share[6:8, 0:HEAD_SIZE] = head_gains[...].astype(jnp.float32)
        gain_share[8:16, :] = laurel_own[...].astype(jnp.float32)
        gain_slots[0] = gain_share[...].astype(jnp.bfloat16)

    greet(me, range(1, 8), block, others, own_shares)
    gain_copies = [
        push(gain_lines, gain_slots.at[distance], gain_send.at[distance - 1], gain_recv.at[distance - 1],
             {"fsdp": across_many(me, distance)})
        for distance in range(1, 8)
    ]
    for copy in gain_copies:
        copy.start()
    spread_in = spread_copies(inward_own, inward_slots, in_send, in_recv, me)
    spread_out = spread_copies(outward_own, outward_slots, out_send, out_recv, me)
    for index in range(5):
        spread_in[index].start()
    outward_slots[0] = outward_own[...]

    value = source[...].astype(jnp.float32)
    factor = lax.rsqrt(jnp.mean(value * value, axis=-1, keepdims=True) + epsilon)
    for copy in gain_copies:
        copy.wait_recv()
    lines = gain_slots[...].astype(jnp.float32)
    gains[...] = jnp.sum(lines, axis=0)[0:8]
    laurel_size = 8
    laurel_all[...] = jnp.zeros_like(laurel_all)
    for slot in range(8):
        device = across_many(me, slot)
        laurel_all[pl.ds(pl.multiple_of(device * laurel_size, laurel_size), laurel_size), :] = lines[slot, 8:16]
    value = value * factor * gains[0:1, :]
    normed[...] = value
    normed_low[...] = value.astype(jnp.bfloat16)
    share = width // 8
    for index in range(8):
        features[:, pl.ds(2 * index * share, share)] = normed_low[:, pl.ds(index * share, share)]

    depth = inward_own.shape[0]
    head_rows = width // 8
    written = []

    def add_inward(slot):
        device = across_many(me, slot)
        part = normed_low[:, pl.ds(pl.multiple_of(device * depth, depth), depth)]
        for start in range(0, inward.shape[1], 640):
            span = pl.ds(start, 640)
            product = jnp.dot(part, inward_slots[slot, :, span], preferred_element_type=jnp.float32)
            inward[:, span] = product if slot == 0 else inward[:, span] + product
        copy = pltpu.make_async_copy(
            inward_slots.at[slot], inward_all.at[pl.ds(pl.multiple_of(device * depth, depth), depth)], in_copy.at[slot]
        )
        copy.start()
        written.append(copy)

    def add_outward(slot):
        device = across_many(me, slot)
        part = attended[:, pl.ds(pl.multiple_of(device * head_rows, head_rows), head_rows)]
        for start in range(0, width, 512):
            span = pl.ds(start, 512)
            product = jnp.dot(part, outward_slots[slot, pl.ds(0, head_rows), span], preferred_element_type=jnp.float32)
            lin_sum[:, span] = product if slot == 0 else lin_sum[:, span] + product

    def write_outward(slot):
        device = across_many(me, slot)
        rows = pl.ds(pl.multiple_of(device * head_rows, head_rows), head_rows)
        copy = pltpu.make_async_copy(outward_slots.at[slot], outward_all.at[rows], out_copy.at[slot])
        copy.start()
        written.append(copy)

    add_inward(0)
    spread_in[0].wait_recv()
    add_inward(1)
    spread_in[1].wait_recv()
    spread_in[9].start()
    spread_in[5].start()
    spread_in[2].wait_recv()
    spread_in[6].start()
    spread_in[3].wait_recv()
    spread_in[7].start()
    spread_in[4].wait_recv()
    spread_in[10].start()
    spread_in[8].start()
    for index in range(5):
        spread_out[index].start()
    add_inward(2)
    add_inward(4)
    spread_in[5].wait_recv()
    spread_in[7].wait_recv()
    add_inward(3)
    spread_in[6].wait_recv()
    spread_in[8].wait_recv()
    add_inward(5)
    spread_in[9].wait_recv()
    spread_in[11].start()
    spread_in[10].wait_recv()
    spread_in[12].start()
    add_inward(6)
    spread_in[11].wait_recv()
    spread_in[12].wait_recv()
    add_inward(7)

    query_width, key_width = QUERY_HEADS * HEAD_SIZE, KEY_VALUE_HEADS * HEAD_SIZE
    own_rows = pl.ds(0, rows_of)

    def head(start, gain):
        lane = inward[:, pl.ds(start, HEAD_SIZE)]
        scale = lax.rsqrt(jnp.mean(lane * lane, axis=-1, keepdims=True) + epsilon)
        return turn(lane * scale * gain, cosine[...], sine[...]).astype(jnp.bfloat16)

    for index in range(KEY_VALUE_HEADS):
        key_value[own_rows, pl.ds(index * HEAD_SIZE, HEAD_SIZE)] = head(
            query_width + index * HEAD_SIZE, gains[7:8, 0:HEAD_SIZE]
        )
    key_value[own_rows, pl.ds(key_width, key_width)] = inward[:, pl.ds(query_width + key_width, key_width)].astype(
        jnp.bfloat16
    )
    for distance in range(1, reach + 1):
        copy = push(
            key_value.at[own_rows],
            key_value.at[pl.ds(distance * rows_of, rows_of)],
            kv_send.at[distance - 1],
            kv_recv.at[distance - 1],
            {"ctx": (block + distance) % (others + 1)},
        )

        @pl.when(block + distance <= others)
        def _():
            copy.start()

        @pl.when(block < distance)
        def _():
            key_value[pl.ds(distance * rows_of, rows_of), :] = jnp.zeros((rows_of, 2 * key_width), jnp.bfloat16)

    for index in range(QUERY_HEADS):
        query_low[:, pl.ds(index * HEAD_SIZE, HEAD_SIZE)] = head(index * HEAD_SIZE, gains[6:7, 0:HEAD_SIZE])
    linear[...] = inward[:, pl.ds(0, query_width + key_width)]
    middle[...] = inward[:, pl.ds(query_width + 2 * key_width, middle.shape[1])].astype(jnp.bfloat16)

    spread_out[0].wait_recv()
    spread_out[1].wait_recv()
    spread_out[9].start()
    spread_out[5].start()
    spread_out[2].wait_recv()
    spread_out[6].start()
    for distance in range(1, reach + 1):
        copy = push(
            key_value.at[own_rows],
            key_value.at[pl.ds(distance * rows_of, rows_of)],
            kv_send.at[distance - 1],
            kv_recv.at[distance - 1],
            {"ctx": (block + distance) % (others + 1)},
        )

        @pl.when(block >= distance)
        def _():
            copy.wait_recv()

    allowed = window_mask(positions[...], rows_of, reach + 1)
    per_group = QUERY_HEADS // KEY_VALUE_HEADS
    for index in range(QUERY_HEADS):
        group = index // per_group
        columns = pl.ds(index * HEAD_SIZE, HEAD_SIZE)
        scores = product_back(query_low[:, columns], key_value[:, pl.ds(group * HEAD_SIZE, HEAD_SIZE)])
        scores = jnp.where(allowed, scores * HEAD_SIZE ** (-0.5), -1e30)
        grown = jnp.exp(scores - jnp.max(scores, axis=-1, keepdims=True))
        soft = (grown / jnp.sum(grown, axis=-1, keepdims=True)).astype(jnp.bfloat16)
        attended[:, columns] = jnp.dot(
            soft, key_value[:, pl.ds(key_width + group * HEAD_SIZE, HEAD_SIZE)], preferred_element_type=jnp.float32
        ).astype(jnp.bfloat16)

    for index in range(8):
        features[:, pl.ds((2 * index + 1) * share, share)] = attended[:, pl.ds(index * share, share)]
    add_outward(0)
    add_outward(1)
    write_outward(0)
    write_outward(1)
    spread_out[3].wait_recv()
    spread_out[7].start()
    spread_out[4].wait_recv()
    spread_out[10].start()
    spread_out[8].start()
    add_outward(2)
    add_outward(4)
    spread_out[5].wait_recv()
    spread_out[7].wait_recv()
    add_outward(3)
    spread_out[6].wait_recv()
    spread_out[8].wait_recv()
    add_outward(5)
    for slot in range(2, 6):
        write_outward(slot)
    spread_out[9].wait_recv()
    spread_out[11].start()
    spread_out[10].wait_recv()
    spread_out[12].start()
    add_outward(6)
    write_outward(6)
    spread_out[11].wait_recv()
    spread_out[12].wait_recv()
    add_outward(7)
    write_outward(7)
    attn_lin[...] = lin_sum[...]
    for copy in gain_copies + spread_in + spread_out:
        copy.wait_send()
    for copy in written:
        copy.wait()
    for distance in range(1, reach + 1):
        copy = push(
            key_value.at[own_rows],
            key_value.at[pl.ds(distance * rows_of, rows_of)],
            kv_send.at[distance - 1],
            kv_recv.at[distance - 1],
            {"ctx": (block + distance) % (others + 1)},
        )

        @pl.when(block + distance <= others)
        def _():
            copy.wait_send()


def attend_call(reach, source, gains, head_gains, laurel_own, positions, cosine, sine, inward_own, outward_own):
    rows_of, width = source.shape
    others = lax.axis_size("ctx") - 1
    low, full = jnp.bfloat16, jnp.float32
    hbm = pl.BlockSpec(memory_space=pl.ANY)
    vmem = pl.BlockSpec(memory_space=pltpu.VMEM)
    dma = pltpu.SemaphoreType.DMA
    depth = inward_own[0].shape[0]
    columns = sum(piece.shape[1] for piece in inward_own[:3]) + inward_own[3].shape[0]
    columns += -columns % 128
    gain_shape = (16, width)
    query_width, key_width = QUERY_HEADS * HEAD_SIZE, KEY_VALUE_HEADS * HEAD_SIZE
    tail = columns - query_width - 2 * key_width
    shapes = [
        jax.ShapeDtypeStruct((rows_of, width), full),
        jax.ShapeDtypeStruct((8, width), full),
        jax.ShapeDtypeStruct((rows_of, query_width + key_width), full),
        jax.ShapeDtypeStruct((rows_of, query_width), low),
        jax.ShapeDtypeStruct(((reach + 1) * rows_of, 2 * key_width), low),
        jax.ShapeDtypeStruct((rows_of, 2 * width), low),
        jax.ShapeDtypeStruct((rows_of, tail), low),
        jax.ShapeDtypeStruct((rows_of, width), full),
        jax.ShapeDtypeStruct((tail, width), full),
        jax.ShapeDtypeStruct((8 * depth, columns), low),
        jax.ShapeDtypeStruct((8 * outward_own.shape[0], width), low),
    ]
    return pl.pallas_call(
        functools.partial(attend_kernel, others, reach),
        out_shape=shapes,
        in_specs=[vmem] * 17,
        out_specs=[vmem] * 9 + [hbm] * 2,
        scratch_shapes=[
            pltpu.VMEM(gain_shape, full),
            pltpu.VMEM((8, *gain_shape), low),
            pltpu.VMEM((8, depth, columns), low),
            pltpu.VMEM((8, *outward_own.shape), low),
            pltpu.VMEM((rows_of, width), low),
            pltpu.VMEM((rows_of, query_width), low),
            pltpu.VMEM((rows_of, columns), full),
            pltpu.VMEM((rows_of, width), full),
            dma((7,)),
            dma((7,)),
            dma((13,)),
            dma((13,)),
            dma((13,)),
            dma((13,)),
            dma((max(reach, 1),)),
            dma((max(reach, 1),)),
            dma((8,)),
            dma((8,)),
        ],
        compiler_params=pltpu.CompilerParams(collective_id=3, has_side_effects=True, vmem_limit_bytes=56 * 2**20),
        cost_estimate=pl.CostEstimate(
            flops=60 * rows_of * width * columns, bytes_accessed=20 * depth * columns, transcendentals=0
        ),
        name="attend_forward",
    )(source, *gains, head_gains, laurel_own, positions, cosine, sine, *inward_own, outward_own)


def turn_norm_grad(upstream, linear, gain, cosine, sine):
    scale = lax.rsqrt(jnp.mean(linear * linear, axis=-1, keepdims=True) + epsilon)
    unit = linear * scale
    back = turn(upstream, cosine, sine, -1.0)
    grad_gain = jnp.sum(back * unit, axis=0, keepdims=True)
    back = back * gain
    return scale * (back - unit * jnp.mean(back * unit, axis=-1, keepdims=True)), grad_gain


def attend_back_kernel(
    others, reach, d_ffn_in, mixed, d_residual, laurel_lin, attn_lin, laurel, gain_part,
    query_low, key_value, linear, gains, positions, cosine, sine, middle, features,
    source, residual, d_vector, gated_value, d_back, outward_all, inward_all, d_rows,
    d_source, grad_wide, grad_small, near_hbm,
    d_lin, d_half, d_laurel, d_middle, gain_rows,
    outward, inward, d_attended, d_key_value, parcel, arrived, d_query, d_rest, lin_slots, query_slots, rest_slots,
    ordered, d_normed, gain_parcel, gain_arrived, load_sem, lin_send, lin_recv, query_send, query_recv, rest_send, rest_recv, kv_send, kv_recv, gain_send, gain_recv, near_send, near_recv,
    gate_in, gate_sum, gate_arrived, out_in, out_sum, out_arrived, pair_send, pair_recv, chip_send, chip_recv,
    gate_parts, out_parts, laurel_rows, laurel_in, laurel_sum, laurel_arrived,
):
    rows_of, width = source.shape
    me, block = lax.axis_index("fsdp"), lax.axis_index("ctx")
    query_width, key_width = QUERY_HEADS * HEAD_SIZE, KEY_VALUE_HEADS * HEAD_SIZE
    per_group = QUERY_HEADS // KEY_VALUE_HEADS
    depth = width // 8
    loads = [
        pltpu.make_async_copy(outward_all.at[pl.ds(index * depth, depth)], outward.at[index % 2], load_sem.at[index])
        for index in range(8)
    ]
    loads.append(pltpu.make_async_copy(inward_all, inward, load_sem.at[8]))
    for index in (0, 1, 8):
        loads[index].start()

    def before_attention():
        d_mixed, grad_before = norm_rows_grad(mixed[...], gains[3:4, :], d_ffn_in[...])
        d_half[...] = (d_residual[...] + d_mixed) * inv_root
        d_branch, grad_laurel_gain = norm_rows_grad(laurel_lin[...], gains[2:3, :], d_half[...])
        d_laurel[...] = d_branch.astype(jnp.bfloat16)
        d_middle[...] = product_back(d_laurel[...], laurel[...].astype(jnp.bfloat16)).astype(jnp.bfloat16)
        d_branch, grad_attention = norm_rows_grad(attn_lin[...], gains[1:2, :], d_half[...])
        d_lin[...] = d_branch.astype(jnp.bfloat16)
        gain_rows[...] = gain_part[...]
        gain_rows[1:2, :] = grad_attention
        gain_rows[2:3, :] = grad_laurel_gain
        gain_rows[3:4, :] = grad_before

    greet(me, range(1, 8), block, others, before_attention)
    mine, theirs = pl.ds(0, rows_of), pl.ds(rows_of, rows_of)
    near = [
        push(
            d_rows.at[pl.ds(group * 2 * rows_of, rows_of)],
            near_hbm.at[group, mine],
            near_send.at[group],
            near_recv.at[group],
            {"ctx": across(block, 1)},
        )
        for group in range(4)
    ]
    near_share = [
        push(
            near_hbm.at[group, mine],
            near_hbm.at[group, theirs],
            near_send.at[4 + group],
            near_recv.at[4 + group],
            {"fsdp": across(me, 1)},
        )
        for group in range(4)
    ]
    for copy in near[:2]:
        copy.start()
    vector_parts = (
        (gate_parts, gate_in, gate_sum, gate_arrived),
        (out_parts, out_in, out_sum, out_arrived),
        (laurel_rows, laurel_in, laurel_sum, laurel_arrived),
    )
    chips = (0, 2, 4, 6)
    pair_copies = []
    chip_copies = []
    for kind, (parts, pair_in, pair_sum, arrived_parts) in enumerate(vector_parts):
        for index, chip in enumerate(chips):
            place = 4 * kind + index
            pair_copies.append(
                push(
                    parts.at[across_many(me, chip + 1)],
                    pair_in.at[index],
                    pair_send.at[place],
                    pair_recv.at[place],
                    {"fsdp": across(me, 1)},
                )
            )
            if chip:
                place = 3 * kind + index - 1
                chip_copies.append(
                    push(
                        pair_sum.at[index - 1],
                        arrived_parts.at[index - 1],
                        chip_send.at[place],
                        chip_recv.at[place],
                        {"fsdp": across_many(me, chip)},
                    )
                )
    spread_lin = spread_copies(d_lin, lin_slots, lin_send, lin_recv, me)
    spread_query = spread_copies(d_query, query_slots, query_send, query_recv, me)
    spread_rest = spread_copies(d_rest, rest_slots, rest_send, rest_recv, me)
    for index in range(5):
        spread_lin[index].start()
    lin_slots[0] = d_lin[...]
    for index in range(8):
        gate_parts[index] = product_rows(residual[:, pl.ds(index * depth, depth)], d_vector[...]).astype(jnp.bfloat16)
    out_parts[...] = product_rows(gated_value[...], d_back[...]).reshape(out_parts.shape).astype(jnp.bfloat16)
    laurel_rows[...] = product_rows(middle[...], d_laurel[...])[0 : 8 * laurel_rows.shape[1]].reshape(laurel_rows.shape)
    for copy in pair_copies:
        copy.start()
    for slot in range(8):
        device = across_many(me, slot)
        ordered[pl.ds(slot * rows_of, rows_of), :] = features[
            pl.ds(pl.multiple_of(device * rows_of, rows_of), rows_of), :
        ]
    for index in range(8):
        loads[index].wait()
        d_attended[:, pl.ds(index * depth, depth)] = product_back(d_lin[...], outward[index % 2]).astype(jnp.bfloat16)
        if index + 2 < 8:
            loads[index + 2].start()

    allowed = window_mask(positions[...], rows_of, reach + 1)
    scale = HEAD_SIZE ** (-0.5)

    def one_head(index):
        group = index // per_group
        columns = pl.ds(index * HEAD_SIZE, HEAD_SIZE)
        keys = pl.ds(group * HEAD_SIZE, HEAD_SIZE)
        values = pl.ds(key_width + group * HEAD_SIZE, HEAD_SIZE)
        scores = product_back(query_low[:, columns], key_value[:, keys])
        scores = jnp.where(allowed, scores * scale, -1e30)
        grown = jnp.exp(scores - jnp.max(scores, axis=-1, keepdims=True))
        soft = grown / jnp.sum(grown, axis=-1, keepdims=True)
        d_soft = product_back(d_attended[:, columns], key_value[:, values])
        d_scores = (soft * (d_soft - jnp.sum(soft * d_soft, axis=-1, keepdims=True))).astype(jnp.bfloat16)
        upstream = scale * jnp.dot(d_scores, key_value[:, keys], preferred_element_type=jnp.float32)
        d_key = scale * product_rows(d_scores, query_low[:, columns])
        d_value = product_rows(soft.astype(jnp.bfloat16), d_attended[:, columns])
        if index % per_group == 0:
            d_key_value[:, keys] = d_key
            d_key_value[:, values] = d_value
        else:
            d_key_value[:, keys] += d_key
            d_key_value[:, values] += d_value
        d_head, grad_gain = turn_norm_grad(upstream, linear[:, columns], gains[6:7, 0:HEAD_SIZE], cosine[...], sine[...])
        d_query[:, columns] = d_head.astype(jnp.bfloat16)
        return grad_gain

    query_gain = one_head(0)
    for index in range(1, per_group):
        query_gain = query_gain + one_head(index)
    spread_lin[0].wait_recv()
    spread_lin[1].wait_recv()
    spread_lin[9].start()
    spread_lin[5].start()
    spread_lin[2].wait_recv()
    spread_lin[6].start()
    for index in range(per_group, QUERY_HEADS):
        query_gain = query_gain + one_head(index)
    parcel[...] = d_key_value[pl.ds(rows_of, reach * rows_of), :].astype(jnp.bfloat16)

    def return_copy(distance):
        span = pl.ds((distance - 1) * rows_of, rows_of)
        return push(
            parcel.at[span],
            arrived.at[span],
            kv_send.at[distance - 1],
            kv_recv.at[distance - 1],
            {"ctx": (block + others + 1 - distance) % (others + 1)},
        )

    for distance in range(1, reach + 1):
        copy = return_copy(distance)

        @pl.when(block >= distance)
        def _():
            copy.start()

        @pl.when(block + distance > others)
        def _():
            arrived[pl.ds((distance - 1) * rows_of, rows_of), :] = jnp.zeros((rows_of, 2 * key_width), jnp.bfloat16)

    for copy in near[2:]:
        copy.start()
    spread_lin[3].wait_recv()
    spread_lin[7].start()
    spread_lin[4].wait_recv()
    spread_lin[10].start()
    spread_lin[8].start()
    for index in range(5):
        spread_query[index].start()
    for copy in pair_copies:
        copy.wait_recv()
    for parts, pair_in, pair_sum, arrived_parts in vector_parts:
        for index, chip in enumerate(chips):
            if chip:
                pair_sum[index - 1] = (
                    parts[across_many(me, chip)].astype(jnp.float32) + pair_in[index].astype(jnp.float32)
                ).astype(pair_sum.dtype)
    for copy in chip_copies:
        copy.start()
    query_slots[0] = d_query[...]
    loads[8].wait()
    d_normed[...] = product_back(d_query[...], inward[:, pl.ds(0, query_width)])
    spread_lin[9].wait_recv()
    spread_lin[11].start()
    spread_lin[10].wait_recv()
    spread_lin[12].start()
    spread_query[0].wait_recv()
    spread_query[1].wait_recv()
    spread_query[9].start()
    spread_query[5].start()
    spread_query[2].wait_recv()
    spread_query[6].start()
    for index in (5, 6, 7, 8, 11, 12):
        spread_lin[index].wait_recv()
    grad_wide[:, pl.ds(inward.shape[1], width)] = product_rows(
        ordered[:, pl.ds(depth, depth)], lin_slots[...].reshape(8 * rows_of, width)
    ).astype(jnp.bfloat16)

    for distance in range(1, reach + 1):
        copy = return_copy(distance)

        @pl.when(block + distance <= others)
        def _():
            copy.wait_recv()

    total = d_key_value[pl.ds(0, rows_of), :]
    for distance in range(1, reach + 1):
        total = total + arrived[pl.ds((distance - 1) * rows_of, rows_of), :].astype(jnp.float32)
    for index in range(KEY_VALUE_HEADS):
        columns = pl.ds(index * HEAD_SIZE, HEAD_SIZE)
        d_head, grad_gain = turn_norm_grad(
            total[:, index * HEAD_SIZE : (index + 1) * HEAD_SIZE],
            linear[:, pl.ds(query_width + index * HEAD_SIZE, HEAD_SIZE)],
            gains[7:8, 0:HEAD_SIZE],
            cosine[...],
            sine[...],
        )
        d_rest[:, columns] = d_head.astype(jnp.bfloat16)
        key_gain = grad_gain if index == 0 else key_gain + grad_gain
    d_rest[:, pl.ds(key_width, key_width)] = total[:, key_width:].astype(jnp.bfloat16)
    d_rest[:, pl.ds(2 * key_width, d_middle.shape[1])] = d_middle[...]
    spread_query[3].wait_recv()
    spread_query[7].start()
    spread_query[4].wait_recv()
    spread_query[10].start()
    spread_query[8].start()
    for index in range(5):
        spread_rest[index].start()
    rest_slots[0] = d_rest[...]
    rest_width = d_rest.shape[1]
    d_normed[...] += product_back(d_rest[...], inward[:, pl.ds(query_width, rest_width)])
    value = source[...].astype(jnp.float32)
    factor = lax.rsqrt(jnp.mean(value * value, axis=-1, keepdims=True) + epsilon)
    unit = value * factor
    upstream = d_half[...] + d_normed[...]
    for index in range(8):
        columns = slice(index * depth, (index + 1) * depth)
        gain_parcel[index, 0:8, :] = gain_rows[0:8, columns]
        gain_parcel[index, 0:1, :] = jnp.sum(upstream[:, columns] * unit[:, columns], axis=0, keepdims=True)
        gain_parcel[index, 6:7, :] = query_gain
        gain_parcel[index, 7:8, :] = key_gain
    gain_copies = [
        push(
            gain_parcel.at[across_many(me, distance)],
            gain_arrived.at[distance],
            gain_send.at[distance - 1],
            gain_recv.at[distance - 1],
            {"fsdp": across_many(me, distance)},
        )
        for distance in range(1, 8)
    ]
    for copy in gain_copies:
        copy.start()
    gain_arrived[0] = gain_parcel[me]
    upstream = upstream * gains[0:1, :]
    d_source[...] = d_half[...] + factor * (upstream - unit * jnp.mean(upstream * unit, axis=-1, keepdims=True))
    spread_rest[0].wait_recv()
    spread_rest[1].wait_recv()
    spread_rest[9].start()
    spread_rest[5].start()
    spread_rest[2].wait_recv()
    spread_rest[6].start()
    spread_query[9].wait_recv()
    spread_query[11].start()
    spread_query[10].wait_recv()
    spread_query[12].start()
    spread_rest[3].wait_recv()
    spread_rest[7].start()
    spread_rest[4].wait_recv()
    spread_rest[10].start()
    spread_rest[8].start()
    for index in (5, 6, 7, 8, 11, 12):
        spread_query[index].wait_recv()
    grad_wide[:, pl.ds(0, query_width)] = product_rows(
        ordered[:, pl.ds(0, depth)], query_slots[...].reshape(8 * rows_of, query_width)
    ).astype(jnp.bfloat16)
    spread_rest[9].wait_recv()
    spread_rest[11].start()
    spread_rest[10].wait_recv()
    spread_rest[12].start()
    for index in (5, 6, 7, 8, 11, 12):
        spread_rest[index].wait_recv()
    grad_wide[:, pl.ds(query_width, rest_width)] = product_rows(
        ordered[:, pl.ds(0, depth)], rest_slots[...].reshape(8 * rows_of, rest_width)
    ).astype(jnp.bfloat16)
    for copy, share in zip(near, near_share):
        copy.wait_recv()
        share.start()
    for copy in gain_copies + chip_copies:
        copy.wait_recv()
    totals = []
    for parts, pair_in, pair_sum, arrived_parts in vector_parts:
        total = parts[me].astype(jnp.float32) + pair_in[0].astype(jnp.float32)
        for index in range(3):
            total = total + arrived_parts[index].astype(jnp.float32)
        totals.append(total)
    grad_wide[:, pl.ds(inward.shape[1] + width, totals[0].shape[1])] = totals[0].astype(jnp.bfloat16)
    laurel_size = laurel_rows.shape[1]
    tail = jnp.concatenate(
        [totals[2], jnp.pad(jnp.sum(gain_arrived[...], axis=0), ((0, 0), (0, width - depth)))],
        axis=0,
    )
    out_size = totals[1].shape[0]
    grad_small[pl.ds(0, out_size), :] = totals[1].astype(jnp.bfloat16)
    grad_small[pl.ds(out_size, laurel_size + 8), :] = tail.astype(jnp.bfloat16)
    for copy in near_share:
        copy.wait_recv()
    for copy in (
        spread_lin + spread_query + spread_rest + gain_copies + near + near_share + pair_copies + chip_copies
    ):
        copy.wait_send()
    for distance in range(1, reach + 1):
        copy = return_copy(distance)

        @pl.when(block >= distance)
        def _():
            copy.wait_send()


def attend_back_call(
    reach, d_ffn_in, mixed, d_residual, laurel_lin, attn_lin, laurel, gain_part,
    query_low, key_value, linear, gains, positions, cosine, sine, middle, features,
    source, residual, d_vector, gated_value, d_back, outward_all, inward_all, d_rows,
):
    rows_of, width = source.shape
    others = lax.axis_size("ctx") - 1
    low, full = jnp.bfloat16, jnp.float32
    hbm = pl.BlockSpec(memory_space=pl.ANY)
    vmem = pl.BlockSpec(memory_space=pltpu.VMEM)
    dma = pltpu.SemaphoreType.DMA
    columns = inward_all.shape[1]
    query_width, key_width = QUERY_HEADS * HEAD_SIZE, KEY_VALUE_HEADS * HEAD_SIZE
    rest_width = columns - query_width
    depth = width // 8
    vector_width = d_vector.shape[1]
    part_shapes = ((depth, vector_width), (vector_width // 8, width))
    shapes = [
        jax.ShapeDtypeStruct((rows_of, width), full),
        jax.ShapeDtypeStruct((depth, columns + width + vector_width), low),
        jax.ShapeDtypeStruct((vector_width // 8 + 16, width), low),
        jax.ShapeDtypeStruct((4, 2 * rows_of, width), low),
    ]
    spans = max(reach, 1)
    return pl.pallas_call(
        functools.partial(attend_back_kernel, others, reach),
        out_shape=shapes,
        in_specs=[vmem] * 21 + [hbm] * 3,
        out_specs=[vmem] * 3 + [hbm],
        scratch_shapes=[
            pltpu.VMEM((rows_of, width), low),
            pltpu.VMEM((rows_of, width), full),
            pltpu.VMEM((rows_of, width), low),
            pltpu.VMEM(middle.shape, low),
            pltpu.VMEM((8, width), full),
            pltpu.VMEM((2, depth, width), low),
            pltpu.VMEM((width, columns), low),
            pltpu.VMEM((rows_of, query_width), low),
            pltpu.VMEM(((reach + 1) * rows_of, 2 * key_width), full),
            pltpu.VMEM((spans * rows_of, 2 * key_width), low),
            pltpu.VMEM((spans * rows_of, 2 * key_width), low),
            pltpu.VMEM((rows_of, query_width), low),
            pltpu.VMEM((rows_of, rest_width), low),
            pltpu.VMEM((8, rows_of, width), low),
            pltpu.VMEM((8, rows_of, query_width), low),
            pltpu.VMEM((8, rows_of, rest_width), low),
            pltpu.VMEM((8 * rows_of, 2 * depth), low),
            pltpu.VMEM((rows_of, width), full),
            pltpu.VMEM((8, 8, depth), full),
            pltpu.VMEM((8, 8, depth), full),
            dma((9,)),
            dma((13,)),
            dma((13,)),
            dma((13,)),
            dma((13,)),
            dma((13,)),
            dma((13,)),
            dma((spans,)),
            dma((spans,)),
            dma((7,)),
            dma((7,)),
            dma((8,)),
            dma((8,)),
        ]
        + [
            pltpu.VMEM((count, *shape), low)
            for shape in part_shapes
            for count in (4, 3, 3)
        ]
        + [dma((12,)), dma((12,)), dma((9,)), dma((9,))]
        + [pltpu.VMEM((8, *shape), low) for shape in part_shapes]
        + [pltpu.VMEM((count, 8, width), full) for count in (8, 4, 3, 3)],
        compiler_params=pltpu.CompilerParams(collective_id=4, has_side_effects=True, vmem_limit_bytes=60 * 2**20),
        cost_estimate=pl.CostEstimate(
            flops=40 * rows_of * width * columns, bytes_accessed=6 * width * columns, transcendentals=0
        ),
        name="attend_backward",
    )(
        d_ffn_in, mixed, d_residual, laurel_lin, attn_lin, laurel, gain_part,
        query_low, key_value, linear, gains, positions, cosine, sine, middle, features,
        source, residual, d_vector, gated_value, d_back, outward_all, inward_all, d_rows,
    )


def feed_call(forward, prelude, weights, kept=(), features=None, forward_rows=None, hidden_rows=None, vectors=()):
    rows_of, width = prelude[0].shape
    hidden = weights[0].shape[0]
    all_rows = 8 * rows_of
    others = lax.axis_size("ctx") - 1
    low, full = jnp.bfloat16, jnp.float32
    count_made = 3 if forward else 2
    hbm = pl.BlockSpec(memory_space=pl.ANY)
    vmem = pl.BlockSpec(memory_space=pltpu.VMEM)
    half = rows_of // 2
    dma = pltpu.SemaphoreType.DMA

    def shape(columns, kind, rows=rows_of):
        return jax.ShapeDtypeStruct((rows, columns), kind)

    operands = (*prelude, *weights, *kept)
    operand_specs = [vmem] * len(prelude) + [hbm] * (3 + len(kept))
    shapes = [shape(width, full)]
    extra = []
    if forward:
        shapes += [shape(width, full)] * 2
        operands += (features, *vectors)
        operand_specs += [vmem] * 3
        extra = (
            [dma((7,)), dma((7,)), dma]
            + [pltpu.VMEM((8, *value.shape), low) for value in vectors]
            + [dma((13,))] * 4
            + [dma((8,))] * 2
        )
    else:
        vector_width = prelude[5].shape[1]
        shapes += [shape(width, low), shape(vector_width, full), shape(width, low), shape(vector_width, low)]
        shapes += [shape(vector_width, low), shape(width, low), shape(width, full), shape(width, full, 8)]
        operands += (forward_rows, hidden_rows)
        operand_specs += [hbm] * 2
        extra = [
            pltpu.VMEM((all_rows, hidden), low),
            pltpu.VMEM((all_rows, width), low),
            pltpu.VMEM((2, hidden, 512), full),
            dma,
            dma,
            dma((3 * (width // 512),)),
        ]
    count_vmem = len(shapes)
    shapes += [
        shape(width, low, all_rows),
        jax.ShapeDtypeStruct((2, rows_of, width), low),
        jax.ShapeDtypeStruct((2, 2 * rows_of, width), low),
    ]
    if forward:
        shapes += [jax.ShapeDtypeStruct((8, rows_of, features.shape[1] // 8), low)]
        shapes += [shape(value.shape[1], low, 8 * value.shape[0]) for value in vectors]
    else:
        shapes += [shape(width, full, hidden)] * 3
    shapes += [shape(hidden, low, all_rows)] * count_made
    return pl.pallas_call(
        functools.partial(feed_kernel, forward, rows_of, others),
        out_shape=shapes,
        in_specs=operand_specs,
        out_specs=[vmem] * count_vmem + [hbm] * (len(shapes) - count_vmem),
        scratch_shapes=[pltpu.VMEM((hidden, width), low)] * 3
        + [pltpu.VMEM((all_rows, hidden), low)] * (len(kept) + count_made)
        + [
            pltpu.VMEM((rows_of, width), low),
            pltpu.VMEM((4, 2 * rows_of, width), low),
            pltpu.VMEM((4, 2 * rows_of, width), low),
            pltpu.VMEM((4, rows_of, width), low),
            pltpu.VMEM((3, rows_of, width), low),
            pltpu.VMEM((2, half, width), low),
            pltpu.VMEM((2, half, width), low),
            pltpu.VMEM((4, half, width), low),
            dma((20,)),
            dma((20,)),
            dma((3 + len(kept),)),
            dma((4 * (1 + count_made),)),
            dma((2,)),
            dma((2,)),
            dma((4,)),
            dma((4,)),
        ]
        + extra,
        compiler_params=pltpu.CompilerParams(
            collective_id=1 if forward else 2,
            has_side_effects=True,
            vmem_limit_bytes=62 * 2**20,
        ),
        cost_estimate=pl.CostEstimate(
            flops=40 * all_rows * hidden * width // 2,
            bytes_accessed=6 * hidden * width + 8 * all_rows * width,
            transcendentals=0,
        ),
        name="feed_forward" if forward else "feed_backward",
    )(*operands)


def other_rows(rows, d_rows, weights, tiles, arrive):
    gate, up, down = weights
    hidden_tile, d_gate_tile, d_up_tile = tiles
    tile = min(512, gate.shape[0])
    for index in range(3):
        arrive(index)

    def body(index, carry):
        span = pl.ds(pl.multiple_of(index * tile, tile), tile)
        gate_value = product_back(gate[span, :], rows[...])
        up_value = product_back(up[span, :], rows[...])
        d_hidden = product_back(down[span, :], d_rows[...])
        value, slope = gelu_parts(gate_value)
        hidden_tile[span, :] = (value * up_value).astype(jnp.bfloat16)
        d_gate_tile[span, :] = (d_hidden * up_value * slope).astype(jnp.bfloat16)
        d_up_tile[span, :] = (d_hidden * value).astype(jnp.bfloat16)
        return carry

    lax.fori_loop(0, gate.shape[0] // tile, body, 0)


def add_weight_grads(grads, tiles, rows, d_rows, last, done):
    hidden_tile, d_gate_tile, d_up_tile = tiles
    terms = list(zip(grads, (d_gate_tile, d_up_tile, hidden_tile), (rows, rows, d_rows)))

    @pl.when(jnp.logical_not(last))
    def _():
        for grad, tile, right in terms:
            grad[...] += matrix_product(tile[...], right[...])

    @pl.when(last)
    def _():
        for index, (grad, tile, right) in enumerate(terms):
            grad[...] += matrix_product(tile[...], right[...])
            done(index)


def weight_moves(step, last, weights_hbm, weights, parts_hbm, grads, grads_hbm, weight_sem, part_sem, out_sem):
    weight_loads, part_loads, out_copies = [
        [pltpu.make_async_copy(source, target, sem.at[index]) for index, (source, target) in enumerate(zip(sources, targets))]
        for sources, targets, sem in (
            (weights_hbm, weights, weight_sem),
            (parts_hbm, grads, part_sem),
            (grads, grads_hbm, out_sem),
        )
    ]

    @pl.when(step == 0)
    def _():
        for load in weight_loads + part_loads:
            load.start()

    def arrive(index):
        @pl.when(step == 0)
        def _():
            weight_loads[index].wait()

    def begin_sums():
        @pl.when(step == 0)
        def _():
            for load in part_loads:
                load.wait()

    def done(index):
        out_copies[index].start()

    def finish():
        @pl.when(step == last)
        def _():
            for copy in out_copies:
                copy.wait()

    return arrive, begin_sums, done, finish


def weight_part_kernel(
    near_steps, gate_hbm, up_hbm, down_hbm, rows_near, rows_next, d_rows_near, gate_part, up_part, down_part, far_own,
    gate_out, up_out, down_out, far_all,
    gate, up, down, grad_gate, grad_up, grad_down, hidden_tile, d_gate_tile, d_up_tile,
    send_sem, recv_sem, own_sem, weight_sem, part_sem, out_sem,
):
    step = pl.program_id(0)
    last = near_steps - 1
    me = lax.axis_index("fsdp")
    grads = (grad_gate, grad_up, grad_down)
    tiles = (hidden_tile, d_gate_tile, d_up_tile)

    sibling, beside, above = across(me, 1), across(me, 2), across(me, 4)
    diagonal = across(beside, 4)
    plan = [(far_own, far_all.at[me], sibling)]
    for part in range(2):
        plan += [(far_own.at[part], far_all.at[me, part], beside), (far_own.at[part], far_all.at[me, part], above)]
    for part in range(2):
        plan += [(far_all.at[device, part], far_all.at[device, part], sibling) for device in (beside, above)]
    plan.append((far_all.at[beside, 0], far_all.at[beside, 0], above))
    plan.append((far_all.at[above, 1], far_all.at[above, 1], beside))
    plan += [(far_all.at[diagonal, part], far_all.at[diagonal, part], sibling) for part in range(2)]
    copies = [
        push(source, target, send_sem.at[index], recv_sem.at[index], {"fsdp": partner})
        for index, (source, target, partner) in enumerate(plan)
    ]
    own_copy = pltpu.make_async_copy(far_own, far_all.at[me], own_sem)

    arrive, begin_sums, done, finish = weight_moves(
        step, last, (gate_hbm, up_hbm, down_hbm), (gate, up, down), (gate_part, up_part, down_part), grads,
        (gate_out, up_out, down_out), weight_sem, part_sem, out_sem,
    )

    @pl.when(step == 0)
    def _():
        greet(me, (1, 2, 4), 0, 0)
        own_copy.start()
        for index in range(5):
            copies[index].start()

    @pl.when(step == last - 1)
    def _():
        copies[0].wait_recv()
        copies[1].wait_recv()
        copies[9].start()
        copies[5].start()
        copies[2].wait_recv()
        copies[6].start()

    @pl.when(step == last)
    def _():
        copies[3].wait_recv()
        copies[7].start()
        copies[4].wait_recv()
        copies[10].start()
        copies[8].start()

    weights = (gate, up, down)

    @pl.when(step < near_steps // 2)
    def _():
        other_rows(rows_near, d_rows_near, weights, tiles, arrive)
        begin_sums()
        add_weight_grads(grads, tiles, rows_near, d_rows_near, step == last, done)

    @pl.when(step >= near_steps // 2)
    def _():
        other_rows(rows_next, d_rows_near, weights, tiles, arrive)
        add_weight_grads(grads, tiles, rows_next, d_rows_near, step == last, done)

    @pl.when(step == last)
    def _():
        copies[9].wait_recv()
        copies[11].start()
        copies[10].wait_recv()
        copies[12].start()

    @pl.when(step == last)
    def _():
        for index in (5, 6, 7, 8, 11, 12):
            copies[index].wait_recv()
        own_copy.wait()
        for copy in copies:
            copy.wait_send()

    finish()


def weight_rest_kernel(
    steps, gate_hbm, up_hbm, down_hbm, rows, d_rows, gate_part, up_part, down_part,
    gate_out, up_out, down_out,
    gate, up, down, grad_gate, grad_up, grad_down, hidden_tile, d_gate_tile, d_up_tile, weight_sem, part_sem, out_sem,
):
    grads = (grad_gate, grad_up, grad_down)
    tiles = (hidden_tile, d_gate_tile, d_up_tile)
    arrive, begin_sums, done, finish = weight_moves(
        pl.program_id(0), steps - 1, (gate_hbm, up_hbm, down_hbm), (gate, up, down), (gate_part, up_part, down_part),
        grads, (gate_out, up_out, down_out), weight_sem, part_sem, out_sem,
    )
    other_rows(rows, d_rows, (gate, up, down), tiles, arrive)
    begin_sums()
    add_weight_grads(grads, tiles, rows, d_rows, pl.program_id(0) == steps - 1, done)
    finish()


def weight_grad_calls(
    gate, up, down, own_parts, rows_near, rows_next, d_rows_near, rows_far, far_own, tok=256, far_tok=512
):
    size, width = gate.shape
    low = jnp.bfloat16
    near_steps = d_rows_near.shape[0] // tok
    hbm = pl.BlockSpec(memory_space=pl.ANY)
    dma = pltpu.SemaphoreType.DMA

    def stream(first, steps):
        return pl.BlockSpec((tok, width), lambda s: (jnp.clip(s - first, 0, steps - 1), 0))

    buffers = [pltpu.VMEM((size, width), low)] * 3 + [pltpu.VMEM((size, width), jnp.float32)] * 3
    near_one, near_two = stream(0, near_steps // 2), stream(near_steps // 2, near_steps // 2)
    near = stream(0, near_steps)
    grad = jax.ShapeDtypeStruct((size, width), jnp.float32)
    *parts, far_all = pl.pallas_call(
        functools.partial(weight_part_kernel, near_steps),
        grid=(near_steps,),
        in_specs=[hbm] * 3 + [near_one, near_two, near] + [hbm] * 4,
        out_specs=[hbm] * 4,
        out_shape=[grad] * 3 + [jax.ShapeDtypeStruct((8, *far_own.shape), low)],
        scratch_shapes=buffers
        + [pltpu.VMEM((size, tok), low)] * 3
        + [dma((13,)), dma((13,)), dma, dma((3,)), dma((3,)), dma((3,))],
        compiler_params=pltpu.CompilerParams(
            dimension_semantics=("arbitrary",), vmem_limit_bytes=62 * 2**20, collective_id=5, has_side_effects=True
        ),
        cost_estimate=pl.CostEstimate(
            flops=12 * size * width * d_rows_near.shape[0], bytes_accessed=80 * 2**20, transcendentals=0
        ),
        name="weight_grads_part",
    )(gate, up, down, rows_near, rows_next, d_rows_near, *own_parts, far_own)
    far = pl.BlockSpec((far_tok, width), lambda s: (s, 0))
    return pl.pallas_call(
        functools.partial(weight_rest_kernel, rows_far.shape[0] // far_tok),
        grid=(rows_far.shape[0] // far_tok,),
        in_specs=[hbm] * 3 + [far] * 2 + [hbm] * 3,
        out_specs=[hbm] * 3,
        out_shape=[grad] * 3,
        scratch_shapes=buffers + [pltpu.VMEM((size, far_tok), low)] * 3 + [dma((3,)), dma((3,)), dma((3,))],
        compiler_params=pltpu.CompilerParams(dimension_semantics=("arbitrary",), vmem_limit_bytes=62 * 2**20),
        cost_estimate=pl.CostEstimate(
            flops=12 * size * width * rows_far.shape[0], bytes_accessed=80 * 2**20, transcendentals=0
        ),
        name="weight_grads_rest",
    )(gate, up, down, rows_far, far_all.reshape(-1, width), *parts)


def finish_kernel(
    key_width, wide, small, result_in, d_vectors_in, d_source_in,
    result, d_source, d_vectors, query, key, value, output, down, up, gate, out,
    gain_one, gain_two, gain_three, gain_four, gain_five, gain_six, query_gain, key_gain,
):
    result[...] = result_in[...]
    d_vectors[...] = d_vectors_in[...]
    d_source[...] = d_source_in[...]
    query_width = query.shape[1]
    start = 0
    for target, columns in (
        (query, query_width),
        (key, key_width),
        (value, key_width),
        (down, down.shape[1]),
    ):
        target[...] = wide[:, start : start + columns].astype(jnp.float32)
        start += columns
    start += -start % 128
    output[...] = wide[:, start : start + output.shape[1]].astype(jnp.float32)
    start += output.shape[1]
    gate[...] = wide[:, start : start + gate.shape[1]].astype(jnp.float32)
    lines = small[...].astype(jnp.float32)
    first = out.shape[0]
    out[...] = lines[0:first]
    up[...] = lines[first : first + up.shape[0]]
    first += up.shape[0]
    for index, target in enumerate((gain_one, gain_two, gain_three, gain_four, gain_five, gain_six)):
        target[...] = lines[first + index : first + index + 1, 0 : target.shape[1]]
    me = lax.axis_index("fsdp")
    for index, target in enumerate((query_gain, key_gain)):
        size = target.shape[1]
        line = lines[first + 6 + index : first + 7 + index, 0 : 8 * size]
        total = jnp.zeros((1, size), jnp.float32)
        for device in range(8):
            total = total + jnp.where(me == device, line[:, device * size : (device + 1) * size], 0.0)
        target[...] = total


def finish_call(wide, small, result, d_vectors, d_source, shapes, key_width):
    vmem = pl.BlockSpec(memory_space=pltpu.VMEM)
    kinds = [jnp.bfloat16] + [jnp.float32] * (len(shapes) - 1)
    return pl.pallas_call(
        functools.partial(finish_kernel, key_width),
        out_shape=[jax.ShapeDtypeStruct(shape, kind) for shape, kind in zip(shapes, kinds)],
        in_specs=[vmem] * 5,
        out_specs=[vmem] * len(shapes),
        compiler_params=pltpu.CompilerParams(vmem_limit_bytes=40 * 2**20),
        name="finish",
    )(wide, small, result, d_vectors, d_source)


def per_device(
    tokens,
    per_layer,
    segments,
    positions,
    cotangent,
    query_weight,
    key_matrix,
    value_matrix,
    output_weight,
    laurel_down,
    laurel_up,
    vector_gate,
    vector_out,
    norm_input,
    norm_attention,
    norm_laurel,
    norm_before,
    norm_after,
    norm_vector,
    query_norm_gain,
    norm_key,
    hidden_gate,
    hidden_up,
    hidden_down,
):
    count_of_rows = tokens.shape[0]
    shards = lax.axis_size("fsdp")
    width = tokens.shape[1]
    heads_per_group = QUERY_HEADS // KEY_VALUE_HEADS
    reach_blocks = min((WINDOW + count_of_rows - 2) // count_of_rows, lax.axis_size("ctx") - 1)
    score_scale = HEAD_SIZE ** (-0.5)
    fused = shards == 8 and lax.axis_size("ctx") == 4
    query_width = query_weight.shape[1]
    key_width = key_matrix.shape[1]

    gain_shards = (
        norm_input,
        norm_attention,
        norm_laurel,
        norm_before,
        norm_after,
        norm_vector,
        query_norm_gain,
        norm_key,
    )
    gain_sizes = [gain.shape[0] for gain in gain_shards]
    gain_starts = [sum(gain_sizes[:index]) for index in range(len(gain_sizes))]
    source = tokens.astype(jnp.float32)
    vectors = per_layer.astype(jnp.float32)
    rank = laurel_down.shape[1]
    unused, allowed = window(positions, count_of_rows, reach_blocks)

    def head_facing(linear, gain):
        return rotary_apply(root_mean_norm(linear, gain), positions)

    if fused:
        me = lax.axis_index("fsdp")
        head_gains = jnp.stack([query_norm_gain, norm_key])
        place = jnp.arange(HEAD_SIZE) // head_gains.shape[1] == me
        head_gains = jnp.where(place[None, :], jnp.tile(head_gains, (1, shards)), 0).astype(jnp.bfloat16)
        cosine, sine_part = rotary_tables(positions, HEAD_SIZE)
        (
            normed,
            gains_all,
            linear,
            query_lowered,
            key_value,
            features,
            middle_low,
            attn_lin,
            full_laurel_up,
            full_inward,
            full_output,
        ) = attend_call(
            reach_blocks,
            tokens,
            [gain.reshape(-1, 128) for gain in gain_shards[:6]],
            head_gains,
            laurel_up,
            positions[None, :],
            cosine,
            sine_part,
            (query_weight, key_matrix, value_matrix, laurel_down.T),
            output_weight,
        )
    else:
        gain_line = jnp.concatenate(gain_shards)
        gain_line = jnp.pad(gain_line, (0, -gain_line.shape[0] % 2048)).reshape(-1, 128)
        gains_all = gather(gain_line, "fsdp").reshape(shards, -1)
        gains = [
            gains_all[:, start : start + size].reshape(-1).astype(jnp.float32)
            for start, size in zip(gain_starts, gain_sizes)
        ]
        inward_weight = jnp.concatenate([query_weight, key_matrix, value_matrix, laurel_down], axis=1)
        inward_weight = jnp.pad(inward_weight, ((0, 0), (0, -inward_weight.shape[1] % 128)))
        full_inward = gather(inward_weight, "fsdp")
        full_output, full_vector_gate, full_vector_out, full_laurel_up = [
            gather(value, "fsdp") for value in (output_weight, vector_gate, vector_out, laurel_up)
        ]
        normed = root_mean_norm(source, gains[0])
        lowered_normed = normed.astype(jnp.bfloat16)
        inward = matrix_product(lowered_normed, full_inward)
        linear = inward[:, : query_width + key_width]
        value_lowered = inward[:, query_width + key_width : query_width + 2 * key_width].astype(jnp.bfloat16)
        laurel_mid = inward[:, query_width + 2 * key_width :][:, :rank].astype(jnp.bfloat16)
        query_lowered = head_facing(
            linear[:, :query_width].reshape(count_of_rows, QUERY_HEADS, HEAD_SIZE), gains[6]
        ).astype(jnp.bfloat16)
        key_lowered = head_facing(
            linear[:, query_width:].reshape(count_of_rows, KEY_VALUE_HEADS, HEAD_SIZE), gains[7]
        ).astype(jnp.bfloat16)
        key_value = jnp.stack([key_lowered.reshape(count_of_rows, -1), value_lowered])
        pair_blocks = [key_value]
        for distance in range(1, reach_blocks + 1):
            pair_blocks.append(from_behind(key_value, "ctx", distance))
        window_couple = jnp.concatenate(pair_blocks, axis=1)
        window_keys, window_values = window_couple[0], window_couple[1]
    if fused:
        (
            feed_value,
            mixed,
            laurel_lin,
            rows_all,
            rows_far,
            rows_near,
            slices,
            full_vector_gate,
            full_vector_out,
            hidden_all,
            lift_all,
            bend_all,
        ) = feed_call(
            True,
            (tokens, normed, attn_lin, middle_low, full_laurel_up, gains_all),
            (hidden_gate, hidden_up, hidden_down),
            features=features,
            vectors=(vector_gate, vector_out),
        )
        slices = slices.reshape(shards * count_of_rows, -1)
        rows_far = gather(rows_far.reshape(-1, width), "fsdp")
        (
            d_ffn_in,
            result,
            d_vectors,
            residual_low,
            d_vector_lin_low,
            gated_low,
            d_vector_back_low,
            d_residual,
            gain_rows,
            d_rows_all,
            d_rows_far,
            rows_next,
            *own_parts,
            unused,
            unused,
        ) = feed_call(
            False,
            (feed_value, mixed, gains_all, full_vector_gate, full_vector_out, per_layer, cotangent),
            (hidden_down, hidden_gate, hidden_up),
            (lift_all, bend_all),
            forward_rows=rows_all,
            hidden_rows=hidden_all,
        )
        d_ffn_in, rows_far = lax.optimization_barrier((d_ffn_in, rows_far))
        d_source, grad_wide, grad_small, d_rows_near = attend_back_call(
            reach_blocks, d_ffn_in, mixed, d_residual, laurel_lin, attn_lin, full_laurel_up, gain_rows,
            query_lowered, key_value, linear, gains_all, positions[None, :], cosine, sine_part, middle_low, slices,
            tokens, residual_low, d_vector_lin_low, gated_low, d_vector_back_low, full_output, full_inward, d_rows_all,
        )
        grad_hidden_gate, grad_hidden_up, grad_hidden_down = weight_grad_calls(
            hidden_gate,
            hidden_up,
            hidden_down,
            own_parts,
            rows_near.reshape(-1, width),
            rows_next.reshape(-1, width),
            d_rows_near.reshape(-1, width),
            rows_far,
            d_rows_far,
        )
    else:
        (
            gain_input,
            gain_attention,
            gain_laurel,
            gain_before,
            gain_after,
            gain_vector,
            gain_query,
            key_norm_gain,
        ) = gains
        query_linear = linear[:, :query_width].reshape(count_of_rows, QUERY_HEADS, HEAD_SIZE)
        key_linear = linear[:, query_width:].reshape(count_of_rows, KEY_VALUE_HEADS, HEAD_SIZE)
        query_lowered = query_lowered.reshape(count_of_rows, KEY_VALUE_HEADS, heads_per_group, HEAD_SIZE)
        window_keys = window_keys.reshape(-1, KEY_VALUE_HEADS, HEAD_SIZE)
        window_values = window_values.reshape(-1, KEY_VALUE_HEADS, HEAD_SIZE)

        def masked_scores():
            raw_scores = score_scale * jnp.einsum(
                "tgfd,kgd->gftk", query_lowered, window_keys, preferred_element_type=jnp.float32
            )
            return jnp.where(allowed, raw_scores, -1e30)

        scores_first = masked_scores()
        row_peak = jnp.max(scores_first, axis=-1, keepdims=True)
        exp_scores = jnp.exp(scores_first - row_peak)
        row_total = jnp.sum(exp_scores, axis=-1, keepdims=True)
        log_total = row_peak + jnp.log(row_total)
        soft_low = (exp_scores / row_total).astype(jnp.bfloat16)
        attended_low = (
            jnp.einsum("gftk,kgd->tgfd", soft_low, window_values, preferred_element_type=jnp.float32)
            .reshape(count_of_rows, QUERY_HEADS * HEAD_SIZE)
            .astype(jnp.bfloat16)
        )
        attn_lin = matrix_product(attended_low, full_output)
        residual_one = source + root_mean_norm(attn_lin, gain_attention)
        laurel_lin = matrix_product(laurel_mid, full_laurel_up)
        mixed = (residual_one + normed + root_mean_norm(laurel_lin, gain_laurel)) * inv_root
        ffn_in = root_mean_norm(mixed, gain_before).astype(jnp.bfloat16)
        normed_slices = feature_slices(lowered_normed)
        attended_slices = feature_slices(attended_low)
        rows_all = gather(ffn_in, "fsdp")
        gate_all = product_back(rows_all, hidden_gate)
        up_all = product_back(rows_all, hidden_up)
        hidden_all = gated(gate_all, up_all).astype(jnp.bfloat16)
        feed_value = scatter_sum(matrix_product(hidden_all, hidden_down))
        residual_two = mixed + root_mean_norm(feed_value, gain_after)
        residual_low = residual_two.astype(jnp.bfloat16)
        vector_lin = matrix_product(residual_low, full_vector_gate)
        gated_low = gated(vector_lin, vectors).astype(jnp.bfloat16)
        vector_back = matrix_product(gated_low, full_vector_out)
        result = residual_two + root_mean_norm(vector_back, gain_vector)
        upstream = cotangent.astype(jnp.float32)
        d_vector_back, grad_gain_vector = norm_grad(vector_back, gain_vector, upstream)
        d_vector_back_low = d_vector_back.astype(jnp.bfloat16)
        grad_vector_out = product_rows(gated_low, d_vector_back_low)
        d_gated = product_back(d_vector_back_low, full_vector_out)
        d_vector_lin, d_vectors = gated_grad(vector_lin, vectors, d_gated)
        d_vector_lin_low = d_vector_lin.astype(jnp.bfloat16)
        grad_vector_gate = product_rows(residual_low, d_vector_lin_low)
        d_residual = upstream + product_back(d_vector_lin_low, full_vector_gate)
        d_feed, grad_gain_after = norm_grad(feed_value, gain_after, d_residual)
        d_feed_low = d_feed.astype(jnp.bfloat16)
        d_rows_all = gather(d_feed_low, "fsdp")
        d_hidden = product_back(d_rows_all, hidden_down)
        d_gate_all, d_up_all = gated_grad(gate_all, up_all, d_hidden)
        d_gate_low = d_gate_all.astype(jnp.bfloat16)
        d_up_low = d_up_all.astype(jnp.bfloat16)
        d_ffn_in = scatter_sum(
            matrix_product(d_gate_low, hidden_gate) + matrix_product(d_up_low, hidden_up)
        )

        grad_hidden_gate, grad_hidden_up, grad_hidden_down = [
            lax.psum(grad.astype(jnp.bfloat16), "ctx").astype(jnp.float32)
            for grad in (
                product_rows(d_gate_low, rows_all),
                product_rows(d_up_low, rows_all),
                product_rows(hidden_all, d_rows_all),
            )
        ]

        d_mixed_part, grad_gain_before = norm_grad(mixed, gain_before, d_ffn_in)
        d_half = (d_residual + d_mixed_part) * inv_root
        d_laurel_lin, grad_gain_laurel = norm_grad(laurel_lin, gain_laurel, d_half)
        d_laurel_low = d_laurel_lin.astype(jnp.bfloat16)
        grad_laurel_up = product_rows(laurel_mid, d_laurel_low)
        d_laurel_mid = product_back(d_laurel_low, full_laurel_up).astype(jnp.bfloat16)
        d_attn_lin, grad_gain_attention = norm_grad(attn_lin, gain_attention, d_half)
        d_attn_low = d_attn_lin.astype(jnp.bfloat16)
        d_attended = (
            product_back(d_attn_low, full_output)
            .astype(jnp.bfloat16)
            .reshape(count_of_rows, KEY_VALUE_HEADS, heads_per_group, HEAD_SIZE)
        )
        soft_again = jnp.exp(masked_scores() - log_total)
        d_soft = jnp.einsum(
            "tgfd,kgd->gftk", d_attended, window_values, preferred_element_type=jnp.float32
        )
        d_scores = (
            soft_again * (d_soft - jnp.sum(soft_again * d_soft, axis=-1, keepdims=True))
        ).astype(jnp.bfloat16)
        d_query = score_scale * jnp.einsum(
            "gftk,kgd->tgfd", d_scores, window_keys, preferred_element_type=jnp.float32
        )
        grad_key_rows = score_scale * jnp.einsum(
            "gftk,tgfd->kgd", d_scores, query_lowered, preferred_element_type=jnp.float32
        )
        grad_value_rows = jnp.einsum(
            "gftk,tgfd->kgd",
            soft_again.astype(jnp.bfloat16),
            d_attended,
            preferred_element_type=jnp.float32,
        )
        grad_window_couple = jnp.stack(
            [
                grad_key_rows.reshape(-1, KEY_VALUE_HEADS * HEAD_SIZE),
                grad_value_rows.reshape(-1, KEY_VALUE_HEADS * HEAD_SIZE),
            ]
        )
        grad_own_part = grad_window_couple[:, :count_of_rows]
        for distance in range(1, reach_blocks + 1):
            grad_own_part = grad_own_part + from_behind(
                grad_window_couple[:, distance * count_of_rows : (distance + 1) * count_of_rows].astype(
                    jnp.bfloat16
                ),
                "ctx",
                -distance,
            ).astype(jnp.float32)
        unused, query_pull = jax.vjp(head_facing, query_linear, gain_query)
        d_query_lin, grad_gain_query = query_pull(
            d_query.reshape(count_of_rows, QUERY_HEADS, HEAD_SIZE)
        )
        unused, key_pullback_fn = jax.vjp(head_facing, key_linear, key_norm_gain)
        grad_key_linear, grad_key_norm_gain = key_pullback_fn(
            grad_own_part[0].reshape(count_of_rows, KEY_VALUE_HEADS, HEAD_SIZE)
        )
        d_inward = jnp.concatenate(
            [
                d_query_lin.reshape(count_of_rows, QUERY_HEADS * HEAD_SIZE).astype(jnp.bfloat16),
                grad_key_linear.reshape(count_of_rows, KEY_VALUE_HEADS * HEAD_SIZE).astype(
                    jnp.bfloat16
                ),
                grad_own_part[1].astype(jnp.bfloat16),
                d_laurel_mid,
                jnp.zeros((count_of_rows, full_inward.shape[1] - query_width - 2 * key_width - rank), jnp.bfloat16),
            ],
            axis=1,
        )
        grad_inward = product_rows(normed_slices, gather(d_inward, "fsdp")).astype(jnp.bfloat16)
        grad_output = product_rows(attended_slices, gather(d_attn_low, "fsdp")).astype(jnp.bfloat16)
        grad_wide = jnp.concatenate([grad_inward, grad_output], axis=1)
        small_rows = jnp.concatenate(
            [
                grad_vector_gate.reshape(shards, -1, width),
                grad_vector_out.reshape(shards, -1, width),
                grad_laurel_up.reshape(shards, -1, width),
            ],
            axis=1,
        ).astype(jnp.bfloat16)
        grad_small = lax.psum_scatter(small_rows, "fsdp", scatter_dimension=0, tiled=False)
        d_normed = d_half + product_back(d_inward, full_inward)
        d_source_part, grad_gain_input = norm_grad(source, gain_input, d_normed)
        d_source = d_half + d_source_part
        gain_lines = jnp.concatenate(
            [
                grad.reshape(shards, -1)
                for grad in (
                    grad_gain_input,
                    grad_gain_attention,
                    grad_gain_laurel,
                    grad_gain_before,
                    grad_gain_after,
                    grad_gain_vector,
                    grad_gain_query,
                    grad_key_norm_gain,
                )
            ],
            axis=1,
        )
        gain_share = lax.psum_scatter(gain_lines, "fsdp", scatter_dimension=0, tiled=False)
        gain_count = gain_share.shape[0]
        gain_share = jnp.pad(gain_share, (0, -gain_count % width)).astype(jnp.bfloat16)
        grad_small = jnp.concatenate([grad_small, gain_share.reshape(-1, width)], axis=0)

    grad_wide, grad_small = lax.psum((grad_wide, grad_small), "ctx")
    hidden_grads = (grad_hidden_gate, grad_hidden_up, grad_hidden_down)
    if fused:
        weights = (query_weight, key_matrix, value_matrix, output_weight, laurel_down, laurel_up, vector_gate, vector_out)
        shapes = [tokens.shape, tokens.shape, per_layer.shape] + [weight.shape for weight in weights]
        shapes += [(1, size) for size in gain_sizes]
        finished = finish_call(grad_wide, grad_small, result, d_vectors, d_source, shapes, key_width)
        gains_from = len(shapes) - len(gain_sizes)
        return tuple(finished[:gains_from]) + tuple(gain.reshape(-1) for gain in finished[gains_from:]) + hidden_grads
    grad_wide, grad_small = grad_wide.astype(jnp.float32), grad_small.astype(jnp.float32)
    inward_width = full_inward.shape[1]
    grad_inward = grad_wide[:, :inward_width]
    grad_output = grad_wide[:, inward_width:]
    out_rows, laurel_rows = vector_out.shape[0], laurel_up.shape[0]
    gate_rows = vector_gate.shape[0] * vector_gate.shape[1] // width
    share_vector_gate = grad_small[:gate_rows].reshape(vector_gate.shape)
    share_vector_out = grad_small[gate_rows : gate_rows + out_rows]
    gain_start = gate_rows + out_rows + laurel_rows
    share_laurel_up = grad_small[gate_rows + out_rows : gain_start]
    gain_share = grad_small[gain_start:].reshape(-1)
    gain_grads = tuple(gain_share[start : start + size] for start, size in zip(gain_starts, gain_sizes))
    value_start = query_width + key_width
    return (
        (
            result.astype(jnp.bfloat16),
            d_source,
            d_vectors,
            grad_inward[:, :query_width],
            grad_inward[:, query_width:value_start],
            grad_inward[:, value_start : value_start + key_width],
            grad_output,
            grad_inward[:, value_start + key_width : value_start + key_width + rank],
            share_laurel_up,
            share_vector_gate,
            share_vector_out,
        )
        + gain_grads
        + hidden_grads
    )


def solution(mesh):
    rows = P(("fsdp", "ctx"), None)
    line = P(("fsdp", "ctx"))
    weight = P("fsdp", None)
    gain = P("fsdp")
    return jax.shard_map(
        per_device,
        mesh=mesh,
        in_specs=(rows, rows, line, line, rows) + (weight,) * 8 + (gain,) * 8 + (weight,) * 3,
        out_specs=(rows,) * 3 + (weight,) * 8 + (gain,) * 8 + (weight,) * 3,
        check_vma=False,
    )
```
